32 devices in a mesh: row: 2 (over x), seq: 16 (over z, y, core).
Axes of the slice: x: 2, y: 2, z: 4, core: 2. Of those that a mesh axis runs over, the one named last changes fastest.
Arguments:
- tokens: bfloat16 [2, 2048, 1024], P('row', 'seq'), may hold values from -6 to 6
- attention_gain: bfloat16 [1024], P(('row', 'seq')), may hold values from 0.099609375 to 1.8984375
- expert_gain: bfloat16 [1024], P(('row', 'seq')), may hold values from 0.099609375 to 1.8984375
- query_weight: bfloat16 [1024, 1024], P(('row', 'seq')), may hold values from -0.1875 to 0.1875
- key_matrix: bfloat16 [1024, 512], P(('row', 'seq')), may hold values from -0.1875 to 0.1875
- value_matrix: bfloat16 [1024, 512], P(('row', 'seq')), may hold values from -0.1875 to 0.1875
- output_weight: bfloat16 [1024, 1024], P(('row', 'seq')), may hold values from -6 to 6
- router_weight: bfloat16 [1024, 16], P(('row', 'seq')), may hold values from -0.09375 to 0.09375
- gate_weight: bfloat16 [1024, 16, 512], P(('row', 'seq')), may hold values from -0.1875 to 0.1875
- up_weight: bfloat16 [1024, 16, 512], P(('row', 'seq')), may hold values from -0.1875 to 0.1875
- down_weight: bfloat16 [1024, 16, 512], P(('row', 'seq')), may hold values from -2 to 2
- routes: int32 [2, 2048, 8], P('row', 'seq'), may hold values from 0 to 15, all different within a row; in each aligned block of 128 rows (0 to 127, 128 to 255, ..., all dimensions but the last counted through in order) at most 96 rows name the same one
- segments: int32 [2, 2048], P('row', 'seq'), may hold values from 0 to 2, as said below
- rope_index: int32 [2], P('row'), may hold values from 0 to 3
- cotangent: bfloat16 [2, 2048, 1024], P('row', 'seq'), may hold values from -6 to 6
Outputs:
- mixed: bfloat16 [2, 2048, 1024], P('row', 'seq')
- grad_tokens: float32 [2, 2048, 1024], P('row', 'seq')
- grad_attention_gain: float32 [1024], P(('row', 'seq'))
- grad_expert_gain: float32 [1024], P(('row', 'seq'))
- grad_query_weight: float32 [1024, 1024], P(('row', 'seq'))
- grad_key_weight: float32 [1024, 512], P(('row', 'seq'))
- grad_value_weight: float32 [1024, 512], P(('row', 'seq'))
- grad_output_weight: float32 [1024, 1024], P(('row', 'seq'))
- grad_router_weight: float32 [1024, 16], P(('row', 'seq'))
- grad_gate_weight: float32 [1024, 16, 512], P(('row', 'seq'))
- grad_up_weight: float32 [1024, 16, 512], P(('row', 'seq'))
- grad_down_weight: float32 [1024, 16, 512], P(('row', 'seq'))
The draws below stay inside these ranges and needn't reach their ends.
Inputs may be any that keep to these rules, and one draw needn't show every extreme that they name: `routes`: each token names 8 different experts; in each aligned block of 128 positions of a row no expert is named by more than 96 of its tokens. `segments`: along each row the numbers never fall; number 0 ends within the row's first 128 positions and number 2 begins within its last 128, so that document 1 runs from the row's first device to its last.
All inputs are finite; a program needn't handle non-finite values.
Results may differ from the reference program's by a relative error of at most 0.028.
Values may be sent and summed in bfloat16 or wider, within the bound.
A program may use at most 384 MiB of HBM per device.

```python
import math
import jax
import jax.numpy as jnp
import numpy as np
from jax import lax

MODEL_WIDTH = 1024
QUERY_HEADS = 16
KEY_VALUE_HEADS = 8
HEAD_SIZE = 64
F = 512
E = 16
K = 8
SEQ_TOK = 128
CAP = 96
LEN = 2048
BATCH = 2


def draw_segments(key, part):
    key = jax.random.fold_in(key, 11)
    first_key, last_key = jax.random.split(key)
    first_end = jax.random.randint(first_key, (BATCH, 1), 1, SEQ_TOK)
    last_start = LEN - jax.random.randint(last_key, (BATCH, 1), 1, SEQ_TOK)
    spots = jnp.arange(LEN, dtype=jnp.int32)[None, :]
    return (spots >= first_end).astype(jnp.int32) + (spots >= last_start).astype(jnp.int32)


def block_scale(key, extent, pieces, least, high):
    def one(position, blocks):
        steps = jax.random.uniform(jax.random.fold_in(jax.random.fold_in(key, 6), position), (blocks,), jnp.float32, least / len(pieces), high / len(pieces))
        return jnp.repeat(jnp.exp(steps), extent[position] // blocks).reshape((-1,) + (1,) * (len(extent) - position - 1))

    factor_of = one(*pieces[0])
    for cut in pieces[1:]:
        factor_of = factor_of * one(*cut)
    return factor_of


def assign_block(own_key, own, number, rows, number_of, top, limit, slope):
    sequence = jax.random.permutation(own_key, number_of)
    heavy_load, ordinary = shares(number_of, rows * top, limit, slope, True), shares(number_of, rows * top, limit, slope, False)
    places = jnp.arange(number_of)

    def named(lengths, rotation):
        used = int((lengths > 0).sum())
        fixed = max(1, used // 4)
        passed = fixed + (places - fixed + rotation * (used - fixed)) % max(1, number_of - fixed)
        return jnp.zeros((number_of,), jnp.int32).at[sequence[jnp.where(places < fixed, places, passed)]].set(jnp.asarray(lengths, jnp.int32))

    lengths = jnp.where(number % 4 == 0, named(heavy_load, number // 4), named(ordinary, number - number // 4 - 1))
    mixed = jax.random.permutation(jax.random.fold_in(own, 3), number_of)
    giver, sink = mixed[0:number_of // 2 * 2:2], mixed[1:number_of // 2 * 2:2]
    margin = jnp.minimum(lengths[giver] - 1, limit - lengths[sink]) // 2
    margin = jnp.where((giver == sequence[0]) | (sink == sequence[0]) | (lengths[sink] == 0), 0, jnp.maximum(margin, 0))
    passed = jax.random.randint(jax.random.fold_in(own, 4), (number_of // 2,), 0, 1 << 20) % (margin + 1)
    lengths = lengths.at[giver].add(-passed).at[sink].add(passed)
    members = jnp.searchsorted(jnp.cumsum(lengths), jnp.arange(rows * top), side="right").astype(jnp.int32)
    grid = members.reshape(top, rows).T
    grid = grid[jax.random.permutation(jax.random.fold_in(own, 1), rows)]
    rotation = jax.random.randint(jax.random.fold_in(own, 2), (rows, 1), 0, top)
    return jnp.take_along_axis(grid, (jnp.arange(top)[None, :] + rotation) % top, axis=1)


def shares(count, total, bound, slope, full):
    weights = [(1 << 20) // math.isqrt(standing ** slope) + 1 for standing in range(1, count + 1)]
    largest = bound if full else min(bound, max(-(-total // count), total * weights[0] // sum(weights)))
    least = 1 if total - largest >= count - 1 else 0
    holding, rest = [largest] + [least] * (count - 1), total - largest - least * (count - 1)
    while rest > 0:
        free = [i for i in range(1, count) if holding[i] < largest] or [i for i in range(1, count) if holding[i] < bound]
        mass, budget = sum([weights[i] for i in free]), rest
        for i in free:
            addition = min(bound - holding[i], max(1, budget * weights[i] // mass), rest)
            holding[i] = holding[i] + addition
            rest = rest - addition
    return np.array(holding)


def noise(own_key, shape, spread, reach, cuts=(), held_as=jnp.bfloat16):
    gain = block_scale(own_key, shape, cuts, -0.22, 0.18) if cuts else 1.0
    entries = jax.random.normal(own_key, shape, jnp.float32) * spread * gain
    return jnp.minimum(jnp.maximum(entries, -reach), reach).astype(held_as)


def setup_inputs(seed: int = 0) -> dict:
    splits = jax.random.split(jax.random.key(seed), 16)
    tokens = noise(splits[0], (BATCH, LEN, MODEL_WIDTH), 1.0, 6.0, ((0, 2), (1, 16)))
    attention_gain = jnp.clip(1.0 + 0.18 * jax.random.normal(splits[1], (MODEL_WIDTH,), jnp.float32), 0.099609375, 1.8984375).astype(jnp.bfloat16)
    expert_gain = jnp.clip(1.0 + 0.18 * jax.random.normal(splits[2], (MODEL_WIDTH,), jnp.float32), 0.099609375, 1.8984375).astype(jnp.bfloat16)
    query_weight = noise(splits[3], (MODEL_WIDTH, QUERY_HEADS * HEAD_SIZE), MODEL_WIDTH ** -0.5, 0.1875, ((0, 32),))
    key_matrix = noise(splits[4], (MODEL_WIDTH, KEY_VALUE_HEADS * HEAD_SIZE), MODEL_WIDTH ** -0.5, 0.1875, ((0, 32),))
    value_matrix = noise(splits[5], (MODEL_WIDTH, KEY_VALUE_HEADS * HEAD_SIZE), MODEL_WIDTH ** -0.5, 0.1875, ((0, 32),))
    output_weight = noise(splits[6], (MODEL_WIDTH, QUERY_HEADS * HEAD_SIZE), (max(1, 2 * MODEL_WIDTH // LEN)) ** -0.5, 6.0, ((0, 32),))
    router_weight = noise(splits[7], (MODEL_WIDTH, E), (4 * MODEL_WIDTH) ** -0.5, 0.09375, ((0, 32),))
    gate_weight = noise(splits[8], (MODEL_WIDTH, E, F), MODEL_WIDTH ** -0.5, 0.1875, ((0, 32),))
    up_weight = noise(splits[9], (MODEL_WIDTH, E, F), MODEL_WIDTH ** -0.5, 0.1875, ((0, 32),))
    down_weight = noise(splits[10], (MODEL_WIDTH, E, F), (max(1, F // 64)) ** -0.5, 2.0, ((0, 32),))
    routes_keys = jax.random.split(jax.random.fold_in(splits[11], 1), BATCH * LEN // SEQ_TOK)
    routes_turns = jax.random.permutation(jax.random.fold_in(splits[11], 3), BATCH * LEN // SEQ_TOK)
    routes = jax.vmap(lambda own, number: assign_block(jax.random.fold_in(splits[11], 2), own, number, SEQ_TOK, E, K, CAP, 1))(routes_keys, routes_turns).reshape((BATCH, LEN, K))
    segments = draw_segments(jax.random.fold_in(splits[15], 71), 0)
    rope_index = jax.random.randint(splits[13], (BATCH,), 0, 4).astype(jnp.int32)
    cotangent = noise(splits[14], (BATCH, LEN, MODEL_WIDTH), 1.0, 6.0, ((0, 2), (1, 16)))
    return dict(tokens=tokens, attention_gain=attention_gain, expert_gain=expert_gain, query_weight=query_weight, key_matrix=key_matrix, value_matrix=value_matrix, output_weight=output_weight, router_weight=router_weight, gate_weight=gate_weight, up_weight=up_weight, down_weight=down_weight, routes=routes, segments=segments, rope_index=rope_index, cotangent=cotangent)


@jax.custom_vjp
def reduced_precision(v):
    return lax.optimization_barrier(v.astype(jnp.bfloat16)).astype(jnp.float32)

@jax.custom_vjp
def low_back(v):
    return v

def low_keep(v):
    return (reduced_precision(v), None)

def low_pass(kept, grad):
    return (grad,)

def back_keep(v):
    return (v, None)

def back_low(kept, grad):
    return (reduced_precision(grad),)
reduced_precision.defvjp(low_keep, low_pass)
low_back.defvjp(back_keep, back_low)
EPSILON = 1e-05
ROPE_BASE = 10000.0
MASKED = -1e+30
HIGHEST = lax.Precision.HIGHEST

def rms_scale(values):
    return lax.rsqrt(lax.optimization_barrier(jnp.mean(values * values, axis=-1, keepdims=True)) + EPSILON)

def frequencies(head_dim):
    halves = head_dim // 2
    return jnp.power(ROPE_BASE, -jnp.arange(halves, dtype=jnp.float32) * (2.0 / head_dim))

def apply_rotary(values, cosine_lookup, sine_lookup):
    halves = values.shape[-1] // 2
    first_half = values[..., :halves]
    second_half = values[..., halves:]
    return jnp.concatenate([first_half * cosine_lookup - second_half * sine_lookup, second_half * cosine_lookup + first_half * sine_lookup], axis=-1)

def one_sequence(params, inputs, seg_ids, route_ids, factor):
    attention_gain, expert_gain, query_weight, key_matrix, value_matrix, output_weight, router_weight, gate_weight, up_weight, down_weight = params
    sequence_length = inputs.shape[0]
    queries_per_group = QUERY_HEADS // KEY_VALUE_HEADS
    scaling = 1.0 / math.sqrt(HEAD_SIZE)
    normed_first = inputs * rms_scale(inputs)
    hidden_first = reduced_precision(normed_first * attention_gain)
    query_unrotated = low_back(jnp.dot(hidden_first, query_weight, precision=HIGHEST))
    key_unrotated = low_back(jnp.dot(hidden_first, key_matrix, precision=HIGHEST))
    value_reduced = reduced_precision(low_back(jnp.dot(hidden_first, value_matrix, precision=HIGHEST)))
    positions = jnp.arange(sequence_length, dtype=jnp.float32) / factor
    angles = positions[:, None] * frequencies(HEAD_SIZE)[None, :]
    cosine_lookup = jnp.cos(angles)[:, None, :]
    sine_lookup = jnp.sin(angles)[:, None, :]
    query_turned = reduced_precision(apply_rotary(query_unrotated.reshape(sequence_length, QUERY_HEADS, HEAD_SIZE), cosine_lookup, sine_lookup)).reshape(sequence_length, KEY_VALUE_HEADS, queries_per_group, HEAD_SIZE)
    key_turned = reduced_precision(apply_rotary(key_unrotated.reshape(sequence_length, KEY_VALUE_HEADS, HEAD_SIZE), cosine_lookup, sine_lookup))
    value_head_rows = value_reduced.reshape(sequence_length, KEY_VALUE_HEADS, HEAD_SIZE)
    block_size = math.gcd(sequence_length, 512)
    key_pos = jnp.arange(sequence_length, dtype=jnp.int32)

    def attend_block(first_row):
        query_block = lax.dynamic_slice_in_dim(query_turned, first_row, block_size, 0)
        query_pos = first_row + jnp.arange(block_size, dtype=jnp.int32)
        query_seg = lax.dynamic_slice_in_dim(seg_ids, first_row, block_size, 0)
        allowed = (key_pos[None, :] <= query_pos[:, None]) & (seg_ids[None, :] == query_seg[:, None])
        scores = low_back(jnp.einsum('qkgd,jkd->kgqj', query_block, key_turned, precision=HIGHEST) * scaling)
        probs = reduced_precision(jax.nn.softmax(jnp.where(allowed, scores, MASKED), axis=-1))
        return jnp.einsum('kgqj,jkd->qkgd', probs, value_head_rows, precision=HIGHEST)
    starts = jnp.arange(sequence_length // block_size, dtype=jnp.int32) * block_size
    attn_rows = lax.map(jax.checkpoint(attend_block), starts).reshape(sequence_length, QUERY_HEADS * HEAD_SIZE)
    attn_low = reduced_precision(low_back(attn_rows))
    branch = low_back(jnp.einsum('qc,dc->qd', attn_low, output_weight, precision=HIGHEST))
    residual = inputs + branch
    normed_second = residual * rms_scale(residual)
    hidden_second = reduced_precision(normed_second * expert_gain)
    logits = low_back(jnp.dot(hidden_second, router_weight, precision=HIGHEST))
    router_probs = jax.nn.softmax(logits, axis=-1)
    blocks = sequence_length // SEQ_TOK
    route_blocks = route_ids.reshape(blocks, SEQ_TOK, K)
    picked = route_blocks[..., None] == jnp.arange(E, dtype=jnp.int32)
    picked_int = picked.astype(jnp.int32).reshape(blocks, SEQ_TOK * K, E)
    earlier = jnp.cumsum(picked_int, axis=1, dtype=jnp.int32) - picked_int
    slot_ids = lax.optimization_barrier(jnp.sum(earlier * picked_int, axis=-1, dtype=jnp.int32)).reshape(blocks, SEQ_TOK, K)
    destination = route_blocks * CAP + slot_ids
    chosen = destination[..., None] == jnp.arange(E * CAP, dtype=jnp.int32)
    gate_probs = lax.optimization_barrier(jnp.sum(jnp.where(picked, router_probs.reshape(blocks, SEQ_TOK, 1, E), 0.0), axis=-1))
    dispatch = lax.optimization_barrier(jnp.sum(chosen.astype(jnp.float32), axis=2)).reshape(blocks, SEQ_TOK, E, CAP)
    combine = lax.optimization_barrier(jnp.sum(jnp.where(chosen, gate_probs[..., None], 0.0), axis=2)).reshape(blocks, SEQ_TOK, E, CAP)
    routed = jnp.einsum('btec,btd->ebcd', dispatch, hidden_second.reshape(blocks, SEQ_TOK, MODEL_WIDTH), precision=HIGHEST).reshape(E, blocks * CAP, MODEL_WIDTH)
    gate_pre = low_back(jnp.einsum('erd,def->erf', routed, gate_weight, precision=HIGHEST))
    up_pre = low_back(jnp.einsum('erd,def->erf', routed, up_weight, precision=HIGHEST))
    hidden_low = reduced_precision(jax.nn.silu(gate_pre) * up_pre)
    expert_out = low_back(jnp.einsum('erf,def->erd', hidden_low, down_weight, precision=HIGHEST)).reshape(E, blocks, CAP, MODEL_WIDTH)
    expert_mix = jnp.einsum('btec,ebcd->btd', combine, expert_out, precision=HIGHEST).reshape(sequence_length, MODEL_WIDTH)
    return residual + expert_mix

def reference(tokens, attention_gain, expert_gain, query_weight, key_matrix, value_matrix, output_weight, router_weight, gate_weight, up_weight, down_weight, routes, segments, rope_index, cotangent):
    params = tuple((weight_item.astype(jnp.float32) for weight_item in (attention_gain, expert_gain, query_weight, key_matrix, value_matrix, output_weight, router_weight, gate_weight, up_weight, down_weight)))
    inputs = tokens.astype(jnp.float32)
    factors = jnp.power(2.0, rope_index.astype(jnp.float32))
    checked = jax.checkpoint(one_sequence)

    def forward(layer_inputs, layer_params):

        def advance(carried, items):
            return (carried, checked(layer_params, items[0], items[1], items[2], items[3]))
        return lax.scan(advance, jnp.zeros((), jnp.float32), (layer_inputs, segments, routes, factors))[1]
    outputs, pull_back = jax.vjp(forward, inputs, params)
    grad_inputs, grads = pull_back(cotangent.astype(jnp.float32))
    return (outputs.astype(jnp.bfloat16), grad_inputs, grads[0], grads[1], grads[2], grads[3], grads[4], grads[5], grads[6], grads[7], grads[8], grads[9])
```

```python
from functools import partial
import math

import jax
import jax.numpy as jnp
from jax import lax
from jax.experimental import pallas as pl
from jax.experimental.pallas import tpu as pltpu
from jax.sharding import PartitionSpec as P

MODEL_WIDTH = 1024
QUERY_HEADS = 16
KEY_VALUE_HEADS = 8
HEAD_SIZE = 64
F = 512
E = 16
K = 8
CAP = 96

EPSILON = 1e-05
ROPE_BASE = 10000.0
MASKED = -1e30
MESH = pl.DeviceIdType.MESH
VM = pltpu.VMEM
BF = jnp.bfloat16
F32 = jnp.float32
DMA = pltpu.SemaphoreType.DMA
UP, DOWN, SIDE, CORE = range(4)
VMEM_LIMIT = 60 * 1024 * 1024

NN = (((1,), (0,)), ((), ()))
NT = (((1,), (1,)), ((), ()))
TN = (((0,), (0,)), ((), ()))


def dot(a, b, dims=NN):
    return lax.dot_general(a, b, dims, preferred_element_type=F32)


def when(cond, f):
    if cond is None:
        f()
    else:
        pl.when(cond)(f)


def both(a, b):
    if a is None:
        return b
    return a if b is None else a & b


def place():
    x = lax.axis_index("row")
    s = lax.axis_index("seq")
    return x, s, s // 4, (s // 2) % 2, s % 2


def seat(z, y, c):
    return z * 4 + y * 2 + c


def remote(src, dst, send, recv, dev):
    return pltpu.make_async_remote_copy(src, dst, send, recv, device_id=dev, device_id_type=MESH)


def barrier_all():
    x, s = lax.axis_index("row"), lax.axis_index("seq")
    sem = pltpu.get_barrier_semaphore()
    for k in range(1, 16):
        pl.semaphore_signal(sem, inc=1, device_id=(x, (s + k) % 16), device_id_type=MESH)
    for k in range(16):
        pl.semaphore_signal(sem, inc=1, device_id=(1 - x, (s + k) % 16), device_id_type=MESH)
    pl.semaphore_wait(sem, 31)


def barrier_row(partner=False):
    x, s = lax.axis_index("row"), lax.axis_index("seq")
    sem = pltpu.get_barrier_semaphore()
    for k in range(1, 16):
        pl.semaphore_signal(sem, inc=1, device_id=(x, (s + k) % 16), device_id_type=MESH)
    if partner:
        pl.semaphore_signal(sem, inc=1, device_id=(1 - x, s), device_id_type=MESH)
    pl.semaphore_wait(sem, 16 if partner else 15)


def barrier_near():
    x, s, z, y, c = place()
    sem = pltpu.get_barrier_semaphore()
    for cond, dev in (
        (z < 3, (x, seat(z + 1, y, c))),
        (z > 0, (x, seat(z - 1, y, c))),
        (None, (x, seat(z, 1 - y, c))),
        (None, (x, seat(z, y, 1 - c))),
    ):
        when(cond, lambda dev=dev: pl.semaphore_signal(sem, inc=1, device_id=dev, device_id_type=MESH))
    pl.semaphore_wait(sem, 2 + (z < 3).astype(jnp.int32) + (z > 0).astype(jnp.int32))


class Gather:
    def __init__(self, own, at, send, recv):
        self.own, self.at, self.send, self.recv = own, at, send, recv
        self.sent = []
        self.x, self.s, self.z, self.y, self.c = place()

    def device(self, k):
        x, z, y, c = self.x, self.z, self.y, self.c
        return {
            UP: (x, seat(z + 1, y, c)),
            DOWN: (x, seat(z - 1, y, c)),
            SIDE: (x, seat(z, 1 - y, c)),
            CORE: (x, seat(z, y, 1 - c)),
        }[k]

    def copy(self, src, h, k, own):
        ref = self.own(h) if own else self.at(src, h)
        return remote(ref, self.at(src, h), self.send.at[src, h, k], self.recv.at[src, h], self.device(k))

    def go(self, src, h, k, cond=None, own=False):
        if k == UP:
            cond = both(cond, self.z < 3)
        if k == DOWN:
            cond = both(cond, self.z > 0)
        when(cond, lambda: self.copy(src, h, k, own).start())
        self.sent.append((cond, src, h, k, own))

    def wait(self, src, h, cond=None):
        when(cond, lambda: self.copy(src, h, SIDE, False).wait_recv())

    def begin(self):
        own = self.own is not None
        for h, k in ((0, UP), (0, DOWN), (1, SIDE), (0, SIDE), (1, UP), (1, DOWN), (0, CORE), (1, CORE)):
            self.go(self.s, h, k, own=own)

    def near(self):
        src = seat(self.z, 1 - self.y, self.c)
        self.wait(src, 1)
        for k in (UP, DOWN, CORE):
            self.go(src, 1, k)
        self.wait(src, 0)
        self.go(src, 0, CORE)

    def step(self, t):
        z, y, c = self.z, self.y, self.c
        for cond, zz, k in ((z - t >= 0, z - t, UP), (z + t <= 3, z + t, DOWN)):
            mine, other = seat(zz, y, c), seat(zz, 1 - y, c)
            self.wait(mine, 0, cond)
            for way in (k, SIDE, CORE):
                self.go(mine, 0, way, cond)
            self.wait(mine, 1, cond)
            for way in (k, CORE):
                self.go(mine, 1, way, cond)
            self.wait(other, 1, cond)
            for way in (k, CORE):
                self.go(other, 1, way, cond)

    def step_side(self, t):
        z, y, c = self.z, self.y, self.c
        for cond, zz in ((z - t >= 0, z - t), (z + t <= 3, z + t)):
            other = seat(zz, 1 - y, c)
            self.wait(other, 0, cond)
            self.go(other, 0, CORE, cond)

    def end_core(self):
        for zz in range(4):
            for yy in range(2):
                for h in range(2):
                    self.wait(seat(zz, yy, 1 - self.c), h)

    def end_sends(self):
        for cond, src, h, k, own in self.sent:
            when(cond, lambda: self.copy(src, h, k, own).wait_send())


GATHER_SEMS = [DMA((16, 2, 4)), DMA((16, 2))]


def run_gathers(gathers):
    for g in gathers:
        g.begin()
    for g in gathers:
        g.near()
    for t in (1, 2, 3):
        for g in gathers:
            g.step(t)
    for t in (1, 2, 3):
        for g in gathers:
            g.step_side(t)
    for g in gathers:
        g.end_core()
    for g in gathers:
        g.end_sends()


class Exchange:
    def __init__(self, src, dst, send, recv, wide=False):
        x, s = lax.axis_index("row"), lax.axis_index("seq")
        self.me = x * 16 + s if wide else s
        self.n = 32 if wide else 16
        self.device = (lambda r: (r // 16, r % 16)) if wide else (lambda r: (x, r))
        self.src, self.dst, self.send, self.recv = src, dst, send, recv

    def copy(self, k):
        to = (self.me + k) % self.n
        return remote(self.src(to), self.dst(self.me), self.send.at[k], self.recv.at[k], self.device(to))

    def begin(self):
        self.local = pltpu.make_async_copy(self.src(self.me), self.dst(self.me), self.recv.at[0])
        self.local.start()
        for k in range(1, self.n):
            self.copy(k).start()

    def arrive(self, k):
        frm = (self.me + self.n - k) % self.n
        remote(self.src(self.me), self.dst(frm), self.send.at[k], self.recv.at[k], self.device(frm)).wait_recv()
        return frm

    def end(self, arrivals=True):
        self.local.wait()
        for k in range(1, self.n):
            if arrivals:
                self.arrive(k)
            self.copy(k).wait_send()


def comm_call(body, outs, ins, sems, cid, scratch=()):
    return pl.pallas_call(
        body,
        out_shape=outs,
        in_specs=[pl.BlockSpec(memory_space=VM)] * len(ins),
        out_specs=[pl.BlockSpec(memory_space=VM)] * len(outs),
        scratch_shapes=list(scratch) + list(sems),
        compiler_params=pltpu.CompilerParams(
            collective_id=cid, has_side_effects=True, vmem_limit_bytes=VMEM_LIMIT
        ),
    )(*ins)


def compute_call(body, outs, ins, scratch=()):
    return pl.pallas_call(
        body,
        out_shape=outs,
        in_specs=[pl.BlockSpec(memory_space=VM)] * len(ins),
        out_specs=[pl.BlockSpec(memory_space=VM)] * len(outs),
        scratch_shapes=list(scratch),
        compiler_params=pltpu.CompilerParams(vmem_limit_bytes=VMEM_LIMIT),
    )(*ins)


def sds(shape, dtype):
    return jax.ShapeDtypeStruct(shape, dtype)


def gather_first(tok, wperm, small, wo, tok_all, w_mine, small_all, wo_all, *sems):
    x, s, z, y, c = place()
    t_send, t_recv, o_send, o_recv, w_send, w_recv, s_send, s_recv, x_sem = sems
    barrier_all()
    over = remote(wo, wo_all.at[x, s], x_sem.at[0], x_sem.at[1], (1 - x, s))
    over.start()
    tokens = Gather(lambda h: tok.at[h], lambda src, h: tok_all.at[src, h], t_send, t_recv)
    tokens.begin()
    keep_tok = pltpu.make_async_copy(tok, tok_all.at[s], x_sem.at[2])
    keep_tok.start()
    keep = pltpu.make_async_copy(wo, wo_all.at[x, s], x_sem.at[3])
    keep.start()
    minor = Exchange(lambda r: small, lambda r: small_all.at[r], s_send, s_recv, wide=True)
    minor.begin()
    slices = Exchange(
        lambda r: wperm.at[:, pl.ds(pl.multiple_of(((r % 16) // 2) * 256, 256), 256)],
        lambda r: w_mine.at[r],
        w_send,
        w_recv,
        wide=True,
    )
    slices.begin()
    keep.wait()
    remote(wo, wo_all.at[1 - x, s], x_sem.at[0], x_sem.at[1], (1 - x, s)).wait_recv()
    outw = Gather(None, lambda src, h: wo_all.at[h, src], o_send, o_recv)
    outw.begin()
    tokens.near()
    outw.near()
    for t in (1, 2, 3):
        tokens.step(t)
        outw.step(t)
    for t in (1, 2, 3):
        tokens.step_side(t)
        outw.step_side(t)
    tokens.end_core()
    outw.end_core()
    minor.end()
    slices.end()
    tokens.end_sends()
    outw.end_sends()
    keep_tok.wait()
    over.wait_send()


QB = 256


def allowed_mask(first_key, first_query, start_row):
    key = first_key + lax.broadcasted_iota(jnp.int32, (QB, QB), 0)
    query = first_query + lax.broadcasted_iota(jnp.int32, (QB, QB), 1)
    return (key <= query) & (key >= start_row)


def lane_block(i, size=QB):
    return pl.ds(pl.multiple_of(i * size, size), size)


SCORE = math.log2(math.e) / math.sqrt(HEAD_SIZE)


def attention_forward(
    tok, w_mine, small, cos, sin, start, hid, q_t, k_t, v_t, o_t, lse, o_low, k_n, gain, w_t
):
    core = lax.axis_index("seq") % 2
    gain[...] = jnp.transpose(small[...].astype(F32))
    w_t[...] = jnp.transpose(w_mine[...].astype(F32)).astype(BF)

    def project(i, _):
        rows = lane_block(i, 512)
        values = tok[rows, :].astype(F32)
        scale = lax.rsqrt(jnp.mean(values * values, axis=-1, keepdims=True) + EPSILON)
        hidden = (values * scale * gain[E : E + 1, :]).astype(BF)
        hid[rows, :] = hidden
        made = dot(w_t[...], hidden, NT)
        co, si = cos[:, rows], sin[:, rows]
        own = jnp.where(core == 0, made[0:64], made[128:192])
        for ref, part in ((q_t, own), (k_t, made[64:128])):
            a, b = part[:32], part[32:]
            ref[0:32, rows] = (a * co - b * si).astype(BF)
            ref[32:64, rows] = (b * co + a * si).astype(BF)
        v_t[:, rows] = made[192:256].astype(BF)
        k_n[rows, :] = jnp.transpose(k_t[:, rows].astype(F32)).astype(BF)
        return 0

    lax.fori_loop(0, 4, project, 0)

    def query_block(i, _):
        cols = lane_block(i)
        queries = q_t[:, cols]
        begin = start[:, cols]

        def key_block(j, carried):
            top, total, acc = carried
            rows = lane_block(j)
            scores = dot(k_n[rows, :], queries) * SCORE
            scores = jnp.where(allowed_mask(j * QB, i * QB, begin), scores, MASKED)
            fresh = jnp.maximum(top, jnp.max(scores, axis=0, keepdims=True))
            weights = jnp.exp2(scores - fresh)
            decay = jnp.exp2(top - fresh)
            total = total * decay + jnp.sum(weights, axis=0, keepdims=True)
            acc = acc * decay + dot(v_t[:, rows], weights.astype(BF))
            return fresh, total, acc

        top, total, acc = lax.fori_loop(
            0,
            i + 1,
            key_block,
            (jnp.full((1, QB), MASKED, F32), jnp.zeros((1, QB), F32), jnp.zeros((HEAD_SIZE, QB), F32)),
        )
        out = acc / total
        o_t[:, cols] = out
        o_low[:, cols] = out.astype(BF)
        lse[:, cols] = top + jnp.log2(total)
        return 0

    lax.fori_loop(0, tok.shape[0] // QB, query_block, 0)


def heads_to_tokens(o_low, w3, att_t, wexp, *sems):
    a_send, a_recv, w_send, w_recv, x_send, x_recv = sems
    x, s, z, y, c = place()
    barrier_row(partner=True)
    heads = Exchange(lambda t: o_low.at[:, lane_block(t, 128)], lambda h: att_t.at[h], a_send, a_recv)
    heads.begin()
    weights = Exchange(lambda e: w3.at[e], lambda r: wexp.at[:, x * 16 + r], w_send, w_recv)
    weights.begin()
    over = []

    def cross(k, src, row):
        copy = remote(src, wexp.at[:, x * 16 + row], x_send.at[k], x_recv.at[k], (1 - x, s))
        copy.start()
        over.append(copy)

    cross(0, w3.at[s], s)
    for k in range(1, 16):
        frm = weights.arrive(k)
        cross(k, wexp.at[:, x * 16 + frm], frm)
    heads.end()
    weights.end(arrivals=False)
    for k, copy in enumerate(over):
        copy.wait_send()
        frm = (s + 16 - k) % 16
        remote(
            wexp.at[:, 0], wexp.at[:, (1 - x) * 16 + frm], x_send.at[k], x_recv.at[k], (1 - x, s)
        ).wait_recv()


def between(tok, att_t, wo, small, routes, residual, normed, scale_out, h2, att, probs, picked, p_t):
    gain = jnp.transpose(small[...].astype(F32))[E + 1 : E + 2, :]
    att[...] = jnp.transpose(att_t[...].astype(F32)).astype(BF)
    res = tok[...].astype(F32) + dot(att[...], wo[...], NT)
    residual[...] = res
    scale = lax.rsqrt(jnp.mean(res * res, axis=-1, keepdims=True) + EPSILON)
    norm = res * scale
    normed[...] = norm
    scale_out[...] = jnp.broadcast_to(scale, scale_out.shape)
    hidden = (norm * gain).astype(BF)
    h2[...] = hidden
    lanes = lax.broadcasted_iota(jnp.int32, (128, 128), 1)
    logits = jnp.where(lanes < E, dot(hidden, small[...]), MASKED)
    top = jnp.max(logits, axis=-1, keepdims=True)
    weights = jnp.exp(logits - top)
    prob = weights / jnp.sum(weights, axis=-1, keepdims=True)
    probs[...] = prob
    mask = jnp.zeros((128, 128), F32)
    for k in range(K):
        mask = mask + jnp.where(lanes == routes[:, k : k + 1], 1.0, 0.0)
    picked[...] = mask
    p_t[...] = jnp.transpose(prob * mask)[0:E, :]


def gather_second(h2, p_t, h_all, p_all, *sems):
    h_send, h_recv, p_send, p_recv, keep_sem = sems
    x, s, z, y, c = place()
    barrier_row()
    hidden = Gather(lambda h: h2.at[h], lambda src, h: h_all.at[src, h], h_send, h_recv)
    hidden.begin()
    keep = pltpu.make_async_copy(h2, h_all.at[s], keep_sem.at[0])
    keep.start()
    minor = Exchange(lambda r: p_t, lambda r: p_all.at[r], p_send, p_recv)
    minor.begin()
    hidden.near()
    for t in (1, 2, 3):
        hidden.step(t)
    for t in (1, 2, 3):
        hidden.step_side(t)
    hidden.end_core()
    hidden.end_sends()
    minor.end()
    keep.wait()


TB = 512


def expert_body(h_all, cot, p_all, wexp, mixp, backp, gg, dw, acc):
    e = lax.axis_index("seq")
    acc[...] = jnp.zeros(acc.shape, F32)

    def chunk(i, _):
        rows = lane_block(i, TB)
        hidden, grad = h_all[rows, :], cot[rows, :]
        cols = [jnp.broadcast_to(p_all[i * 4 + b, pl.ds(e, 1), :], (128, 128)) for b in range(4)]
        prob = jnp.concatenate([jnp.transpose(v)[:, 0:1] for v in cols], axis=0)
        gate = dot(hidden, wexp[0])
        up = dot(hidden, wexp[1])
        sig = 1.0 / (1.0 + jnp.exp(-gate))
        silu = gate * sig
        act = silu * up
        low = act.astype(BF)
        out = dot(low, wexp[2], NT)
        mixp[rows, :] = (prob * out).astype(BF)
        back = dot(grad, wexp[2])
        seen = jnp.sum(low.astype(F32) * back, axis=-1, keepdims=True)
        for b in range(4):
            line = jnp.transpose(jnp.broadcast_to(seen[b * 128 : b * 128 + 128], (128, 128)))[0:8]
            gg[i * 4 + b] = line
        grad_hidden = back * prob
        grad_gate = (grad_hidden * up * (sig * (1.0 + gate * (1.0 - sig)))).astype(BF)
        grad_up = (grad_hidden * silu).astype(BF)
        backp[rows, :] = (dot(grad_gate, wexp[0], NT) + dot(grad_up, wexp[1], NT)).astype(BF)
        acc[0] += dot(hidden, grad_gate, TN)
        acc[1] += dot(hidden, grad_up, TN)
        acc[2] += dot(grad, (prob * low.astype(F32)).astype(BF), TN)
        return 0

    lax.fori_loop(0, h_all.shape[0] // TB, chunk, 0)
    dw[...] = acc[...].astype(BF)


class Reduce:
    def __init__(self, part, out, bufs, sems):
        self.part, self.out = part, out
        self.r1, self.ra, self.ua, self.da, self.ub, self.db, self.rb = bufs
        (self.s1, self.q1, self.sa, self.qa, self.su, self.qu, self.sd, self.qd, self.sb) = sems
        self.x, self.s, self.z, self.y, self.c = place()
        self.pending = []

    @staticmethod
    def bufs(rows, width):
        b = (rows, width)
        return [
            VM((4, 2, 2) + b, BF),
            VM((4,) + b, BF),
            VM((4,) + b, BF),
            VM((4,) + b, BF),
            VM((2, 4) + b, BF),
            VM((2, 4) + b, BF),
            VM(b, BF),
        ]

    SEMS = [DMA((4, 2)), DMA((4, 2)), DMA((4,)), DMA((4,)), DMA((3, 4)), DMA((3, 4)), DMA((3, 4)), DMA((3, 4)), DMA((2,))]

    def add(self, dst, src):
        dst[...] = (dst[...].astype(F32) + src[...].astype(F32)).astype(BF)

    def first(self, zz, yy):
        return remote(
            self.part.at[seat(zz, yy, 1 - self.c)],
            self.r1.at[zz, yy],
            self.s1.at[zz, yy],
            self.q1.at[zz, yy],
            (self.x, seat(self.z, self.y, 1 - self.c)),
        )

    def side(self, zz):
        return remote(
            self.r1.at[zz, 1 - self.y, 0],
            self.ra.at[zz],
            self.sa.at[zz],
            self.qa.at[zz],
            (self.x, seat(self.z, 1 - self.y, self.c)),
        )

    def line(self, lane, zz, up):
        z, y, c = self.z, self.y, self.c
        src = self.ra.at[zz] if lane == 0 else self.r1.at[zz, lane - 1, 1]
        if up:
            dst = self.ua.at[zz] if lane == 0 else self.ub.at[lane - 1, zz]
            return remote(src, dst, self.su.at[lane, zz], self.qu.at[lane, zz], (self.x, seat(z + 1, y, c)))
        dst = self.da.at[zz] if lane == 0 else self.db.at[lane - 1, zz]
        return remote(src, dst, self.sd.at[lane, zz], self.qd.at[lane, zz], (self.x, seat(z - 1, y, c)))

    def landed(self, lane, zz, up):
        if lane == 0:
            return (self.ua if up else self.da).at[zz]
        return (self.ub if up else self.db).at[lane - 1, zz]

    def held(self, lane, zz):
        return self.ra.at[zz] if lane == 0 else self.r1.at[zz, lane - 1, 1]

    def order(self):
        z = self.z
        for t in (3, 2, 1):
            yield z + t <= 3, z + t, True
            yield z - t >= 0, z - t, False
        yield None, z, None

    def begin(self):
        for cond, zz, _ in self.order():
            for yy in range(2):
                when(cond, lambda: self.first(zz, yy).start())

    def pass_on(self, lane, zz, up, cond):
        def go():
            def add():
                self.line(lane, zz, up).wait_recv()
                self.add(self.held(lane, zz), self.landed(lane, zz, up))

            pl.when(self.z > 0 if up else self.z < 3)(add)
            self.line(lane, zz, up).start()

        when(cond, go)

    def core_step(self, cond, zz):
        def go():
            for yy in range(2):
                self.first(zz, yy).wait_recv()
                mine = self.part.at[seat(zz, yy, self.c)]
                self.add(self.r1.at[zz, yy], mine)
            self.side(zz).start()

        when(cond, go)

    def run(self):
        order = list(self.order())
        for cond, zz, up in order:
            self.core_step(cond, zz)
            if up is not None:
                for lane in (1, 2):
                    at_end = (self.z == 0) if up else (self.z == 3)
                    when(both(cond, at_end), lambda: self.line(lane, zz, up).start())
        for cond, zz, up in order:

            def ready():
                self.side(zz).wait_recv()
                self.add(self.ra.at[zz], self.r1.at[zz, self.y, 0])

            when(cond, ready)
            if up is None:
                continue
            inner = (self.z > 0) if up else (self.z < 3)
            for lane in (1, 2):
                self.pass_on(lane, zz, up, both(cond, inner))
            self.pass_on(0, zz, up, cond)
        z = self.z
        for lane in (1, 2, 0):
            for up, cond in ((True, z > 0), (False, z < 3)):

                def take():
                    self.line(lane, z, up).wait_recv()
                    self.add(self.held(lane, z), self.landed(lane, z, up))

                when(cond, take)
            if lane == 2:
                self.last().start()
        self.out[0] = self.ra[z]
        self.last().wait_recv()
        self.out[1] = (self.r1[z, self.y, 1].astype(F32) + self.rb[...].astype(F32)).astype(BF)

    def last(self):
        return remote(
            self.r1.at[self.z, 1 - self.y, 1],
            self.rb,
            self.sb.at[0],
            self.sb.at[1],
            (self.x, seat(self.z, 1 - self.y, self.c)),
        )

    def end(self):
        for cond, zz, up in self.order():
            for yy in range(2):
                when(cond, lambda: self.first(zz, yy).wait_send())
            when(cond, lambda: self.side(zz).wait_send())
            if up is not None:
                for lane in range(3):
                    when(cond, lambda: self.line(lane, zz, up).wait_send())
        self.last().wait_send()


NBUF = 7
NSEM = 9


def reduce_rows(backp, mixp, gg, back, mix, g_all, *rest):
    bufs_a, bufs_b = rest[:NBUF], rest[NBUF : 2 * NBUF]
    sems = rest[2 * NBUF :]
    barrier_row()
    one = Reduce(backp, back, bufs_a, sems[:NSEM])
    two = Reduce(mixp, mix, bufs_b, sems[NSEM : 2 * NSEM])
    g_send, g_recv = sems[2 * NSEM :]
    one.begin()
    minor = Exchange(lambda r: gg.at[r], lambda r: g_all.at[r], g_send, g_recv)
    minor.begin()
    one.run()
    two.begin()
    two.run()
    one.end()
    two.end()
    minor.end()


def back_between(
    back, g_all, cot, probs, picked, normed, scale, small, wo, att, h2, g_res, ga_t, dwo
):
    gain = jnp.transpose(small[...].astype(F32))[E + 1 : E + 2, :]
    seen = jnp.concatenate([g_all[e, 0:1, :] for e in range(E)] + [jnp.zeros((128 - E, 128), F32)], axis=0)
    grad_probs = jnp.transpose(seen) * picked[...]
    prob = probs[...]
    grad_logits = (prob * (grad_probs - jnp.sum(prob * grad_probs, axis=-1, keepdims=True))).astype(BF)
    grad_second = back[...].astype(F32) + dot(grad_logits, small[...], NT)
    u = grad_second * gain
    norm = normed[...]
    grad = cot[...].astype(F32) + scale[:, 0:1] * (u - norm * jnp.mean(u * norm, axis=-1, keepdims=True))
    g_res[...] = grad
    branch = grad.astype(BF)
    ga_t[...] = jnp.transpose(dot(branch, wo[...])).astype(BF)
    dwo[:, 0:1024] = dot(jnp.transpose(grad).astype(BF), att[...]).astype(BF)
    dwo[:, 1024:1152] = dot(h2[...], grad_logits, TN).astype(BF)


def grads_out(ga_t, dw, dwo, go_t, dw_all, dwo_sum, *rest):
    bufs = rest[:NBUF]
    dwx, dwo_x = rest[NBUF : NBUF + 2]
    sems = rest[NBUF + 2 :]
    a_send, a_recv, w_send, w_recv, x_sem = sems[NSEM:]
    x, s, z, y, c = place()
    barrier_row(partner=True)
    heads = Exchange(lambda h: ga_t.at[h], lambda t: go_t.at[:, lane_block(t, 128)], a_send, a_recv)
    heads.begin()
    over = remote(dw.at[:, 1 - x], dwx, x_sem.at[0], x_sem.at[1], (1 - x, s))
    over.start()
    over_o = remote(dwo.at[1 - x], dwo_x, x_sem.at[2], x_sem.at[3], (1 - x, s))
    over_o.start()
    over_o.wait_recv()
    dwo_x[...] = (dwo_x[...].astype(F32) + dwo[x].astype(F32)).astype(BF)
    out = Reduce(dwo_x, dwo_sum, bufs, sems[:NSEM])
    out.begin()
    out.run()
    over.wait_recv()
    dwx[...] = (dwx[...].astype(F32) + dw[:, x].astype(F32)).astype(BF)
    weights = Exchange(lambda r: dwx.at[:, r], lambda e: dw_all.at[e], w_send, w_recv)
    weights.begin()
    weights.end()
    heads.end()
    out.end()
    over.wait_send()
    over_o.wait_send()


def attention_backward(q_t, k_t, v_t, lse, o_t, go_t, start, gq_t, gkv_t, k_n, v_n, delta):
    k_n[...] = jnp.transpose(k_t[...].astype(F32)).astype(BF)
    v_n[...] = jnp.transpose(v_t[...].astype(F32)).astype(BF)
    gkv_t[...] = jnp.zeros(gkv_t.shape, F32)
    delta[...] = jnp.sum(go_t[...].astype(F32) * o_t[...], axis=0, keepdims=True)

    def query_block(i, _):
        cols = lane_block(i)
        queries, grads = q_t[:, cols], go_t[:, cols]
        begin, log_total, shift = start[:, cols], lse[:, cols], delta[:, cols]

        def key_block(j, acc):
            rows = lane_block(j)
            scores = dot(k_n[rows, :], queries) * SCORE
            weights = jnp.where(
                allowed_mask(j * QB, i * QB, begin), jnp.exp2(scores - log_total), 0.0
            )
            moved = dot(v_n[rows, :], grads)
            grad_scores = (weights * (moved - shift)).astype(BF)
            gkv_t[0:64, rows] += dot(queries, grad_scores, NT)
            gkv_t[64:128, rows] += dot(grads, weights.astype(BF), NT)
            return acc + dot(k_t[:, rows], grad_scores)

        gq_t[:, cols] = lax.fori_loop(0, i + 1, key_block, jnp.zeros((HEAD_SIZE, QB), F32))
        return 0

    lax.fori_loop(0, q_t.shape[1] // QB, query_block, 0)


def share_pair(gkv, got, send, recv):
    x, s, z, y, c = place()
    sem = pltpu.get_barrier_semaphore()
    mate = (x, seat(z, y, 1 - c))
    pl.semaphore_signal(sem, inc=1, device_id=mate, device_id_type=MESH)
    pl.semaphore_wait(sem, 1)
    copy = remote(gkv.at[1 - c], got, send, recv, mate)
    copy.start()
    copy.wait()


def back_projection(gq_t, gkv, got, hid, cos, sin, g_t, wg):
    core = lax.axis_index("seq") % 2
    scaling = 1.0 / math.sqrt(HEAD_SIZE)
    co, si = cos[...], sin[...]

    def unturn(part):
        a, b = part[:32], part[32:]
        return jnp.concatenate([a * co + b * si, b * co - a * si], axis=0)

    g_t[0:64, :] = unturn(gq_t[...] * scaling).astype(BF)
    mine = gkv[core] + got[...]
    g_t[64:128, :] = jnp.where(core == 0, unturn(mine * scaling), mine).astype(BF)
    wg[...] = jnp.transpose(dot(g_t[...], hid[...])).astype(BF)


def last_exchange(g_t, wg, g_mine, wg_all, *sems):
    a_send, a_recv, w_send, w_recv = sems
    barrier_all()
    heads = Exchange(lambda t: g_t.at[:, lane_block(t, 128)], lambda h: g_mine.at[h], a_send, a_recv)
    heads.begin()
    weights = Exchange(lambda r: wg.at[r], lambda r: wg_all.at[r], w_send, w_recv, wide=True)
    weights.begin()
    heads.end()
    weights.end()


def last_rows(g_mine, wp, tok, small, g_res, grad_tokens):
    gain = jnp.transpose(small[...].astype(F32))[E : E + 1, :]
    first = jnp.transpose(dot(wp[...], g_mine[...]))
    values = tok[...].astype(F32)
    scale = lax.rsqrt(jnp.mean(values * values, axis=-1, keepdims=True) + EPSILON)
    norm = values * scale
    w = first * gain
    grad_tokens[...] = g_res[...] + scale * (w - norm * jnp.mean(w * norm, axis=-1, keepdims=True))


def frequencies(head_dim):
    halves = head_dim // 2
    return jnp.power(ROPE_BASE, -jnp.arange(halves, dtype=F32) * (2.0 / head_dim))


def sixteen_seats(
    tokens,
    attention_gain,
    expert_gain,
    query_weight,
    key_matrix,
    value_matrix,
    output_weight,
    router_weight,
    gate_weight,
    up_weight,
    down_weight,
    routes,
    segments,
    rope_index,
    cotangent,
):
    D = MODEL_WIDTH
    rows = tokens.shape[1]
    length = 16 * rows
    pair = jnp.stack([key_matrix.reshape(32, 8, 64), value_matrix.reshape(32, 8, 64)], axis=2).reshape(32, 16, 64)
    wperm = jnp.concatenate([query_weight.reshape(32, 16, 64), pair], axis=2).reshape(32, 2048)
    small = jnp.concatenate(
        [router_weight, attention_gain[:, None], expert_gain[:, None], jnp.zeros((32, 128 - E - 2), BF)], axis=1
    )
    w3 = jnp.stack([gate_weight, up_weight, down_weight]).transpose(2, 0, 1, 3)
    angle = (
        jnp.arange(length, dtype=F32)[None, :] / jnp.power(2.0, rope_index.astype(F32))[:, None]
    ) * frequencies(HEAD_SIZE)[:, None]
    cos, sin = jnp.cos(angle), jnp.sin(angle)
    segment_all = lax.all_gather(segments.astype(jnp.int32), "seq", axis=1, tiled=True)
    start = jnp.sum((segment_all[:, None, :] < segment_all[:, :, None]).astype(jnp.int32), axis=-1, dtype=jnp.int32)
    wp_all = lax.all_gather(wperm, ("row", "seq"), axis=0, tiled=True)
    cot_all = lax.all_gather(cotangent[0], "seq", axis=0, tiled=True)

    tok_all, w_mine, small_all, wo_all = comm_call(
        gather_first,
        [sds((16, 2, rows // 2, D), BF), sds((32, 32, 256), BF), sds((32, 32, 128), BF), sds((2, 16, 32, D), BF)],
        [tokens.reshape(2, rows // 2, D), wperm, small, output_weight],
        GATHER_SEMS * 2 + [DMA((32,))] * 4 + [DMA((4,))],
        0,
    )
    small_all = small_all.reshape(D, 128)
    wo_all = wo_all.reshape(D, D)
    hid, q_t, k_t, v_t, o_t, lse, o_low = compute_call(
        attention_forward,
        [
            sds((length, D), BF),
            sds((64, length), BF),
            sds((64, length), BF),
            sds((64, length), BF),
            sds((64, length), F32),
            sds((1, length), F32),
            sds((64, length), BF),
        ],
        [tok_all.reshape(length, D), w_mine.reshape(D, 256), small_all, cos, sin, start],
        [VM((length, 64), BF), VM((128, D), F32), VM((256, D), BF)],
    )
    att_t, wexp = comm_call(
        heads_to_tokens,
        [sds((16, 64, rows), BF), sds((3, 32, 32, F), BF)],
        [o_low, w3],
        [DMA((16,))] * 6,
        1,
    )
    tok_mine = tokens.reshape(rows, D)
    residual, normed, scale, h2, att, probs, picked, p_t = compute_call(
        between,
        [
            sds((rows, D), F32),
            sds((rows, D), F32),
            sds((rows, 128), F32),
            sds((rows, D), BF),
            sds((rows, D), BF),
            sds((rows, 128), F32),
            sds((rows, 128), F32),
            sds((E, rows), F32),
        ],
        [tok_mine, att_t.reshape(D, rows), wo_all, small_all, routes.reshape(rows, K)],
    )
    h_all, p_all = comm_call(
        gather_second,
        [sds((16, 2, rows // 2, D), BF), sds((16, E, rows), F32)],
        [h2.reshape(2, rows // 2, D), p_t],
        GATHER_SEMS + [DMA((16,))] * 2 + [DMA((1,))],
        2,
    )
    mixp, backp, gg, dw = compute_call(
        expert_body,
        [sds((length, D), BF), sds((length, D), BF), sds((16, 8, 128), F32), sds((3, D, F), BF)],
        [h_all.reshape(length, D), cot_all, p_all, wexp.reshape(3, D, F)],
        [VM((3, D, F), F32)],
    )
    back, mix, g_all = comm_call(
        reduce_rows,
        [sds((2, rows // 2, D), BF), sds((2, rows // 2, D), BF), sds((16, 8, 128), F32)],
        [backp.reshape(16, 2, rows // 2, D), mixp.reshape(16, 2, rows // 2, D), gg],
        Reduce.SEMS * 2 + [DMA((16,))] * 2,
        3,
        Reduce.bufs(rows // 2, D) * 2,
    )
    mixed = (residual + mix.reshape(rows, D).astype(F32)).astype(BF)
    g_res, ga_t, dwo = compute_call(
        back_between,
        [sds((rows, D), F32), sds((D, rows), BF), sds((D, D + 128), BF)],
        [
            back.reshape(rows, D),
            g_all,
            cotangent.reshape(rows, D),
            probs,
            picked,
            normed,
            scale,
            small_all,
            wo_all,
            att,
            h2,
        ],
    )
    go_t, dw_all, dwo_sum = comm_call(
        grads_out,
        [sds((64, length), BF), sds((16, 3, 32, F), BF), sds((2, 16, D + 128), BF)],
        [ga_t.reshape(16, 64, rows), dw.reshape(3, 2, 16, 32, F), dwo.reshape(2, 16, 2, 16, D + 128)],
        Reduce.SEMS + [DMA((16,))] * 4 + [DMA((4,))],
        4,
        Reduce.bufs(16, D + 128) + [VM((3, 16, 32, F), BF), VM((16, 2, 16, D + 128), BF)],
    )
    gq_t, gkv_t = compute_call(
        attention_backward,
        [sds((64, length), F32), sds((128, length), F32)],
        [q_t, k_t, v_t, lse, o_t, go_t, start],
        [VM((length, 64), BF), VM((length, 64), BF), VM((1, length), F32)],
    )
    gkv = gkv_t.reshape(2, 64, length)
    (got,) = comm_call(share_pair, [sds((64, length), F32)], [gkv], [DMA, DMA], 5)
    g_t, wg = compute_call(
        back_projection, [sds((128, length), BF), sds((D, 128), BF)], [gq_t, gkv, got, hid, cos, sin]
    )
    g_mine, wg_all = comm_call(
        last_exchange,
        [sds((16, 128, rows), BF), sds((32, 32, 128), BF)],
        [g_t, wg.reshape(32, 32, 128)],
        [DMA((16,))] * 2 + [DMA((32,))] * 2,
        6,
    )
    (grad_tokens,) = compute_call(
        last_rows, [sds((rows, D), F32)], [g_mine.reshape(2 * D, rows), wp_all, tok_mine, small_all, g_res]
    )
    wg_sum = wg_all.reshape(2, 16, 32, 128).astype(F32).sum(axis=0).transpose(1, 0, 2)
    grad_query_weight = wg_sum[:, :, :64].reshape(32, D)
    grad_key_weight = wg_sum[:, 0::2, 64:].reshape(32, 512)
    grad_value_weight = wg_sum[:, 1::2, 64:].reshape(32, 512)
    own_o = dwo_sum.reshape(32, D + 128).astype(F32)
    grad_output_weight, grad_router_weight = own_o[:, :D], own_o[:, D : D + E]
    expert_grads = dw_all.transpose(1, 2, 0, 3).astype(F32)
    grad_gate_weight, grad_up_weight, grad_down_weight = expert_grads[0], expert_grads[1], expert_grads[2]
    grad_attention_gain = (
        jnp.sum(grad_query_weight * query_weight.astype(F32), axis=1)
        + jnp.sum(grad_key_weight * key_matrix.astype(F32), axis=1)
        + jnp.sum(grad_value_weight * value_matrix.astype(F32), axis=1)
    ) / attention_gain.astype(F32)
    grad_expert_gain = (
        jnp.sum(grad_gate_weight * gate_weight.astype(F32) + grad_up_weight * up_weight.astype(F32), axis=(1, 2))
        + jnp.sum(grad_router_weight * router_weight.astype(F32), axis=1)
    ) / expert_gain.astype(F32)
    return (
        mixed.reshape(tokens.shape),
        grad_tokens.reshape(tokens.shape),
        grad_attention_gain,
        grad_expert_gain,
        grad_query_weight,
        grad_key_weight,
        grad_value_weight,
        grad_output_weight,
        grad_router_weight,
        grad_gate_weight,
        grad_up_weight,
        grad_down_weight,
    )


def rms_scale(values):
    return lax.rsqrt(jnp.mean(values * values, axis=-1, keepdims=True) + EPSILON)


def apply_rotary(values, cosine_lookup, sine_lookup):
    halves = values.shape[-1] // 2
    first_half = values[..., :halves]
    second_half = values[..., halves:]
    return jnp.concatenate(
        [
            first_half * cosine_lookup - second_half * sine_lookup,
            second_half * cosine_lookup + first_half * sine_lookup,
        ],
        axis=-1,
    )


def unrotate(values, cosine_lookup, sine_lookup):
    halves = values.shape[-1] // 2
    first_half = values[..., :halves]
    second_half = values[..., halves:]
    return jnp.concatenate(
        [
            first_half * cosine_lookup + second_half * sine_lookup,
            second_half * cosine_lookup - first_half * sine_lookup,
        ],
        axis=-1,
    )


def block_mask(key_start, block_size, query_pos, query_seg, seg_block):
    key_pos = key_start + jnp.arange(block_size, dtype=jnp.int32)
    causal = key_pos[None, :] <= query_pos[:, None]
    same_doc = seg_block[:, None, :] == query_seg[:, :, None]
    return (causal[None] & same_doc)[:, None, None]


def attend_piece(running, pieces, first_key, queries, query_pos, query_seg, scaling):
    key_rows, value_rows, key_segments = pieces
    sequence_count, key_span = (key_rows.shape[0], key_rows.shape[1])
    block_size = math.gcd(key_span, 512)
    kv_heads, head_dim = (queries.shape[2], queries.shape[4])

    def advance(block_index, carried):
        top_score, denominator, numerator = carried
        offset = block_index * block_size
        key_block = lax.dynamic_slice_in_dim(key_rows, offset, block_size, 1).reshape(
            sequence_count, block_size, kv_heads, head_dim
        )
        value_block = lax.dynamic_slice_in_dim(value_rows, offset, block_size, 1).reshape(
            sequence_count, block_size, kv_heads, head_dim
        )
        seg_block = lax.dynamic_slice_in_dim(key_segments, offset, block_size, 1).astype(jnp.int32)
        allowed = block_mask(offset, block_size, query_pos, query_seg, seg_block)
        scores = (
            jnp.einsum("sqkgd,sjkd->skgqj", queries, key_block, preferred_element_type=jnp.float32)
            * scaling
        )
        fresh_top = jnp.maximum(top_score, jnp.max(jnp.where(allowed, scores, MASKED), axis=-1))
        weights = jnp.where(allowed, jnp.exp(scores - fresh_top[..., None]), 0.0)
        decay_factor = jnp.exp(top_score - fresh_top)
        denominator = denominator * decay_factor + jnp.sum(weights, axis=-1)
        numerator = numerator * decay_factor[..., None] + jnp.einsum(
            "skgqj,sjkd->skgqd",
            weights.astype(jnp.bfloat16),
            value_block,
            preferred_element_type=jnp.float32,
        )
        return (fresh_top, denominator, numerator)

    return lax.fori_loop(0, key_span // block_size, advance, running)


def attend_back(pieces, queries, query_pos, query_seg, grad_attn, log_total, row_delta, scaling):
    key_rows, value_rows, key_segments = pieces
    sequence_count, key_span, key_value_width = key_rows.shape
    block_size = math.gcd(key_span, 512)
    kv_heads, head_dim = (queries.shape[2], queries.shape[4])

    def advance(block_index, carried):
        grad_queries, gradient_couples = carried
        offset = block_index * block_size
        key_block = lax.dynamic_slice_in_dim(key_rows, offset, block_size, 1).reshape(
            sequence_count, block_size, kv_heads, head_dim
        )
        value_block = lax.dynamic_slice_in_dim(value_rows, offset, block_size, 1).reshape(
            sequence_count, block_size, kv_heads, head_dim
        )
        seg_block = lax.dynamic_slice_in_dim(key_segments, offset, block_size, 1).astype(jnp.int32)
        allowed = block_mask(offset, block_size, query_pos, query_seg, seg_block)
        scores = (
            jnp.einsum("sqkgd,sjkd->skgqj", queries, key_block, preferred_element_type=jnp.float32)
            * scaling
        )
        weights = jnp.where(allowed, jnp.exp(scores - log_total[..., None]), 0.0)
        grad_weights = jnp.einsum(
            "sqkgd,sjkd->skgqj", grad_attn, value_block, preferred_element_type=jnp.float32
        )
        grad_scores = (weights * (grad_weights - row_delta[..., None])).astype(jnp.bfloat16)
        grad_queries = grad_queries + jnp.einsum(
            "skgqj,sjkd->sqkgd", grad_scores, key_block, preferred_element_type=jnp.float32
        )
        grad_keys = (
            jnp.einsum(
                "skgqj,sqkgd->sjkd", grad_scores, queries, preferred_element_type=jnp.float32
            )
            * scaling
        )
        grad_values = jnp.einsum(
            "skgqj,sqkgd->sjkd",
            weights.astype(jnp.bfloat16),
            grad_attn,
            preferred_element_type=jnp.float32,
        )
        produced = jnp.concatenate(
            [
                grad_keys.reshape(sequence_count, block_size, key_value_width),
                grad_values.reshape(sequence_count, block_size, key_value_width),
            ],
            axis=-1,
        )
        return (
            grad_queries,
            lax.dynamic_update_slice_in_dim(gradient_couples, produced, offset, 1),
        )

    starting = (
        jnp.zeros(queries.shape, jnp.float32),
        jnp.zeros((sequence_count, key_span, 2 * key_value_width), jnp.float32),
    )
    grad_queries, gradient_couples = lax.fori_loop(0, key_span // block_size, advance, starting)
    return (grad_queries * scaling, gradient_couples)


def project_in(pieces, routed):
    gate_rows, up_rows = pieces
    return (
        jnp.einsum("erd,def->erf", routed, gate_rows, preferred_element_type=jnp.float32),
        jnp.einsum("erd,def->erf", routed, up_rows, preferred_element_type=jnp.float32),
    )


def project_out(down_rows, hidden):
    produced = jnp.einsum("erf,def->erd", hidden, down_rows, preferred_element_type=jnp.float32)
    return produced


def back_through_down(down_rows, grad_output):
    return jnp.einsum("erd,def->erf", grad_output, down_rows, preferred_element_type=jnp.float32)


def back_through_in(pieces, grad_gate, grad_up):
    gate_rows, up_rows = pieces
    produced = jnp.einsum(
        "erf,def->erd", grad_gate, gate_rows, preferred_element_type=jnp.float32
    ) + jnp.einsum("erf,def->erd", grad_up, up_rows, preferred_element_type=jnp.float32)
    return produced


def take_slots(slot_data, destination):
    experts, width = (slot_data.shape[0], slot_data.shape[-1])
    sequence_count, sequence_rows, picks = destination.shape
    flat = jnp.transpose(
        slot_data.reshape(experts, sequence_count, -1, width), (1, 0, 2, 3)
    ).reshape(sequence_count, -1, width)
    taken = jax.vmap(lambda table, spots: table[spots])(
        flat, destination.reshape(sequence_count, sequence_rows * picks)
    )
    return taken.reshape(sequence_count, sequence_rows, picks, width)


def place_slots(values, destination, experts, capacity):
    sequence_count, width = (values.shape[0], values.shape[-1])
    empty = jnp.zeros((sequence_count, experts * capacity, width), values.dtype)
    filled = jax.vmap(lambda table, spots, rows: table.at[spots].set(rows))(
        empty, destination.reshape(sequence_count, -1), values.reshape(sequence_count, -1, width)
    )
    return jnp.transpose(
        filled.reshape(sequence_count, experts, capacity, width), (1, 0, 2, 3)
    ).reshape(experts, sequence_count * capacity, width)


def any_seats(
    tokens,
    attention_gain,
    expert_gain,
    query_weight,
    key_matrix,
    value_matrix,
    output_weight,
    router_weight,
    gate_weight,
    up_weight,
    down_weight,
    routes,
    segments,
    rope_index,
    cotangent,
):
    sequence_count, sequence_rows = (tokens.shape[0], tokens.shape[1])
    queries_per_group = QUERY_HEADS // KEY_VALUE_HEADS
    key_value_width = KEY_VALUE_HEADS * HEAD_SIZE
    scaling = 1.0 / math.sqrt(HEAD_SIZE)
    experts_slots = E * CAP
    gathered = (
        lax.all_gather(attention_gain, ("row", "seq"), axis=0, tiled=True),
        lax.all_gather(expert_gain, ("row", "seq"), axis=0, tiled=True),
        lax.all_gather(query_weight, ("row", "seq"), axis=0, tiled=True),
        lax.all_gather(key_matrix, ("row", "seq"), axis=0, tiled=True),
        lax.all_gather(value_matrix, ("row", "seq"), axis=0, tiled=True),
        lax.all_gather(output_weight, ("row", "seq"), axis=0, tiled=True),
        lax.all_gather(router_weight, ("row", "seq"), axis=0, tiled=True),
    )
    gain_first = gathered[0].astype(jnp.float32)
    gain_second = gathered[1].astype(jnp.float32)
    full_query, full_key, full_value, full_output, full_router = gathered[2:]
    inputs = tokens.astype(jnp.float32)
    scale_first = rms_scale(inputs)
    normed_first = inputs * scale_first
    hidden_first = (normed_first * gain_first).astype(jnp.bfloat16)
    query_unrotated = jnp.einsum(
        "sqd,dc->sqc", hidden_first, full_query, preferred_element_type=jnp.float32
    )
    key_unrotated = jnp.einsum(
        "sqd,dc->sqc", hidden_first, full_key, preferred_element_type=jnp.float32
    )
    value_raw = jnp.einsum(
        "sqd,dc->sqc", hidden_first, full_value, preferred_element_type=jnp.float32
    )
    positions = lax.axis_index("seq") * sequence_rows + jnp.arange(sequence_rows, dtype=jnp.int32)
    factor = jnp.power(2.0, rope_index.astype(jnp.float32))
    angles = (positions.astype(jnp.float32)[None, :] / factor[:, None])[..., None] * frequencies(
        HEAD_SIZE
    )
    cosine_lookup = jnp.cos(angles)[:, :, None, :]
    sine_lookup = jnp.sin(angles)[:, :, None, :]
    query_turned = (
        apply_rotary(
            query_unrotated.reshape(sequence_count, sequence_rows, QUERY_HEADS, HEAD_SIZE),
            cosine_lookup,
            sine_lookup,
        )
        .astype(jnp.bfloat16)
        .reshape(sequence_count, sequence_rows, KEY_VALUE_HEADS, queries_per_group, HEAD_SIZE)
    )
    key_turned = (
        apply_rotary(
            key_unrotated.reshape(sequence_count, sequence_rows, KEY_VALUE_HEADS, HEAD_SIZE),
            cosine_lookup,
            sine_lookup,
        )
        .astype(jnp.bfloat16)
        .reshape(sequence_count, sequence_rows, key_value_width)
    )
    value_reduced = value_raw.astype(jnp.bfloat16)
    segment_low = segments.astype(jnp.float32).astype(jnp.bfloat16)
    statistic_shape = (sequence_count, KEY_VALUE_HEADS, queries_per_group, sequence_rows)
    starting = (
        jnp.full(statistic_shape, MASKED, jnp.float32),
        jnp.zeros(statistic_shape, jnp.float32),
        jnp.zeros(statistic_shape + (HEAD_SIZE,), jnp.float32),
    )
    attend = partial(
        attend_piece, queries=query_turned, query_pos=positions, query_seg=segments, scaling=scaling
    )
    top_score, denominator, numerator = attend(
        starting,
        (
            lax.all_gather(key_turned, "seq", axis=1, tiled=True),
            lax.all_gather(value_reduced, "seq", axis=1, tiled=True),
            lax.all_gather(segment_low, "seq", axis=1, tiled=True),
        ),
        jnp.int32(0),
    )
    attn_heads = numerator / denominator[..., None]
    log_total = top_score + jnp.log(denominator)
    attn_rows = jnp.transpose(attn_heads, (0, 3, 1, 2, 4))
    attn_low = attn_rows.astype(jnp.bfloat16).reshape(
        sequence_count, sequence_rows, QUERY_HEADS * HEAD_SIZE
    )
    branch = jnp.einsum("sqc,dc->sqd", attn_low, full_output, preferred_element_type=jnp.float32)
    residual = inputs + branch
    scale_second = rms_scale(residual)
    normed_second = residual * scale_second
    hidden_second = (normed_second * gain_second).astype(jnp.bfloat16)
    logits = jnp.einsum(
        "sqd,de->sqe", hidden_second, full_router, preferred_element_type=jnp.float32
    )
    router_probs = jax.nn.softmax(logits, axis=-1)
    picked = routes[..., None] == jnp.arange(E, dtype=jnp.int32)
    picked_int = picked.astype(jnp.int32).reshape(sequence_count, sequence_rows * K, E)
    earlier = jnp.cumsum(picked_int, axis=1, dtype=jnp.int32) - picked_int
    slot_ids = jnp.sum(earlier * picked_int, axis=-1, dtype=jnp.int32).reshape(
        sequence_count, sequence_rows, K
    )
    destination = routes * CAP + slot_ids
    chosen = destination[..., None] == jnp.arange(experts_slots, dtype=jnp.int32)
    gate_probs = jnp.sum(jnp.where(picked, router_probs[:, :, None, :], 0.0), axis=-1)
    dispatch = jnp.sum(chosen, axis=2, dtype=jnp.float32).reshape(
        sequence_count, sequence_rows, E, CAP
    )
    slot_rows = sequence_count * CAP
    routed = (
        jnp.einsum(
            "sqec,sqd->escd",
            dispatch.astype(jnp.bfloat16),
            hidden_second,
            preferred_element_type=jnp.float32,
        )
        .astype(jnp.bfloat16)
        .reshape(E, slot_rows, MODEL_WIDTH)
    )
    grad_mixed = cotangent.astype(jnp.float32)
    grad_slot_values = (gate_probs[..., None] * grad_mixed[:, :, None, :]).astype(jnp.bfloat16)
    grad_expert = place_slots(grad_slot_values, destination, E, CAP)
    groups = 4
    width = E // groups

    def some_experts(_, given):
        rows, grads, gate_part, up_part, down_part = given
        pieces = (
            lax.all_gather(gate_part, ("row", "seq"), axis=0, tiled=True),
            lax.all_gather(up_part, ("row", "seq"), axis=0, tiled=True),
        )
        down_rows = lax.all_gather(down_part, ("row", "seq"), axis=0, tiled=True)
        gate_pre, up_pre = project_in(pieces, routed=rows)
        hidden_low = (jax.nn.silu(gate_pre) * up_pre).astype(jnp.bfloat16)
        expert_out = project_out(down_rows, hidden=hidden_low)
        grad_hidden = back_through_down(down_rows, grad_output=grads)
        sigmoid_gate = jax.nn.sigmoid(gate_pre)
        grad_gate = (
            grad_hidden * up_pre * sigmoid_gate * (1.0 + gate_pre * (1.0 - sigmoid_gate))
        ).astype(jnp.bfloat16)
        grad_up = (grad_hidden * (gate_pre * sigmoid_gate)).astype(jnp.bfloat16)
        grad_routed = back_through_in(pieces, grad_gate=grad_gate, grad_up=grad_up)
        made = [
            lax.psum_scatter(
                jnp.einsum("erd,erf->def", left, right, preferred_element_type=jnp.float32),
                ("row", "seq"),
                scatter_dimension=0,
                tiled=True,
            )
            for left, right in ((rows, grad_gate), (rows, grad_up), (grads, hidden_low))
        ]
        return None, (expert_out, grad_routed, *made)

    def grouped(weight):
        return jnp.moveaxis(weight.reshape(weight.shape[0], groups, width, F), 1, 0)

    _, (expert_out, grad_routed, *expert_grads) = lax.scan(
        some_experts,
        None,
        (
            routed.reshape(groups, width, slot_rows, MODEL_WIDTH),
            grad_expert.reshape(groups, width, slot_rows, MODEL_WIDTH),
            grouped(gate_weight),
            grouped(up_weight),
            grouped(down_weight),
        ),
    )
    expert_out = expert_out.reshape(E, slot_rows, MODEL_WIDTH)
    grad_routed = grad_routed.reshape(E, slot_rows, MODEL_WIDTH)
    grad_gate_weight, grad_up_weight, grad_down_weight = [
        jnp.moveaxis(grad, 0, 1).reshape(gate_weight.shape) for grad in expert_grads
    ]
    taken_out = take_slots(expert_out, destination)
    expert_mix = jnp.sum(gate_probs[..., None] * taken_out, axis=2)
    mixed = (residual + expert_mix).astype(jnp.bfloat16)
    grad_gates = jnp.sum(taken_out * grad_mixed[:, :, None, :], axis=-1)
    grad_probs = jnp.sum(jnp.where(picked, grad_gates[..., None], 0.0), axis=2)
    grad_logits = (
        router_probs * (grad_probs - jnp.sum(router_probs * grad_probs, axis=-1, keepdims=True))
    ).astype(jnp.bfloat16)
    grad_second = jnp.sum(take_slots(grad_routed, destination), axis=2) + jnp.einsum(
        "sqe,de->sqd", grad_logits, full_router, preferred_element_type=jnp.float32
    )
    grad_gain_second = jnp.sum(grad_second * normed_second, axis=(0, 1))
    scaled_second = grad_second * gain_second
    grad_residual = grad_mixed + scale_second * (
        scaled_second
        - normed_second * jnp.mean(scaled_second * normed_second, axis=-1, keepdims=True)
    )
    grad_branch = grad_residual.astype(jnp.bfloat16)
    grad_attn = (
        jnp.einsum("sqd,dc->sqc", grad_branch, full_output, preferred_element_type=jnp.float32)
        .astype(jnp.bfloat16)
        .reshape(sequence_count, sequence_rows, KEY_VALUE_HEADS, queries_per_group, HEAD_SIZE)
    )
    row_delta = jnp.transpose(
        jnp.sum(grad_attn.astype(jnp.float32) * attn_rows, axis=-1), (0, 2, 3, 1)
    )
    keys_back = (
        lax.all_gather(key_turned, "seq", axis=1, tiled=True),
        lax.all_gather(value_reduced, "seq", axis=1, tiled=True),
        lax.all_gather(segment_low, "seq", axis=1, tiled=True),
    )
    grad_query_rot, grad_pair_rows = attend_back(
        keys_back, query_turned, positions, segments, grad_attn, log_total, row_delta, scaling
    )
    gradient_couples = lax.psum_scatter(grad_pair_rows, "seq", scatter_dimension=1, tiled=True)
    grad_query = (
        unrotate(
            grad_query_rot.reshape(sequence_count, sequence_rows, QUERY_HEADS, HEAD_SIZE),
            cosine_lookup,
            sine_lookup,
        )
        .astype(jnp.bfloat16)
        .reshape(sequence_count, sequence_rows, QUERY_HEADS * HEAD_SIZE)
    )
    grad_key = (
        unrotate(
            gradient_couples[..., :key_value_width].reshape(
                sequence_count, sequence_rows, KEY_VALUE_HEADS, HEAD_SIZE
            ),
            cosine_lookup,
            sine_lookup,
        )
        .astype(jnp.bfloat16)
        .reshape(sequence_count, sequence_rows, key_value_width)
    )
    grad_value = gradient_couples[..., key_value_width:].astype(jnp.bfloat16)
    grad_first = (
        jnp.einsum("sqc,dc->sqd", grad_query, full_query, preferred_element_type=jnp.float32)
        + jnp.einsum("sqc,dc->sqd", grad_key, full_key, preferred_element_type=jnp.float32)
        + jnp.einsum("sqc,dc->sqd", grad_value, full_value, preferred_element_type=jnp.float32)
    )
    grad_gain_first = jnp.sum(grad_first * normed_first, axis=(0, 1))
    scaled_first = grad_first * gain_first
    grad_tokens = grad_residual + scale_first * (
        scaled_first - normed_first * jnp.mean(scaled_first * normed_first, axis=-1, keepdims=True)
    )
    attention_grads = lax.psum_scatter(
        jnp.concatenate(
            [
                jnp.einsum(
                    "sqd,sqc->dc", hidden_first, grad_query, preferred_element_type=jnp.float32
                ),
                jnp.einsum(
                    "sqd,sqc->dc", hidden_first, grad_key, preferred_element_type=jnp.float32
                ),
                jnp.einsum(
                    "sqd,sqc->dc", hidden_first, grad_value, preferred_element_type=jnp.float32
                ),
                jnp.einsum(
                    "sqd,sqc->dc", grad_branch, attn_low, preferred_element_type=jnp.float32
                ),
                jnp.einsum(
                    "sqd,sqe->de", hidden_second, grad_logits, preferred_element_type=jnp.float32
                ),
                grad_gain_first[:, None],
                grad_gain_second[:, None],
            ],
            axis=1,
        ),
        ("row", "seq"),
        scatter_dimension=0,
        tiled=True,
    )
    query_cols = QUERY_HEADS * HEAD_SIZE
    edge_two = query_cols + key_value_width
    edge_three = edge_two + key_value_width
    edge_four = edge_three + query_cols
    edge_five = edge_four + E
    return (
        mixed,
        grad_tokens,
        attention_grads[:, edge_five],
        attention_grads[:, edge_five + 1],
        attention_grads[:, :query_cols],
        attention_grads[:, query_cols:edge_two],
        attention_grads[:, edge_two:edge_three],
        attention_grads[:, edge_three:edge_four],
        attention_grads[:, edge_four:edge_five],
        grad_gate_weight,
        grad_up_weight,
        grad_down_weight,
    )


def solution(mesh):
    first = P(("row", "seq"))
    in_specs = (
        (P("row", "seq", None), first, first)
        + (P(("row", "seq"), None),) * 5
        + (P(("row", "seq"), None, None),) * 3
        + (P("row", "seq", None), P("row", "seq"), P("row"), P("row", "seq", None))
    )
    out_specs = (
        (P("row", "seq", None), P("row", "seq", None), first, first)
        + (P(("row", "seq"), None),) * 5
        + (P(("row", "seq"), None, None),) * 3
    )
    body = sixteen_seats if dict(mesh.shape) == {"row": 2, "seq": 16} else any_seats
    return jax.shard_map(body, mesh=mesh, in_specs=in_specs, out_specs=out_specs, check_vma=False)
```

```python
from functools import partial
import math

import jax
import jax.numpy as jnp
from jax import lax
from jax.experimental import pallas as pl
from jax.experimental.pallas import tpu as pltpu
from jax.sharding import PartitionSpec as P

MODEL_WIDTH = 1024
QUERY_HEADS = 16
KEY_VALUE_HEADS = 8
HEAD_SIZE = 64
F = 512
E = 16
K = 8
CAP = 96

EPSILON = 1e-05
ROPE_BASE = 10000.0
MASKED = -1e30
MESH = pl.DeviceIdType.MESH
VM = pltpu.VMEM
BF = jnp.bfloat16
F32 = jnp.float32
DMA = pltpu.SemaphoreType.DMA
UP, DOWN, SIDE, CORE = range(4)
VMEM_LIMIT = 60 * 1024 * 1024

NN = (((1,), (0,)), ((), ()))
NT = (((1,), (1,)), ((), ()))
TN = (((0,), (0,)), ((), ()))


def dot(a, b, dims=NN):
    return lax.dot_general(a, b, dims, preferred_element_type=F32)


def when(cond, f):
    if cond is None:
        f()
    else:
        pl.when(cond)(f)


def both(a, b):
    if a is None:
        return b
    return a if b is None else a & b


def place():
    x = lax.axis_index("row")
    s = lax.axis_index("seq")
    return x, s, s // 4, (s // 2) % 2, s % 2


def seat(z, y, c):
    return z * 4 + y * 2 + c


def remote(src, dst, send, recv, dev):
    return pltpu.make_async_remote_copy(src, dst, send, recv, device_id=dev, device_id_type=MESH)


def barrier_all():
    x, s = lax.axis_index("row"), lax.axis_index("seq")
    sem = pltpu.get_barrier_semaphore()
    for k in range(1, 16):
        pl.semaphore_signal(sem, inc=1, device_id=(x, (s + k) % 16), device_id_type=MESH)
    for k in range(16):
        pl.semaphore_signal(sem, inc=1, device_id=(1 - x, (s + k) % 16), device_id_type=MESH)
    pl.semaphore_wait(sem, 31)


def barrier_row(partner=False):
    x, s = lax.axis_index("row"), lax.axis_index("seq")
    sem = pltpu.get_barrier_semaphore()
    for k in range(1, 16):
        pl.semaphore_signal(sem, inc=1, device_id=(x, (s + k) % 16), device_id_type=MESH)
    if partner:
        pl.semaphore_signal(sem, inc=1, device_id=(1 - x, s), device_id_type=MESH)
    pl.semaphore_wait(sem, 16 if partner else 15)


def barrier_near():
    x, s, z, y, c = place()
    sem = pltpu.get_barrier_semaphore()
    for cond, dev in (
        (z < 3, (x, seat(z + 1, y, c))),
        (z > 0, (x, seat(z - 1, y, c))),
        (None, (x, seat(z, 1 - y, c))),
        (None, (x, seat(z, y, 1 - c))),
    ):
        when(cond, lambda dev=dev: pl.semaphore_signal(sem, inc=1, device_id=dev, device_id_type=MESH))
    pl.semaphore_wait(sem, 2 + (z < 3).astype(jnp.int32) + (z > 0).astype(jnp.int32))


QB = 256


def lane_block(i, size=QB):
    return pl.ds(pl.multiple_of(i * size, size), size)


class Gather:
    def __init__(self, own, at, send, recv):
        self.own, self.at, self.send, self.recv = own, at, send, recv
        self.ending = False
        self.x, self.s, self.z, self.y, self.c = place()

    def device(self, k):
        x, z, y, c = self.x, self.z, self.y, self.c
        return {
            UP: (x, seat(z + 1, y, c)),
            DOWN: (x, seat(z - 1, y, c)),
            SIDE: (x, seat(z, 1 - y, c)),
            CORE: (x, seat(z, y, 1 - c)),
        }[k]

    def copy(self, src, h, k, own):
        ref = self.own(h) if own else self.at(src, h)
        return remote(ref, self.at(src, h), self.send.at[src, h, k], self.recv.at[src, h], self.device(k))

    def go(self, src, h, k, cond=None, own=False):
        if k == UP:
            cond = both(cond, self.z < 3)
        if k == DOWN:
            cond = both(cond, self.z > 0)
        act = (lambda c: c.wait_send()) if self.ending else (lambda c: c.start())
        when(cond, lambda: act(self.copy(src, h, k, own)))

    def wait(self, src, h, cond=None):
        if self.ending:
            return
        when(cond, lambda: self.copy(src, h, SIDE, False).wait_recv())

    def begin(self):
        own = self.own is not None
        for h, k in ((0, UP), (0, DOWN), (1, SIDE), (0, SIDE), (1, UP), (1, DOWN), (0, CORE), (1, CORE)):
            self.go(self.s, h, k, own=own)

    def near(self):
        src = seat(self.z, 1 - self.y, self.c)
        self.wait(src, 1)
        for k in (UP, DOWN, CORE):
            self.go(src, 1, k)
        self.wait(src, 0)
        self.go(src, 0, CORE)

    def step(self, t):
        z, y, c = self.z, self.y, self.c
        for cond, zz, k in ((z - t >= 0, z - t, UP), (z + t <= 3, z + t, DOWN)):
            mine, other = seat(zz, y, c), seat(zz, 1 - y, c)
            self.wait(mine, 0, cond)
            for way in (k, SIDE, CORE):
                self.go(mine, 0, way, cond)
            self.wait(mine, 1, cond)
            for way in (k, CORE):
                self.go(mine, 1, way, cond)
            self.wait(other, 1, cond)
            for way in (k, CORE):
                self.go(other, 1, way, cond)

    def step_side(self, t):
        z, y, c = self.z, self.y, self.c
        for cond, zz in ((z - t >= 0, z - t), (z + t <= 3, z + t)):
            other = seat(zz, 1 - y, c)
            self.wait(other, 0, cond)
            self.go(other, 0, CORE, cond)

    def plane(self, zz, cond=None):
        for yy in range(2):
            for h in range(2):
                self.wait(seat(zz, yy, 1 - self.c), h, cond)

    def planes(self, t):
        self.step_side(t)
        for cond, zz in ((self.z - t >= 0, self.z - t), (self.z + t <= 3, self.z + t)):
            self.plane(zz, cond)

    def end_core(self):
        for zz in range(4):
            self.plane(zz)

    def end_sends(self):
        self.ending = True
        self.begin()
        self.near()
        for t in (1, 2, 3):
            self.step(t)
            self.step_side(t)


GATHER_SEMS = [DMA((16, 2, 4)), DMA((16, 2))]


def run_gathers(gathers):
    for g in gathers:
        g.begin()
    for g in gathers:
        g.near()
    for t in (1, 2, 3):
        for g in gathers:
            g.step(t)
    for t in (1, 2, 3):
        for g in gathers:
            g.step_side(t)
    for g in gathers:
        g.end_core()
    for g in gathers:
        g.end_sends()


class Exchange:
    def __init__(self, src, dst, send, recv, wide=False):
        self.x, self.s, self.z, self.y, self.c = place()
        self.wide, self.n = wide, 32 if wide else 16
        self.src, self.dst, self.send, self.recv = src, dst, send, recv

    def seat(self, k, back=False):
        dz = (k // 4) % 4
        if back:
            dz = (4 - dz) % 4
        x = (self.x + k // 16) % 2
        s = seat((self.z + dz) % 4, (self.y + k // 2) % 2, (self.c + k) % 2)
        return x, s

    def index(self, seat_of):
        x, s = seat_of
        return x * 16 + s if self.wide else s

    def copy(self, k):
        to, me = self.seat(k), self.index((self.x, self.s))
        return remote(self.src(self.index(to)), self.dst(me), self.send.at[k], self.recv.at[k], to)

    def begin(self, ks=None):
        for k in range(self.n) if ks is None else ks:
            if k == 0:
                me = self.index((self.x, self.s))
                self.local = pltpu.make_async_copy(self.src(me), self.dst(me), self.recv.at[0])
                self.local.start()
            else:
                self.copy(k).start()

    def arrive(self, k):
        frm = self.seat(k, back=True)
        me = self.index((self.x, self.s))
        remote(self.src(me), self.dst(self.index(frm)), self.send.at[k], self.recv.at[k], frm).wait_recv()
        return self.index(frm)

    def end(self, arrivals=True):
        self.local.wait()
        for k in range(1, self.n):
            if arrivals:
                self.arrive(k)
            self.copy(k).wait_send()


class Slices:
    def __init__(self, src, got, send, recv):
        self.x, self.s, self.z, self.y, self.c = place()
        self.src, self.got, self.send, self.recv = src, got, send, recv

    def block(self, pair):
        return self.src.at[:, lane_block(pair, 256)]

    def copy(self, k):
        z, y = (self.z + k // 2) % 4, (self.y + k) % 2
        dst = self.got.at[self.x, self.s // 2, self.c]
        return remote(self.block(z * 2 + y), dst, self.send.at[k], self.recv.at[k], (self.x, seat(z, y, self.c)))

    def begin(self):
        self.local = pltpu.make_async_copy(
            self.block(self.s // 2), self.got.at[self.x, self.s // 2, self.c], self.recv.at[0]
        )
        self.local.start()
        for k in range(1, 8):
            self.copy(k).start()

    def over_x(self):
        ref = self.got.at[self.x, :, self.c]
        return remote(ref, ref, self.send.at[8], self.recv.at[8], (1 - self.x, self.s))

    def over_core(self, k):
        ref = self.got.at[self.x if k == 9 else 1 - self.x, :, self.c]
        return remote(ref, ref, self.send.at[k], self.recv.at[k], (self.x, seat(self.z, self.y, 1 - self.c)))

    def share(self):
        self.local.wait()
        for k in range(1, 8):
            z, y = (self.z + 4 - k // 2) % 4, (self.y + k) % 2
            dst = self.got.at[self.x, z * 2 + y, self.c]
            remote(
                self.block(z * 2 + y), dst, self.send.at[k], self.recv.at[k], (self.x, seat(z, y, self.c))
            ).wait_recv()
        self.over_x().start()
        self.over_core(9).start()

    def end(self):
        self.over_x().wait_recv()
        self.over_core(10).start()
        self.over_core(9).wait_recv()
        self.over_core(10).wait_recv()
        for k in range(1, 8):
            self.copy(k).wait_send()
        self.over_x().wait_send()
        self.over_core(9).wait_send()
        self.over_core(10).wait_send()


def comm_call(body, outs, ins, sems, cid, scratch=()):
    return pl.pallas_call(
        body,
        out_shape=outs,
        in_specs=[pl.BlockSpec(memory_space=VM)] * len(ins),
        out_specs=[pl.BlockSpec(memory_space=VM)] * len(outs),
        scratch_shapes=list(scratch) + list(sems),
        compiler_params=pltpu.CompilerParams(
            collective_id=cid, has_side_effects=True, vmem_limit_bytes=VMEM_LIMIT
        ),
    )(*ins)


def sds(shape, dtype):
    return jax.ShapeDtypeStruct(shape, dtype)


def allowed_mask(first_key, first_query, start_row):
    key = first_key + lax.broadcasted_iota(jnp.int32, (QB, QB), 0)
    query = first_query + lax.broadcasted_iota(jnp.int32, (QB, QB), 1)
    return (key <= query) & (key >= start_row)


SCORE = math.log2(math.e) / math.sqrt(HEAD_SIZE)


def front(
    tok, wperm, wo, w3, seg, routes, cos, sin,
    hid, q_t, k_t, v_t, o_t, lse, start, wexp, wo_all,
    residual, normed, scale_out, h2, att, probs, picked, p_t,
    tok_all, w_mine, seg_all, o_low, att_t, k_n, w_t,
    t_send, t_recv, o_send, o_recv, w_send, w_recv, g_send, g_recv,
    a_send, a_recv, e_send, e_recv, x_send, x_recv, x_sem,
):
    x, s, z, y, c = place()
    half = tok.shape[1]
    length = hid.shape[0]
    barrier_all()
    slices = Slices(wperm, w_mine, w_send, w_recv)
    slices.begin()
    over = remote(wo, wo_all.at[x, s], x_sem.at[0], x_sem.at[1], (1 - x, s))
    over.start()
    tokens = Gather(lambda h: tok.at[h], lambda src, h: tok_all.at[src, h], t_send, t_recv)
    tokens.begin()
    keep_tok = pltpu.make_async_copy(tok, tok_all.at[s], x_sem.at[2])
    keep_tok.start()
    keep = pltpu.make_async_copy(wo, wo_all.at[x, s], x_sem.at[3])
    keep.start()
    documents = Exchange(lambda r: seg, lambda r: seg_all.at[r], g_send, g_recv)
    documents.begin()
    weights = Exchange(lambda e: w3.at[e], lambda r: wexp.at[:, x * 16 + r], e_send, e_recv)
    weights.begin(range(4))
    tokens.near()
    for t in (1, 2, 3):
        tokens.step(t)
    for t in (1, 2, 3):
        tokens.step_side(t)
    documents.end()
    slices.share()
    keep.wait()
    remote(wo, wo_all.at[1 - x, s], x_sem.at[0], x_sem.at[1], (1 - x, s)).wait_recv()
    outw = Gather(None, lambda src, h: wo_all.at[h, src], o_send, o_recv)
    outw.begin()

    def cross(k, begin=True):
        row = weights.index(weights.seat(k, back=True))
        if begin and k:
            weights.arrive(k)
        src = w3.at[s] if k == 0 else wexp.at[:, x * 16 + row]
        copy = remote(src, wexp.at[:, x * 16 + row], x_send.at[k], x_recv.at[k], (1 - x, s))
        if begin:
            copy.start()
        else:
            copy.wait_send()
            remote(src, wexp.at[:, (1 - x) * 16 + row], x_send.at[k], x_recv.at[k], (1 - x, s)).wait_recv()

    width = tok.shape[2]
    slices.end()
    w_t[...] = jnp.transpose(w_mine[...].reshape(width, 256).astype(F32)).astype(BF)
    numbers = seg_all[:, 0, :]
    ends = [jnp.sum((numbers < n).astype(jnp.int32)) for n in (1, 2)]
    for b in range(16):
        line = numbers[b : b + 1]
        first = jnp.where(line == 0, 0, jnp.where(line == 1, ends[0], ends[1]))
        start[:, b * 128 : b * 128 + 128] = first
    tokens.end_core()
    keep_tok.wait()
    weights.begin(range(4, 8))
    for k in range(4):
        cross(k)

    def project(i, _):
        rows = lane_block(i, 512)
        values = tok_all[pl.ds(i * 4, 4)].reshape(512, width).astype(F32)
        scale = lax.rsqrt(jnp.mean(values * values, axis=-1, keepdims=True) + EPSILON)
        hidden = (values * scale).astype(BF)
        hid[rows, :] = hidden
        made = dot(w_t[...], hidden, NT)
        co, si = cos[:, rows], sin[:, rows]
        own = jnp.where(c == 0, made[0:64], made[64:128])
        for ref, part in ((q_t, own), (k_t, made[128:192])):
            a, b = part[:32], part[32:]
            ref[0:32, rows] = (a * co - b * si).astype(BF)
            ref[32:64, rows] = (b * co + a * si).astype(BF)
        v_t[:, rows] = made[192:256].astype(BF)
        k_n[rows, :] = jnp.transpose(k_t[:, rows].astype(F32)).astype(BF)
        return 0

    lax.fori_loop(0, length // 512, project, 0)
    outw.near()
    outw.step(1)
    weights.begin(range(8, 12))

    def query_block(i, _):
        cols = lane_block(i)
        queries = q_t[:, cols]
        begin = start[:, cols]

        def key_block(j, carried):
            top, total, acc = carried
            rows = lane_block(j)
            scores = dot(k_n[rows, :], queries) * SCORE
            scores = jnp.where(allowed_mask(j * QB, i * QB, begin), scores, MASKED)
            fresh = jnp.maximum(top, jnp.max(scores, axis=0, keepdims=True))
            powers = jnp.exp2(scores - fresh)
            decay = jnp.exp2(top - fresh)
            total = total * decay + jnp.sum(powers, axis=0, keepdims=True)
            acc = acc * decay + dot(v_t[:, rows], powers.astype(BF))
            return fresh, total, acc

        top, total, acc = lax.fori_loop(
            0,
            i + 1,
            key_block,
            (jnp.full((1, QB), MASKED, F32), jnp.zeros((1, QB), F32), jnp.zeros((HEAD_SIZE, QB), F32)),
        )
        out = acc / total
        o_t[:, cols] = out
        o_low[:, cols] = out.astype(BF)
        lse[:, cols] = top + jnp.log2(total)
        return 0

    blocks = length // QB
    cut = (5 * blocks) // 8
    lax.fori_loop(0, cut, query_block, 0)
    outw.step(2)
    outw.step(3)
    for t in (1, 2, 3):
        outw.step_side(t)
    for k in range(4, 8):
        cross(k)
    weights.begin(range(12, 16))
    lax.fori_loop(cut, blocks, query_block, 0)
    heads = Exchange(lambda t: o_low.at[:, lane_block(t, 128)], lambda h: att_t.at[h], a_send, a_recv)
    heads.begin()
    outw.end_core()
    for k in range(8, 12):
        cross(k)
    heads.end()

    att[...] = jnp.transpose(att_t[...].reshape(width, 2 * half).astype(F32)).astype(BF)
    res = tok[...].reshape(2 * half, width).astype(F32) + dot(att[...], wo_all[:, :, :, 0:width].reshape(width, width), NT)
    residual[...] = res
    scale = lax.rsqrt(jnp.mean(res * res, axis=-1, keepdims=True) + EPSILON)
    norm = res * scale
    normed[...] = norm
    scale_out[...] = jnp.broadcast_to(scale, scale_out.shape)
    hidden = norm.astype(BF)
    h2[...] = hidden
    lanes = lax.broadcasted_iota(jnp.int32, (128, 128), 1)
    logits = jnp.where(lanes < E, dot(hidden, wo_all[:, :, :, width : width + 128].reshape(width, 128)), MASKED)
    top = jnp.max(logits, axis=-1, keepdims=True)
    powers = jnp.exp(logits - top)
    prob = powers / jnp.sum(powers, axis=-1, keepdims=True)
    probs[...] = prob
    mask = jnp.zeros((128, 128), F32)
    for k in range(K):
        mask = mask + jnp.where(lanes == routes[:, k : k + 1], 1.0, 0.0)
    picked[...] = mask
    p_t[...] = jnp.transpose(prob * mask)[0:E, :]

    for k in range(12, 16):
        cross(k)
    weights.end(arrivals=False)
    for k in range(16):
        cross(k, begin=False)
    tokens.end_sends()
    outw.end_sends()
    over.wait_send()


class Reduce:
    def __init__(self, part, out, bufs, sems):
        self.part, self.out = part, out
        self.r1, self.ra, self.ua, self.da, self.ub, self.db, self.rb = bufs
        (self.s1, self.q1, self.sa, self.qa, self.su, self.qu, self.sd, self.qd, self.sb) = sems
        self.x, self.s, self.z, self.y, self.c = place()
        self.pending = []

    @staticmethod
    def bufs(rows, width):
        b = (rows, width)
        return [
            VM((4, 2, 2) + b, BF),
            VM((4,) + b, BF),
            VM((4,) + b, BF),
            VM((4,) + b, BF),
            VM((2, 4) + b, BF),
            VM((2, 4) + b, BF),
            VM(b, BF),
        ]

    SEMS = [DMA((4, 2)), DMA((4, 2)), DMA((4,)), DMA((4,)), DMA((3, 4)), DMA((3, 4)), DMA((3, 4)), DMA((3, 4)), DMA((2,))]

    def add(self, dst, src):
        dst[...] = (dst[...].astype(F32) + src[...].astype(F32)).astype(BF)

    def first(self, zz, yy):
        return remote(
            self.part.at[seat(zz, yy, 1 - self.c)],
            self.r1.at[zz, yy],
            self.s1.at[zz, yy],
            self.q1.at[zz, yy],
            (self.x, seat(self.z, self.y, 1 - self.c)),
        )

    def side(self, zz):
        return remote(
            self.r1.at[zz, 1 - self.y, 0],
            self.ra.at[zz],
            self.sa.at[zz],
            self.qa.at[zz],
            (self.x, seat(self.z, 1 - self.y, self.c)),
        )

    def line(self, lane, zz, up):
        z, y, c = self.z, self.y, self.c
        src = self.ra.at[zz] if lane == 0 else self.r1.at[zz, lane - 1, 1]
        if up:
            dst = self.ua.at[zz] if lane == 0 else self.ub.at[lane - 1, zz]
            return remote(src, dst, self.su.at[lane, zz], self.qu.at[lane, zz], (self.x, seat(z + 1, y, c)))
        dst = self.da.at[zz] if lane == 0 else self.db.at[lane - 1, zz]
        return remote(src, dst, self.sd.at[lane, zz], self.qd.at[lane, zz], (self.x, seat(z - 1, y, c)))

    def landed(self, lane, zz, up):
        if lane == 0:
            return (self.ua if up else self.da).at[zz]
        return (self.ub if up else self.db).at[lane - 1, zz]

    def held(self, lane, zz):
        return self.ra.at[zz] if lane == 0 else self.r1.at[zz, lane - 1, 1]

    def order(self):
        z = self.z
        for t in (3, 2, 1):
            yield z + t <= 3, z + t, True
            yield z - t >= 0, z - t, False
        yield None, z, None

    def begin(self):
        for cond, zz, _ in self.order():
            for yy in range(2):
                when(cond, lambda: self.first(zz, yy).start())

    def pass_on(self, lane, zz, up, cond):
        def go():
            def add():
                self.line(lane, zz, up).wait_recv()
                self.add(self.held(lane, zz), self.landed(lane, zz, up))

            pl.when(self.z > 0 if up else self.z < 3)(add)
            self.line(lane, zz, up).start()

        when(cond, go)

    def begin_plane(self, zz, cond=None):
        for yy in range(2):
            when(cond, lambda: self.first(zz, yy).start())

    def fold(self, zz, cond=None):
        z = self.z

        def go():
            for yy in range(2):
                self.first(zz, yy).wait_recv()
                self.add(self.r1.at[zz, yy], self.part.at[seat(zz, yy, self.c)])
            self.side(zz).start()
            for lane in (1, 2):
                pl.when((zz > z) & (z == 0))(lambda: self.line(lane, zz, True).start())
                pl.when((zz < z) & (z == 3))(lambda: self.line(lane, zz, False).start())

        when(cond, go)

    def flow(self):
        z = self.z
        for cond, zz, up in self.order():

            def ready():
                self.side(zz).wait_recv()
                self.add(self.ra.at[zz], self.r1.at[zz, self.y, 0])

            when(cond, ready)
            if up is None:
                continue
            inner = (z > 0) if up else (z < 3)
            for lane in (1, 2):
                self.pass_on(lane, zz, up, both(cond, inner))
            self.pass_on(0, zz, up, cond)
        for lane in (1, 2, 0):
            for up, cond in ((True, z > 0), (False, z < 3)):

                def take():
                    self.line(lane, z, up).wait_recv()
                    self.add(self.held(lane, z), self.landed(lane, z, up))

                when(cond, take)
            if lane == 2:
                self.last().start()
        self.out[0] = self.ra[z]
        self.last().wait_recv()
        self.out[1] = (self.r1[z, self.y, 1].astype(F32) + self.rb[...].astype(F32)).astype(BF)

    def run(self):
        for cond, zz, _ in self.order():
            self.fold(zz, cond)
        self.flow()

    def last(self):
        return remote(
            self.r1.at[self.z, 1 - self.y, 1],
            self.rb,
            self.sb.at[0],
            self.sb.at[1],
            (self.x, seat(self.z, 1 - self.y, self.c)),
        )

    def end(self):
        for cond, zz, up in self.order():
            for yy in range(2):
                when(cond, lambda: self.first(zz, yy).wait_send())
            when(cond, lambda: self.side(zz).wait_send())
            if up is not None:
                for lane in range(3):
                    when(cond, lambda: self.line(lane, zz, up).wait_send())
        self.last().wait_send()


NBUF = 7
NSEM = 9
TB = 512


def middle(h2, p_t, cot, wexp, back, mix, g_all, dwx, h_all, p_all, backp, mixp, gg, dw, acc, *rest):
    bufs_a, bufs_b = rest[:NBUF], rest[NBUF : 2 * NBUF]
    sems = rest[2 * NBUF :]
    h_send, h_recv, p_send, p_recv, keep_sem, g_send, g_recv, x_sem = sems[2 * NSEM :]
    x, s, z, y, c = place()
    barrier_row(partner=True)
    hidden = Gather(lambda h: h2.at[h], lambda src, h: h_all.at[src, h], h_send, h_recv)
    hidden.begin()
    keep = pltpu.make_async_copy(h2, h_all.at[s], keep_sem.at[0])
    keep.start()
    minor = Exchange(lambda r: p_t, lambda r: p_all.at[r], p_send, p_recv)
    minor.begin()
    one = Reduce(backp, back, bufs_a, sems[:NSEM])
    two = Reduce(mixp, mix, bufs_b, sems[NSEM : 2 * NSEM])
    acc[...] = jnp.zeros(acc.shape, F32)
    hidden.near()
    keep.wait()
    minor.end()
    hidden.plane(z)
    hidden.step(1)
    far = z // 2
    order = (z, z + 1 - 2 * far, 2 - 2 * z + 5 * far, 3 - 3 * far)
    width = h2.shape[2]

    def chunk(i, _):
        zz = jnp.where(i == 0, order[0], jnp.where(i == 1, order[1], jnp.where(i == 2, order[2], order[3])))

        @pl.when(i == 1)
        def _():
            hidden.planes(1)
            hidden.step(2)

        @pl.when(i == 2)
        def _():
            hidden.planes(2)
            hidden.step(3)
            one.fold(order[0])

        @pl.when(i == 3)
        def _():
            hidden.planes(3)
            one.fold(order[1])

        four = pl.ds(zz * 4, 4)
        rows = lane_block(zz, TB)
        rest = h_all[four].reshape(TB, width)
        grad = cot[rows, :]
        cols = [jnp.broadcast_to(p_all[zz * 4 + b, pl.ds(s, 1), :], (128, 128)) for b in range(4)]
        prob = jnp.concatenate([jnp.transpose(v)[:, 0:1] for v in cols], axis=0)
        gate = dot(rest, wexp[0])
        up = dot(rest, wexp[1])
        sig = 1.0 / (1.0 + jnp.exp(-gate))
        silu = gate * sig
        low = (silu * up).astype(BF)
        out = dot(low, wexp[2], NT)
        mixp[four] = (prob * out).astype(BF).reshape(4, 2, TB // 8, width)
        moved = dot(grad, wexp[2])
        seen = jnp.sum(low.astype(F32) * moved, axis=-1, keepdims=True)
        for b in range(4):
            line = jnp.transpose(jnp.broadcast_to(seen[b * 128 : b * 128 + 128], (128, 128)))[0:8]
            gg[zz * 4 + b] = line
        grad_hidden = moved * prob
        grad_gate = (grad_hidden * up * (sig * (1.0 + gate * (1.0 - sig)))).astype(BF)
        grad_up = (grad_hidden * silu).astype(BF)
        below = dot(grad_gate, wexp[0], NT) + dot(grad_up, wexp[1], NT)
        backp[four] = below.astype(BF).reshape(4, 2, TB // 8, width)
        one.begin_plane(zz)
        two.begin_plane(zz)
        acc[0] += dot(rest, grad_gate, TN)
        acc[1] += dot(rest, grad_up, TN)
        acc[2] += dot(grad, (prob * low.astype(F32)).astype(BF), TN)
        return 0

    lax.fori_loop(0, 4, chunk, 0)
    seen_out = Exchange(lambda r: gg.at[r], lambda r: g_all.at[r], g_send, g_recv)
    seen_out.begin()
    one.fold(order[2])
    one.fold(order[3])
    dw[...] = acc[...].astype(BF).reshape(dw.shape)
    over = remote(dw.at[:, 1 - x], dwx, x_sem.at[0], x_sem.at[1], (1 - x, s))
    over.start()
    one.flow()
    two.run()
    hidden.end_sends()
    seen_out.end()
    one.end()
    two.end()
    over.wait()
    dwx[...] = (dwx[...].astype(F32) + dw[:, x].astype(F32)).astype(BF)


def rear(
    back, g_all, cot, probs, picked, normed, scale, wo, att, h2, dwx, q_t, k_t, v_t, lse, o_t, start, hid, cos, sin,
    wp, tok,
    grad_tokens, dw_all, dwo_sum, wg_all,
    g_res, ga_t, dwo, dwo_x, go_t, gq_t, gkv, k_n, v_n, delta, got, g_t, wg, g_mine,
    *rest,
):
    bufs = rest[:NBUF]
    sems = rest[NBUF:]
    a_send, a_recv, w_send, w_recv, b_send, b_recv, v_send, v_recv, x_sem = sems[NSEM:]
    x, s, z, y, c = place()
    width = att.shape[1]
    length = hid.shape[0]
    barrier_all()

    seen = jnp.concatenate([g_all[e, 0:1, :] for e in range(E)] + [jnp.zeros((128 - E, 128), F32)], axis=0)
    grad_probs = jnp.transpose(seen) * picked[...]
    prob = probs[...]
    grad_logits = (prob * (grad_probs - jnp.sum(prob * grad_probs, axis=-1, keepdims=True))).astype(BF)
    u = back[...].astype(F32) + dot(grad_logits, wo[:, width : width + 128], NT)
    norm = normed[...]
    grad = cot[...].astype(F32) + scale[:, 0:1] * (u - norm * jnp.mean(u * norm, axis=-1, keepdims=True))
    g_res[...] = grad
    branch = grad.astype(BF)
    ga_t[...] = jnp.transpose(dot(branch, wo[:, 0:width])).astype(BF).reshape(ga_t.shape)
    heads = Exchange(lambda h: ga_t.at[h], lambda t: go_t.at[:, lane_block(t, 128)], a_send, a_recv)
    heads.begin()
    dwo[:, :, :, :, 0:width] = dot(jnp.transpose(grad).astype(BF), att[...]).astype(BF).reshape(2, 16, 2, 16, width)
    dwo[:, :, :, :, width : width + 128] = dot(h2[...], grad_logits, TN).astype(BF).reshape(2, 16, 2, 16, 128)
    over_o = remote(dwo.at[1 - x], dwo_x, x_sem.at[0], x_sem.at[1], (1 - x, s))
    over_o.start()
    k_n[...] = jnp.transpose(k_t[...].astype(F32)).astype(BF)
    v_n[...] = jnp.transpose(v_t[...].astype(F32)).astype(BF)
    gkv[...] = jnp.zeros(gkv.shape, F32)
    weights = Exchange(lambda r: dwx.at[:, r], lambda e: dw_all.at[e], w_send, w_recv)
    heads.end()
    weights.begin(range(8))
    delta[...] = jnp.sum(go_t[...].astype(F32) * o_t[...], axis=0, keepdims=True)

    def query_block(i, _):
        cols = lane_block(i)
        queries, grads = q_t[:, cols], go_t[:, cols]
        begin, log_total, shift = start[:, cols], lse[:, cols], delta[:, cols]

        def key_block(j, sofar):
            rows = lane_block(j)
            scores = dot(k_n[rows, :], queries) * SCORE
            powers = jnp.where(allowed_mask(j * QB, i * QB, begin), jnp.exp2(scores - log_total), 0.0)
            moved = dot(v_n[rows, :], grads)
            grad_scores = (powers * (moved - shift)).astype(BF)
            gkv[0, :, rows] += dot(queries, grad_scores, NT)
            gkv[1, :, rows] += dot(grads, powers.astype(BF), NT)
            return sofar + dot(k_t[:, rows], grad_scores)

        gq_t[:, cols] = lax.fori_loop(0, i + 1, key_block, jnp.zeros((HEAD_SIZE, QB), F32))
        return 0

    blocks = length // QB
    cut = (5 * blocks) // 8
    lax.fori_loop(0, cut, query_block, 0)
    over_o.wait_recv()
    dwo_x[...] = (dwo_x[...].astype(F32) + dwo[x].astype(F32)).astype(BF)
    out = Reduce(dwo_x, dwo_sum, bufs, sems[:NSEM])
    out.begin()
    weights.begin(range(8, 16))
    lax.fori_loop(cut, blocks, query_block, 0)

    pair = remote(gkv.at[1 - c], got, x_sem.at[2], x_sem.at[3], (x, seat(z, y, 1 - c)))
    pair.start()
    for cond, zz, _ in out.order():
        out.fold(zz, cond)
    scaling = 1.0 / math.sqrt(HEAD_SIZE)
    co, si = cos[...], sin[...]

    def unturn(part):
        a, b = part[:32], part[32:]
        return jnp.concatenate([a * co + b * si, b * co - a * si], axis=0)

    g_t[0] = unturn(gq_t[...] * scaling).astype(BF)
    pair.wait()
    mine = gkv[c] + got[...]
    g_t[1] = jnp.where(c == 0, unturn(mine * scaling), mine).astype(BF)
    tokens = Exchange(
        lambda t: g_t.at[:, :, lane_block(t, 128)], lambda h: g_mine.at[h // 2, :, h % 2], b_send, b_recv
    )
    tokens.begin()
    wg[...] = jnp.transpose(dot(g_t[...].reshape(128, length), hid[...])).astype(BF).reshape(wg.shape)
    columns = Exchange(lambda r: wg.at[r], lambda r: wg_all.at[r], v_send, v_recv, wide=True)
    columns.begin()
    tokens.end()
    w = jnp.transpose(dot(wp[...], g_mine[...].reshape(2 * width, 128)))
    values = tok[...].astype(F32)
    scale_first = lax.rsqrt(jnp.mean(values * values, axis=-1, keepdims=True) + EPSILON)
    norm = values * scale_first
    grad_tokens[...] = g_res[...] + scale_first * (w - norm * jnp.mean(w * norm, axis=-1, keepdims=True))
    out.flow()
    out.end()
    columns.end()
    weights.end()
    over_o.wait_send()


def frequencies(head_dim):
    halves = head_dim // 2
    return jnp.power(ROPE_BASE, -jnp.arange(halves, dtype=F32) * (2.0 / head_dim))


def sixteen_seats(
    tokens,
    attention_gain,
    expert_gain,
    query_weight,
    key_matrix,
    value_matrix,
    output_weight,
    router_weight,
    gate_weight,
    up_weight,
    down_weight,
    routes,
    segments,
    rope_index,
    cotangent,
):
    D = MODEL_WIDTH
    rows = tokens.shape[1]
    length = 16 * rows
    gain_first, gain_second = attention_gain.astype(F32)[:, None], expert_gain.astype(F32)[:, None]
    scaled_query = (query_weight.astype(F32) * gain_first).astype(BF).reshape(32, 8, 128)
    scaled_key = (key_matrix.astype(F32) * gain_first).astype(BF).reshape(32, 8, 64)
    scaled_value = (value_matrix.astype(F32) * gain_first).astype(BF).reshape(32, 8, 64)
    wperm = jnp.concatenate([scaled_query, scaled_key, scaled_value], axis=2).reshape(32, 2048)
    scaled_router = (router_weight.astype(F32) * gain_second).astype(BF)
    wo_router = jnp.concatenate([output_weight, scaled_router, jnp.zeros((32, 128 - E), BF)], axis=1)
    w3 = jnp.stack(
        [
            (gate_weight.astype(F32) * gain_second[..., None]).astype(BF),
            (up_weight.astype(F32) * gain_second[..., None]).astype(BF),
            down_weight,
        ]
    ).transpose(2, 0, 1, 3)
    angle = (
        jnp.arange(length, dtype=F32)[None, :] / jnp.power(2.0, rope_index.astype(F32))[:, None]
    ) * frequencies(HEAD_SIZE)[:, None]
    cos, sin = jnp.cos(angle), jnp.sin(angle)
    wp_all = lax.all_gather(wperm, ("row", "seq"), axis=0, tiled=True)
    cot_all = lax.all_gather(cotangent[0], "seq", axis=0, tiled=True)

    tok_mine = tokens.reshape(rows, D)
    (
        hid, q_t, k_t, v_t, o_t, lse, start, wexp, wo_all,
        residual, normed, scale, h2, att, probs, picked, p_t,
    ) = comm_call(
        front,
        [sds((length, D), BF)]
        + [sds((64, length), BF)] * 3
        + [sds((64, length), F32), sds((1, length), F32), sds((1, length), jnp.int32)]
        + [sds((3, 32, 32, F), BF), sds((2, 16, 32, D + 128), BF)]
        + [sds((rows, D), F32), sds((rows, D), F32), sds((rows, 128), F32), sds((rows, D), BF), sds((rows, D), BF)]
        + [sds((rows, 128), F32), sds((rows, 128), F32), sds((E, rows), F32)],
        [
            tokens.reshape(2, rows // 2, D),
            wperm,
            wo_router,
            w3,
            jnp.broadcast_to(segments.astype(jnp.int32), (8, rows)),
            routes.reshape(rows, K),
            cos,
            sin,
        ],
        GATHER_SEMS * 2 + [DMA((16,))] * 10 + [DMA((4,))],
        0,
        [
            VM((16, 2, rows // 2, D), BF),
            VM((2, 8, 2, 32, 256), BF),
            VM((16, 8, rows), jnp.int32),
            VM((64, length), BF),
            VM((16, 64, rows), BF),
            VM((length, 64), BF),
            VM((256, D), BF),
        ],
    )
    wo_all = wo_all.reshape(D, D + 128)
    back, mix, g_all, dwx = comm_call(
        middle,
        [
            sds((2, rows // 2, D), BF),
            sds((2, rows // 2, D), BF),
            sds((16, 8, rows), F32),
            sds((3, 16, 32, F), BF),
        ],
        [h2.reshape(2, rows // 2, D), p_t, cot_all, wexp.reshape(3, D, F)],
        Reduce.SEMS * 2 + GATHER_SEMS + [DMA((16,))] * 2 + [DMA((1,))] + [DMA((16,))] * 2 + [DMA((2,))],
        1,
        [
            VM((16, 2, rows // 2, D), BF),
            VM((16, E, rows), F32),
            VM((16, 2, rows // 2, D), BF),
            VM((16, 2, rows // 2, D), BF),
            VM((16, 8, rows), F32),
            VM((3, 2, 16, 32, F), BF),
            VM((3, D, F), F32),
        ]
        + Reduce.bufs(rows // 2, D) * 2,
    )
    mixed = (residual + mix.reshape(rows, D).astype(F32)).astype(BF)
    grad_tokens, dw_all, dwo_sum, wg_all = comm_call(
        rear,
        [sds((rows, D), F32), sds((16, 3, 32, F), BF), sds((2, 16, D + 128), BF), sds((32, 32, 128), BF)],
        [
            back.reshape(rows, D),
            g_all,
            cotangent.reshape(rows, D),
            probs,
            picked,
            normed,
            scale,
            wo_all,
            att,
            h2,
            dwx,
            q_t,
            k_t,
            v_t,
            lse,
            o_t,
            start,
            hid,
            cos,
            sin,
            wp_all,
            tok_mine,
        ],
        Reduce.SEMS + [DMA((16,))] * 6 + [DMA((32,))] * 2 + [DMA((4,))],
        2,
        [
            VM((rows, D), F32),
            VM((16, 64, rows), BF),
            VM((2, 16, 2, 16, D + 128), BF),
            VM((16, 2, 16, D + 128), BF),
            VM((64, length), BF),
            VM((64, length), F32),
            VM((2, 64, length), F32),
            VM((length, 64), BF),
            VM((length, 64), BF),
            VM((1, length), F32),
            VM((64, length), F32),
            VM((2, 64, length), BF),
            VM((32, 32, 128), BF),
            VM((8, 2, 2, 64, rows), BF),
        ]
        + Reduce.bufs(16, D + 128),
    )
    wg_sum = wg_all.reshape(2, 16, 32, 128).astype(F32).sum(axis=0).transpose(1, 0, 2)
    plain_query = wg_sum[:, :, :64].reshape(32, D)
    plain_key = wg_sum[:, 0::2, 64:].reshape(32, 512)
    plain_value = wg_sum[:, 1::2, 64:].reshape(32, 512)
    own_o = dwo_sum.reshape(32, D + 128).astype(F32)
    plain_router = own_o[:, D : D + E]
    expert_grads = dw_all.transpose(1, 2, 0, 3).astype(F32)
    plain_gate, plain_up = expert_grads[0], expert_grads[1]
    grad_attention_gain = (
        jnp.sum(plain_query * query_weight.astype(F32), axis=1)
        + jnp.sum(plain_key * key_matrix.astype(F32), axis=1)
        + jnp.sum(plain_value * value_matrix.astype(F32), axis=1)
    )
    grad_expert_gain = jnp.sum(
        plain_gate * gate_weight.astype(F32) + plain_up * up_weight.astype(F32), axis=(1, 2)
    ) + jnp.sum(plain_router * router_weight.astype(F32), axis=1)
    return (
        mixed.reshape(tokens.shape),
        grad_tokens.reshape(tokens.shape),
        grad_attention_gain,
        grad_expert_gain,
        plain_query * gain_first,
        plain_key * gain_first,
        plain_value * gain_first,
        own_o[:, :D],
        plain_router * gain_second,
        plain_gate * gain_second[..., None],
        plain_up * gain_second[..., None],
        expert_grads[2],
    )


def rms_scale(values):
    return lax.rsqrt(jnp.mean(values * values, axis=-1, keepdims=True) + EPSILON)


def apply_rotary(values, cosine_lookup, sine_lookup):
    halves = values.shape[-1] // 2
    first_half = values[..., :halves]
    second_half = values[..., halves:]
    return jnp.concatenate(
        [
            first_half * cosine_lookup - second_half * sine_lookup,
            second_half * cosine_lookup + first_half * sine_lookup,
        ],
        axis=-1,
    )


def unrotate(values, cosine_lookup, sine_lookup):
    halves = values.shape[-1] // 2
    first_half = values[..., :halves]
    second_half = values[..., halves:]
    return jnp.concatenate(
        [
            first_half * cosine_lookup + second_half * sine_lookup,
            second_half * cosine_lookup - first_half * sine_lookup,
        ],
        axis=-1,
    )


def block_mask(key_start, block_size, query_pos, query_seg, seg_block):
    key_pos = key_start + jnp.arange(block_size, dtype=jnp.int32)
    causal = key_pos[None, :] <= query_pos[:, None]
    same_doc = seg_block[:, None, :] == query_seg[:, :, None]
    return (causal[None] & same_doc)[:, None, None]


def attend_piece(running, pieces, first_key, queries, query_pos, query_seg, scaling):
    key_rows, value_rows, key_segments = pieces
    sequence_count, key_span = (key_rows.shape[0], key_rows.shape[1])
    block_size = math.gcd(key_span, 512)
    kv_heads, head_dim = (queries.shape[2], queries.shape[4])

    def advance(block_index, carried):
        top_score, denominator, numerator = carried
        offset = block_index * block_size
        key_block = lax.dynamic_slice_in_dim(key_rows, offset, block_size, 1).reshape(
            sequence_count, block_size, kv_heads, head_dim
        )
        value_block = lax.dynamic_slice_in_dim(value_rows, offset, block_size, 1).reshape(
            sequence_count, block_size, kv_heads, head_dim
        )
        seg_block = lax.dynamic_slice_in_dim(key_segments, offset, block_size, 1).astype(jnp.int32)
        allowed = block_mask(offset, block_size, query_pos, query_seg, seg_block)
        scores = (
            jnp.einsum("sqkgd,sjkd->skgqj", queries, key_block, preferred_element_type=jnp.float32)
            * scaling
        )
        fresh_top = jnp.maximum(top_score, jnp.max(jnp.where(allowed, scores, MASKED), axis=-1))
        weights = jnp.where(allowed, jnp.exp(scores - fresh_top[..., None]), 0.0)
        decay_factor = jnp.exp(top_score - fresh_top)
        denominator = denominator * decay_factor + jnp.sum(weights, axis=-1)
        numerator = numerator * decay_factor[..., None] + jnp.einsum(
            "skgqj,sjkd->skgqd",
            weights.astype(jnp.bfloat16),
            value_block,
            preferred_element_type=jnp.float32,
        )
        return (fresh_top, denominator, numerator)

    return lax.fori_loop(0, key_span // block_size, advance, running)


def attend_back(pieces, queries, query_pos, query_seg, grad_attn, log_total, row_delta, scaling):
    key_rows, value_rows, key_segments = pieces
    sequence_count, key_span, key_value_width = key_rows.shape
    block_size = math.gcd(key_span, 512)
    kv_heads, head_dim = (queries.shape[2], queries.shape[4])

    def advance(block_index, carried):
        grad_queries, gradient_couples = carried
        offset = block_index * block_size
        key_block = lax.dynamic_slice_in_dim(key_rows, offset, block_size, 1).reshape(
            sequence_count, block_size, kv_heads, head_dim
        )
        value_block = lax.dynamic_slice_in_dim(value_rows, offset, block_size, 1).reshape(
            sequence_count, block_size, kv_heads, head_dim
        )
        seg_block = lax.dynamic_slice_in_dim(key_segments, offset, block_size, 1).astype(jnp.int32)
        allowed = block_mask(offset, block_size, query_pos, query_seg, seg_block)
        scores = (
            jnp.einsum("sqkgd,sjkd->skgqj", queries, key_block, preferred_element_type=jnp.float32)
            * scaling
        )
        weights = jnp.where(allowed, jnp.exp(scores - log_total[..., None]), 0.0)
        grad_weights = jnp.einsum(
            "sqkgd,sjkd->skgqj", grad_attn, value_block, preferred_element_type=jnp.float32
        )
        grad_scores = (weights * (grad_weights - row_delta[..., None])).astype(jnp.bfloat16)
        grad_queries = grad_queries + jnp.einsum(
            "skgqj,sjkd->sqkgd", grad_scores, key_block, preferred_element_type=jnp.float32
        )
        grad_keys = (
            jnp.einsum(
                "skgqj,sqkgd->sjkd", grad_scores, queries, preferred_element_type=jnp.float32
            )
            * scaling
        )
        grad_values = jnp.einsum(
            "skgqj,sqkgd->sjkd",
            weights.astype(jnp.bfloat16),
            grad_attn,
            preferred_element_type=jnp.float32,
        )
        produced = jnp.concatenate(
            [
                grad_keys.reshape(sequence_count, block_size, key_value_width),
                grad_values.reshape(sequence_count, block_size, key_value_width),
            ],
            axis=-1,
        )
        return (
            grad_queries,
            lax.dynamic_update_slice_in_dim(gradient_couples, produced, offset, 1),
        )

    starting = (
        jnp.zeros(queries.shape, jnp.float32),
        jnp.zeros((sequence_count, key_span, 2 * key_value_width), jnp.float32),
    )
    grad_queries, gradient_couples = lax.fori_loop(0, key_span // block_size, advance, starting)
    return (grad_queries * scaling, gradient_couples)


def project_in(pieces, routed):
    gate_rows, up_rows = pieces
    return (
        jnp.einsum("erd,def->erf", routed, gate_rows, preferred_element_type=jnp.float32),
        jnp.einsum("erd,def->erf", routed, up_rows, preferred_element_type=jnp.float32),
    )


def project_out(down_rows, hidden):
    produced = jnp.einsum("erf,def->erd", hidden, down_rows, preferred_element_type=jnp.float32)
    return produced


def back_through_down(down_rows, grad_output):
    return jnp.einsum("erd,def->erf", grad_output, down_rows, preferred_element_type=jnp.float32)


def back_through_in(pieces, grad_gate, grad_up):
    gate_rows, up_rows = pieces
    produced = jnp.einsum(
        "erf,def->erd", grad_gate, gate_rows, preferred_element_type=jnp.float32
    ) + jnp.einsum("erf,def->erd", grad_up, up_rows, preferred_element_type=jnp.float32)
    return produced


def take_slots(slot_data, destination):
    experts, width = (slot_data.shape[0], slot_data.shape[-1])
    sequence_count, sequence_rows, picks = destination.shape
    flat = jnp.transpose(
        slot_data.reshape(experts, sequence_count, -1, width), (1, 0, 2, 3)
    ).reshape(sequence_count, -1, width)
    taken = jax.vmap(lambda table, spots: table[spots])(
        flat, destination.reshape(sequence_count, sequence_rows * picks)
    )
    return taken.reshape(sequence_count, sequence_rows, picks, width)


def place_slots(values, destination, experts, capacity):
    sequence_count, width = (values.shape[0], values.shape[-1])
    empty = jnp.zeros((sequence_count, experts * capacity, width), values.dtype)
    filled = jax.vmap(lambda table, spots, rows: table.at[spots].set(rows))(
        empty, destination.reshape(sequence_count, -1), values.reshape(sequence_count, -1, width)
    )
    return jnp.transpose(
        filled.reshape(sequence_count, experts, capacity, width), (1, 0, 2, 3)
    ).reshape(experts, sequence_count * capacity, width)


def any_seats(
    tokens,
    attention_gain,
    expert_gain,
    query_weight,
    key_matrix,
    value_matrix,
    output_weight,
    router_weight,
    gate_weight,
    up_weight,
    down_weight,
    routes,
    segments,
    rope_index,
    cotangent,
):
    sequence_count, sequence_rows = (tokens.shape[0], tokens.shape[1])
    queries_per_group = QUERY_HEADS // KEY_VALUE_HEADS
    key_value_width = KEY_VALUE_HEADS * HEAD_SIZE
    scaling = 1.0 / math.sqrt(HEAD_SIZE)
    experts_slots = E * CAP
    gathered = (
        lax.all_gather(attention_gain, ("row", "seq"), axis=0, tiled=True),
        lax.all_gather(expert_gain, ("row", "seq"), axis=0, tiled=True),
        lax.all_gather(query_weight, ("row", "seq"), axis=0, tiled=True),
        lax.all_gather(key_matrix, ("row", "seq"), axis=0, tiled=True),
        lax.all_gather(value_matrix, ("row", "seq"), axis=0, tiled=True),
        lax.all_gather(output_weight, ("row", "seq"), axis=0, tiled=True),
        lax.all_gather(router_weight, ("row", "seq"), axis=0, tiled=True),
    )
    gain_first = gathered[0].astype(jnp.float32)
    gain_second = gathered[1].astype(jnp.float32)
    full_query, full_key, full_value, full_output, full_router = gathered[2:]
    inputs = tokens.astype(jnp.float32)
    scale_first = rms_scale(inputs)
    normed_first = inputs * scale_first
    hidden_first = (normed_first * gain_first).astype(jnp.bfloat16)
    query_unrotated = jnp.einsum(
        "sqd,dc->sqc", hidden_first, full_query, preferred_element_type=jnp.float32
    )
    key_unrotated = jnp.einsum(
        "sqd,dc->sqc", hidden_first, full_key, preferred_element_type=jnp.float32
    )
    value_raw = jnp.einsum(
        "sqd,dc->sqc", hidden_first, full_value, preferred_element_type=jnp.float32
    )
    positions = lax.axis_index("seq") * sequence_rows + jnp.arange(sequence_rows, dtype=jnp.int32)
    factor = jnp.power(2.0, rope_index.astype(jnp.float32))
    angles = (positions.astype(jnp.float32)[None, :] / factor[:, None])[..., None] * frequencies(
        HEAD_SIZE
    )
    cosine_lookup = jnp.cos(angles)[:, :, None, :]
    sine_lookup = jnp.sin(angles)[:, :, None, :]
    query_turned = (
        apply_rotary(
            query_unrotated.reshape(sequence_count, sequence_rows, QUERY_HEADS, HEAD_SIZE),
            cosine_lookup,
            sine_lookup,
        )
        .astype(jnp.bfloat16)
        .reshape(sequence_count, sequence_rows, KEY_VALUE_HEADS, queries_per_group, HEAD_SIZE)
    )
    key_turned = (
        apply_rotary(
            key_unrotated.reshape(sequence_count, sequence_rows, KEY_VALUE_HEADS, HEAD_SIZE),
            cosine_lookup,
            sine_lookup,
        )
        .astype(jnp.bfloat16)
        .reshape(sequence_count, sequence_rows, key_value_width)
    )
    value_reduced = value_raw.astype(jnp.bfloat16)
    segment_low = segments.astype(jnp.float32).astype(jnp.bfloat16)
    statistic_shape = (sequence_count, KEY_VALUE_HEADS, queries_per_group, sequence_rows)
    starting = (
        jnp.full(statistic_shape, MASKED, jnp.float32),
        jnp.zeros(statistic_shape, jnp.float32),
        jnp.zeros(statistic_shape + (HEAD_SIZE,), jnp.float32),
    )
    attend = partial(
        attend_piece, queries=query_turned, query_pos=positions, query_seg=segments, scaling=scaling
    )
    top_score, denominator, numerator = attend(
        starting,
        (
            lax.all_gather(key_turned, "seq", axis=1, tiled=True),
            lax.all_gather(value_reduced, "seq", axis=1, tiled=True),
            lax.all_gather(segment_low, "seq", axis=1, tiled=True),
        ),
        jnp.int32(0),
    )
    attn_heads = numerator / denominator[..., None]
    log_total = top_score + jnp.log(denominator)
    attn_rows = jnp.transpose(attn_heads, (0, 3, 1, 2, 4))
    attn_low = attn_rows.astype(jnp.bfloat16).reshape(
        sequence_count, sequence_rows, QUERY_HEADS * HEAD_SIZE
    )
    branch = jnp.einsum("sqc,dc->sqd", attn_low, full_output, preferred_element_type=jnp.float32)
    residual = inputs + branch
    scale_second = rms_scale(residual)
    normed_second = residual * scale_second
    hidden_second = (normed_second * gain_second).astype(jnp.bfloat16)
    logits = jnp.einsum(
        "sqd,de->sqe", hidden_second, full_router, preferred_element_type=jnp.float32
    )
    router_probs = jax.nn.softmax(logits, axis=-1)
    picked = routes[..., None] == jnp.arange(E, dtype=jnp.int32)
    picked_int = picked.astype(jnp.int32).reshape(sequence_count, sequence_rows * K, E)
    earlier = jnp.cumsum(picked_int, axis=1, dtype=jnp.int32) - picked_int
    slot_ids = jnp.sum(earlier * picked_int, axis=-1, dtype=jnp.int32).reshape(
        sequence_count, sequence_rows, K
    )
    destination = routes * CAP + slot_ids
    chosen = destination[..., None] == jnp.arange(experts_slots, dtype=jnp.int32)
    gate_probs = jnp.sum(jnp.where(picked, router_probs[:, :, None, :], 0.0), axis=-1)
    dispatch = jnp.sum(chosen, axis=2, dtype=jnp.float32).reshape(
        sequence_count, sequence_rows, E, CAP
    )
    slot_rows = sequence_count * CAP
    routed = (
        jnp.einsum(
            "sqec,sqd->escd",
            dispatch.astype(jnp.bfloat16),
            hidden_second,
            preferred_element_type=jnp.float32,
        )
        .astype(jnp.bfloat16)
        .reshape(E, slot_rows, MODEL_WIDTH)
    )
    grad_mixed = cotangent.astype(jnp.float32)
    grad_slot_values = (gate_probs[..., None] * grad_mixed[:, :, None, :]).astype(jnp.bfloat16)
    grad_expert = place_slots(grad_slot_values, destination, E, CAP)
    groups = 4
    width = E // groups

    def some_experts(_, given):
        rows, grads, gate_part, up_part, down_part = given
        pieces = (
            lax.all_gather(gate_part, ("row", "seq"), axis=0, tiled=True),
            lax.all_gather(up_part, ("row", "seq"), axis=0, tiled=True),
        )
        down_rows = lax.all_gather(down_part, ("row", "seq"), axis=0, tiled=True)
        gate_pre, up_pre = project_in(pieces, routed=rows)
        hidden_low = (jax.nn.silu(gate_pre) * up_pre).astype(jnp.bfloat16)
        expert_out = project_out(down_rows, hidden=hidden_low)
        grad_hidden = back_through_down(down_rows, grad_output=grads)
        sigmoid_gate = jax.nn.sigmoid(gate_pre)
        grad_gate = (
            grad_hidden * up_pre * sigmoid_gate * (1.0 + gate_pre * (1.0 - sigmoid_gate))
        ).astype(jnp.bfloat16)
        grad_up = (grad_hidden * (gate_pre * sigmoid_gate)).astype(jnp.bfloat16)
        grad_routed = back_through_in(pieces, grad_gate=grad_gate, grad_up=grad_up)
        made = [
            lax.psum_scatter(
                jnp.einsum("erd,erf->def", left, right, preferred_element_type=jnp.float32),
                ("row", "seq"),
                scatter_dimension=0,
                tiled=True,
            )
            for left, right in ((rows, grad_gate), (rows, grad_up), (grads, hidden_low))
        ]
        return None, (expert_out, grad_routed, *made)

    def grouped(weight):
        return jnp.moveaxis(weight.reshape(weight.shape[0], groups, width, F), 1, 0)

    _, (expert_out, grad_routed, *expert_grads) = lax.scan(
        some_experts,
        None,
        (
            routed.reshape(groups, width, slot_rows, MODEL_WIDTH),
            grad_expert.reshape(groups, width, slot_rows, MODEL_WIDTH),
            grouped(gate_weight),
            grouped(up_weight),
            grouped(down_weight),
        ),
    )
    expert_out = expert_out.reshape(E, slot_rows, MODEL_WIDTH)
    grad_routed = grad_routed.reshape(E, slot_rows, MODEL_WIDTH)
    grad_gate_weight, grad_up_weight, grad_down_weight = [
        jnp.moveaxis(grad, 0, 1).reshape(gate_weight.shape) for grad in expert_grads
    ]
    taken_out = take_slots(expert_out, destination)
    expert_mix = jnp.sum(gate_probs[..., None] * taken_out, axis=2)
    mixed = (residual + expert_mix).astype(jnp.bfloat16)
    grad_gates = jnp.sum(taken_out * grad_mixed[:, :, None, :], axis=-1)
    grad_probs = jnp.sum(jnp.where(picked, grad_gates[..., None], 0.0), axis=2)
    grad_logits = (
        router_probs * (grad_probs - jnp.sum(router_probs * grad_probs, axis=-1, keepdims=True))
    ).astype(jnp.bfloat16)
    grad_second = jnp.sum(take_slots(grad_routed, destination), axis=2) + jnp.einsum(
        "sqe,de->sqd", grad_logits, full_router, preferred_element_type=jnp.float32
    )
    grad_gain_second = jnp.sum(grad_second * normed_second, axis=(0, 1))
    scaled_second = grad_second * gain_second
    grad_residual = grad_mixed + scale_second * (
        scaled_second
        - normed_second * jnp.mean(scaled_second * normed_second, axis=-1, keepdims=True)
    )
    grad_branch = grad_residual.astype(jnp.bfloat16)
    grad_attn = (
        jnp.einsum("sqd,dc->sqc", grad_branch, full_output, preferred_element_type=jnp.float32)
        .astype(jnp.bfloat16)
        .reshape(sequence_count, sequence_rows, KEY_VALUE_HEADS, queries_per_group, HEAD_SIZE)
    )
    row_delta = jnp.transpose(
        jnp.sum(grad_attn.astype(jnp.float32) * attn_rows, axis=-1), (0, 2, 3, 1)
    )
    keys_back = (
        lax.all_gather(key_turned, "seq", axis=1, tiled=True),
        lax.all_gather(value_reduced, "seq", axis=1, tiled=True),
        lax.all_gather(segment_low, "seq", axis=1, tiled=True),
    )
    grad_query_rot, grad_pair_rows = attend_back(
        keys_back, query_turned, positions, segments, grad_attn, log_total, row_delta, scaling
    )
    gradient_couples = lax.psum_scatter(grad_pair_rows, "seq", scatter_dimension=1, tiled=True)
    grad_query = (
        unrotate(
            grad_query_rot.reshape(sequence_count, sequence_rows, QUERY_HEADS, HEAD_SIZE),
            cosine_lookup,
            sine_lookup,
        )
        .astype(jnp.bfloat16)
        .reshape(sequence_count, sequence_rows, QUERY_HEADS * HEAD_SIZE)
    )
    grad_key = (
        unrotate(
            gradient_couples[..., :key_value_width].reshape(
                sequence_count, sequence_rows, KEY_VALUE_HEADS, HEAD_SIZE
            ),
            cosine_lookup,
            sine_lookup,
        )
        .astype(jnp.bfloat16)
        .reshape(sequence_count, sequence_rows, key_value_width)
    )
    grad_value = gradient_couples[..., key_value_width:].astype(jnp.bfloat16)
    grad_first = (
        jnp.einsum("sqc,dc->sqd", grad_query, full_query, preferred_element_type=jnp.float32)
        + jnp.einsum("sqc,dc->sqd", grad_key, full_key, preferred_element_type=jnp.float32)
        + jnp.einsum("sqc,dc->sqd", grad_value, full_value, preferred_element_type=jnp.float32)
    )
    grad_gain_first = jnp.sum(grad_first * normed_first, axis=(0, 1))
    scaled_first = grad_first * gain_first
    grad_tokens = grad_residual + scale_first * (
        scaled_first - normed_first * jnp.mean(scaled_first * normed_first, axis=-1, keepdims=True)
    )
    attention_grads = lax.psum_scatter(
        jnp.concatenate(
            [
                jnp.einsum(
                    "sqd,sqc->dc", hidden_first, grad_query, preferred_element_type=jnp.float32
                ),
                jnp.einsum(
                    "sqd,sqc->dc", hidden_first, grad_key, preferred_element_type=jnp.float32
                ),
                jnp.einsum(
                    "sqd,sqc->dc", hidden_first, grad_value, preferred_element_type=jnp.float32
                ),
                jnp.einsum(
                    "sqd,sqc->dc", grad_branch, attn_low, preferred_element_type=jnp.float32
                ),
                jnp.einsum(
                    "sqd,sqe->de", hidden_second, grad_logits, preferred_element_type=jnp.float32
                ),
                grad_gain_first[:, None],
                grad_gain_second[:, None],
            ],
            axis=1,
        ),
        ("row", "seq"),
        scatter_dimension=0,
        tiled=True,
    )
    query_cols = QUERY_HEADS * HEAD_SIZE
    edge_two = query_cols + key_value_width
    edge_three = edge_two + key_value_width
    edge_four = edge_three + query_cols
    edge_five = edge_four + E
    return (
        mixed,
        grad_tokens,
        attention_grads[:, edge_five],
        attention_grads[:, edge_five + 1],
        attention_grads[:, :query_cols],
        attention_grads[:, query_cols:edge_two],
        attention_grads[:, edge_two:edge_three],
        attention_grads[:, edge_three:edge_four],
        attention_grads[:, edge_four:edge_five],
        grad_gate_weight,
        grad_up_weight,
        grad_down_weight,
    )


def solution(mesh):
    first = P(("row", "seq"))
    in_specs = (
        (P("row", "seq", None), first, first)
        + (P(("row", "seq"), None),) * 5
        + (P(("row", "seq"), None, None),) * 3
        + (P("row", "seq", None), P("row", "seq"), P("row"), P("row", "seq", None))
    )
    out_specs = (
        (P("row", "seq", None), P("row", "seq", None), first, first)
        + (P(("row", "seq"), None),) * 5
        + (P(("row", "seq"), None, None),) * 3
    )
    body = sixteen_seats if dict(mesh.shape) == {"row": 2, "seq": 16} else any_seats
    return jax.shard_map(body, mesh=mesh, in_specs=in_specs, out_specs=out_specs, check_vma=False)
```

```python
from functools import partial
import math

import jax
import jax.numpy as jnp
from jax import lax
from jax.experimental import pallas as pl
from jax.experimental.pallas import tpu as pltpu
from jax.sharding import PartitionSpec as P

MODEL_WIDTH = 1024
QUERY_HEADS = 16
KEY_VALUE_HEADS = 8
HEAD_SIZE = 64
F = 512
E = 16
K = 8
CAP = 96

EPSILON = 1e-05
ROPE_BASE = 10000.0
MASKED = -1e30
MESH = pl.DeviceIdType.MESH
VM = pltpu.VMEM
BF = jnp.bfloat16
F32 = jnp.float32
DMA = pltpu.SemaphoreType.DMA
UP, DOWN, SIDE, CORE = range(4)
VMEM_LIMIT = 60 * 1024 * 1024

NN = (((1,), (0,)), ((), ()))
NT = (((1,), (1,)), ((), ()))
TN = (((0,), (0,)), ((), ()))


def dot(a, b, dims=NN):
    return lax.dot_general(a, b, dims, preferred_element_type=F32)


def when(cond, f):
    if cond is None:
        f()
    else:
        pl.when(cond)(f)


def both(a, b):
    if a is None:
        return b
    return a if b is None else a & b


def place():
    x = lax.axis_index("row")
    s = lax.axis_index("seq")
    return x, s, s // 4, (s // 2) % 2, s % 2


def seat(z, y, c):
    return z * 4 + y * 2 + c


def remote(src, dst, send, recv, dev):
    return pltpu.make_async_remote_copy(src, dst, send, recv, device_id=dev, device_id_type=MESH)


def barrier_all():
    x, s = lax.axis_index("row"), lax.axis_index("seq")
    sem = pltpu.get_barrier_semaphore()
    for k in range(1, 16):
        pl.semaphore_signal(sem, inc=1, device_id=(x, (s + k) % 16), device_id_type=MESH)
    for k in range(16):
        pl.semaphore_signal(sem, inc=1, device_id=(1 - x, (s + k) % 16), device_id_type=MESH)
    pl.semaphore_wait(sem, 31)


def barrier_row(partner=False):
    x, s = lax.axis_index("row"), lax.axis_index("seq")
    sem = pltpu.get_barrier_semaphore()
    for k in range(1, 16):
        pl.semaphore_signal(sem, inc=1, device_id=(x, (s + k) % 16), device_id_type=MESH)
    if partner:
        pl.semaphore_signal(sem, inc=1, device_id=(1 - x, s), device_id_type=MESH)
    pl.semaphore_wait(sem, 16 if partner else 15)


def barrier_near():
    x, s, z, y, c = place()
    sem = pltpu.get_barrier_semaphore()
    for cond, dev in (
        (z < 3, (x, seat(z + 1, y, c))),
        (z > 0, (x, seat(z - 1, y, c))),
        (None, (x, seat(z, 1 - y, c))),
        (None, (x, seat(z, y, 1 - c))),
    ):
        when(cond, lambda dev=dev: pl.semaphore_signal(sem, inc=1, device_id=dev, device_id_type=MESH))
    pl.semaphore_wait(sem, 2 + (z < 3).astype(jnp.int32) + (z > 0).astype(jnp.int32))


QB = 256


def lane_block(i, size=QB):
    return pl.ds(pl.multiple_of(i * size, size), size)


class Gather:
    def __init__(self, own, at, send, recv):
        self.own, self.at, self.send, self.recv = own, at, send, recv
        self.ending = False
        self.x, self.s, self.z, self.y, self.c = place()

    def device(self, k):
        x, z, y, c = self.x, self.z, self.y, self.c
        return {
            UP: (x, seat(z + 1, y, c)),
            DOWN: (x, seat(z - 1, y, c)),
            SIDE: (x, seat(z, 1 - y, c)),
            CORE: (x, seat(z, y, 1 - c)),
        }[k]

    def copy(self, src, k, own=False):
        ref = self.own if own else self.at(src)
        return remote(ref, self.at(src), self.send.at[src, k], self.recv.at[src], self.device(k))

    def go(self, src, k, cond=None, own=False):
        if k == UP:
            cond = both(cond, self.z < 3)
        if k == DOWN:
            cond = both(cond, self.z > 0)
        act = (lambda c: c.wait_send()) if self.ending else (lambda c: c.start())
        when(cond, lambda: act(self.copy(src, k, own)))

    def wait(self, src, cond=None):
        if self.ending:
            return
        when(cond, lambda: self.copy(src, SIDE).wait_recv())

    def sides(self, t):
        if t == 0:
            return ((None, self.z, None),)
        return ((self.z - t >= 0, self.z - t, UP), (self.z + t <= 3, self.z + t, DOWN))

    def begin(self):
        for k in (UP, DOWN, SIDE, CORE):
            self.go(self.s, k, own=self.own is not None)

    def line(self, t):
        for cond, zz, k in self.sides(t):
            src = seat(zz, self.y, self.c)
            self.wait(src, cond)
            for way in (k, SIDE, CORE):
                self.go(src, way, cond)

    def over(self, t):
        for cond, zz, _ in self.sides(t):
            src = seat(zz, 1 - self.y, self.c)
            self.wait(src, cond)
            self.go(src, CORE, cond)

    def done(self, t):
        for cond, zz, _ in self.sides(t):
            for yy in range(2):
                self.wait(seat(zz, yy, 1 - self.c), cond)

    def end(self):
        self.ending = True
        self.begin()
        for t in range(4):
            if t:
                self.line(t)
            self.over(t)


GATHER_SEMS = [DMA((16, 4)), DMA((16,))]


class Exchange:
    def __init__(self, src, dst, send, recv, wide=False):
        self.x, self.s, self.z, self.y, self.c = place()
        self.wide, self.n = wide, 32 if wide else 16
        self.src, self.dst, self.send, self.recv = src, dst, send, recv

    def seat(self, k, back=False):
        dz = (k // 4) % 4
        if back:
            dz = (4 - dz) % 4
        x = (self.x + k // 16) % 2
        s = seat((self.z + dz) % 4, (self.y + k // 2) % 2, (self.c + k) % 2)
        return x, s

    def index(self, seat_of):
        x, s = seat_of
        return x * 16 + s if self.wide else s

    def copy(self, k):
        to, me = self.seat(k), self.index((self.x, self.s))
        return remote(self.src(self.index(to)), self.dst(me), self.send.at[k], self.recv.at[k], to)

    def begin(self, ks=None):
        for k in range(self.n) if ks is None else ks:
            if k == 0:
                me = self.index((self.x, self.s))
                self.local = pltpu.make_async_copy(self.src(me), self.dst(me), self.recv.at[0])
                self.local.start()
            else:
                self.copy(k).start()

    def arrive(self, k):
        frm = self.seat(k, back=True)
        me = self.index((self.x, self.s))
        remote(self.src(me), self.dst(self.index(frm)), self.send.at[k], self.recv.at[k], frm).wait_recv()
        return self.index(frm)

    def end(self, arrivals=True):
        self.local.wait()
        for k in range(1, self.n):
            if arrivals:
                self.arrive(k)
            self.copy(k).wait_send()


class Slices:
    def __init__(self, src, got, send, recv):
        self.x, self.s, self.z, self.y, self.c = place()
        self.src, self.got, self.send, self.recv = src, got, send, recv

    def block(self, pair):
        return self.src.at[:, lane_block(pair, 256)]

    def copy(self, k):
        z, y = (self.z + k // 2) % 4, (self.y + k) % 2
        dst = self.got.at[self.x, self.s // 2, self.c]
        return remote(self.block(z * 2 + y), dst, self.send.at[k], self.recv.at[k], (self.x, seat(z, y, self.c)))

    def begin(self):
        self.local = pltpu.make_async_copy(
            self.block(self.s // 2), self.got.at[self.x, self.s // 2, self.c], self.recv.at[0]
        )
        self.local.start()
        for k in range(1, 8):
            self.copy(k).start()

    def over_x(self):
        ref = self.got.at[self.x, :, self.c]
        return remote(ref, ref, self.send.at[8], self.recv.at[8], (1 - self.x, self.s))

    def over_core(self, k):
        ref = self.got.at[self.x if k == 9 else 1 - self.x, :, self.c]
        return remote(ref, ref, self.send.at[k], self.recv.at[k], (self.x, seat(self.z, self.y, 1 - self.c)))

    def share(self):
        self.local.wait()
        for k in range(1, 8):
            z, y = (self.z + 4 - k // 2) % 4, (self.y + k) % 2
            dst = self.got.at[self.x, z * 2 + y, self.c]
            remote(
                self.block(z * 2 + y), dst, self.send.at[k], self.recv.at[k], (self.x, seat(z, y, self.c))
            ).wait_recv()
        self.over_x().start()
        self.over_core(9).start()

    def end(self):
        self.over_x().wait_recv()
        self.over_core(10).start()
        self.over_core(9).wait_recv()
        self.over_core(10).wait_recv()
        for k in range(1, 8):
            self.copy(k).wait_send()
        self.over_x().wait_send()
        self.over_core(9).wait_send()
        self.over_core(10).wait_send()


ANY = pl.ANY
SM = pltpu.SMEM


def comm_call(body, outs, ins, sems, cid, scratch=(), out_spaces=None, in_spaces=None):
    return pl.pallas_call(
        body,
        out_shape=outs,
        in_specs=[pl.BlockSpec(memory_space=m) for m in in_spaces or [VM] * len(ins)],
        out_specs=[pl.BlockSpec(memory_space=m) for m in out_spaces or [VM] * len(outs)],
        scratch_shapes=list(scratch) + list(sems),
        compiler_params=pltpu.CompilerParams(
            collective_id=cid, has_side_effects=True, vmem_limit_bytes=VMEM_LIMIT
        ),
    )(*ins)


def sds(shape, dtype):
    return jax.ShapeDtypeStruct(shape, dtype)


def allowed_mask(first_key, first_query, start_row):
    key = first_key + lax.broadcasted_iota(jnp.int32, (QB, QB), 0)
    query = first_query + lax.broadcasted_iota(jnp.int32, (QB, QB), 1)
    return (key <= query) & (key >= start_row)


SCORE = math.log2(math.e) / math.sqrt(HEAD_SIZE)


def column(line):
    n = line.shape[1]
    same = lax.broadcasted_iota(jnp.int32, (n, n), 0) == lax.broadcasted_iota(jnp.int32, (n, n), 1)
    return jnp.sum(jnp.where(same, jnp.broadcast_to(line.astype(F32), (n, n)), 0.0), axis=1, keepdims=True)


def front(
    tok, query_w, key_w, value_w, out_w, router_w, gate_w, up_w, down_w, gain_a, gain_e, seg, routes, cot, rope, freq,
    hid, wexp, wo_all, cot_all, q_t, k_t, v_t, o_t, lse, start, cos, sin,
    residual, normed, scale_out, h2, att, probs, picked, p_t, wperm,
    wo, w3, spread, seg_mine, tok_all, w_mine, seg_all, o_low, att_t, k_n, w_t, hid_v, wo_v,
    t_send, t_recv, o_send, o_recv, c_send, c_recv, w_send, w_recv, g_send, g_recv,
    a_send, a_recv, e_send, e_recv, x_send, x_recv, x_sem,
):
    x, s, z, y, c = place()
    rows, width = tok.shape
    length = hid.shape[0]
    barrier_all()
    tokens = Gather(tok, lambda src: tok_all.at[src], t_send, t_recv)
    tokens.begin()
    keep_tok = pltpu.make_async_copy(tok, tok_all.at[s], x_sem.at[2])
    keep_tok.start()
    seg_mine[...] = jnp.broadcast_to(seg[...], seg_mine.shape)
    documents = Exchange(lambda r: seg_mine, lambda r: seg_all.at[r], g_send, g_recv)
    documents.begin()
    by_first = column(gain_a[...])
    for j in range(8):
        wperm[:, 256 * j : 256 * j + 128] = (query_w[:, 128 * j : 128 * j + 128].astype(F32) * by_first).astype(BF)
        pair = [ref[:, 64 * j : 64 * j + 64].astype(F32) for ref in (key_w, value_w)]
        wperm[:, 256 * j + 128 : 256 * j + 256] = (jnp.concatenate(pair, axis=1) * by_first).astype(BF)
    slices = Slices(wperm, w_mine, w_send, w_recv)
    slices.begin()
    by_second = column(gain_e[...])
    wo[:, 0:width] = out_w[...]
    router = (router_w[...].astype(F32) * by_second).astype(F32)
    wo[:, width : width + 128] = jnp.concatenate([router, jnp.zeros((32, 128 - E), F32)], axis=1).astype(BF)
    over = remote(wo, wo_v.at[x, s], x_sem.at[0], x_sem.at[1], (1 - x, s))
    over.start()
    keep = pltpu.make_async_copy(wo, wo_v.at[x, s], x_sem.at[3])
    keep.start()
    for m, ref in enumerate((gate_w, up_w, down_w)):
        plain = ref[...].astype(F32).reshape(32 * E, F)
        for b in range(F // 128):
            lanes = slice(b * 128, b * 128 + 128)
            spread[b] = plain[:, lanes]
            for e in range(E):
                part = spread[b, pl.ds(e, 32, stride=E), :]
                w3[e, m, :, lanes] = (part * by_second if m < 2 else part).astype(BF)
    weights = Exchange(lambda e: w3.at[e], lambda r: wexp.at[:, x * 16 + r], e_send, e_recv)
    weights.begin(range(4))
    def cross(k, begin=True):
        row = weights.index(weights.seat(k, back=True))
        if begin and k:
            weights.arrive(k)
        src = w3.at[s] if k == 0 else wexp.at[:, x * 16 + row]
        copy = remote(src, wexp.at[:, x * 16 + row], x_send.at[k], x_recv.at[k], (1 - x, s))
        if begin:
            copy.start()
        else:
            copy.wait_send()
            remote(src, wexp.at[:, (1 - x) * 16 + row], x_send.at[k], x_recv.at[k], (1 - x, s)).wait_recv()

    factor = jnp.exp2(rope[0].astype(F32))
    for b in range(length // 128):
        position = (b * 128 + lax.broadcasted_iota(jnp.int32, (32, 128), 1)).astype(F32)
        angle = position / factor * freq[...]
        cos[:, b * 128 : b * 128 + 128] = jnp.cos(angle)
        sin[:, b * 128 : b * 128 + 128] = jnp.sin(angle)
    tokens.over(0)
    tokens.line(1)
    slices.share()
    tokens.over(1)
    tokens.line(2)
    keep.wait()
    remote(wo, wo_v.at[1 - x, s], x_sem.at[0], x_sem.at[1], (1 - x, s)).wait_recv()
    outw = Gather(None, lambda src: wo_v.at[:, src], o_send, o_recv)
    outw.begin()
    for k in range(4):
        cross(k)
    slices.end()
    w_t[...] = jnp.transpose(w_mine[...].reshape(width, 256).astype(F32)).astype(BF)
    tokens.over(2)
    tokens.line(3)
    outw.over(0)
    outw.line(1)
    documents.end()
    numbers = seg_all[:, 0, :]
    ends = [jnp.sum((numbers < n).astype(jnp.int32)) for n in (1, 2)]
    for b in range(16):
        line = numbers[b : b + 1]
        start[:, b * 128 : b * 128 + 128] = jnp.where(line == 0, 0, jnp.where(line == 1, ends[0], ends[1]))
    tokens.over(3)
    outw.over(1)
    outw.line(2)
    weights.begin(range(4, 8))
    for t in range(4):
        tokens.done(t)
    keep_tok.wait()

    def project(i, _):
        cols = lane_block(i, 512)
        values = tok_all[pl.ds(i * 4, 4)].reshape(512, width).astype(F32)
        scale = lax.rsqrt(jnp.mean(values * values, axis=-1, keepdims=True) + EPSILON)
        hidden = (values * scale).astype(BF)
        hid_v[cols, :] = hidden
        made = dot(w_t[...], hidden, NT)
        co, si = cos[:, cols], sin[:, cols]
        own = jnp.where(c == 0, made[0:64], made[64:128])
        for ref, part in ((q_t, own), (k_t, made[128:192])):
            a, b = part[:32], part[32:]
            ref[0:32, cols] = (a * co - b * si).astype(BF)
            ref[32:64, cols] = (b * co + a * si).astype(BF)
        v_t[:, cols] = made[192:256].astype(BF)
        k_n[cols, :] = jnp.transpose(k_t[:, cols].astype(F32)).astype(BF)
        return 0

    lax.fori_loop(0, length // 512, project, 0)
    keep_hid = pltpu.make_async_copy(hid_v, hid, x_sem.at[4])
    keep_hid.start()
    outw.over(2)
    outw.line(3)
    weights.begin(range(8, 12))

    def query_block(i, _):
        cols = lane_block(i)
        queries = q_t[:, cols]
        begin = start[:, cols]

        def key_block(j, carried):
            top, total, acc = carried
            keys = lane_block(j)
            scores = dot(k_n[keys, :], queries) * SCORE
            scores = jnp.where(allowed_mask(j * QB, i * QB, begin), scores, MASKED)
            fresh = jnp.maximum(top, jnp.max(scores, axis=0, keepdims=True))
            powers = jnp.exp2(scores - fresh)
            decay = jnp.exp2(top - fresh)
            total = total * decay + jnp.sum(powers, axis=0, keepdims=True)
            acc = acc * decay + dot(v_t[:, keys], powers.astype(BF))
            return fresh, total, acc

        top, total, acc = lax.fori_loop(
            0,
            i + 1,
            key_block,
            (jnp.full((1, QB), MASKED, F32), jnp.zeros((1, QB), F32), jnp.zeros((HEAD_SIZE, QB), F32)),
        )
        out = acc / total
        o_t[:, cols] = out
        o_low[:, cols] = out.astype(BF)
        lse[:, cols] = top + jnp.log2(total)
        return 0

    blocks = length // QB
    cut = (5 * blocks) // 8
    lax.fori_loop(0, cut, query_block, 0)
    outw.over(3)
    for k in range(4, 8):
        cross(k)
    lax.fori_loop(cut, blocks, query_block, 0)
    heads = Exchange(lambda t: o_low.at[:, lane_block(t, 128)], lambda h: att_t.at[h], a_send, a_recv)
    heads.begin()
    weights.begin(range(12, 16))
    cots = Gather(cot, lambda src: cot_all.at[src], c_send, c_recv)
    cots.begin()
    keep_cot = pltpu.make_async_copy(cot, cot_all.at[s], x_sem.at[6])
    keep_cot.start()
    for t in range(4):
        outw.done(t)
    keep_wo = pltpu.make_async_copy(wo_v, wo_all, x_sem.at[5])
    keep_wo.start()
    for k in range(8, 12):
        cross(k)
    heads.end()
    cots.over(0)
    cots.line(1)

    att[...] = jnp.transpose(att_t[...].reshape(width, rows).astype(F32)).astype(BF)
    res = tok[...].astype(F32) + dot(att[...], wo_v[:, :, :, 0:width].reshape(width, width), NT)
    residual[...] = res
    scale = lax.rsqrt(jnp.mean(res * res, axis=-1, keepdims=True) + EPSILON)
    norm = res * scale
    normed[...] = norm
    scale_out[...] = jnp.broadcast_to(scale, scale_out.shape)
    hidden = norm.astype(BF)
    h2[...] = hidden
    lanes = lax.broadcasted_iota(jnp.int32, (128, 128), 1)
    logits = jnp.where(lanes < E, dot(hidden, wo_v[:, :, :, width : width + 128].reshape(width, 128)), MASKED)
    top = jnp.max(logits, axis=-1, keepdims=True)
    powers = jnp.exp(logits - top)
    prob = powers / jnp.sum(powers, axis=-1, keepdims=True)
    probs[...] = prob
    mask = jnp.zeros((128, 128), F32)
    for k in range(K):
        mask = mask + jnp.where(lanes == routes[:, k : k + 1], 1.0, 0.0)
    picked[...] = mask
    p_t[...] = jnp.transpose(prob * mask)[0:E, :]

    cots.over(1)
    cots.line(2)
    for k in range(12, 16):
        cross(k)
    cots.over(2)
    cots.line(3)
    cots.over(3)
    for t in range(4):
        cots.done(t)
    weights.end(arrivals=False)
    for k in range(16):
        cross(k, begin=False)
    for g in (tokens, outw, cots):
        g.end()
    over.wait_send()
    for copy in (keep_hid, keep_wo, keep_cot):
        copy.wait()


class Reduce:
    def __init__(self, part, out, bufs, sems):
        self.part, self.out = part, out
        self.r1, self.ra, self.ua, self.da = bufs
        self.s1, self.q1, self.sa, self.qa, self.su, self.qu, self.sd, self.qd = sems
        self.x, self.s, self.z, self.y, self.c = place()

    @staticmethod
    def bufs(rows, width):
        return [VM((4, 2, rows, width), BF)] + [VM((4, rows, width), BF)] * 3

    SEMS = [DMA((4, 2))] * 2 + [DMA((4,))] * 6

    def add(self, dst, src):
        dst[...] = (dst[...].astype(F32) + src[...].astype(F32)).astype(BF)

    def first(self, zz, yy):
        return remote(
            self.part.at[seat(zz, yy, 1 - self.c)],
            self.r1.at[zz, yy],
            self.s1.at[zz, yy],
            self.q1.at[zz, yy],
            (self.x, seat(self.z, self.y, 1 - self.c)),
        )

    def side(self, zz):
        return remote(
            self.r1.at[zz, 1 - self.y],
            self.ra.at[zz],
            self.sa.at[zz],
            self.qa.at[zz],
            (self.x, seat(self.z, 1 - self.y, self.c)),
        )

    def line(self, zz, up):
        z, y, c = self.z, self.y, self.c
        if up:
            return remote(self.ra.at[zz], self.ua.at[zz], self.su.at[zz], self.qu.at[zz], (self.x, seat(z + 1, y, c)))
        return remote(self.ra.at[zz], self.da.at[zz], self.sd.at[zz], self.qd.at[zz], (self.x, seat(z - 1, y, c)))

    def order(self):
        z = self.z
        for t in (3, 2, 1):
            yield z + t <= 3, z + t, True
            yield z - t >= 0, z - t, False
        yield None, z, None

    def begin_plane(self, zz, cond=None):
        for yy in range(2):
            when(cond, lambda: self.first(zz, yy).start())

    def begin(self):
        for cond, zz, _ in self.order():
            self.begin_plane(zz, cond)

    def fold(self, zz, cond=None):
        def go():
            for yy in range(2):
                self.first(zz, yy).wait_recv()
                self.add(self.r1.at[zz, yy], self.part.at[seat(zz, yy, self.c)])
            self.side(zz).start()

        when(cond, go)

    def flow(self):
        z = self.z
        for cond, zz, up in self.order():

            def go():
                self.side(zz).wait_recv()
                self.add(self.ra.at[zz], self.r1.at[zz, self.y])
                if up is None:
                    return

                def take():
                    self.line(zz, up).wait_recv()
                    self.add(self.ra.at[zz], (self.ua if up else self.da).at[zz])

                pl.when(z > 0 if up else z < 3)(take)
                self.line(zz, up).start()

            when(cond, go)
        for up, cond in ((True, z > 0), (False, z < 3)):

            def take():
                self.line(z, up).wait_recv()
                self.add(self.ra.at[z], (self.ua if up else self.da).at[z])

            when(cond, take)
        self.out[...] = self.ra[z]

    def run(self):
        for cond, zz, _ in self.order():
            self.fold(zz, cond)
        self.flow()

    def end(self):
        for cond, zz, up in self.order():
            for yy in range(2):
                when(cond, lambda: self.first(zz, yy).wait_send())
            when(cond, lambda: self.side(zz).wait_send())
            if up is not None:
                when(cond, lambda: self.line(zz, up).wait_send())


NBUF = 4
NSEM = 8
TB = 512


def middle(
    h2, p_t, cot_in, wexp_in, residual,
    back, mixed, g_all, dwx,
    h_all, p_all, cot, wexp, backp, mixp, mix, gg, dw, acc,
    *rest,
):
    bufs_a, bufs_b = rest[:NBUF], rest[NBUF : 2 * NBUF]
    sems = rest[2 * NBUF :]
    h_send, h_recv, p_send, p_recv, g_send, g_recv, x_sem = sems[2 * NSEM :]
    x, s, z, y, c = place()
    loads = [
        pltpu.make_async_copy(wexp_in, wexp, x_sem.at[2]),
        pltpu.make_async_copy(cot_in, cot, x_sem.at[3]),
    ]
    for copy in loads:
        copy.start()
    barrier_row(partner=True)
    hidden = Gather(h2, lambda src: h_all.at[src], h_send, h_recv)
    hidden.begin()
    keep = pltpu.make_async_copy(h2, h_all.at[s], x_sem.at[4])
    keep.start()
    minor = Exchange(lambda r: p_t, lambda r: p_all.at[r], p_send, p_recv)
    minor.begin()
    one = Reduce(backp, back, bufs_a, sems[:NSEM])
    two = Reduce(mixp, mix, bufs_b, sems[NSEM : 2 * NSEM])
    acc[...] = jnp.zeros(acc.shape, F32)
    hidden.over(0)
    keep.wait()
    minor.end()
    for copy in loads:
        copy.wait()
    hidden.done(0)
    hidden.line(1)
    far = z // 2
    order = (z, z + 1 - 2 * far, 2 - 2 * z + 5 * far, 3 - 3 * far)
    width = h2.shape[1]
    rows = h2.shape[0]

    def chunk(i, _):
        zz = jnp.where(i == 0, order[0], jnp.where(i == 1, order[1], jnp.where(i == 2, order[2], order[3])))

        @pl.when(i == 1)
        def _():
            hidden.over(1)
            hidden.done(1)
            hidden.line(2)
            one.fold(order[0])

        @pl.when(i == 2)
        def _():
            hidden.over(2)
            hidden.done(2)
            hidden.line(3)
            one.fold(order[1])

        @pl.when(i == 3)
        def _():
            hidden.over(3)
            hidden.done(3)
            one.fold(order[2])

        four = pl.ds(zz * 4, 4)
        some = h_all[four].reshape(4 * rows, width)
        grad = cot[four].reshape(4 * rows, width)
        cols = [jnp.broadcast_to(p_all[zz * 4 + b, pl.ds(s, 1), :], (128, 128)) for b in range(4)]
        prob = jnp.concatenate([jnp.transpose(v)[:, 0:1] for v in cols], axis=0)
        gate = dot(some, wexp[0])
        up = dot(some, wexp[1])
        sig = 1.0 / (1.0 + jnp.exp(-gate))
        silu = gate * sig
        low = (silu * up).astype(BF)
        moved = dot(grad, wexp[2])
        seen = jnp.sum(low.astype(F32) * moved, axis=-1, keepdims=True)
        for b in range(4):
            line = jnp.transpose(jnp.broadcast_to(seen[b * 128 : b * 128 + 128], (128, 128)))[0:8]
            gg[zz * 4 + b] = line
        grad_hidden = moved * prob
        grad_gate = (grad_hidden * up * (sig * (1.0 + gate * (1.0 - sig)))).astype(BF)
        grad_up = (grad_hidden * silu).astype(BF)
        below = dot(grad_gate, wexp[0], NT) + dot(grad_up, wexp[1], NT)
        backp[four] = below.astype(BF).reshape(4, rows, width)
        one.begin_plane(zz)
        out = dot(low, wexp[2], NT)
        mixp[four] = (prob * out).astype(BF).reshape(4, rows, width)
        two.begin_plane(zz)
        acc[0] += dot(some, grad_gate, TN)
        acc[1] += dot(some, grad_up, TN)
        acc[2] += dot(grad, (prob * low.astype(F32)).astype(BF), TN)
        return 0

    lax.fori_loop(0, 4, chunk, 0)
    one.fold(order[3])
    seen_out = Exchange(lambda r: gg.at[r], lambda r: g_all.at[r], g_send, g_recv)
    seen_out.begin()
    dw[...] = acc[...].astype(BF).reshape(dw.shape)
    over = remote(dw.at[:, 1 - x], dwx, x_sem.at[0], x_sem.at[1], (1 - x, s))
    over.start()
    one.flow()
    two.run()
    mixed[...] = (residual[...] + mix[...].astype(F32)).astype(BF)
    hidden.end()
    seen_out.end()
    one.end()
    two.end()
    over.wait()
    dwx[...] = (dwx[...].astype(F32) + dw[:, x].astype(F32)).astype(BF)


def rear(
    back, g_all, cot, probs, picked, normed, scale, wo, att, h2, dwx, q_t, k_t, v_t, lse, o_t, start, hid, cos, sin,
    wperm, tok,
    grad_tokens, dw_all, dwo_sum, wg_all,
    g_res, ga_t, dwo, dwo_x, go_t, gq_t, gkv, k_n, v_n, delta, got, g_t, wg, g_mine, wp,
    *rest,
):
    bufs = rest[:NBUF]
    sems = rest[NBUF:]
    a_send, a_recv, w_send, w_recv, b_send, b_recv, v_send, v_recv, p_send, p_recv, x_sem = sems[NSEM:]
    x, s, z, y, c = place()
    width = att.shape[1]
    length = hid.shape[0]
    barrier_all()
    over_w = remote(wperm, wp.at[x, s], x_sem.at[4], x_sem.at[5], (1 - x, s))
    over_w.start()
    keep_w = pltpu.make_async_copy(wperm, wp.at[x, s], x_sem.at[6])
    keep_w.start()

    seen = jnp.concatenate([g_all[e, 0:1, :] for e in range(E)] + [jnp.zeros((128 - E, 128), F32)], axis=0)
    grad_probs = jnp.transpose(seen) * picked[...]
    prob = probs[...]
    grad_logits = (prob * (grad_probs - jnp.sum(prob * grad_probs, axis=-1, keepdims=True))).astype(BF)
    u = back[...].astype(F32) + dot(grad_logits, wo[:, width : width + 128], NT)
    norm = normed[...]
    grad = cot[...].astype(F32) + scale[:, 0:1] * (u - norm * jnp.mean(u * norm, axis=-1, keepdims=True))
    g_res[...] = grad
    branch = grad.astype(BF)
    ga_t[...] = jnp.transpose(dot(branch, wo[:, 0:width])).astype(BF).reshape(ga_t.shape)
    heads = Exchange(lambda h: ga_t.at[h], lambda t: go_t.at[:, lane_block(t, 128)], a_send, a_recv)
    heads.begin()
    dwo[:, :, :, 0:width] = dot(jnp.transpose(grad).astype(BF), att[...]).astype(BF).reshape(2, 16, 32, width)
    dwo[:, :, :, width : width + 128] = dot(h2[...], grad_logits, TN).astype(BF).reshape(2, 16, 32, 128)
    over_o = remote(dwo.at[1 - x], dwo_x, x_sem.at[0], x_sem.at[1], (1 - x, s))
    over_o.start()
    k_n[...] = jnp.transpose(k_t[...].astype(F32)).astype(BF)
    v_n[...] = jnp.transpose(v_t[...].astype(F32)).astype(BF)
    gkv[...] = jnp.zeros(gkv.shape, F32)
    weights = Exchange(lambda r: dwx.at[:, r], lambda e: dw_all.at[e], w_send, w_recv)
    heads.end()
    keep_w.wait()
    remote(wperm, wp.at[1 - x, s], x_sem.at[4], x_sem.at[5], (1 - x, s)).wait_recv()
    columns_all = Gather(None, lambda src: wp.at[:, src], p_send, p_recv)
    columns_all.begin()
    weights.begin(range(8))
    delta[...] = jnp.sum(go_t[...].astype(F32) * o_t[...], axis=0, keepdims=True)

    def query_block(i, _):
        cols = lane_block(i)
        queries, grads = q_t[:, cols], go_t[:, cols]
        begin, log_total, shift = start[:, cols], lse[:, cols], delta[:, cols]

        def key_block(j, sofar):
            rows = lane_block(j)
            scores = dot(k_n[rows, :], queries) * SCORE
            powers = jnp.where(allowed_mask(j * QB, i * QB, begin), jnp.exp2(scores - log_total), 0.0)
            moved = dot(v_n[rows, :], grads)
            grad_scores = (powers * (moved - shift)).astype(BF)
            gkv[0, :, rows] += dot(queries, grad_scores, NT)
            gkv[1, :, rows] += dot(grads, powers.astype(BF), NT)
            return sofar + dot(k_t[:, rows], grad_scores)

        gq_t[:, cols] = lax.fori_loop(0, i + 1, key_block, jnp.zeros((HEAD_SIZE, QB), F32))
        return 0

    blocks = length // QB
    cut = (5 * blocks) // 8
    lax.fori_loop(0, cut, query_block, 0)
    columns_all.over(0)
    columns_all.line(1)
    over_o.wait_recv()
    dwo_x[...] = (dwo_x[...].astype(F32) + dwo[x].astype(F32)).astype(BF)
    out = Reduce(dwo_x, dwo_sum, bufs, sems[:NSEM])
    out.begin()
    weights.begin(range(8, 16))
    lax.fori_loop(cut, blocks, query_block, 0)

    pair = remote(gkv.at[1 - c], got, x_sem.at[2], x_sem.at[3], (x, seat(z, y, 1 - c)))
    pair.start()
    columns_all.over(1)
    columns_all.line(2)
    for cond, zz, _ in out.order():
        out.fold(zz, cond)
    scaling = 1.0 / math.sqrt(HEAD_SIZE)
    co, si = cos[...], sin[...]

    def unturn(part):
        a, b = part[:32], part[32:]
        return jnp.concatenate([a * co + b * si, b * co - a * si], axis=0)

    g_t[0] = unturn(gq_t[...] * scaling).astype(BF)
    pair.wait()
    mine = gkv[c] + got[...]
    g_t[1] = jnp.where(c == 0, unturn(mine * scaling), mine).astype(BF)
    tokens = Exchange(
        lambda t: g_t.at[:, :, lane_block(t, 128)], lambda h: g_mine.at[h // 2, :, h % 2], b_send, b_recv
    )
    tokens.begin()
    wg[...] = jnp.transpose(dot(g_t[...].reshape(128, length), hid[...])).astype(BF).reshape(wg.shape)
    columns = Exchange(lambda r: wg.at[r], lambda r: wg_all.at[r], v_send, v_recv, wide=True)
    columns.begin()
    columns_all.over(2)
    columns_all.line(3)
    columns_all.over(3)
    for t in range(4):
        columns_all.done(t)
    tokens.end()
    w = jnp.transpose(dot(wp[...].reshape(width, 2 * width), g_mine[...].reshape(2 * width, 128)))
    values = tok[...].astype(F32)
    scale_first = lax.rsqrt(jnp.mean(values * values, axis=-1, keepdims=True) + EPSILON)
    norm = values * scale_first
    grad_tokens[...] = g_res[...] + scale_first * (w - norm * jnp.mean(w * norm, axis=-1, keepdims=True))
    out.flow()
    out.end()
    columns.end()
    weights.end()
    over_o.wait_send()
    over_w.wait_send()
    columns_all.end()


def frequencies(head_dim):
    halves = head_dim // 2
    return jnp.power(ROPE_BASE, -jnp.arange(halves, dtype=F32) * (2.0 / head_dim))


def sixteen_seats(
    tokens,
    attention_gain,
    expert_gain,
    query_weight,
    key_matrix,
    value_matrix,
    output_weight,
    router_weight,
    gate_weight,
    up_weight,
    down_weight,
    routes,
    segments,
    rope_index,
    cotangent,
):
    D = MODEL_WIDTH
    rows = tokens.shape[1]
    length = 16 * rows
    gain_first, gain_second = attention_gain.astype(F32)[:, None], expert_gain.astype(F32)[:, None]
    tok_mine = tokens.reshape(rows, D)
    cot_mine = cotangent.reshape(rows, D)
    freq = jnp.broadcast_to(frequencies(HEAD_SIZE)[:, None], (32, 128))
    (
        hid, wexp, wo_all, cot_all, q_t, k_t, v_t, o_t, lse, start, cos, sin,
        residual, normed, scale, h2, att, probs, picked, p_t, wperm,
    ) = comm_call(
        front,
        [sds((length, D), BF), sds((3, 32, 32, F), BF), sds((2, 16, 32, D + 128), BF), sds((16, rows, D), BF)]
        + [sds((64, length), BF)] * 3
        + [sds((64, length), F32), sds((1, length), F32), sds((1, length), jnp.int32)]
        + [sds((32, length), F32)] * 2
        + [sds((rows, D), F32), sds((rows, D), F32), sds((rows, 128), F32), sds((rows, D), BF), sds((rows, D), BF)]
        + [sds((rows, 128), F32), sds((rows, 128), F32), sds((E, rows), F32), sds((32, 2 * D), BF)],
        [
            tok_mine,
            query_weight,
            key_matrix,
            value_matrix,
            output_weight,
            router_weight,
            gate_weight,
            up_weight,
            down_weight,
            attention_gain.reshape(1, 32),
            expert_gain.reshape(1, 32),
            segments.astype(jnp.int32),
            routes.reshape(rows, K),
            cot_mine,
            rope_index.astype(jnp.int32),
            freq,
        ],
        GATHER_SEMS * 3 + [DMA((16,))] * 10 + [DMA((8,))],
        0,
        [
            VM((32, D + 128), BF),
            VM((E, 3, 32, F), BF),
            VM((F // 128, 32 * E, 128), F32),
            VM((8, rows), jnp.int32),
            VM((16, rows, D), BF),
            VM((2, 8, 2, 32, 256), BF),
            VM((16, 8, rows), jnp.int32),
            VM((64, length), BF),
            VM((16, 64, rows), BF),
            VM((length, 64), BF),
            VM((256, D), BF),
            VM((length, D), BF),
            VM((2, 16, 32, D + 128), BF),
        ],
        [ANY] * 4 + [VM] * 17,
        [VM] * 14 + [SM, VM],
    )
    wo_all = wo_all.reshape(D, D + 128)
    back, mixed, g_all, dwx = comm_call(
        middle,
        [sds((rows, D), BF), sds((rows, D), BF), sds((16, 8, rows), F32), sds((3, 16, 32, F), BF)],
        [h2, p_t, cot_all, wexp.reshape(3, D, F), residual],
        Reduce.SEMS * 2 + GATHER_SEMS + [DMA((16,))] * 4 + [DMA((8,))],
        1,
        [
            VM((16, rows, D), BF),
            VM((16, E, rows), F32),
            VM((16, rows, D), BF),
            VM((3, D, F), BF),
            VM((16, rows, D), BF),
            VM((16, rows, D), BF),
            VM((rows, D), BF),
            VM((16, 8, rows), F32),
            VM((3, 2, 16, 32, F), BF),
            VM((3, D, F), F32),
        ]
        + Reduce.bufs(rows, D) * 2,
        None,
        [VM, VM, ANY, ANY, VM],
    )
    grad_tokens, dw_all, dwo_sum, wg_all = comm_call(
        rear,
        [sds((rows, D), F32), sds((16, 3, 32, F), BF), sds((32, D + 128), BF), sds((32, 32, 128), BF)],
        [
            back,
            g_all,
            cot_mine,
            probs,
            picked,
            normed,
            scale,
            wo_all,
            att,
            h2,
            dwx,
            q_t,
            k_t,
            v_t,
            lse,
            o_t,
            start,
            hid,
            cos,
            sin,
            wperm,
            tok_mine,
        ],
        Reduce.SEMS + [DMA((16,))] * 6 + [DMA((32,))] * 2 + GATHER_SEMS + [DMA((8,))],
        2,
        [
            VM((rows, D), F32),
            VM((16, 64, rows), BF),
            VM((2, 16, 32, D + 128), BF),
            VM((16, 32, D + 128), BF),
            VM((64, length), BF),
            VM((64, length), F32),
            VM((2, 64, length), F32),
            VM((length, 64), BF),
            VM((length, 64), BF),
            VM((1, length), F32),
            VM((64, length), F32),
            VM((2, 64, length), BF),
            VM((32, 32, 128), BF),
            VM((8, 2, 2, 64, rows), BF),
            VM((2, 16, 32, 2 * D), BF),
        ]
        + Reduce.bufs(32, D + 128),
    )
    wg_sum = wg_all.reshape(2, 16, 32, 128).astype(F32).sum(axis=0).transpose(1, 0, 2)
    plain_query = wg_sum[:, :, :64].reshape(32, D)
    plain_key = wg_sum[:, 0::2, 64:].reshape(32, 512)
    plain_value = wg_sum[:, 1::2, 64:].reshape(32, 512)
    own_o = dwo_sum.astype(F32)
    plain_router = own_o[:, D : D + E]
    expert_grads = dw_all.transpose(1, 2, 0, 3).astype(F32)
    plain_gate, plain_up = expert_grads[0], expert_grads[1]
    grad_attention_gain = (
        jnp.sum(plain_query * query_weight.astype(F32), axis=1)
        + jnp.sum(plain_key * key_matrix.astype(F32), axis=1)
        + jnp.sum(plain_value * value_matrix.astype(F32), axis=1)
    )
    grad_expert_gain = jnp.sum(
        plain_gate * gate_weight.astype(F32) + plain_up * up_weight.astype(F32), axis=(1, 2)
    ) + jnp.sum(plain_router * router_weight.astype(F32), axis=1)
    return (
        mixed.reshape(tokens.shape),
        grad_tokens.reshape(tokens.shape),
        grad_attention_gain,
        grad_expert_gain,
        plain_query * gain_first,
        plain_key * gain_first,
        plain_value * gain_first,
        own_o[:, :D],
        plain_router * gain_second,
        plain_gate * gain_second[..., None],
        plain_up * gain_second[..., None],
        expert_grads[2],
    )


def rms_scale(values):
    return lax.rsqrt(jnp.mean(values * values, axis=-1, keepdims=True) + EPSILON)


def apply_rotary(values, cosine_lookup, sine_lookup):
    halves = values.shape[-1] // 2
    first_half = values[..., :halves]
    second_half = values[..., halves:]
    return jnp.concatenate(
        [
            first_half * cosine_lookup - second_half * sine_lookup,
            second_half * cosine_lookup + first_half * sine_lookup,
        ],
        axis=-1,
    )


def unrotate(values, cosine_lookup, sine_lookup):
    halves = values.shape[-1] // 2
    first_half = values[..., :halves]
    second_half = values[..., halves:]
    return jnp.concatenate(
        [
            first_half * cosine_lookup + second_half * sine_lookup,
            second_half * cosine_lookup - first_half * sine_lookup,
        ],
        axis=-1,
    )


def block_mask(key_start, block_size, query_pos, query_seg, seg_block):
    key_pos = key_start + jnp.arange(block_size, dtype=jnp.int32)
    causal = key_pos[None, :] <= query_pos[:, None]
    same_doc = seg_block[:, None, :] == query_seg[:, :, None]
    return (causal[None] & same_doc)[:, None, None]


def attend_piece(running, pieces, first_key, queries, query_pos, query_seg, scaling):
    key_rows, value_rows, key_segments = pieces
    sequence_count, key_span = (key_rows.shape[0], key_rows.shape[1])
    block_size = math.gcd(key_span, 512)
    kv_heads, head_dim = (queries.shape[2], queries.shape[4])

    def advance(block_index, carried):
        top_score, denominator, numerator = carried
        offset = block_index * block_size
        key_block = lax.dynamic_slice_in_dim(key_rows, offset, block_size, 1).reshape(
            sequence_count, block_size, kv_heads, head_dim
        )
        value_block = lax.dynamic_slice_in_dim(value_rows, offset, block_size, 1).reshape(
            sequence_count, block_size, kv_heads, head_dim
        )
        seg_block = lax.dynamic_slice_in_dim(key_segments, offset, block_size, 1).astype(jnp.int32)
        allowed = block_mask(offset, block_size, query_pos, query_seg, seg_block)
        scores = (
            jnp.einsum("sqkgd,sjkd->skgqj", queries, key_block, preferred_element_type=jnp.float32)
            * scaling
        )
        fresh_top = jnp.maximum(top_score, jnp.max(jnp.where(allowed, scores, MASKED), axis=-1))
        weights = jnp.where(allowed, jnp.exp(scores - fresh_top[..., None]), 0.0)
        decay_factor = jnp.exp(top_score - fresh_top)
        denominator = denominator * decay_factor + jnp.sum(weights, axis=-1)
        numerator = numerator * decay_factor[..., None] + jnp.einsum(
            "skgqj,sjkd->skgqd",
            weights.astype(jnp.bfloat16),
            value_block,
            preferred_element_type=jnp.float32,
        )
        return (fresh_top, denominator, numerator)

    return lax.fori_loop(0, key_span // block_size, advance, running)


def attend_back(pieces, queries, query_pos, query_seg, grad_attn, log_total, row_delta, scaling):
    key_rows, value_rows, key_segments = pieces
    sequence_count, key_span, key_value_width = key_rows.shape
    block_size = math.gcd(key_span, 512)
    kv_heads, head_dim = (queries.shape[2], queries.shape[4])

    def advance(block_index, carried):
        grad_queries, gradient_couples = carried
        offset = block_index * block_size
        key_block = lax.dynamic_slice_in_dim(key_rows, offset, block_size, 1).reshape(
            sequence_count, block_size, kv_heads, head_dim
        )
        value_block = lax.dynamic_slice_in_dim(value_rows, offset, block_size, 1).reshape(
            sequence_count, block_size, kv_heads, head_dim
        )
        seg_block = lax.dynamic_slice_in_dim(key_segments, offset, block_size, 1).astype(jnp.int32)
        allowed = block_mask(offset, block_size, query_pos, query_seg, seg_block)
        scores = (
            jnp.einsum("sqkgd,sjkd->skgqj", queries, key_block, preferred_element_type=jnp.float32)
            * scaling
        )
        weights = jnp.where(allowed, jnp.exp(scores - log_total[..., None]), 0.0)
        grad_weights = jnp.einsum(
            "sqkgd,sjkd->skgqj", grad_attn, value_block, preferred_element_type=jnp.float32
        )
        grad_scores = (weights * (grad_weights - row_delta[..., None])).astype(jnp.bfloat16)
        grad_queries = grad_queries + jnp.einsum(
            "skgqj,sjkd->sqkgd", grad_scores, key_block, preferred_element_type=jnp.float32
        )
        grad_keys = (
            jnp.einsum(
                "skgqj,sqkgd->sjkd", grad_scores, queries, preferred_element_type=jnp.float32
            )
            * scaling
        )
        grad_values = jnp.einsum(
            "skgqj,sqkgd->sjkd",
            weights.astype(jnp.bfloat16),
            grad_attn,
            preferred_element_type=jnp.float32,
        )
        produced = jnp.concatenate(
            [
                grad_keys.reshape(sequence_count, block_size, key_value_width),
                grad_values.reshape(sequence_count, block_size, key_value_width),
            ],
            axis=-1,
        )
        return (
            grad_queries,
            lax.dynamic_update_slice_in_dim(gradient_couples, produced, offset, 1),
        )

    starting = (
        jnp.zeros(queries.shape, jnp.float32),
        jnp.zeros((sequence_count, key_span, 2 * key_value_width), jnp.float32),
    )
    grad_queries, gradient_couples = lax.fori_loop(0, key_span // block_size, advance, starting)
    return (grad_queries * scaling, gradient_couples)


def project_in(pieces, routed):
    gate_rows, up_rows = pieces
    return (
        jnp.einsum("erd,def->erf", routed, gate_rows, preferred_element_type=jnp.float32),
        jnp.einsum("erd,def->erf", routed, up_rows, preferred_element_type=jnp.float32),
    )


def project_out(down_rows, hidden):
    produced = jnp.einsum("erf,def->erd", hidden, down_rows, preferred_element_type=jnp.float32)
    return produced


def back_through_down(down_rows, grad_output):
    return jnp.einsum("erd,def->erf", grad_output, down_rows, preferred_element_type=jnp.float32)


def back_through_in(pieces, grad_gate, grad_up):
    gate_rows, up_rows = pieces
    produced = jnp.einsum(
        "erf,def->erd", grad_gate, gate_rows, preferred_element_type=jnp.float32
    ) + jnp.einsum("erf,def->erd", grad_up, up_rows, preferred_element_type=jnp.float32)
    return produced


def take_slots(slot_data, destination):
    experts, width = (slot_data.shape[0], slot_data.shape[-1])
    sequence_count, sequence_rows, picks = destination.shape
    flat = jnp.transpose(
        slot_data.reshape(experts, sequence_count, -1, width), (1, 0, 2, 3)
    ).reshape(sequence_count, -1, width)
    taken = jax.vmap(lambda table, spots: table[spots])(
        flat, destination.reshape(sequence_count, sequence_rows * picks)
    )
    return taken.reshape(sequence_count, sequence_rows, picks, width)


def place_slots(values, destination, experts, capacity):
    sequence_count, width = (values.shape[0], values.shape[-1])
    empty = jnp.zeros((sequence_count, experts * capacity, width), values.dtype)
    filled = jax.vmap(lambda table, spots, rows: table.at[spots].set(rows))(
        empty, destination.reshape(sequence_count, -1), values.reshape(sequence_count, -1, width)
    )
    return jnp.transpose(
        filled.reshape(sequence_count, experts, capacity, width), (1, 0, 2, 3)
    ).reshape(experts, sequence_count * capacity, width)


def any_seats(
    tokens,
    attention_gain,
    expert_gain,
    query_weight,
    key_matrix,
    value_matrix,
    output_weight,
    router_weight,
    gate_weight,
    up_weight,
    down_weight,
    routes,
    segments,
    rope_index,
    cotangent,
):
    sequence_count, sequence_rows = (tokens.shape[0], tokens.shape[1])
    queries_per_group = QUERY_HEADS // KEY_VALUE_HEADS
    key_value_width = KEY_VALUE_HEADS * HEAD_SIZE
    scaling = 1.0 / math.sqrt(HEAD_SIZE)
    experts_slots = E * CAP
    gathered = (
        lax.all_gather(attention_gain, ("row", "seq"), axis=0, tiled=True),
        lax.all_gather(expert_gain, ("row", "seq"), axis=0, tiled=True),
        lax.all_gather(query_weight, ("row", "seq"), axis=0, tiled=True),
        lax.all_gather(key_matrix, ("row", "seq"), axis=0, tiled=True),
        lax.all_gather(value_matrix, ("row", "seq"), axis=0, tiled=True),
        lax.all_gather(output_weight, ("row", "seq"), axis=0, tiled=True),
        lax.all_gather(router_weight, ("row", "seq"), axis=0, tiled=True),
    )
    gain_first = gathered[0].astype(jnp.float32)
    gain_second = gathered[1].astype(jnp.float32)
    full_query, full_key, full_value, full_output, full_router = gathered[2:]
    inputs = tokens.astype(jnp.float32)
    scale_first = rms_scale(inputs)
    normed_first = inputs * scale_first
    hidden_first = (normed_first * gain_first).astype(jnp.bfloat16)
    query_unrotated = jnp.einsum(
        "sqd,dc->sqc", hidden_first, full_query, preferred_element_type=jnp.float32
    )
    key_unrotated = jnp.einsum(
        "sqd,dc->sqc", hidden_first, full_key, preferred_element_type=jnp.float32
    )
    value_raw = jnp.einsum(
        "sqd,dc->sqc", hidden_first, full_value, preferred_element_type=jnp.float32
    )
    positions = lax.axis_index("seq") * sequence_rows + jnp.arange(sequence_rows, dtype=jnp.int32)
    factor = jnp.power(2.0, rope_index.astype(jnp.float32))
    angles = (positions.astype(jnp.float32)[None, :] / factor[:, None])[..., None] * frequencies(
        HEAD_SIZE
    )
    cosine_lookup = jnp.cos(angles)[:, :, None, :]
    sine_lookup = jnp.sin(angles)[:, :, None, :]
    query_turned = (
        apply_rotary(
            query_unrotated.reshape(sequence_count, sequence_rows, QUERY_HEADS, HEAD_SIZE),
            cosine_lookup,
            sine_lookup,
        )
        .astype(jnp.bfloat16)
        .reshape(sequence_count, sequence_rows, KEY_VALUE_HEADS, queries_per_group, HEAD_SIZE)
    )
    key_turned = (
        apply_rotary(
            key_unrotated.reshape(sequence_count, sequence_rows, KEY_VALUE_HEADS, HEAD_SIZE),
            cosine_lookup,
            sine_lookup,
        )
        .astype(jnp.bfloat16)
        .reshape(sequence_count, sequence_rows, key_value_width)
    )
    value_reduced = value_raw.astype(jnp.bfloat16)
    segment_low = segments.astype(jnp.float32).astype(jnp.bfloat16)
    statistic_shape = (sequence_count, KEY_VALUE_HEADS, queries_per_group, sequence_rows)
    starting = (
        jnp.full(statistic_shape, MASKED, jnp.float32),
        jnp.zeros(statistic_shape, jnp.float32),
        jnp.zeros(statistic_shape + (HEAD_SIZE,), jnp.float32),
    )
    attend = partial(
        attend_piece, queries=query_turned, query_pos=positions, query_seg=segments, scaling=scaling
    )
    top_score, denominator, numerator = attend(
        starting,
        (
            lax.all_gather(key_turned, "seq", axis=1, tiled=True),
            lax.all_gather(value_reduced, "seq", axis=1, tiled=True),
            lax.all_gather(segment_low, "seq", axis=1, tiled=True),
        ),
        jnp.int32(0),
    )
    attn_heads = numerator / denominator[..., None]
    log_total = top_score + jnp.log(denominator)
    attn_rows = jnp.transpose(attn_heads, (0, 3, 1, 2, 4))
    attn_low = attn_rows.astype(jnp.bfloat16).reshape(
        sequence_count, sequence_rows, QUERY_HEADS * HEAD_SIZE
    )
    branch = jnp.einsum("sqc,dc->sqd", attn_low, full_output, preferred_element_type=jnp.float32)
    residual = inputs + branch
    scale_second = rms_scale(residual)
    normed_second = residual * scale_second
    hidden_second = (normed_second * gain_second).astype(jnp.bfloat16)
    logits = jnp.einsum(
        "sqd,de->sqe", hidden_second, full_router, preferred_element_type=jnp.float32
    )
    router_probs = jax.nn.softmax(logits, axis=-1)
    picked = routes[..., None] == jnp.arange(E, dtype=jnp.int32)
    picked_int = picked.astype(jnp.int32).reshape(sequence_count, sequence_rows * K, E)
    earlier = jnp.cumsum(picked_int, axis=1, dtype=jnp.int32) - picked_int
    slot_ids = jnp.sum(earlier * picked_int, axis=-1, dtype=jnp.int32).reshape(
        sequence_count, sequence_rows, K
    )
    destination = routes * CAP + slot_ids
    chosen = destination[..., None] == jnp.arange(experts_slots, dtype=jnp.int32)
    gate_probs = jnp.sum(jnp.where(picked, router_probs[:, :, None, :], 0.0), axis=-1)
    dispatch = jnp.sum(chosen, axis=2, dtype=jnp.float32).reshape(
        sequence_count, sequence_rows, E, CAP
    )
    slot_rows = sequence_count * CAP
    routed = (
        jnp.einsum(
            "sqec,sqd->escd",
            dispatch.astype(jnp.bfloat16),
            hidden_second,
            preferred_element_type=jnp.float32,
        )
        .astype(jnp.bfloat16)
        .reshape(E, slot_rows, MODEL_WIDTH)
    )
    grad_mixed = cotangent.astype(jnp.float32)
    grad_slot_values = (gate_probs[..., None] * grad_mixed[:, :, None, :]).astype(jnp.bfloat16)
    grad_expert = place_slots(grad_slot_values, destination, E, CAP)
    groups = 4
    width = E // groups

    def some_experts(_, given):
        rows, grads, gate_part, up_part, down_part = given
        pieces = (
            lax.all_gather(gate_part, ("row", "seq"), axis=0, tiled=True),
            lax.all_gather(up_part, ("row", "seq"), axis=0, tiled=True),
        )
        down_rows = lax.all_gather(down_part, ("row", "seq"), axis=0, tiled=True)
        gate_pre, up_pre = project_in(pieces, routed=rows)
        hidden_low = (jax.nn.silu(gate_pre) * up_pre).astype(jnp.bfloat16)
        expert_out = project_out(down_rows, hidden=hidden_low)
        grad_hidden = back_through_down(down_rows, grad_output=grads)
        sigmoid_gate = jax.nn.sigmoid(gate_pre)
        grad_gate = (
            grad_hidden * up_pre * sigmoid_gate * (1.0 + gate_pre * (1.0 - sigmoid_gate))
        ).astype(jnp.bfloat16)
        grad_up = (grad_hidden * (gate_pre * sigmoid_gate)).astype(jnp.bfloat16)
        grad_routed = back_through_in(pieces, grad_gate=grad_gate, grad_up=grad_up)
        made = [
            lax.psum_scatter(
                jnp.einsum("erd,erf->def", left, right, preferred_element_type=jnp.float32),
                ("row", "seq"),
                scatter_dimension=0,
                tiled=True,
            )
            for left, right in ((rows, grad_gate), (rows, grad_up), (grads, hidden_low))
        ]
        return None, (expert_out, grad_routed, *made)

    def grouped(weight):
        return jnp.moveaxis(weight.reshape(weight.shape[0], groups, width, F), 1, 0)

    _, (expert_out, grad_routed, *expert_grads) = lax.scan(
        some_experts,
        None,
        (
            routed.reshape(groups, width, slot_rows, MODEL_WIDTH),
            grad_expert.reshape(groups, width, slot_rows, MODEL_WIDTH),
            grouped(gate_weight),
            grouped(up_weight),
            grouped(down_weight),
        ),
    )
    expert_out = expert_out.reshape(E, slot_rows, MODEL_WIDTH)
    grad_routed = grad_routed.reshape(E, slot_rows, MODEL_WIDTH)
    grad_gate_weight, grad_up_weight, grad_down_weight = [
        jnp.moveaxis(grad, 0, 1).reshape(gate_weight.shape) for grad in expert_grads
    ]
    taken_out = take_slots(expert_out, destination)
    expert_mix = jnp.sum(gate_probs[..., None] * taken_out, axis=2)
    mixed = (residual + expert_mix).astype(jnp.bfloat16)
    grad_gates = jnp.sum(taken_out * grad_mixed[:, :, None, :], axis=-1)
    grad_probs = jnp.sum(jnp.where(picked, grad_gates[..., None], 0.0), axis=2)
    grad_logits = (
        router_probs * (grad_probs - jnp.sum(router_probs * grad_probs, axis=-1, keepdims=True))
    ).astype(jnp.bfloat16)
    grad_second = jnp.sum(take_slots(grad_routed, destination), axis=2) + jnp.einsum(
        "sqe,de->sqd", grad_logits, full_router, preferred_element_type=jnp.float32
    )
    grad_gain_second = jnp.sum(grad_second * normed_second, axis=(0, 1))
    scaled_second = grad_second * gain_second
    grad_residual = grad_mixed + scale_second * (
        scaled_second
        - normed_second * jnp.mean(scaled_second * normed_second, axis=-1, keepdims=True)
    )
    grad_branch = grad_residual.astype(jnp.bfloat16)
    grad_attn = (
        jnp.einsum("sqd,dc->sqc", grad_branch, full_output, preferred_element_type=jnp.float32)
        .astype(jnp.bfloat16)
        .reshape(sequence_count, sequence_rows, KEY_VALUE_HEADS, queries_per_group, HEAD_SIZE)
    )
    row_delta = jnp.transpose(
        jnp.sum(grad_attn.astype(jnp.float32) * attn_rows, axis=-1), (0, 2, 3, 1)
    )
    keys_back = (
        lax.all_gather(key_turned, "seq", axis=1, tiled=True),
        lax.all_gather(value_reduced, "seq", axis=1, tiled=True),
        lax.all_gather(segment_low, "seq", axis=1, tiled=True),
    )
    grad_query_rot, grad_pair_rows = attend_back(
        keys_back, query_turned, positions, segments, grad_attn, log_total, row_delta, scaling
    )
    gradient_couples = lax.psum_scatter(grad_pair_rows, "seq", scatter_dimension=1, tiled=True)
    grad_query = (
        unrotate(
            grad_query_rot.reshape(sequence_count, sequence_rows, QUERY_HEADS, HEAD_SIZE),
            cosine_lookup,
            sine_lookup,
        )
        .astype(jnp.bfloat16)
        .reshape(sequence_count, sequence_rows, QUERY_HEADS * HEAD_SIZE)
    )
    grad_key = (
        unrotate(
            gradient_couples[..., :key_value_width].reshape(
                sequence_count, sequence_rows, KEY_VALUE_HEADS, HEAD_SIZE
            ),
            cosine_lookup,
            sine_lookup,
        )
        .astype(jnp.bfloat16)
        .reshape(sequence_count, sequence_rows, key_value_width)
    )
    grad_value = gradient_couples[..., key_value_width:].astype(jnp.bfloat16)
    grad_first = (
        jnp.einsum("sqc,dc->sqd", grad_query, full_query, preferred_element_type=jnp.float32)
        + jnp.einsum("sqc,dc->sqd", grad_key, full_key, preferred_element_type=jnp.float32)
        + jnp.einsum("sqc,dc->sqd", grad_value, full_value, preferred_element_type=jnp.float32)
    )
    grad_gain_first = jnp.sum(grad_first * normed_first, axis=(0, 1))
    scaled_first = grad_first * gain_first
    grad_tokens = grad_residual + scale_first * (
        scaled_first - normed_first * jnp.mean(scaled_first * normed_first, axis=-1, keepdims=True)
    )
    attention_grads = lax.psum_scatter(
        jnp.concatenate(
            [
                jnp.einsum(
                    "sqd,sqc->dc", hidden_first, grad_query, preferred_element_type=jnp.float32
                ),
                jnp.einsum(
                    "sqd,sqc->dc", hidden_first, grad_key, preferred_element_type=jnp.float32
                ),
                jnp.einsum(
                    "sqd,sqc->dc", hidden_first, grad_value, preferred_element_type=jnp.float32
                ),
                jnp.einsum(
                    "sqd,sqc->dc", grad_branch, attn_low, preferred_element_type=jnp.float32
                ),
                jnp.einsum(
                    "sqd,sqe->de", hidden_second, grad_logits, preferred_element_type=jnp.float32
                ),
                grad_gain_first[:, None],
                grad_gain_second[:, None],
            ],
            axis=1,
        ),
        ("row", "seq"),
        scatter_dimension=0,
        tiled=True,
    )
    query_cols = QUERY_HEADS * HEAD_SIZE
    edge_two = query_cols + key_value_width
    edge_three = edge_two + key_value_width
    edge_four = edge_three + query_cols
    edge_five = edge_four + E
    return (
        mixed,
        grad_tokens,
        attention_grads[:, edge_five],
        attention_grads[:, edge_five + 1],
        attention_grads[:, :query_cols],
        attention_grads[:, query_cols:edge_two],
        attention_grads[:, edge_two:edge_three],
        attention_grads[:, edge_three:edge_four],
        attention_grads[:, edge_four:edge_five],
        grad_gate_weight,
        grad_up_weight,
        grad_down_weight,
    )


def solution(mesh):
    first = P(("row", "seq"))
    in_specs = (
        (P("row", "seq", None), first, first)
        + (P(("row", "seq"), None),) * 5
        + (P(("row", "seq"), None, None),) * 3
        + (P("row", "seq", None), P("row", "seq"), P("row"), P("row", "seq", None))
    )
    out_specs = (
        (P("row", "seq", None), P("row", "seq", None), first, first)
        + (P(("row", "seq"), None),) * 5
        + (P(("row", "seq"), None, None),) * 3
    )
    body = sixteen_seats if dict(mesh.shape) == {"row": 2, "seq": 16} else any_seats
    return jax.shard_map(body, mesh=mesh, in_specs=in_specs, out_specs=out_specs, check_vma=False)
```

```python
from functools import partial
import math

import jax
import jax.numpy as jnp
import numpy as np
from jax import lax
from jax.experimental import pallas as pl
from jax.experimental.pallas import tpu as pltpu
from jax.sharding import PartitionSpec as P

MODEL_WIDTH = 1024
QUERY_HEADS = 16
KEY_VALUE_HEADS = 8
HEAD_SIZE = 64
F = 512
E = 16
K = 8
CAP = 96

EPSILON = 1e-05
ROPE_BASE = 10000.0
MASKED = -1e30
MESH = pl.DeviceIdType.MESH
VM = pltpu.VMEM
BF = jnp.bfloat16
F32 = jnp.float32
DMA = pltpu.SemaphoreType.DMA
UP, DOWN, SIDE, CORE, ACROSS = range(5)
VMEM_LIMIT = 60 * 1024 * 1024

NN = (((1,), (0,)), ((), ()))
NT = (((1,), (1,)), ((), ()))
TN = (((0,), (0,)), ((), ()))


def dot(a, b, dims=NN):
    return lax.dot_general(a, b, dims, preferred_element_type=F32)


def when(cond, f):
    if cond is None:
        f()
    else:
        pl.when(cond)(f)


def both(a, b):
    if a is None:
        return b
    return a if b is None else a & b


def place():
    x = lax.axis_index("row")
    s = lax.axis_index("seq")
    return x, s, s // 4, (s // 2) % 2, s % 2


def seat(z, y, c):
    return z * 4 + y * 2 + c


def remote(src, dst, send, recv, dev):
    return pltpu.make_async_remote_copy(src, dst, send, recv, device_id=dev, device_id_type=MESH)


def barrier_all():
    x, s = lax.axis_index("row"), lax.axis_index("seq")
    sem = pltpu.get_barrier_semaphore()
    for k in range(1, 16):
        pl.semaphore_signal(sem, inc=1, device_id=(x, (s + k) % 16), device_id_type=MESH)
    for k in range(16):
        pl.semaphore_signal(sem, inc=1, device_id=(1 - x, (s + k) % 16), device_id_type=MESH)
    pl.semaphore_wait(sem, 31)


def barrier_row(partner=False):
    x, s = lax.axis_index("row"), lax.axis_index("seq")
    sem = pltpu.get_barrier_semaphore()
    for k in range(1, 16):
        pl.semaphore_signal(sem, inc=1, device_id=(x, (s + k) % 16), device_id_type=MESH)
    if partner:
        pl.semaphore_signal(sem, inc=1, device_id=(1 - x, s), device_id_type=MESH)
    pl.semaphore_wait(sem, 16 if partner else 15)


def barrier_near():
    x, s, z, y, c = place()
    sem = pltpu.get_barrier_semaphore()
    for cond, dev in (
        (z < 3, (x, seat(z + 1, y, c))),
        (z > 0, (x, seat(z - 1, y, c))),
        (None, (x, seat(z, 1 - y, c))),
        (None, (x, seat(z, y, 1 - c))),
    ):
        when(cond, lambda dev=dev: pl.semaphore_signal(sem, inc=1, device_id=dev, device_id_type=MESH))
    pl.semaphore_wait(sem, 2 + (z < 3).astype(jnp.int32) + (z > 0).astype(jnp.int32))


QB = 256


def lane_block(i, size=QB):
    return pl.ds(pl.multiple_of(i * size, size), size)


class Gather:
    def __init__(self, own, at, send, recv):
        self.own, self.at, self.send, self.recv = own, at, send, recv
        self.ending = False
        self.x, self.s, self.z, self.y, self.c = place()

    def device(self, k):
        x, z, y, c = self.x, self.z, self.y, self.c
        return {
            UP: (x, seat(z + 1, y, c)),
            DOWN: (x, seat(z - 1, y, c)),
            SIDE: (x, seat(z, 1 - y, c)),
            CORE: (x, seat(z, y, 1 - c)),
        }[k]

    def copy(self, src, k, own=False):
        ref = self.own if own else self.at(src)
        return remote(ref, self.at(src), self.send.at[src, k], self.recv.at[src], self.device(k))

    def go(self, src, k, cond=None, own=False):
        if k == UP:
            cond = both(cond, self.z < 3)
        if k == DOWN:
            cond = both(cond, self.z > 0)
        act = (lambda c: c.wait_send()) if self.ending else (lambda c: c.start())
        when(cond, lambda: act(self.copy(src, k, own)))

    def wait(self, src, cond=None):
        if self.ending:
            return
        when(cond, lambda: self.copy(src, SIDE).wait_recv())

    def sides(self, t):
        if t == 0:
            return ((None, self.z, None),)
        return ((self.z - t >= 0, self.z - t, UP), (self.z + t <= 3, self.z + t, DOWN))

    def begin(self):
        for k in (UP, DOWN, SIDE, CORE):
            self.go(self.s, k, own=self.own is not None)

    def line(self, t):
        for cond, zz, k in self.sides(t):
            src = seat(zz, self.y, self.c)
            self.wait(src, cond)
            for way in (k, SIDE, CORE):
                self.go(src, way, cond)

    def over(self, t):
        for cond, zz, _ in self.sides(t):
            src = seat(zz, 1 - self.y, self.c)
            self.wait(src, cond)
            self.go(src, CORE, cond)

    def done(self, t):
        for cond, zz, _ in self.sides(t):
            for yy in range(2):
                self.wait(seat(zz, yy, 1 - self.c), cond)

    def end(self):
        self.ending = True
        self.begin()
        for t in range(4):
            if t:
                self.line(t)
            self.over(t)


GATHER_SEMS = [DMA((16, 4)), DMA((16,))]


class GatherAll(Gather):
    def device(self, k):
        return (1 - self.x, self.s) if k == ACROSS else Gather.device(self, k)

    def copy(self, src, k, own=False, x=None):
        x = self.x if x is None else x
        ref = self.own if own else self.at(x, src)
        return remote(ref, self.at(x, src), self.send.at[x, src, k], self.recv.at[x, src], self.device(k))

    def begin(self):
        for k in (UP, DOWN, SIDE, ACROSS, CORE):
            self.go(self.s, k, own=True)

    def line(self, t):
        for cond, zz, k in self.sides(t):
            src = seat(zz, self.y, self.c)
            self.wait(src, cond)
            for way in (k, SIDE, ACROSS, CORE):
                self.go(src, way, cond)

    def over(self, t):
        for cond, zz, _ in self.sides(t):
            src = seat(zz, 1 - self.y, self.c)
            self.wait(src, cond)
            for way in (ACROSS, CORE):
                self.go(src, way, cond)

    def across(self, t):
        x = 1 - self.x
        for cond, zz, _ in self.sides(t):
            for yy in range(2):
                src = seat(zz, yy, self.c)
                if not self.ending:
                    when(cond, lambda: self.copy(src, SIDE, x=x).wait_recv())
                act = (lambda c: c.wait_send()) if self.ending else (lambda c: c.start())
                when(cond, lambda: act(self.copy(src, CORE, x=x)))

    def done(self, t):
        for cond, zz, _ in self.sides(t):
            for yy in range(2):
                src = seat(zz, yy, 1 - self.c)
                for x in (self.x, 1 - self.x):
                    when(cond, lambda: self.copy(src, SIDE, x=x).wait_recv())

    def end(self):
        Gather.end(self)
        for t in range(4):
            self.across(t)


GATHER_ALL_SEMS = [DMA((2, 16, 5)), DMA((2, 16))]


class Exchange:
    def __init__(self, src, dst, send, recv, wide=False):
        self.x, self.s, self.z, self.y, self.c = place()
        self.wide, self.n = wide, 32 if wide else 16
        self.src, self.dst, self.send, self.recv = src, dst, send, recv

    def seat(self, k, back=False):
        dz = (k // 4) % 4
        if back:
            dz = (4 - dz) % 4
        x = (self.x + k // 16) % 2
        s = seat((self.z + dz) % 4, (self.y + k // 2) % 2, (self.c + k) % 2)
        return x, s

    def index(self, seat_of):
        x, s = seat_of
        return x * 16 + s if self.wide else s

    def copy(self, k):
        to, me = self.seat(k), self.index((self.x, self.s))
        return remote(self.src(self.index(to)), self.dst(me), self.send.at[k], self.recv.at[k], to)

    def keep(self):
        me = self.index((self.x, self.s))
        return pltpu.make_async_copy(self.src(me), self.dst(me), self.recv.at[0])

    def begin(self, ks=None):
        for k in range(self.n) if ks is None else ks:
            if k == 0:
                self.keep().start()
            else:
                self.copy(k).start()

    def arrive(self, k):
        frm = self.seat(k, back=True)
        me = self.index((self.x, self.s))
        remote(self.src(me), self.dst(self.index(frm)), self.send.at[k], self.recv.at[k], frm).wait_recv()
        return self.index(frm)

    def end(self):
        self.keep().wait()
        for k in range(1, self.n):
            self.arrive(k)
        self.end_sends()

    def end_sends(self):
        for k in range(1, self.n):
            self.copy(k).wait_send()


class Slices:
    def __init__(self, src, got, send, recv):
        self.x, self.s, self.z, self.y, self.c = place()
        self.src, self.got, self.send, self.recv = src, got, send, recv

    def block(self, pair):
        return self.src.at[:, lane_block(pair, 256)]

    def copy(self, k):
        z, y = (self.z + k // 2) % 4, (self.y + k) % 2
        dst = self.got.at[self.x, self.s // 2, self.c]
        return remote(self.block(z * 2 + y), dst, self.send.at[k], self.recv.at[k], (self.x, seat(z, y, self.c)))

    def begin(self):
        self.local = pltpu.make_async_copy(
            self.block(self.s // 2), self.got.at[self.x, self.s // 2, self.c], self.recv.at[0]
        )
        self.local.start()
        for k in range(1, 8):
            self.copy(k).start()

    def over_x(self):
        ref = self.got.at[self.x, :, self.c]
        return remote(ref, ref, self.send.at[8], self.recv.at[8], (1 - self.x, self.s))

    def over_core(self, k):
        ref = self.got.at[self.x if k == 9 else 1 - self.x, :, self.c]
        return remote(ref, ref, self.send.at[k], self.recv.at[k], (self.x, seat(self.z, self.y, 1 - self.c)))

    def share(self):
        self.local.wait()
        for k in range(1, 8):
            z, y = (self.z + 4 - k // 2) % 4, (self.y + k) % 2
            dst = self.got.at[self.x, z * 2 + y, self.c]
            remote(
                self.block(z * 2 + y), dst, self.send.at[k], self.recv.at[k], (self.x, seat(z, y, self.c))
            ).wait_recv()
        self.over_x().start()
        self.over_core(9).start()

    def end(self):
        self.over_x().wait_recv()
        self.over_core(10).start()
        self.over_core(9).wait_recv()
        self.over_core(10).wait_recv()
        for k in range(1, 8):
            self.copy(k).wait_send()
        self.over_x().wait_send()
        self.over_core(9).wait_send()
        self.over_core(10).wait_send()


ANY = pl.ANY
SM = pltpu.SMEM


def comm_call(body, outs, ins, sems, cid, scratch=(), out_spaces=None, in_spaces=None):
    return pl.pallas_call(
        body,
        out_shape=outs,
        in_specs=[pl.BlockSpec(memory_space=m) for m in in_spaces or [VM] * len(ins)],
        out_specs=[pl.BlockSpec(memory_space=m) for m in out_spaces or [VM] * len(outs)],
        scratch_shapes=list(scratch) + list(sems),
        compiler_params=pltpu.CompilerParams(
            collective_id=cid, has_side_effects=True, vmem_limit_bytes=VMEM_LIMIT
        ),
    )(*ins)


def sds(shape, dtype):
    return jax.ShapeDtypeStruct(shape, dtype)


class Reduce:
    def __init__(self, part, out, bufs, sems):
        self.part, self.out = part, out
        self.r1, self.ra, self.ua, self.da = bufs
        self.s1, self.q1, self.sa, self.qa, self.su, self.qu, self.sd, self.qd = sems
        self.x, self.s, self.z, self.y, self.c = place()

    @staticmethod
    def bufs(rows, width):
        return [VM((4, 2, rows, width), BF)] + [VM((4, rows, width), BF)] * 3

    SEMS = [DMA((4, 2))] * 8

    def add(self, dst, src):
        dst[...] = (dst[...].astype(F32) + src[...].astype(F32)).astype(BF)

    def piece(self, p):
        rows = self.ra.shape[1] // 2
        return slice(p * rows, p * rows + rows)

    def first(self, zz, yy):
        return remote(
            self.part.at[seat(zz, yy, 1 - self.c)],
            self.r1.at[zz, yy],
            self.s1.at[zz, yy],
            self.q1.at[zz, yy],
            (self.x, seat(self.z, self.y, 1 - self.c)),
        )

    def side(self, zz, p):
        part = self.piece(p)
        return remote(
            self.r1.at[zz, 1 - self.y, part],
            self.ra.at[zz, part],
            self.sa.at[zz, p],
            self.qa.at[zz, p],
            (self.x, seat(self.z, 1 - self.y, self.c)),
        )

    def line(self, zz, p, up):
        z, y, c = self.z, self.y, self.c
        src = self.ra.at[zz, self.piece(p)]
        dst = (self.ua if up else self.da).at[zz, self.piece(p)]
        send, recv = (self.su, self.qu) if up else (self.sd, self.qd)
        return remote(src, dst, send.at[zz, p], recv.at[zz, p], (self.x, seat(z + 1 if up else z - 1, y, c)))

    def order(self):
        z = self.z
        for t in (3, 2, 1):
            yield z + t <= 3, z + t, True
            yield z - t >= 0, z - t, False
        yield None, z, None

    def begin_plane(self, zz, cond=None):
        for yy in range(2):
            when(cond, lambda: self.first(zz, yy).start())

    def begin(self):
        for cond, zz, _ in self.order():
            self.begin_plane(zz, cond)

    def fold(self, zz, cond=None):
        def go():
            for yy in range(2):
                self.first(zz, yy).wait_recv()
                self.add(self.r1.at[zz, yy], self.part.at[seat(zz, yy, self.c)])
            for p in range(2):
                self.side(zz, p).start()

        when(cond, go)

    def take(self, zz, p, up):
        self.line(zz, p, up).wait_recv()
        part = self.piece(p)
        self.add(self.ra.at[zz, part], (self.ua if up else self.da).at[zz, part])

    def flow_plane(self, cond, zz, up):
        z = self.z

        def go():
            for p in range(2):
                part = self.piece(p)
                self.side(zz, p).wait_recv()
                self.add(self.ra.at[zz, part], self.r1.at[zz, self.y, part])
                if up is not None:
                    pl.when(z > 0 if up else z < 3)(lambda: self.take(zz, p, up))
                    self.line(zz, p, up).start()

        when(cond, go)

    def flow(self):
        z = self.z
        for cond, zz, up in self.order():
            self.flow_plane(cond, zz, up)
        for up, cond in ((True, z > 0), (False, z < 3)):
            for p in range(2):
                when(cond, lambda: self.take(z, p, up))
        self.out[...] = self.ra[z]

    def run(self):
        for cond, zz, _ in self.order():
            self.fold(zz, cond)
        self.flow()

    def end(self):
        for cond, zz, up in self.order():
            for yy in range(2):
                when(cond, lambda: self.first(zz, yy).wait_send())
            for p in range(2):
                when(cond, lambda: self.side(zz, p).wait_send())
                if up is not None:
                    when(cond, lambda: self.line(zz, p, up).wait_send())


NBUF = 4
NSEM = 8
TB = 512


def allowed_mask(first_key, first_query, start_row):
    key = first_key + lax.broadcasted_iota(jnp.int32, (QB, QB), 0)
    query = first_query + lax.broadcasted_iota(jnp.int32, (QB, QB), 1)
    return (key <= query) & (key >= start_row)


SCORE = math.log2(math.e) / math.sqrt(HEAD_SIZE)


def as_row(col):
    n = col.shape[0]
    same = lax.broadcasted_iota(jnp.int32, (n, n), 0) == lax.broadcasted_iota(jnp.int32, (n, n), 1)
    return jnp.sum(jnp.where(same, jnp.broadcast_to(col, (n, n)), 0.0), axis=0, keepdims=True)


def column(line):
    n = line.shape[1]
    same = lax.broadcasted_iota(jnp.int32, (n, n), 0) == lax.broadcasted_iota(jnp.int32, (n, n), 1)
    return jnp.sum(jnp.where(same, jnp.broadcast_to(line.astype(F32), (n, n)), 0.0), axis=1, keepdims=True)


def front(
    tok, query_w, key_w, value_w, out_w, router_w, gate_w, up_w, down_w, gain_a, gain_e, seg, routes, cot, rope, freq,
    hid, wo_all, mixp, q_t, k_t, v_t, o_t, lse, start, cos, sin,
    residual, normed, scale_out, h2, att, probs, picked, wperm, back, g_all, dw,
    wo, w3, spread, seg_mine, row_all, w_mine, seg_all, o_low, att_t, k_n, w_t, wo_v,
    wexp, cot_all, p_t, p_all, backp, mix_v, gg, acc,
    *rest,
):
    bufs, sems = rest[:NBUF], rest[NBUF:]
    (
        t_send, t_recv, o_send, o_recv, c_send, c_recv, h_send, h_recv, w_send, w_recv, g_send, g_recv,
        a_send, a_recv, e_send, e_recv, x_send, x_recv, p_send, p_recv, y_send, y_recv, x_sem,
    ) = sems[NSEM:]
    x, s, z, y, c = place()
    rows, width = tok.shape
    length = 16 * rows
    barrier_all()
    tokens = Gather(tok, lambda src: row_all.at[src], t_send, t_recv)
    tokens.begin()
    keep_tok = pltpu.make_async_copy(tok, row_all.at[s], x_sem.at[2])
    keep_tok.start()
    seg_mine[...] = jnp.broadcast_to(seg[...], seg_mine.shape)
    documents = Exchange(lambda r: seg_mine, lambda r: seg_all.at[r], g_send, g_recv)
    documents.begin()
    by_first = column(gain_a[...])
    for j in range(8):
        wperm[:, 256 * j : 256 * j + 128] = (query_w[:, 128 * j : 128 * j + 128].astype(F32) * by_first).astype(BF)
        pair = [ref[:, 64 * j : 64 * j + 64].astype(F32) for ref in (key_w, value_w)]
        wperm[:, 256 * j + 128 : 256 * j + 256] = (jnp.concatenate(pair, axis=1) * by_first).astype(BF)
    slices = Slices(wperm, w_mine, w_send, w_recv)
    slices.begin()
    by_second = column(gain_e[...])
    wo[:, 0:width] = out_w[...]
    router = router_w[...].astype(F32) * gain_e[...].astype(F32)
    router = jnp.concatenate([jnp.concatenate([router, jnp.zeros((128 - E, 32), F32)], axis=0), jnp.zeros((128, 96), F32)], axis=1)
    wo[:, width : width + 128] = jnp.transpose(router)[0:32].astype(BF)
    outw = GatherAll(wo, lambda x, src: wo_v.at[x, src], o_send, o_recv)
    keep = pltpu.make_async_copy(wo, wo_v.at[x, s], x_sem.at[3])
    keep.start()
    for m, ref in enumerate((gate_w, up_w, down_w)):
        plain = ref[...].astype(F32).reshape(32 * E, F)
        for b in range(F // 128):
            lanes = slice(b * 128, b * 128 + 128)
            spread[b] = plain[:, lanes]
            for e in range(E):
                part = spread[b, pl.ds(e, 32, stride=E), :]
                w3[e, m, :, lanes] = (part * by_second if m < 2 else part).astype(BF)
    weights = Exchange(lambda e: w3.at[e], lambda r: wexp.at[:, x * 16 + r], e_send, e_recv)
    cots = Gather(cot, lambda src: cot_all.at[src], c_send, c_recv)

    def cross(k, begin=True):
        row = weights.index(weights.seat(k, back=True))
        if begin and k:
            weights.arrive(k)
        src = w3.at[s] if k == 0 else wexp.at[:, x * 16 + row]
        copy = remote(src, wexp.at[:, x * 16 + row], x_send.at[k], x_recv.at[k], (1 - x, s))
        if begin:
            copy.start()
        else:
            copy.wait_send()
            remote(src, wexp.at[:, (1 - x) * 16 + row], x_send.at[k], x_recv.at[k], (1 - x, s)).wait_recv()

    factor = jnp.exp2(rope[0].astype(F32))
    for b in range(length // 128):
        position = (b * 128 + lax.broadcasted_iota(jnp.int32, (32, 128), 1)).astype(F32)
        angle = position / factor * freq[...]
        cos[:, b * 128 : b * 128 + 128] = jnp.cos(angle)
        sin[:, b * 128 : b * 128 + 128] = jnp.sin(angle)
    tokens.over(0)
    tokens.line(1)
    slices.share()
    tokens.over(1)
    tokens.line(2)
    outw.begin()
    weights.begin(range(8))
    slices.end()
    w_t[...] = jnp.transpose(w_mine[...].reshape(width, 256).astype(F32)).astype(BF)
    tokens.over(2)
    tokens.line(3)
    outw.over(0)
    outw.line(1)
    weights.begin(range(8, 12))
    for k in range(4):
        cross(k)
    documents.end()
    numbers = seg_all[:, 0, :]
    ends = [jnp.sum((numbers < n).astype(jnp.int32)) for n in (1, 2)]
    for b in range(16):
        line = numbers[b : b + 1]
        start[:, b * 128 : b * 128 + 128] = jnp.where(line == 0, 0, jnp.where(line == 1, ends[0], ends[1]))
    tokens.over(3)
    for t in range(4):
        tokens.done(t)
    keep_tok.wait()
    tokens.end()
    acc[...] = jnp.zeros(acc.shape, F32)

    def project(i, _):
        cols = lane_block(i, 512)
        values = row_all[pl.ds(i * 4, 4)].reshape(512, width).astype(F32)
        scale = lax.rsqrt(jnp.mean(values * values, axis=-1, keepdims=True) + EPSILON)
        hidden = (values * scale).astype(BF)
        row_all[pl.ds(i * 4, 4)] = hidden.reshape(4, rows, width)
        made = dot(w_t[...], hidden, NT)
        co, si = cos[:, cols], sin[:, cols]
        own = jnp.where(c == 0, made[0:64], made[64:128])
        for ref, part in ((q_t, own), (k_t, made[128:192])):
            a, b = part[:32], part[32:]
            ref[0:32, cols] = (a * co - b * si).astype(BF)
            ref[32:64, cols] = (b * co + a * si).astype(BF)
        v_t[:, cols] = made[192:256].astype(BF)
        k_n[cols, :] = jnp.transpose(k_t[:, cols].astype(F32)).astype(BF)
        return 0

    lax.fori_loop(0, length // 512, project, 0)
    keep_hid = pltpu.make_async_copy(row_all, hid, x_sem.at[4])
    keep_hid.start()

    def query_block(i, _):
        @pl.when(i == 2)
        def _():
            outw.over(1)
            outw.line(2)

        @pl.when(i == 5)
        def _():
            outw.over(2)
            outw.line(3)
            for k in range(4, 8):
                cross(k)

        @pl.when(i == 6)
        def _():
            cots.begin()

        @pl.when(i == 7)
        def _():
            outw.over(3)

        cols = lane_block(i)
        queries = q_t[:, cols]
        begin = start[:, cols]

        def key_block(j, carried):
            top, total, acc = carried
            keys = lane_block(j)
            scores = dot(k_n[keys, :], queries) * SCORE
            scores = jnp.where(allowed_mask(j * QB, i * QB, begin), scores, MASKED)
            fresh = jnp.maximum(top, jnp.max(scores, axis=0, keepdims=True))
            powers = jnp.exp2(scores - fresh)
            decay = jnp.exp2(top - fresh)
            total = total * decay + jnp.sum(powers, axis=0, keepdims=True)
            acc = acc * decay + dot(v_t[:, keys], powers.astype(BF))
            return fresh, total, acc

        top, total, acc = lax.fori_loop(
            0,
            i + 1,
            key_block,
            (jnp.full((1, QB), MASKED, F32), jnp.zeros((1, QB), F32), jnp.zeros((HEAD_SIZE, QB), F32)),
        )
        out = acc / total
        o_t[:, cols] = out
        o_low[:, cols] = out.astype(BF)
        lse[:, cols] = top + jnp.log2(total)
        return 0

    lax.fori_loop(0, length // QB, query_block, 0)
    keep_hid.wait()
    heads = Exchange(lambda t: o_low.at[:, lane_block(t, 128)], lambda h: att_t.at[h], a_send, a_recv)
    heads.begin()
    keep_cot = pltpu.make_async_copy(cot, cot_all.at[s], x_sem.at[6])
    keep_cot.start()
    cots.over(0)
    cots.line(1)
    for t in range(4):
        outw.across(t)
    for t in range(4):
        outw.done(t)
    keep.wait()
    keep_wo = pltpu.make_async_copy(wo_v, wo_all, x_sem.at[5])
    keep_wo.start()
    weights.begin(range(12, 16))
    heads.end()
    cots.over(1)
    for k in range(8, 12):
        cross(k)

    att[...] = jnp.transpose(att_t[...].reshape(width, rows).astype(F32)).astype(BF)
    res = tok[...].astype(F32) + dot(att[...], wo_v[:, :, :, 0:width].reshape(width, width), NT)
    residual[...] = res
    scale = lax.rsqrt(jnp.mean(res * res, axis=-1, keepdims=True) + EPSILON)
    norm = res * scale
    normed[...] = norm
    scale_out[...] = jnp.broadcast_to(scale, scale_out.shape)
    hidden = norm.astype(BF)
    h2[...] = hidden
    lanes = lax.broadcasted_iota(jnp.int32, (128, 128), 1)
    logits = jnp.where(lanes < E, dot(hidden, wo_v[:, :, :, width : width + 128].reshape(width, 128)), MASKED)
    top = jnp.max(logits, axis=-1, keepdims=True)
    powers = jnp.exp(logits - top)
    prob = powers / jnp.sum(powers, axis=-1, keepdims=True)
    probs[...] = prob
    names = lax.broadcasted_iota(jnp.int32, (128, 128), 0)
    mask = jnp.zeros((128, 128), F32)
    for k in range(K):
        mask = mask + jnp.where(names == routes[k : k + 1, :], 1.0, 0.0)
    mask = jnp.transpose(mask)
    picked[...] = mask
    p_t[...] = jnp.transpose(prob * mask)[0:E, :]

    hidden = Gather(h2, lambda src: row_all.at[src], h_send, h_recv)
    hidden.begin()
    keep = pltpu.make_async_copy(h2, row_all.at[s], x_sem.at[8])
    keep.start()
    minor = Exchange(lambda r: p_t, lambda r: p_all.at[r], p_send, p_recv)
    minor.begin()
    one = Reduce(backp, back, bufs, sems[:NSEM])
    cots.line(2)
    hidden.over(0)
    keep.wait()
    keep_cot.wait()
    for k in range(12, 16):
        cross(k)
    minor.end()
    hidden.line(1)
    weights.keep().wait()
    for k in range(16):
        cross(k, begin=False)
    cots.done(0)
    hidden.done(0)
    far = z // 2
    order = (z, z + 1 - 2 * far, 2 - 2 * z + 5 * far, 3 - 3 * far)

    def chunk(i, _):
        zz = jnp.where(i == 0, order[0], jnp.where(i == 1, order[1], jnp.where(i == 2, order[2], order[3])))

        for t in (1, 2, 3):

            @pl.when(i == t)
            def _():
                cots.done(t)
                hidden.done(t)

        four = pl.ds(zz * 4, 4)
        some = row_all[four].reshape(4 * rows, width)
        grad = cot_all[four].reshape(4 * rows, width)
        cols = [jnp.broadcast_to(p_all[zz * 4 + b, pl.ds(s, 1), :], (128, 128)) for b in range(4)]
        prob = jnp.concatenate([jnp.transpose(v)[:, 0:1] for v in cols], axis=0)
        gate = dot(some, wexp[0].reshape(width, F))
        up = dot(some, wexp[1].reshape(width, F))

        @pl.when(i == 0)
        def _():
            hidden.over(1)
            hidden.line(2)

        @pl.when(i == 1)
        def _():
            hidden.over(2)
            hidden.line(3)

        @pl.when(i == 2)
        def _():
            one.fold(order[0])
            one.fold(order[1])
            hidden.over(3)

        sig = 1.0 / (1.0 + jnp.exp(-gate))
        silu = gate * sig
        low = (silu * up).astype(BF)
        moved = dot(grad, wexp[2].reshape(width, F))
        seen = jnp.sum(low.astype(F32) * moved, axis=-1, keepdims=True)
        for b in range(4):
            line = jnp.transpose(jnp.broadcast_to(seen[b * 128 : b * 128 + 128], (128, 128)))[0:8]
            gg[zz * 4 + b] = line
        grad_hidden = moved * prob
        grad_gate = (grad_hidden * up * (sig * (1.0 + gate * (1.0 - sig)))).astype(BF)
        grad_up = (grad_hidden * silu).astype(BF)
        below = dot(grad_gate, wexp[0].reshape(width, F), NT) + dot(
            grad_up, wexp[1].reshape(width, F), NT
        )
        backp[four] = below.astype(BF).reshape(4, rows, width)
        one.begin_plane(zz)

        @pl.when(i == 0)
        def _():
            cots.over(2)

        @pl.when(i == 3)
        def _():
            one.fold(order[2])

        out = dot(low, wexp[2].reshape(width, F), NT)
        keep_mix = pltpu.make_async_copy(mix_v, mixp.at[four], x_sem.at[7])
        pl.when(i > 0)(lambda: keep_mix.wait())
        mix_v[...] = (prob * out).astype(BF).reshape(4, rows, width)
        keep_mix.start()
        acc[0] += dot(some, grad_gate, TN)
        acc[1] += dot(some, grad_up, TN)
        acc[2] += dot(grad, (prob * low.astype(F32)).astype(BF), TN)

        @pl.when(i == 0)
        def _():
            cots.line(3)

        @pl.when(i == 1)
        def _():
            cots.over(3)

        return 0

    lax.fori_loop(0, 4, chunk, 0)
    one.fold(order[3])
    seen_out = Exchange(lambda r: gg.at[r], lambda r: g_all.at[r], y_send, y_recv)
    seen_out.begin()
    dw[...] = acc[...].astype(BF).reshape(dw.shape)
    one.flow()
    weights.end_sends()
    for g in (outw, cots, hidden):
        g.end()
    keep_wo.wait()
    pltpu.make_async_copy(mix_v, mixp.at[pl.ds(0, 4)], x_sem.at[7]).wait()
    seen_out.end()
    one.end()


def rear(
    back, g_all, cot, probs, picked, normed, scale, wo, att, h2, dw, mixp, q_t, k_t, v_t, lse, o_t, start, hid_in, cos, sin,
    wperm, tok,
    grad_tokens, dw_all, dwo_sum, wg_all, mix,
    g_res, ga_t, dwo, dwo_x, go_t, gq_t, gkv, k_n, v_n, delta, got, g_t, wg, g_mine, wp, hid, dwx,
    *rest,
):
    bufs, bufs_b = rest[:NBUF], rest[NBUF : 2 * NBUF]
    sems = rest[2 * NBUF :]
    (
        a_send, a_recv, b_send, b_recv, w0s, w0r, w1s, w1r, w2s, w2r, v_send, v_recv, p_send, p_recv, d_sem, x_sem,
    ) = sems[2 * NSEM :]
    x, s, z, y, c = place()
    width = att.shape[1]
    length = q_t.shape[1]
    barrier_all()
    two = Reduce(mixp, mix, bufs_b, sems[NSEM : 2 * NSEM])
    two.begin()
    columns_all = GatherAll(wperm, lambda x, src: wp.at[x, src], p_send, p_recv)
    columns_all.begin()
    loads = [
        pltpu.make_async_copy(wperm, wp.at[x, s], x_sem.at[6]),
        pltpu.make_async_copy(hid_in, hid, x_sem.at[4]),
    ]
    for copy in loads:
        copy.start()
    owners = [
        Exchange(
            lambda r, m=m: dwx.at[m, r],
            lambda e, m=m: dw_all.at[e, m],
            (w0s, w1s, w2s)[m],
            (w0r, w1r, w2r)[m],
        )
        for m in range(3)
    ]

    def over_d(m):
        return remote(dw.at[m, 1 - x], dwx.at[m], d_sem.at[0, m], d_sem.at[1, m], (1 - x, s))

    def to_owners(m):
        over_d(m).wait()
        dwx[m] = (dwx[m].astype(F32) + dw[m, x].astype(F32)).astype(BF)
        owners[m].begin()

    over_d(0).start()

    seen = jnp.concatenate([g_all[e, 0:1, :] for e in range(E)] + [jnp.zeros((128 - E, 128), F32)], axis=0)
    grad_probs = jnp.transpose(seen) * picked[...]
    prob = probs[...]
    grad_logits = (prob * (grad_probs - jnp.sum(prob * grad_probs, axis=-1, keepdims=True))).astype(BF)
    u = back[...].astype(F32) + dot(grad_logits, wo[:, width : width + 128], NT)
    norm = normed[...]
    grad = cot[...].astype(F32) + scale[:, 0:1] * (u - norm * jnp.mean(u * norm, axis=-1, keepdims=True))
    g_res[...] = grad
    branch = grad.astype(BF)
    ga_t[...] = jnp.transpose(dot(branch, wo[:, 0:width])).astype(BF).reshape(ga_t.shape)
    heads = Exchange(lambda h: ga_t.at[h], lambda t: go_t.at[:, lane_block(t, 128)], a_send, a_recv)
    heads.begin()
    over_d(1).start()
    over_d(2).start()
    for cond, zz, _ in two.order():
        two.fold(zz, cond)
    dwo[:, :, :, 0:width] = dot(jnp.transpose(grad).astype(BF), att[...]).astype(BF).reshape(2, 16, 32, width)
    dwo[:, :, :, width : width + 128] = dot(h2[...], grad_logits, TN).astype(BF).reshape(2, 16, 32, 128)
    over_o = remote(dwo.at[1 - x], dwo_x, x_sem.at[0], x_sem.at[1], (1 - x, s))
    over_o.start()
    to_owners(0)
    k_n[...] = jnp.transpose(k_t[...].astype(F32)).astype(BF)
    v_n[...] = jnp.transpose(v_t[...].astype(F32)).astype(BF)
    gkv[...] = jnp.zeros(gkv.shape, F32)
    columns_all.over(0)
    heads.end()
    columns_all.line(1)
    delta[...] = jnp.sum(go_t[...].astype(F32) * o_t[...], axis=0, keepdims=True)

    def query_block(i, _):
        pl.when(i == 4)(lambda: to_owners(1))
        cols = lane_block(i)
        queries, grads = q_t[:, cols], go_t[:, cols]
        begin, log_total, shift = start[:, cols], lse[:, cols], delta[:, cols]

        def key_block(j, sofar):
            rows = lane_block(j)
            scores = dot(k_n[rows, :], queries) * SCORE
            powers = jnp.where(allowed_mask(j * QB, i * QB, begin), jnp.exp2(scores - log_total), 0.0)
            moved = dot(v_n[rows, :], grads)
            grad_scores = (powers * (moved - shift)).astype(BF)
            gkv[0, :, rows] += dot(queries, grad_scores, NT)
            gkv[1, :, rows] += dot(grads, powers.astype(BF), NT)
            return sofar + dot(k_t[:, rows], grad_scores)

        gq_t[:, cols] = lax.fori_loop(0, i + 1, key_block, jnp.zeros((HEAD_SIZE, QB), F32))
        return 0

    lax.fori_loop(0, length // QB, query_block, 0)
    columns_all.over(1)
    columns_all.line(2)
    two.flow()

    pair = remote(gkv.at[1 - c], got, x_sem.at[2], x_sem.at[3], (x, seat(z, y, 1 - c)))
    pair.start()
    columns_all.over(2)
    columns_all.line(3)
    columns_all.over(3)
    scaling = 1.0 / math.sqrt(HEAD_SIZE)
    co, si = cos[...], sin[...]

    def unturn(part):
        a, b = part[:32], part[32:]
        return jnp.concatenate([a * co + b * si, b * co - a * si], axis=0)

    g_t[0] = unturn(gq_t[...] * scaling).astype(BF)
    pair.wait()
    mine = gkv[c] + got[...]
    g_t[1] = jnp.where(c == 0, unturn(mine * scaling), mine).astype(BF)
    tokens = Exchange(
        lambda t: g_t.at[:, :, lane_block(t, 128)], lambda h: g_mine.at[h // 2, :, h % 2], b_send, b_recv
    )
    tokens.begin()
    loads[1].wait()
    wg[...] = jnp.transpose(dot(g_t[...].reshape(128, length), hid[...])).astype(BF).reshape(wg.shape)
    columns = Exchange(lambda r: wg.at[r], lambda r: wg_all.at[r], v_send, v_recv, wide=True)
    columns.begin()
    over_o.wait_recv()
    dwo_x[...] = (dwo_x[...].astype(F32) + dwo[x].astype(F32)).astype(BF)
    out = Reduce(dwo_x, dwo_sum, bufs, sems[:NSEM])
    out.begin()
    out.run()
    for t in range(4):
        columns_all.across(t)
    tokens.end()
    for t in range(4):
        columns_all.done(t)
    loads[0].wait()
    w = jnp.transpose(dot(wp[...].reshape(width, 2 * width), g_mine[...].reshape(2 * width, 128)))
    values = tok[...].astype(F32)
    scale_first = lax.rsqrt(jnp.mean(values * values, axis=-1, keepdims=True) + EPSILON)
    norm = values * scale_first
    grad_tokens[...] = g_res[...] + scale_first * (w - norm * jnp.mean(w * norm, axis=-1, keepdims=True))
    to_owners(2)
    out.end()
    columns.end()
    for m in range(3):
        owners[m].end()
    over_o.wait_send()
    two.end()
    columns_all.end()


def finish(
    wg_all, dwo_sum, dw_all, query_w, key_w, value_w, router_w, gate_w, up_w, gain_a, gain_e, mix, residual, g_tok,
    mixed, grad_tokens, grad_a, grad_e, grad_q, grad_k, grad_v, grad_o, grad_r, grad_gate, grad_up, grad_down,
    spread,
):
    width = grad_o.shape[1]
    mixed[...] = (residual[...] + mix[...].astype(F32)).astype(BF)
    grad_tokens[...] = g_tok[...]
    by_first, by_second = column(gain_a[...]), column(gain_e[...])
    head = [wg_all[h].astype(F32) + wg_all[16 + h].astype(F32) for h in range(16)]
    total = jnp.zeros((32, 128), F32)
    for ref, weight, lanes, seats in (
        (grad_q, query_w, slice(0, 64), range(16)),
        (grad_k, key_w, slice(64, 128), range(0, 16, 2)),
        (grad_v, value_w, slice(64, 128), range(1, 16, 2)),
    ):
        for j in range(len(seats) // 2):
            part = jnp.concatenate([head[seats[2 * j]][:, lanes], head[seats[2 * j + 1]][:, lanes]], axis=1)
            cols = slice(128 * j, 128 * j + 128)
            ref[:, cols] = part * by_first
            total = total + part * weight[:, cols].astype(F32)
    grad_a[...] = as_row(jnp.sum(total, axis=1, keepdims=True))
    grad_o[...] = dwo_sum[:, 0:width].astype(F32)
    router = dwo_sum[:, width : width + 128].astype(F32)
    router = jnp.concatenate([router, jnp.zeros((96, 128), F32)], axis=0)
    router = jnp.transpose(router)[0:E, 0:32]
    grad_r[...] = router * gain_e[...].astype(F32)
    total = jnp.zeros((32 * E, 128), F32)
    for m, (ref, weight) in enumerate(((grad_gate, gate_w), (grad_up, up_w), (grad_down, None))):
        for b in range(F // 128):
            lanes = slice(b * 128, b * 128 + 128)
            for e in range(E):
                part = dw_all[e, m, :, lanes].astype(F32)
                spread[b, pl.ds(e, 32, stride=E), :] = part
            plain = spread[b]
            if m == 2:
                ref[:, :, lanes] = plain.reshape(32, E, 128)
            else:
                ref[:, :, lanes] = plain.reshape(32, E, 128) * by_second[:, :, None]
                total = total + plain * weight[:, :, lanes].astype(F32).reshape(32 * E, 128)
    sums = jnp.sum(jnp.sum(total.reshape(32, E, 128), axis=1), axis=1, keepdims=True)
    grad_e[...] = as_row(sums) + jnp.sum(router * router_w[...].astype(F32), axis=0, keepdims=True)


def frequencies(head_dim):
    halves = head_dim // 2
    return jnp.power(ROPE_BASE, -jnp.arange(halves, dtype=F32) * (2.0 / head_dim))


def sixteen_seats(
    tokens,
    attention_gain,
    expert_gain,
    query_weight,
    key_matrix,
    value_matrix,
    output_weight,
    router_weight,
    gate_weight,
    up_weight,
    down_weight,
    routes,
    segments,
    rope_index,
    cotangent,
):
    D = MODEL_WIDTH
    rows = tokens.shape[1]
    length = 16 * rows
    tok_mine = tokens.reshape(rows, D)
    cot_mine = cotangent.reshape(rows, D)
    powers = np.power(np.float32(ROPE_BASE), -np.arange(32, dtype=np.float32) * np.float32(2.0 / HEAD_SIZE))
    freq = jnp.asarray(np.broadcast_to(powers[:, None], (32, 128)).astype(np.float32))
    (
        hid, wo_all, mixp, q_t, k_t, v_t, o_t, lse, start, cos, sin,
        residual, normed, scale, h2, att, probs, picked, wperm, back, g_all, dw,
    ) = comm_call(
        front,
        [sds((16, rows, D), BF), sds((2, 16, 32, D + 128), BF), sds((16, rows, D), BF)]
        + [sds((64, length), BF)] * 3
        + [sds((64, length), F32), sds((1, length), F32), sds((1, length), jnp.int32)]
        + [sds((32, length), F32)] * 2
        + [sds((rows, D), F32), sds((rows, D), F32), sds((rows, 128), F32), sds((rows, D), BF), sds((rows, D), BF)]
        + [sds((rows, 128), F32), sds((rows, 128), F32), sds((32, 2 * D), BF)]
        + [sds((rows, D), BF), sds((16, 8, rows), F32), sds((3, 2, 16, 32, F), BF)],
        [
            tok_mine,
            query_weight,
            key_matrix,
            value_matrix,
            output_weight,
            router_weight.T,
            gate_weight,
            up_weight,
            down_weight,
            attention_gain.reshape(1, 32),
            expert_gain.reshape(1, 32),
            segments.astype(jnp.int32),
            routes.reshape(rows, K).T,
            cot_mine,
            rope_index.astype(jnp.int32),
            freq,
        ],
        Reduce.SEMS + GATHER_SEMS + GATHER_ALL_SEMS + GATHER_SEMS * 2 + [DMA((16,))] * 14 + [DMA((12,))],
        0,
        [
            VM((32, D + 128), BF),
            VM((E, 3, 32, F), BF),
            VM((F // 128, 32 * E, 128), F32),
            VM((8, rows), jnp.int32),
            VM((16, rows, D), BF),
            VM((2, 8, 2, 32, 256), BF),
            VM((16, 8, rows), jnp.int32),
            VM((64, length), BF),
            VM((16, 64, rows), BF),
            VM((length, 64), BF),
            VM((256, D), BF),
            VM((2, 16, 32, D + 128), BF),
            VM((3, 32, 32, F), BF),
            VM((16, rows, D), BF),
            VM((E, rows), F32),
            VM((16, E, rows), F32),
            VM((16, rows, D), BF),
            VM((4, rows, D), BF),
            VM((16, 8, rows), F32),
            VM((3, D, F), F32),
        ]
        + Reduce.bufs(rows, D),
        [ANY] * 3 + [VM] * 19,
        [VM] * 14 + [SM, VM],
    )
    wo_all = wo_all.reshape(D, D + 128)
    hid = hid.reshape(length, D)
    grad_tokens, dw_all, dwo_sum, wg_all, mix = comm_call(
        rear,
        [sds((rows, D), F32), sds((16, 3, 32, F), BF), sds((32, D + 128), BF), sds((32, 32, 128), BF)]
        + [sds((rows, D), BF)],
        [
            back,
            g_all,
            cot_mine,
            probs,
            picked,
            normed,
            scale,
            wo_all,
            att,
            h2,
            dw,
            mixp,
            q_t,
            k_t,
            v_t,
            lse,
            o_t,
            start,
            hid,
            cos,
            sin,
            wperm,
            tok_mine,
        ],
        Reduce.SEMS * 2 + [DMA((16,))] * 10 + [DMA((32,))] * 2 + GATHER_ALL_SEMS + [DMA((2, 3)), DMA((10,))],
        2,
        [
            VM((rows, D), F32),
            VM((16, 64, rows), BF),
            VM((2, 16, 32, D + 128), BF),
            VM((16, 32, D + 128), BF),
            VM((64, length), BF),
            VM((64, length), F32),
            VM((2, 64, length), F32),
            VM((length, 64), BF),
            VM((length, 64), BF),
            VM((1, length), F32),
            VM((64, length), F32),
            VM((2, 64, length), BF),
            VM((32, 32, 128), BF),
            VM((8, 2, 2, 64, rows), BF),
            VM((2, 16, 32, 2 * D), BF),
            VM((length, D), BF),
            VM((3, 16, 32, F), BF),
        ]
        + Reduce.bufs(32, D + 128)
        + Reduce.bufs(rows, D),
        None,
        [VM] * 18 + [ANY] + [VM] * 4,
    )
    (
        mixed, grad_tokens, grad_a, grad_e, grad_q, grad_k, grad_v, grad_o, grad_r, grad_gate, grad_up, grad_down,
    ) = pl.pallas_call(
        finish,
        out_shape=[sds((rows, D), BF), sds((rows, D), F32), sds((1, 32), F32), sds((1, 32), F32)]
        + [sds((32, n), F32) for n in (D, 512, 512, D)]
        + [sds((E, 32), F32)]
        + [sds((32, E, F), F32)] * 3,
        scratch_shapes=[VM((F // 128, 32 * E, 128), F32)],
        compiler_params=pltpu.CompilerParams(vmem_limit_bytes=VMEM_LIMIT),
    )(
        wg_all,
        dwo_sum,
        dw_all,
        query_weight,
        key_matrix,
        value_matrix,
        router_weight.T,
        gate_weight,
        up_weight,
        attention_gain.reshape(1, 32),
        expert_gain.reshape(1, 32),
        mix,
        residual,
        grad_tokens,
    )
    return (
        mixed.reshape(tokens.shape),
        grad_tokens.reshape(tokens.shape),
        grad_a.reshape(32),
        grad_e.reshape(32),
        grad_q,
        grad_k,
        grad_v,
        grad_o,
        grad_r.T,
        grad_gate,
        grad_up,
        grad_down,
    )


def rms_scale(values):
    return lax.rsqrt(jnp.mean(values * values, axis=-1, keepdims=True) + EPSILON)


def apply_rotary(values, cosine_lookup, sine_lookup):
    halves = values.shape[-1] // 2
    first_half = values[..., :halves]
    second_half = values[..., halves:]
    return jnp.concatenate(
        [
            first_half * cosine_lookup - second_half * sine_lookup,
            second_half * cosine_lookup + first_half * sine_lookup,
        ],
        axis=-1,
    )


def unrotate(values, cosine_lookup, sine_lookup):
    halves = values.shape[-1] // 2
    first_half = values[..., :halves]
    second_half = values[..., halves:]
    return jnp.concatenate(
        [
            first_half * cosine_lookup + second_half * sine_lookup,
            second_half * cosine_lookup - first_half * sine_lookup,
        ],
        axis=-1,
    )


def block_mask(key_start, block_size, query_pos, query_seg, seg_block):
    key_pos = key_start + jnp.arange(block_size, dtype=jnp.int32)
    causal = key_pos[None, :] <= query_pos[:, None]
    same_doc = seg_block[:, None, :] == query_seg[:, :, None]
    return (causal[None] & same_doc)[:, None, None]


def attend_piece(running, pieces, first_key, queries, query_pos, query_seg, scaling):
    key_rows, value_rows, key_segments = pieces
    sequence_count, key_span = (key_rows.shape[0], key_rows.shape[1])
    block_size = math.gcd(key_span, 512)
    kv_heads, head_dim = (queries.shape[2], queries.shape[4])

    def advance(block_index, carried):
        top_score, denominator, numerator = carried
        offset = block_index * block_size
        key_block = lax.dynamic_slice_in_dim(key_rows, offset, block_size, 1).reshape(
            sequence_count, block_size, kv_heads, head_dim
        )
        value_block = lax.dynamic_slice_in_dim(value_rows, offset, block_size, 1).reshape(
            sequence_count, block_size, kv_heads, head_dim
        )
        seg_block = lax.dynamic_slice_in_dim(key_segments, offset, block_size, 1).astype(jnp.int32)
        allowed = block_mask(offset, block_size, query_pos, query_seg, seg_block)
        scores = (
            jnp.einsum("sqkgd,sjkd->skgqj", queries, key_block, preferred_element_type=jnp.float32)
            * scaling
        )
        fresh_top = jnp.maximum(top_score, jnp.max(jnp.where(allowed, scores, MASKED), axis=-1))
        weights = jnp.where(allowed, jnp.exp(scores - fresh_top[..., None]), 0.0)
        decay_factor = jnp.exp(top_score - fresh_top)
        denominator = denominator * decay_factor + jnp.sum(weights, axis=-1)
        numerator = numerator * decay_factor[..., None] + jnp.einsum(
            "skgqj,sjkd->skgqd",
            weights.astype(jnp.bfloat16),
            value_block,
            preferred_element_type=jnp.float32,
        )
        return (fresh_top, denominator, numerator)

    return lax.fori_loop(0, key_span // block_size, advance, running)


def attend_back(pieces, queries, query_pos, query_seg, grad_attn, log_total, row_delta, scaling):
    key_rows, value_rows, key_segments = pieces
    sequence_count, key_span, key_value_width = key_rows.shape
    block_size = math.gcd(key_span, 512)
    kv_heads, head_dim = (queries.shape[2], queries.shape[4])

    def advance(block_index, carried):
        grad_queries, gradient_couples = carried
        offset = block_index * block_size
        key_block = lax.dynamic_slice_in_dim(key_rows, offset, block_size, 1).reshape(
            sequence_count, block_size, kv_heads, head_dim
        )
        value_block = lax.dynamic_slice_in_dim(value_rows, offset, block_size, 1).reshape(
            sequence_count, block_size, kv_heads, head_dim
        )
        seg_block = lax.dynamic_slice_in_dim(key_segments, offset, block_size, 1).astype(jnp.int32)
        allowed = block_mask(offset, block_size, query_pos, query_seg, seg_block)
        scores = (
            jnp.einsum("sqkgd,sjkd->skgqj", queries, key_block, preferred_element_type=jnp.float32)
            * scaling
        )
        weights = jnp.where(allowed, jnp.exp(scores - log_total[..., None]), 0.0)
        grad_weights = jnp.einsum(
            "sqkgd,sjkd->skgqj", grad_attn, value_block, preferred_element_type=jnp.float32
        )
        grad_scores = (weights * (grad_weights - row_delta[..., None])).astype(jnp.bfloat16)
        grad_queries = grad_queries + jnp.einsum(
            "skgqj,sjkd->sqkgd", grad_scores, key_block, preferred_element_type=jnp.float32
        )
        grad_keys = (
            jnp.einsum(
                "skgqj,sqkgd->sjkd", grad_scores, queries, preferred_element_type=jnp.float32
            )
            * scaling
        )
        grad_values = jnp.einsum(
            "skgqj,sqkgd->sjkd",
            weights.astype(jnp.bfloat16),
            grad_attn,
            preferred_element_type=jnp.float32,
        )
        produced = jnp.concatenate(
            [
                grad_keys.reshape(sequence_count, block_size, key_value_width),
                grad_values.reshape(sequence_count, block_size, key_value_width),
            ],
            axis=-1,
        )
        return (
            grad_queries,
            lax.dynamic_update_slice_in_dim(gradient_couples, produced, offset, 1),
        )

    starting = (
        jnp.zeros(queries.shape, jnp.float32),
        jnp.zeros((sequence_count, key_span, 2 * key_value_width), jnp.float32),
    )
    grad_queries, gradient_couples = lax.fori_loop(0, key_span // block_size, advance, starting)
    return (grad_queries * scaling, gradient_couples)


def project_in(pieces, routed):
    gate_rows, up_rows = pieces
    return (
        jnp.einsum("erd,def->erf", routed, gate_rows, preferred_element_type=jnp.float32),
        jnp.einsum("erd,def->erf", routed, up_rows, preferred_element_type=jnp.float32),
    )


def project_out(down_rows, hidden):
    produced = jnp.einsum("erf,def->erd", hidden, down_rows, preferred_element_type=jnp.float32)
    return produced


def back_through_down(down_rows, grad_output):
    return jnp.einsum("erd,def->erf", grad_output, down_rows, preferred_element_type=jnp.float32)


def back_through_in(pieces, grad_gate, grad_up):
    gate_rows, up_rows = pieces
    produced = jnp.einsum(
        "erf,def->erd", grad_gate, gate_rows, preferred_element_type=jnp.float32
    ) + jnp.einsum("erf,def->erd", grad_up, up_rows, preferred_element_type=jnp.float32)
    return produced


def take_slots(slot_data, destination):
    experts, width = (slot_data.shape[0], slot_data.shape[-1])
    sequence_count, sequence_rows, picks = destination.shape
    flat = jnp.transpose(
        slot_data.reshape(experts, sequence_count, -1, width), (1, 0, 2, 3)
    ).reshape(sequence_count, -1, width)
    taken = jax.vmap(lambda table, spots: table[spots])(
        flat, destination.reshape(sequence_count, sequence_rows * picks)
    )
    return taken.reshape(sequence_count, sequence_rows, picks, width)


def place_slots(values, destination, experts, capacity):
    sequence_count, width = (values.shape[0], values.shape[-1])
    empty = jnp.zeros((sequence_count, experts * capacity, width), values.dtype)
    filled = jax.vmap(lambda table, spots, rows: table.at[spots].set(rows))(
        empty, destination.reshape(sequence_count, -1), values.reshape(sequence_count, -1, width)
    )
    return jnp.transpose(
        filled.reshape(sequence_count, experts, capacity, width), (1, 0, 2, 3)
    ).reshape(experts, sequence_count * capacity, width)


def any_seats(
    tokens,
    attention_gain,
    expert_gain,
    query_weight,
    key_matrix,
    value_matrix,
    output_weight,
    router_weight,
    gate_weight,
    up_weight,
    down_weight,
    routes,
    segments,
    rope_index,
    cotangent,
):
    sequence_count, sequence_rows = (tokens.shape[0], tokens.shape[1])
    queries_per_group = QUERY_HEADS // KEY_VALUE_HEADS
    key_value_width = KEY_VALUE_HEADS * HEAD_SIZE
    scaling = 1.0 / math.sqrt(HEAD_SIZE)
    experts_slots = E * CAP
    gathered = (
        lax.all_gather(attention_gain, ("row", "seq"), axis=0, tiled=True),
        lax.all_gather(expert_gain, ("row", "seq"), axis=0, tiled=True),
        lax.all_gather(query_weight, ("row", "seq"), axis=0, tiled=True),
        lax.all_gather(key_matrix, ("row", "seq"), axis=0, tiled=True),
        lax.all_gather(value_matrix, ("row", "seq"), axis=0, tiled=True),
        lax.all_gather(output_weight, ("row", "seq"), axis=0, tiled=True),
        lax.all_gather(router_weight, ("row", "seq"), axis=0, tiled=True),
    )
    gain_first = gathered[0].astype(jnp.float32)
    gain_second = gathered[1].astype(jnp.float32)
    full_query, full_key, full_value, full_output, full_router = gathered[2:]
    inputs = tokens.astype(jnp.float32)
    scale_first = rms_scale(inputs)
    normed_first = inputs * scale_first
    hidden_first = (normed_first * gain_first).astype(jnp.bfloat16)
    query_unrotated = jnp.einsum(
        "sqd,dc->sqc", hidden_first, full_query, preferred_element_type=jnp.float32
    )
    key_unrotated = jnp.einsum(
        "sqd,dc->sqc", hidden_first, full_key, preferred_element_type=jnp.float32
    )
    value_raw = jnp.einsum(
        "sqd,dc->sqc", hidden_first, full_value, preferred_element_type=jnp.float32
    )
    positions = lax.axis_index("seq") * sequence_rows + jnp.arange(sequence_rows, dtype=jnp.int32)
    factor = jnp.power(2.0, rope_index.astype(jnp.float32))
    angles = (positions.astype(jnp.float32)[None, :] / factor[:, None])[..., None] * frequencies(
        HEAD_SIZE
    )
    cosine_lookup = jnp.cos(angles)[:, :, None, :]
    sine_lookup = jnp.sin(angles)[:, :, None, :]
    query_turned = (
        apply_rotary(
            query_unrotated.reshape(sequence_count, sequence_rows, QUERY_HEADS, HEAD_SIZE),
            cosine_lookup,
            sine_lookup,
        )
        .astype(jnp.bfloat16)
        .reshape(sequence_count, sequence_rows, KEY_VALUE_HEADS, queries_per_group, HEAD_SIZE)
    )
    key_turned = (
        apply_rotary(
            key_unrotated.reshape(sequence_count, sequence_rows, KEY_VALUE_HEADS, HEAD_SIZE),
            cosine_lookup,
            sine_lookup,
        )
        .astype(jnp.bfloat16)
        .reshape(sequence_count, sequence_rows, key_value_width)
    )
    value_reduced = value_raw.astype(jnp.bfloat16)
    segment_low = segments.astype(jnp.float32).astype(jnp.bfloat16)
    statistic_shape = (sequence_count, KEY_VALUE_HEADS, queries_per_group, sequence_rows)
    starting = (
        jnp.full(statistic_shape, MASKED, jnp.float32),
        jnp.zeros(statistic_shape, jnp.float32),
        jnp.zeros(statistic_shape + (HEAD_SIZE,), jnp.float32),
    )
    attend = partial(
        attend_piece, queries=query_turned, query_pos=positions, query_seg=segments, scaling=scaling
    )
    top_score, denominator, numerator = attend(
        starting,
        (
            lax.all_gather(key_turned, "seq", axis=1, tiled=True),
            lax.all_gather(value_reduced, "seq", axis=1, tiled=True),
            lax.all_gather(segment_low, "seq", axis=1, tiled=True),
        ),
        jnp.int32(0),
    )
    attn_heads = numerator / denominator[..., None]
    log_total = top_score + jnp.log(denominator)
    attn_rows = jnp.transpose(attn_heads, (0, 3, 1, 2, 4))
    attn_low = attn_rows.astype(jnp.bfloat16).reshape(
        sequence_count, sequence_rows, QUERY_HEADS * HEAD_SIZE
    )
    branch = jnp.einsum("sqc,dc->sqd", attn_low, full_output, preferred_element_type=jnp.float32)
    residual = inputs + branch
    scale_second = rms_scale(residual)
    normed_second = residual * scale_second
    hidden_second = (normed_second * gain_second).astype(jnp.bfloat16)
    logits = jnp.einsum(
        "sqd,de->sqe", hidden_second, full_router, preferred_element_type=jnp.float32
    )
    router_probs = jax.nn.softmax(logits, axis=-1)
    picked = routes[..., None] == jnp.arange(E, dtype=jnp.int32)
    picked_int = picked.astype(jnp.int32).reshape(sequence_count, sequence_rows * K, E)
    earlier = jnp.cumsum(picked_int, axis=1, dtype=jnp.int32) - picked_int
    slot_ids = jnp.sum(earlier * picked_int, axis=-1, dtype=jnp.int32).reshape(
        sequence_count, sequence_rows, K
    )
    destination = routes * CAP + slot_ids
    chosen = destination[..., None] == jnp.arange(experts_slots, dtype=jnp.int32)
    gate_probs = jnp.sum(jnp.where(picked, router_probs[:, :, None, :], 0.0), axis=-1)
    dispatch = jnp.sum(chosen, axis=2, dtype=jnp.float32).reshape(
        sequence_count, sequence_rows, E, CAP
    )
    slot_rows = sequence_count * CAP
    routed = (
        jnp.einsum(
            "sqec,sqd->escd",
            dispatch.astype(jnp.bfloat16),
            hidden_second,
            preferred_element_type=jnp.float32,
        )
        .astype(jnp.bfloat16)
        .reshape(E, slot_rows, MODEL_WIDTH)
    )
    grad_mixed = cotangent.astype(jnp.float32)
    grad_slot_values = (gate_probs[..., None] * grad_mixed[:, :, None, :]).astype(jnp.bfloat16)
    grad_expert = place_slots(grad_slot_values, destination, E, CAP)
    groups = 4
    width = E // groups

    def some_experts(_, given):
        rows, grads, gate_part, up_part, down_part = given
        pieces = (
            lax.all_gather(gate_part, ("row", "seq"), axis=0, tiled=True),
            lax.all_gather(up_part, ("row", "seq"), axis=0, tiled=True),
        )
        down_rows = lax.all_gather(down_part, ("row", "seq"), axis=0, tiled=True)
        gate_pre, up_pre = project_in(pieces, routed=rows)
        hidden_low = (jax.nn.silu(gate_pre) * up_pre).astype(jnp.bfloat16)
        expert_out = project_out(down_rows, hidden=hidden_low)
        grad_hidden = back_through_down(down_rows, grad_output=grads)
        sigmoid_gate = jax.nn.sigmoid(gate_pre)
        grad_gate = (
            grad_hidden * up_pre * sigmoid_gate * (1.0 + gate_pre * (1.0 - sigmoid_gate))
        ).astype(jnp.bfloat16)
        grad_up = (grad_hidden * (gate_pre * sigmoid_gate)).astype(jnp.bfloat16)
        grad_routed = back_through_in(pieces, grad_gate=grad_gate, grad_up=grad_up)
        made = [
            lax.psum_scatter(
                jnp.einsum("erd,erf->def", left, right, preferred_element_type=jnp.float32),
                ("row", "seq"),
                scatter_dimension=0,
                tiled=True,
            )
            for left, right in ((rows, grad_gate), (rows, grad_up), (grads, hidden_low))
        ]
        return None, (expert_out, grad_routed, *made)

    def grouped(weight):
        return jnp.moveaxis(weight.reshape(weight.shape[0], groups, width, F), 1, 0)

    _, (expert_out, grad_routed, *expert_grads) = lax.scan(
        some_experts,
        None,
        (
            routed.reshape(groups, width, slot_rows, MODEL_WIDTH),
            grad_expert.reshape(groups, width, slot_rows, MODEL_WIDTH),
            grouped(gate_weight),
            grouped(up_weight),
            grouped(down_weight),
        ),
    )
    expert_out = expert_out.reshape(E, slot_rows, MODEL_WIDTH)
    grad_routed = grad_routed.reshape(E, slot_rows, MODEL_WIDTH)
    grad_gate_weight, grad_up_weight, grad_down_weight = [
        jnp.moveaxis(grad, 0, 1).reshape(gate_weight.shape) for grad in expert_grads
    ]
    taken_out = take_slots(expert_out, destination)
    expert_mix = jnp.sum(gate_probs[..., None] * taken_out, axis=2)
    mixed = (residual + expert_mix).astype(jnp.bfloat16)
    grad_gates = jnp.sum(taken_out * grad_mixed[:, :, None, :], axis=-1)
    grad_probs = jnp.sum(jnp.where(picked, grad_gates[..., None], 0.0), axis=2)
    grad_logits = (
        router_probs * (grad_probs - jnp.sum(router_probs * grad_probs, axis=-1, keepdims=True))
    ).astype(jnp.bfloat16)
    grad_second = jnp.sum(take_slots(grad_routed, destination), axis=2) + jnp.einsum(
        "sqe,de->sqd", grad_logits, full_router, preferred_element_type=jnp.float32
    )
    grad_gain_second = jnp.sum(grad_second * normed_second, axis=(0, 1))
    scaled_second = grad_second * gain_second
    grad_residual = grad_mixed + scale_second * (
        scaled_second
        - normed_second * jnp.mean(scaled_second * normed_second, axis=-1, keepdims=True)
    )
    grad_branch = grad_residual.astype(jnp.bfloat16)
    grad_attn = (
        jnp.einsum("sqd,dc->sqc", grad_branch, full_output, preferred_element_type=jnp.float32)
        .astype(jnp.bfloat16)
        .reshape(sequence_count, sequence_rows, KEY_VALUE_HEADS, queries_per_group, HEAD_SIZE)
    )
    row_delta = jnp.transpose(
        jnp.sum(grad_attn.astype(jnp.float32) * attn_rows, axis=-1), (0, 2, 3, 1)
    )
    keys_back = (
        lax.all_gather(key_turned, "seq", axis=1, tiled=True),
        lax.all_gather(value_reduced, "seq", axis=1, tiled=True),
        lax.all_gather(segment_low, "seq", axis=1, tiled=True),
    )
    grad_query_rot, grad_pair_rows = attend_back(
        keys_back, query_turned, positions, segments, grad_attn, log_total, row_delta, scaling
    )
    gradient_couples = lax.psum_scatter(grad_pair_rows, "seq", scatter_dimension=1, tiled=True)
    grad_query = (
        unrotate(
            grad_query_rot.reshape(sequence_count, sequence_rows, QUERY_HEADS, HEAD_SIZE),
            cosine_lookup,
            sine_lookup,
        )
        .astype(jnp.bfloat16)
        .reshape(sequence_count, sequence_rows, QUERY_HEADS * HEAD_SIZE)
    )
    grad_key = (
        unrotate(
            gradient_couples[..., :key_value_width].reshape(
                sequence_count, sequence_rows, KEY_VALUE_HEADS, HEAD_SIZE
            ),
            cosine_lookup,
            sine_lookup,
        )
        .astype(jnp.bfloat16)
        .reshape(sequence_count, sequence_rows, key_value_width)
    )
    grad_value = gradient_couples[..., key_value_width:].astype(jnp.bfloat16)
    grad_first = (
        jnp.einsum("sqc,dc->sqd", grad_query, full_query, preferred_element_type=jnp.float32)
        + jnp.einsum("sqc,dc->sqd", grad_key, full_key, preferred_element_type=jnp.float32)
        + jnp.einsum("sqc,dc->sqd", grad_value, full_value, preferred_element_type=jnp.float32)
    )
    grad_gain_first = jnp.sum(grad_first * normed_first, axis=(0, 1))
    scaled_first = grad_first * gain_first
    grad_tokens = grad_residual + scale_first * (
        scaled_first - normed_first * jnp.mean(scaled_first * normed_first, axis=-1, keepdims=True)
    )
    attention_grads = lax.psum_scatter(
        jnp.concatenate(
            [
                jnp.einsum(
                    "sqd,sqc->dc", hidden_first, grad_query, preferred_element_type=jnp.float32
                ),
                jnp.einsum(
                    "sqd,sqc->dc", hidden_first, grad_key, preferred_element_type=jnp.float32
                ),
                jnp.einsum(
                    "sqd,sqc->dc", hidden_first, grad_value, preferred_element_type=jnp.float32
                ),
                jnp.einsum(
                    "sqd,sqc->dc", grad_branch, attn_low, preferred_element_type=jnp.float32
                ),
                jnp.einsum(
                    "sqd,sqe->de", hidden_second, grad_logits, preferred_element_type=jnp.float32
                ),
                grad_gain_first[:, None],
                grad_gain_second[:, None],
            ],
            axis=1,
        ),
        ("row", "seq"),
        scatter_dimension=0,
        tiled=True,
    )
    query_cols = QUERY_HEADS * HEAD_SIZE
    edge_two = query_cols + key_value_width
    edge_three = edge_two + key_value_width
    edge_four = edge_three + query_cols
    edge_five = edge_four + E
    return (
        mixed,
        grad_tokens,
        attention_grads[:, edge_five],
        attention_grads[:, edge_five + 1],
        attention_grads[:, :query_cols],
        attention_grads[:, query_cols:edge_two],
        attention_grads[:, edge_two:edge_three],
        attention_grads[:, edge_three:edge_four],
        attention_grads[:, edge_four:edge_five],
        grad_gate_weight,
        grad_up_weight,
        grad_down_weight,
    )


def solution(mesh):
    first = P(("row", "seq"))
    in_specs = (
        (P("row", "seq", None), first, first)
        + (P(("row", "seq"), None),) * 5
        + (P(("row", "seq"), None, None),) * 3
        + (P("row", "seq", None), P("row", "seq"), P("row"), P("row", "seq", None))
    )
    out_specs = (
        (P("row", "seq", None), P("row", "seq", None), first, first)
        + (P(("row", "seq"), None),) * 5
        + (P(("row", "seq"), None, None),) * 3
    )
    body = sixteen_seats if dict(mesh.shape) == {"row": 2, "seq": 16} else any_seats
    return jax.shard_map(body, mesh=mesh, in_specs=in_specs, out_specs=out_specs, check_vma=False)
```

```python
from functools import partial
import math

import jax
import jax.numpy as jnp
import numpy as np
from jax import lax
from jax.experimental import pallas as pl
from jax.experimental.pallas import tpu as pltpu
from jax.sharding import PartitionSpec as P

MODEL_WIDTH = 1024
QUERY_HEADS = 16
KEY_VALUE_HEADS = 8
HEAD_SIZE = 64
F = 512
E = 16
K = 8
CAP = 96

EPSILON = 1e-05
ROPE_BASE = 10000.0
MASKED = -1e30
MESH = pl.DeviceIdType.MESH
VM = pltpu.VMEM
BF = jnp.bfloat16
F32 = jnp.float32
DMA = pltpu.SemaphoreType.DMA
UP, DOWN, SIDE, CORE, ACROSS = range(5)
VMEM_LIMIT = 60 * 1024 * 1024

NN = (((1,), (0,)), ((), ()))
NT = (((1,), (1,)), ((), ()))
TN = (((0,), (0,)), ((), ()))


def dot(a, b, dims=NN):
    return lax.dot_general(a, b, dims, preferred_element_type=F32)


def when(cond, f):
    if cond is None:
        f()
    else:
        pl.when(cond)(f)


def both(a, b):
    if a is None:
        return b
    return a if b is None else a & b


def place():
    x = lax.axis_index("row")
    s = lax.axis_index("seq")
    return x, s, s // 4, (s // 2) % 2, s % 2


def seat(z, y, c):
    return z * 4 + y * 2 + c


def remote(src, dst, send, recv, dev):
    return pltpu.make_async_remote_copy(src, dst, send, recv, device_id=dev, device_id_type=MESH)


def barrier_all():
    x, s = lax.axis_index("row"), lax.axis_index("seq")
    sem = pltpu.get_barrier_semaphore()
    for k in range(1, 16):
        pl.semaphore_signal(sem, inc=1, device_id=(x, (s + k) % 16), device_id_type=MESH)
    for k in range(16):
        pl.semaphore_signal(sem, inc=1, device_id=(1 - x, (s + k) % 16), device_id_type=MESH)
    pl.semaphore_wait(sem, 31)


def barrier_row(partner=False):
    x, s = lax.axis_index("row"), lax.axis_index("seq")
    sem = pltpu.get_barrier_semaphore()
    for k in range(1, 16):
        pl.semaphore_signal(sem, inc=1, device_id=(x, (s + k) % 16), device_id_type=MESH)
    if partner:
        pl.semaphore_signal(sem, inc=1, device_id=(1 - x, s), device_id_type=MESH)
    pl.semaphore_wait(sem, 16 if partner else 15)


def barrier_near():
    x, s, z, y, c = place()
    sem = pltpu.get_barrier_semaphore()
    for cond, dev in (
        (z < 3, (x, seat(z + 1, y, c))),
        (z > 0, (x, seat(z - 1, y, c))),
        (None, (x, seat(z, 1 - y, c))),
        (None, (x, seat(z, y, 1 - c))),
    ):
        when(cond, lambda dev=dev: pl.semaphore_signal(sem, inc=1, device_id=dev, device_id_type=MESH))
    pl.semaphore_wait(sem, 2 + (z < 3).astype(jnp.int32) + (z > 0).astype(jnp.int32))


QB = 256
TOKENS_CUT, COTS_CUT, HIDDEN_CUT = 112, None, 96


def lane_block(i, size=QB):
    return pl.ds(pl.multiple_of(i * size, size), size)


class Gather:
    def __init__(self, own, at, send, recv, cut=None):
        self.own, self.at, self.send, self.recv, self.cut = own, at, send, recv, cut
        self.ending = False
        self.x, self.s, self.z, self.y, self.c = place()

    def device(self, k):
        x, z, y, c = self.x, self.z, self.y, self.c
        return {
            UP: (x, seat(z + 1, y, c)),
            DOWN: (x, seat(z - 1, y, c)),
            SIDE: (x, seat(z, 1 - y, c)),
            CORE: (x, seat(z, y, 1 - c)),
        }[k]

    def part(self, ref, p):
        if self.cut is None:
            return ref
        return ref.at[self.cut : ref.shape[0]] if p else ref.at[0 : self.cut]

    def copy(self, src, k, own=False, p=0):
        ref = self.own if own else self.at(src)
        send, recv = self.send.at[src, k, p], self.recv.at[src, p]
        return remote(self.part(ref, p), self.part(self.at(src), p), send, recv, self.device(k))

    def go(self, src, k, cond=None, own=False, p=0):
        if k == UP:
            cond = both(cond, self.z < 3)
        if k == DOWN:
            cond = both(cond, self.z > 0)
        act = (lambda c: c.wait_send()) if self.ending else (lambda c: c.start())
        when(cond, lambda: act(self.copy(src, k, own, p=p)))

    def wait(self, src, cond=None, p=0):
        if self.ending:
            return
        when(cond, lambda: self.copy(src, SIDE, p=p).wait_recv())

    def sides(self, t):
        if t == 0:
            return ((None, self.z, None),)
        return ((self.z - t >= 0, self.z - t, UP), (self.z + t <= 3, self.z + t, DOWN))

    def begin(self):
        if self.cut is not None:
            self.go(self.s, SIDE, own=True, p=1)
        for k in (UP, DOWN, SIDE, CORE):
            self.go(self.s, k, own=True)
        if self.cut is not None:
            for k in (UP, DOWN, CORE):
                self.go(self.s, k, own=True, p=1)

    def line(self, t):
        for cond, zz, k in self.sides(t):
            mine, other = seat(zz, self.y, self.c), seat(zz, 1 - self.y, self.c)
            parts = ((mine, 0, (k, SIDE, CORE)), (mine, 1, (k, CORE)), (other, 1, (k, CORE)))
            for src, p, ways in parts[: 1 if self.cut is None else 3]:
                self.wait(src, cond, p)
                for way in ways:
                    self.go(src, way, cond, p=p)

    def over(self, t):
        for cond, zz, _ in self.sides(t):
            src = seat(zz, 1 - self.y, self.c)
            if t == 0 and self.cut is not None:
                self.wait(src, cond, 1)
                for way in (UP, DOWN, CORE):
                    self.go(src, way, cond, p=1)
            self.wait(src, cond)
            self.go(src, CORE, cond)

    def done(self, t):
        for cond, zz, _ in self.sides(t):
            for yy in range(2):
                for p in range(1 if self.cut is None else 2):
                    self.wait(seat(zz, yy, 1 - self.c), cond, p)

    def end(self):
        self.ending = True
        self.begin()
        for t in range(4):
            if t:
                self.line(t)
            self.over(t)


GATHER_SEMS = [DMA((16, 4, 2)), DMA((16, 2))]


class GatherAll(Gather):
    def device(self, k):
        return (1 - self.x, self.s) if k == ACROSS else Gather.device(self, k)

    def copy(self, src, k, own=False, x=None, p=0):
        x = self.x if x is None else x
        ref = self.own if own else self.at(x, src)
        return remote(ref, self.at(x, src), self.send.at[x, src, k], self.recv.at[x, src], self.device(k))

    def begin(self):
        for k in (UP, DOWN, SIDE, ACROSS, CORE):
            self.go(self.s, k, own=True)

    def line(self, t):
        for cond, zz, k in self.sides(t):
            src = seat(zz, self.y, self.c)
            self.wait(src, cond)
            for way in (k, SIDE, ACROSS, CORE):
                self.go(src, way, cond)

    def over(self, t):
        for cond, zz, _ in self.sides(t):
            src = seat(zz, 1 - self.y, self.c)
            self.wait(src, cond)
            for way in (ACROSS, CORE):
                self.go(src, way, cond)

    def across(self, t):
        x = 1 - self.x
        for cond, zz, _ in self.sides(t):
            for yy in range(2):
                src = seat(zz, yy, self.c)
                if not self.ending:
                    when(cond, lambda: self.copy(src, SIDE, x=x).wait_recv())
                act = (lambda c: c.wait_send()) if self.ending else (lambda c: c.start())
                when(cond, lambda: act(self.copy(src, CORE, x=x)))

    def done(self, t):
        for cond, zz, _ in self.sides(t):
            for yy in range(2):
                src = seat(zz, yy, 1 - self.c)
                for x in (self.x, 1 - self.x):
                    when(cond, lambda: self.copy(src, SIDE, x=x).wait_recv())

    def end(self):
        Gather.end(self)
        for t in range(4):
            self.across(t)


GATHER_ALL_SEMS = [DMA((2, 16, 5)), DMA((2, 16))]


class Exchange:
    def __init__(self, src, dst, send, recv, wide=False):
        self.x, self.s, self.z, self.y, self.c = place()
        self.wide, self.n = wide, 32 if wide else 16
        self.src, self.dst, self.send, self.recv = src, dst, send, recv

    def seat(self, k, back=False):
        dz = (k // 4) % 4
        if back:
            dz = (4 - dz) % 4
        x = (self.x + k // 16) % 2
        s = seat((self.z + dz) % 4, (self.y + k // 2) % 2, (self.c + k) % 2)
        return x, s

    def index(self, seat_of):
        x, s = seat_of
        return x * 16 + s if self.wide else s

    def copy(self, k):
        to, me = self.seat(k), self.index((self.x, self.s))
        return remote(self.src(self.index(to)), self.dst(me), self.send.at[k], self.recv.at[k], to)

    def keep(self):
        me = self.index((self.x, self.s))
        return pltpu.make_async_copy(self.src(me), self.dst(me), self.recv.at[0])

    def begin(self, ks=None):
        for k in range(self.n) if ks is None else ks:
            if k == 0:
                self.keep().start()
            else:
                self.copy(k).start()

    def arrive(self, k):
        frm = self.seat(k, back=True)
        me = self.index((self.x, self.s))
        remote(self.src(me), self.dst(self.index(frm)), self.send.at[k], self.recv.at[k], frm).wait_recv()
        return self.index(frm)

    def end(self):
        self.keep().wait()
        for k in range(1, self.n):
            self.arrive(k)
        self.end_sends()

    def end_sends(self):
        for k in range(1, self.n):
            self.copy(k).wait_send()


class Swap(Exchange):
    def __init__(self, src, dst, whole, most, send, recv, wide=False):
        Exchange.__init__(self, src, dst, send, recv, wide)
        self.whole, self.most = whole, most

    def keep(self):
        me = self.index((self.x, self.s))
        return pltpu.make_async_copy(self.src(me), self.dst(me), self.recv.at[0])

    def copy(self, k):
        to, me = self.seat(k), self.index((self.x, self.s))
        return remote(self.src(self.index(to)), self.dst(me), self.send.at[0], self.recv.at[0], to)

    def arrived(self):
        remote(self.whole, self.whole, self.send.at[0], self.recv.at[0], self.seat(1)).wait_recv()

    def sent(self):
        remote(self.most, self.most, self.send.at[0], self.recv.at[0], self.seat(1)).wait_send()

    def end(self):
        self.arrived()
        self.sent()


class Slices:
    def __init__(self, src, got, send, recv):
        self.x, self.s, self.z, self.y, self.c = place()
        self.src, self.got, self.send, self.recv = src, got, send, recv

    def block(self, pair):
        return self.src.at[pl.ds((pair // 4) * 32, 32), lane_block(pair % 4, 256)]

    def copy(self, k):
        z, y = (self.z + k // 2) % 4, (self.y + k) % 2
        dst = self.got.at[self.x, self.s // 2, self.c]
        return remote(self.block(z * 2 + y), dst, self.send.at[k], self.recv.at[k], (self.x, seat(z, y, self.c)))

    def begin(self):
        self.local = pltpu.make_async_copy(
            self.block(self.s // 2), self.got.at[self.x, self.s // 2, self.c], self.recv.at[0]
        )
        self.local.start()
        for k in range(1, 8):
            self.copy(k).start()

    def over_x(self):
        ref = self.got.at[self.x, :, self.c]
        return remote(ref, ref, self.send.at[8], self.recv.at[8], (1 - self.x, self.s))

    def over_core(self, k):
        ref = self.got.at[self.x if k == 9 else 1 - self.x, :, self.c]
        return remote(ref, ref, self.send.at[k], self.recv.at[k], (self.x, seat(self.z, self.y, 1 - self.c)))

    def share(self):
        self.local.wait()
        for k in range(1, 8):
            z, y = (self.z + 4 - k // 2) % 4, (self.y + k) % 2
            dst = self.got.at[self.x, z * 2 + y, self.c]
            remote(
                self.block(z * 2 + y), dst, self.send.at[k], self.recv.at[k], (self.x, seat(z, y, self.c))
            ).wait_recv()
        self.over_x().start()
        self.over_core(9).start()

    def end(self):
        self.over_x().wait_recv()
        self.over_core(10).start()
        self.over_core(9).wait_recv()
        self.over_core(10).wait_recv()
        for k in range(1, 8):
            self.copy(k).wait_send()
        self.over_x().wait_send()
        self.over_core(9).wait_send()
        self.over_core(10).wait_send()


ANY = pl.ANY
SM = pltpu.SMEM


def comm_call(body, outs, ins, sems, cid, scratch=(), out_spaces=None, in_spaces=None):
    return pl.pallas_call(
        body,
        out_shape=outs,
        in_specs=[pl.BlockSpec(memory_space=m) for m in in_spaces or [VM] * len(ins)],
        out_specs=[pl.BlockSpec(memory_space=m) for m in out_spaces or [VM] * len(outs)],
        scratch_shapes=list(scratch) + list(sems),
        compiler_params=pltpu.CompilerParams(
            collective_id=cid, has_side_effects=True, vmem_limit_bytes=VMEM_LIMIT
        ),
    )(*ins)


def sds(shape, dtype):
    return jax.ShapeDtypeStruct(shape, dtype)


class Reduce:
    def __init__(self, part, out, bufs, sems, near=None):
        self.part, self.out = part, out
        self.near = part if near is None else near
        self.r1, self.ra, self.ua, self.da = bufs
        self.s1, self.q1, self.sa, self.qa, self.su, self.qu, self.sd, self.qd = sems
        self.x, self.s, self.z, self.y, self.c = place()

    @staticmethod
    def bufs(rows, width):
        return [VM((4, 2, rows, width), BF)] + [VM((4, rows, width), BF)] * 3

    SEMS = [DMA((4, 2))] * 8

    def add(self, dst, src):
        dst[...] = (dst[...].astype(F32) + src[...].astype(F32)).astype(BF)

    def piece(self, p):
        rows = self.ra.shape[1] // 2
        return slice(p * rows, p * rows + rows)

    def first(self, zz, yy):
        return remote(
            self.part.at[seat(zz, yy, 1 - self.c)],
            self.r1.at[zz, yy],
            self.s1.at[zz, yy],
            self.q1.at[zz, yy],
            (self.x, seat(self.z, self.y, 1 - self.c)),
        )

    def side(self, zz, p):
        part = self.piece(p)
        return remote(
            self.r1.at[zz, 1 - self.y, part],
            self.ra.at[zz, part],
            self.sa.at[zz, p],
            self.qa.at[zz, p],
            (self.x, seat(self.z, 1 - self.y, self.c)),
        )

    def line(self, zz, p, up):
        z, y, c = self.z, self.y, self.c
        src = self.ra.at[zz, self.piece(p)]
        dst = (self.ua if up else self.da).at[zz, self.piece(p)]
        send, recv = (self.su, self.qu) if up else (self.sd, self.qd)
        return remote(src, dst, send.at[zz, p], recv.at[zz, p], (self.x, seat(z + 1 if up else z - 1, y, c)))

    def order(self):
        z = self.z
        for t in (3, 2, 1):
            yield z + t <= 3, z + t, True
            yield z - t >= 0, z - t, False
        yield None, z, None

    def begin_plane(self, zz, cond=None):
        for yy in range(2):
            when(cond, lambda: self.first(zz, yy).start())

    def begin(self):
        for cond, zz, _ in self.order():
            self.begin_plane(zz, cond)

    def fold(self, zz, cond=None):
        def go():
            for yy in range(2):
                self.first(zz, yy).wait_recv()
                self.add(self.r1.at[zz, yy], self.near.at[seat(zz, yy, self.c)])
            for p in range(2):
                self.side(zz, p).start()

        when(cond, go)

    def take(self, zz, p, up):
        self.line(zz, p, up).wait_recv()
        part = self.piece(p)
        self.add(self.ra.at[zz, part], (self.ua if up else self.da).at[zz, part])

    def flow_plane(self, cond, zz, up):
        z = self.z

        def go():
            for p in range(2):
                part = self.piece(p)
                self.side(zz, p).wait_recv()
                self.add(self.ra.at[zz, part], self.r1.at[zz, self.y, part])
                if up is not None:
                    pl.when(z > 0 if up else z < 3)(lambda: self.take(zz, p, up))
                    self.line(zz, p, up).start()

        when(cond, go)

    def flow(self):
        z = self.z
        for cond, zz, up in self.order():
            self.flow_plane(cond, zz, up)
        for up, cond in ((True, z > 0), (False, z < 3)):
            for p in range(2):
                when(cond, lambda: self.take(z, p, up))
        self.out[...] = self.ra[z]

    def run(self):
        for cond, zz, _ in self.order():
            self.fold(zz, cond)
        self.flow()

    def end(self):
        for cond, zz, up in self.order():
            for yy in range(2):
                when(cond, lambda: self.first(zz, yy).wait_send())
            for p in range(2):
                when(cond, lambda: self.side(zz, p).wait_send())
                if up is not None:
                    when(cond, lambda: self.line(zz, p, up).wait_send())


NBUF = 4
NSEM = 8
TB = 512


def allowed_mask(first_key, first_query, start_row):
    key = first_key + lax.broadcasted_iota(jnp.int32, (QB, QB), 0)
    query = first_query + lax.broadcasted_iota(jnp.int32, (QB, QB), 1)
    return (key <= query) & (key >= start_row)


SCORE = math.log2(math.e) / math.sqrt(HEAD_SIZE)


def as_row(col):
    n = col.shape[0]
    same = lax.broadcasted_iota(jnp.int32, (n, n), 0) == lax.broadcasted_iota(jnp.int32, (n, n), 1)
    return jnp.sum(jnp.where(same, jnp.broadcast_to(col, (n, n)), 0.0), axis=0, keepdims=True)


def column(line):
    n = line.shape[1]
    same = lax.broadcasted_iota(jnp.int32, (n, n), 0) == lax.broadcasted_iota(jnp.int32, (n, n), 1)
    return jnp.sum(jnp.where(same, jnp.broadcast_to(line.astype(F32), (n, n)), 0.0), axis=1, keepdims=True)


def layer(
    tok, query_w, key_w, value_w, out_w, router_w, gate_w, up_w, down_w, gain_a, gain_e, seg, routes, cot, rope, freq,
    hid, mixp, dw_all, grad_tokens, dwo_sum, wg_all, mix, residual,
    q_t, k_t, v_t, o_t, lse, start, cos, sin, normed, scale_out, h2, att, probs, picked, wperm, back, g_all,
    wo, w3, spread, seg_mine, row_all, w_mine, seg_all, o_low, att_t, k_n, w_t, wo_v,
    wexp, cot_all, p_t, p_all, backp, mix_v, gg, acc,
    g_res, grad_t, router_t, dwo, dwo_x, gkv, v_n, delta, got, g_t, wg, g_mine,
    *rest,
):
    bufs, bufs_o, sems = rest[:NBUF], rest[NBUF : 2 * NBUF], rest[2 * NBUF :]
    (
        t_send, t_recv, o_send, o_recv, c_send, c_recv, h_send, h_recv, q_send, q_recv, w_send, w_recv, e_send, e_recv,
        x_send, x_recv, g_send, g_recv, a_send, a_recv, p_send, p_recv, y_send, y_recv, b_send, b_recv, r_send, r_recv,
        v_send, v_recv, w0s, w0r, w1s, w1r, w2s, w2r, d_sem, x_sem, free,
    ) = sems[3 * NSEM :]
    x, s, z, y, c = place()
    rows, width = tok.shape
    length = 16 * rows
    barrier_all()
    tokens = Gather(tok, lambda src: row_all.at[src], t_send, t_recv, TOKENS_CUT)
    tokens.begin()
    keep_tok = pltpu.make_async_copy(tok, row_all.at[s], x_sem.at[2])
    keep_tok.start()
    seg_mine[...] = jnp.broadcast_to(seg[...], seg_mine.shape)
    documents = Swap(lambda r: seg_mine, lambda r: seg_all.at[r], seg_all, seg_all.at[0:15], g_send, g_recv)
    documents.begin()
    by_first = column(gain_a[...])
    for j in range(8):
        part, lane = slice(32 * (j // 4), 32 * (j // 4) + 32), 256 * (j % 4)
        wperm[part, lane : lane + 128] = (query_w[:, 128 * j : 128 * j + 128].astype(F32) * by_first).astype(BF)
        pair = [ref[:, 64 * j : 64 * j + 64].astype(F32) for ref in (key_w, value_w)]
        wperm[part, lane + 128 : lane + 256] = (jnp.concatenate(pair, axis=1) * by_first).astype(BF)
    slices = Slices(wperm, w_mine, w_send, w_recv)
    slices.begin()
    by_second = column(gain_e[...])
    wo[:, 0:width] = out_w[...]
    router = router_w[...].astype(F32) * gain_e[...].astype(F32)
    router = jnp.concatenate([jnp.concatenate([router, jnp.zeros((128 - E, 32), F32)], axis=0), jnp.zeros((128, 96), F32)], axis=1)
    wo[:, width : width + 128] = jnp.transpose(router)[0:32].astype(BF)
    outw = GatherAll(wo, lambda x, src: wo_v.at[x, src], o_send, o_recv)
    keep = pltpu.make_async_copy(wo, wo_v.at[x, s], x_sem.at[3])
    keep.start()
    for m, ref in enumerate((gate_w, up_w, down_w)):
        plain = ref[...].astype(F32).reshape(32 * E, F)
        for b in range(F // 128):
            lanes = slice(b * 128, b * 128 + 128)
            spread[...] = plain[:, lanes]
            for e in range(E):
                part = spread[pl.ds(e, 32, stride=E), :]
                w3[e, m, :, lanes] = (part * by_second if m < 2 else part).astype(BF)
    weights = Exchange(lambda e: w3.at[e], lambda r: wexp.at[:, x * 16 + r], e_send, e_recv)
    cots = Gather(cot, lambda src: cot_all.at[src], c_send, c_recv, COTS_CUT)

    def cross_copy(k, back=False):
        row = weights.index(weights.seat(k, back=True))
        src = w3.at[s] if k == 0 else wexp.at[:, x * 16 + row]
        dst = wexp.at[:, (1 - x if back else x) * 16 + row]
        return remote(src, dst, x_send.at[k], x_recv.at[k], (1 - x, s))

    def cross(k):
        if k:
            weights.arrive(k)
        cross_copy(k).start()

    factor = jnp.exp2(rope[0].astype(F32))
    for b in range(length // 128):
        position = (b * 128 + lax.broadcasted_iota(jnp.int32, (32, 128), 1)).astype(F32)
        angle = position / factor * freq[...]
        cos[:, b * 128 : b * 128 + 128] = jnp.cos(angle)
        sin[:, b * 128 : b * 128 + 128] = jnp.sin(angle)
    tokens.over(0)
    tokens.line(1)
    slices.share()
    tokens.over(1)
    outw.begin()
    tokens.line(2)
    weights.begin(range(8))
    slices.end()
    w_t[...] = jnp.transpose(w_mine[...].reshape(width, 256).astype(F32)).astype(BF)
    tokens.over(2)
    tokens.line(3)
    outw.over(0)
    outw.line(1)
    weights.begin(range(8, 12))
    documents.end()
    numbers = seg_all[:, 0, :]
    ends = [jnp.sum((numbers < n).astype(jnp.int32)) for n in (1, 2)]
    for b in range(16):
        line = numbers[b : b + 1]
        start[:, b * 128 : b * 128 + 128] = jnp.where(line == 0, 0, jnp.where(line == 1, ends[0], ends[1]))
    tokens.over(3)
    for t in range(4):
        tokens.done(t)
    keep_tok.wait()
    tokens.end()
    acc[...] = jnp.zeros(acc.shape, F32)
    for k in range(4):
        cross(k)

    def project(i, _):
        cols = lane_block(i, 512)
        values = row_all[pl.ds(i * 4, 4)].reshape(512, width).astype(F32)
        scale = lax.rsqrt(jnp.mean(values * values, axis=-1, keepdims=True) + EPSILON)
        hidden = (values * scale).astype(BF)
        row_all[pl.ds(i * 4, 4)] = hidden.reshape(4, rows, width)
        made = dot(w_t[...], hidden, NT)
        co, si = cos[:, cols], sin[:, cols]
        own = jnp.where(c == 0, made[0:64], made[64:128])
        for ref, part in ((q_t, own), (k_t, made[128:192])):
            a, b = part[:32], part[32:]
            ref[0:32, cols] = (a * co - b * si).astype(BF)
            ref[32:64, cols] = (b * co + a * si).astype(BF)
        v_t[:, cols] = made[192:256].astype(BF)
        k_n[cols, :] = jnp.transpose(k_t[:, cols].astype(F32)).astype(BF)
        return 0

    lax.fori_loop(0, length // 512, project, 0)
    keep_hid = pltpu.make_async_copy(row_all, hid, x_sem.at[4])
    keep_hid.start()

    def query_block(i, _):
        @pl.when(i == 2)
        def _():
            outw.over(1)
            outw.line(2)

        @pl.when(i == 5)
        def _():
            outw.over(2)
            outw.line(3)

        @pl.when(i == 6)
        def _():
            cots.begin()

        @pl.when(i == 7)
        def _():
            outw.over(3)

        cols = lane_block(i)
        queries = q_t[:, cols]
        begin = start[:, cols]

        def key_block(j, carried):
            top, total, acc = carried
            keys = lane_block(j)
            scores = dot(k_n[keys, :], queries) * SCORE
            scores = jnp.where(allowed_mask(j * QB, i * QB, begin), scores, MASKED)
            fresh = jnp.maximum(top, jnp.max(scores, axis=0, keepdims=True))
            powers = jnp.exp2(scores - fresh)
            decay = jnp.exp2(top - fresh)
            total = total * decay + jnp.sum(powers, axis=0, keepdims=True)
            acc = acc * decay + dot(v_t[:, keys], powers.astype(BF))
            return fresh, total, acc

        top, total, acc = lax.fori_loop(
            0,
            i + 1,
            key_block,
            (jnp.full((1, QB), MASKED, F32), jnp.zeros((1, QB), F32), jnp.zeros((HEAD_SIZE, QB), F32)),
        )
        out = acc / total
        o_t[:, cols] = out
        o_low[:, cols] = out.astype(BF)
        lse[:, cols] = top + jnp.log2(total)
        return 0

    lax.fori_loop(0, length // QB, query_block, 0)
    for k in range(4, 8):
        cross(k)
    keep_hid.wait()
    heads = Swap(
        lambda t: o_low.at[:, lane_block(t, 128)], lambda h: att_t.at[h], att_t, att_t.at[0:15], a_send, a_recv
    )
    heads.begin()
    keep_cot = pltpu.make_async_copy(cot, cot_all.at[s], x_sem.at[6])
    keep_cot.start()
    for t in range(4):
        outw.across(t)
    for t in range(4):
        outw.done(t)
    keep.wait()
    cots.over(0)
    cots.line(1)
    weights.begin(range(12, 16))
    heads.end()
    for k in range(8, 12):
        cross(k)

    att[...] = jnp.transpose(att_t[...].reshape(width, rows).astype(F32)).astype(BF)
    res = tok[...].astype(F32) + dot(att[...], wo_v[:, :, :, 0:width].reshape(width, width), NT)
    residual[...] = res
    scale = lax.rsqrt(jnp.mean(res * res, axis=-1, keepdims=True) + EPSILON)
    norm = res * scale
    normed[...] = norm
    scale_out[...] = jnp.broadcast_to(scale, scale_out.shape)
    hidden = norm.astype(BF)
    h2[...] = hidden
    lanes = lax.broadcasted_iota(jnp.int32, (128, 128), 1)
    logits = jnp.where(lanes < E, dot(hidden, wo_v[:, :, :, width : width + 128].reshape(width, 128)), MASKED)
    top = jnp.max(logits, axis=-1, keepdims=True)
    powers = jnp.exp(logits - top)
    prob = powers / jnp.sum(powers, axis=-1, keepdims=True)
    probs[...] = prob
    names = lax.broadcasted_iota(jnp.int32, (128, 128), 0)
    mask = jnp.zeros((128, 128), F32)
    for k in range(K):
        mask = mask + jnp.where(names == routes[k : k + 1, :], 1.0, 0.0)
    mask = jnp.transpose(mask)
    picked[...] = mask
    p_t[...] = jnp.transpose(prob * mask)[0:E, :]

    hidden = Gather(h2, lambda src: row_all.at[src], h_send, h_recv, HIDDEN_CUT)
    hidden.begin()
    keep = pltpu.make_async_copy(h2, row_all.at[s], x_sem.at[8])
    keep.start()
    minor = Swap(lambda r: p_t, lambda r: p_all.at[r], p_all, p_all.at[0:15], p_send, p_recv)
    minor.begin()
    one = Reduce(backp, back, bufs, sems[:NSEM])
    hidden.over(0)
    keep.wait()
    keep_cot.wait()
    weights.end_sends()
    weights.keep().wait()
    cross_copy(0).wait_send()
    for k in range(12, 16):
        cross(k)
    minor.end()
    hidden.line(1)
    for k in range(16):
        if k:
            cross_copy(k).wait_send()
        cross_copy(k, back=True).wait_recv()
    cots.done(0)
    hidden.done(0)
    far = z // 2
    order = (z, z + 1 - 2 * far, 2 - 2 * z + 5 * far, 3 - 3 * far)

    def chunk(i, _):
        zz = jnp.where(i == 0, order[0], jnp.where(i == 1, order[1], jnp.where(i == 2, order[2], order[3])))

        for t in (1, 2, 3):

            @pl.when(i == t)
            def _():
                cots.done(t)
                hidden.done(t)

        four = pl.ds(zz * 4, 4)
        some = row_all[four].reshape(4 * rows, width)
        grad = cot_all[four].reshape(4 * rows, width)
        cols = [jnp.broadcast_to(p_all[zz * 4 + b, pl.ds(s, 1), :], (128, 128)) for b in range(4)]
        prob = jnp.concatenate([jnp.transpose(v)[:, 0:1] for v in cols], axis=0)
        gate = dot(some, wexp[0].reshape(width, F))
        up = dot(some, wexp[1].reshape(width, F))

        @pl.when(i == 0)
        def _():
            hidden.over(1)
            hidden.line(2)
            cots.over(1)

        @pl.when(i == 1)
        def _():
            hidden.over(2)
            hidden.line(3)

        @pl.when(i == 2)
        def _():
            one.fold(order[0])
            one.fold(order[1])
            hidden.over(3)

        sig = 1.0 / (1.0 + jnp.exp(-gate))
        silu = gate * sig
        low = (silu * up).astype(BF)
        moved = dot(grad, wexp[2].reshape(width, F))
        seen = jnp.sum(low.astype(F32) * moved, axis=-1, keepdims=True)
        for b in range(4):
            line = jnp.transpose(jnp.broadcast_to(seen[b * 128 : b * 128 + 128], (128, 128)))[0:8]
            gg[zz * 4 + b] = line
        grad_hidden = moved * prob
        grad_gate = (grad_hidden * up * (sig * (1.0 + gate * (1.0 - sig)))).astype(BF)
        grad_up = (grad_hidden * silu).astype(BF)
        below = dot(grad_gate, wexp[0].reshape(width, F), NT) + dot(
            grad_up, wexp[1].reshape(width, F), NT
        )
        backp[four] = below.astype(BF).reshape(4, rows, width)
        one.begin_plane(zz)

        @pl.when(i == 0)
        def _():
            cots.line(2)

        @pl.when(i == 1)
        def _():
            cots.over(2)

        @pl.when(i == 2)
        def _():
            cots.over(3)

        @pl.when(i == 3)
        def _():
            one.fold(order[2])

        out = dot(low, wexp[2].reshape(width, F), NT)
        keep_mix = pltpu.make_async_copy(mix_v, mixp.at[four], x_sem.at[7])
        pl.when(i > 0)(lambda: keep_mix.wait())
        mix_v[...] = (prob * out).astype(BF).reshape(4, rows, width)
        keep_mix.start()
        acc[0] += dot(some, grad_gate, TN)
        acc[1] += dot(some, grad_up, TN)
        acc[2] += dot(grad, (prob * low.astype(F32)).astype(BF), TN)

        @pl.when(i == 1)
        def _():
            cots.line(3)

        return 0

    lax.fori_loop(0, 4, chunk, 0)
    one.fold(order[3])
    seen_out = Swap(lambda r: gg.at[r], lambda r: g_all.at[r], g_all, g_all.at[0:15], y_send, y_recv)
    seen_out.begin()

    def over_d(m):
        part = wexp.at[m, pl.ds((1 - x) * 16, 16)]
        return remote(part, w3.at[:, m], d_sem.at[0, m], d_sem.at[1, m], (1 - x, s))

    for m in range(3):
        wexp[m] = acc[m].astype(BF).reshape(wexp.shape[1:])
        over_d(m).start()
    owners = [
        Swap(
            lambda r, m=m: w3.at[r, m],
            lambda e, m=m: dw_all.at[m, e],
            dw_all.at[m],
            dw_all.at[m, 0:15],
            (w0s, w1s, w2s)[m],
            (w0r, w1r, w2r)[m],
        )
        for m in range(3)
    ]

    def to_owners(m):
        over_d(m).wait()
        w3[:, m] = (w3[:, m].astype(F32) + wexp[m, pl.ds(x * 16, 16)].astype(F32)).astype(BF)
        owners[m].begin()

    for g in (outw, cots, hidden):
        g.end()
    one.flow()
    one.end()
    pltpu.make_async_copy(mix_v, mixp.at[pl.ds(0, 4)], x_sem.at[7]).wait()
    near = (
        (z < 3, (x, seat(z + 1, y, c))),
        (z > 0, (x, seat(z - 1, y, c))),
        (None, (x, seat(z, 1 - y, c))),
        (None, (x, seat(z, y, 1 - c))),
        (None, (1 - x, s)),
    )
    for cond, dev in near:
        when(cond, lambda dev=dev: pl.semaphore_signal(free, inc=1, device_id=dev, device_id_type=MESH))
    loads = [
        pltpu.make_async_copy(hid, row_all, x_sem.at[9]),
        pltpu.make_async_copy(mixp, backp, x_sem.at[10]),
    ]
    for copy in loads:
        copy.start()
    seen_out.end()
    pl.semaphore_wait(free, 3 + (z < 3).astype(jnp.int32) + (z > 0).astype(jnp.int32))
    me = x * 16 + s
    columns_all = GatherAll(
        wperm, lambda x_, src: cot_all.at[x_ * 8 + src // 2, pl.ds((src % 2) * 64, 64)], q_send, q_recv
    )
    columns_all.begin()
    keep_w = pltpu.make_async_copy(wperm, cot_all.at[me // 2, pl.ds((me % 2) * 64, 64)], x_sem.at[11])
    keep_w.start()
    two = Reduce(mixp, mix, bufs, sems[NSEM : 2 * NSEM], backp)
    two.begin()

    seen = jnp.concatenate([g_all[e, 0:1, :] for e in range(E)] + [jnp.zeros((128 - E, 128), F32)], axis=0)
    grad_probs = jnp.transpose(seen) * picked[...]
    prob = probs[...]
    grad_logits = (prob * (grad_probs - jnp.sum(prob * grad_probs, axis=-1, keepdims=True))).astype(BF)
    u = back[...].astype(F32) + dot(
        grad_logits, wo_v[:, :, :, width : width + 128].reshape(width, 128), NT
    )
    norm = normed[...]
    grad = cot[...].astype(F32) + scale_out[:, 0:1] * (u - norm * jnp.mean(u * norm, axis=-1, keepdims=True))
    g_res[...] = grad
    branch = grad.astype(BF)
    att_t[...] = jnp.transpose(dot(branch, wo_v[:, :, :, 0:width].reshape(width, width))).astype(BF).reshape(att_t.shape)
    heads = Swap(
        lambda h: att_t.at[h], lambda t: o_low.at[:, lane_block(t, 128)], o_low, att_t.at[0:15], b_send, b_recv
    )
    heads.begin()
    columns_all.over(0)
    columns_all.line(1)
    loads[1].wait()
    for cond, zz, _ in two.order():
        two.fold(zz, cond)
    grad_t[...] = jnp.transpose(grad).astype(BF)
    other = pl.ds((1 - x) * (width // 2), width // 2)
    router_t[...] = dot(h2[...], grad_logits, TN).astype(BF)
    dwo[:, :, 0:width] = dot(grad_t[other, :], att[...]).astype(BF).reshape(16, 32, width)
    dwo[:, :, width : width + 128] = router_t[other, :].reshape(16, 32, 128)
    over_o = remote(dwo, dwo_x, x_sem.at[12], x_sem.at[13], (1 - x, s))
    over_o.start()
    to_owners(0)
    to_owners(1)
    v_n[...] = jnp.transpose(v_t[...].astype(F32)).astype(BF)
    gkv[...] = jnp.zeros(gkv.shape, F32)
    heads.end()
    delta[...] = jnp.sum(o_low[...].astype(F32) * o_t[...], axis=0, keepdims=True)

    def query_block(i, _):
        @pl.when(i == 3)
        def _():
            two.flow()

        @pl.when(i == 4)
        def _():
            columns_all.over(1)
            to_owners(2)

        @pl.when(i == 5)
        def _():
            columns_all.line(2)

        cols = lane_block(i)
        queries, grads = q_t[:, cols], o_low[:, cols]
        begin, log_total, shift = start[:, cols], lse[:, cols], delta[:, cols]

        def key_block(j, sofar):
            rows = lane_block(j)
            scores = dot(k_n[rows, :], queries) * SCORE
            powers = jnp.where(allowed_mask(j * QB, i * QB, begin), jnp.exp2(scores - log_total), 0.0)
            moved = dot(v_n[rows, :], grads)
            grad_scores = (powers * (moved - shift)).astype(BF)
            gkv[0, :, rows] += dot(queries, grad_scores, NT)
            gkv[1, :, rows] += dot(grads, powers.astype(BF), NT)
            return sofar + dot(k_t[:, rows], grad_scores)

        o_t[:, cols] = lax.fori_loop(0, i + 1, key_block, jnp.zeros((HEAD_SIZE, QB), F32))
        return 0

    lax.fori_loop(0, length // QB, query_block, 0)
    columns_all.over(2)

    pair = remote(gkv.at[1 - c], got, x_sem.at[14], x_sem.at[15], (x, seat(z, y, 1 - c)))
    pair.start()
    columns_all.line(3)
    over_o.wait_recv()
    own = pl.ds(x * (width // 2), width // 2)
    mine = dot(grad_t[own, :], att[...]).reshape(16, 32, width)
    dwo_x[:, :, 0:width] = (dwo_x[:, :, 0:width].astype(F32) + mine).astype(BF)
    mine = router_t[own, :].reshape(16, 32, 128).astype(F32)
    dwo_x[:, :, width : width + 128] = (dwo_x[:, :, width : width + 128].astype(F32) + mine).astype(BF)
    out = Reduce(dwo_x, dwo_sum, bufs_o, sems[2 * NSEM : 3 * NSEM])
    out.begin()
    scaling = 1.0 / math.sqrt(HEAD_SIZE)
    co, si = cos[...], sin[...]

    def unturn(part):
        a, b = part[:32], part[32:]
        return jnp.concatenate([a * co + b * si, b * co - a * si], axis=0)

    g_t[0] = unturn(o_t[...] * scaling).astype(BF)
    pair.wait()
    mine = gkv[c] + got[...]
    g_t[1] = jnp.where(c == 0, unturn(mine * scaling), mine).astype(BF)
    tokens = Swap(
        lambda t: g_t.at[:, :, lane_block(t, 128)],
        lambda h: g_mine.at[h // 2, :, h % 2],
        g_mine,
        g_t.at[:, :, 0 : length - 128],
        r_send,
        r_recv,
    )
    tokens.begin()
    loads[0].wait()
    wg[...] = jnp.transpose(dot(g_t[...].reshape(128, length), row_all[...].reshape(length, width))).astype(BF).reshape(
        wg.shape
    )
    columns = Swap(lambda r: wg.at[r], lambda r: wg_all.at[r], wg_all, wg_all.at[0:31], v_send, v_recv, wide=True)
    columns.begin()
    columns_all.over(3)
    for t in range(4):
        columns_all.across(t)
    for t in range(4):
        columns_all.done(t)
    keep_w.wait()
    for cond, zz, _ in out.order():
        out.fold(zz, cond)
    tokens.end()
    halves = cot_all[...].reshape(32, 2, 32, width)
    w = sum(dot(halves[:, h].reshape(width, width), g_mine[4 * h : 4 * h + 4].reshape(width, 128)) for h in range(2))
    w = jnp.transpose(w)
    values = tok[...].astype(F32)
    scale_first = lax.rsqrt(jnp.mean(values * values, axis=-1, keepdims=True) + EPSILON)
    norm = values * scale_first
    grad_tokens[...] = g_res[...] + scale_first * (w - norm * jnp.mean(w * norm, axis=-1, keepdims=True))
    out.flow()
    out.end()
    columns.end()
    for owner in owners:
        owner.end()
    over_o.wait_send()
    two.end()
    columns_all.end()


def finish(
    wg_all, dwo_sum, dw_all, query_w, key_w, value_w, router_w, gate_w, up_w, gain_a, gain_e, mix, residual, g_tok,
    mixed, grad_tokens, grad_a, grad_e, grad_q, grad_k, grad_v, grad_o, grad_r, grad_gate, grad_up, grad_down,
    spread,
):
    width = grad_o.shape[1]
    mixed[...] = (residual[...] + mix[...].astype(F32)).astype(BF)
    grad_tokens[...] = g_tok[...]
    by_first, by_second = column(gain_a[...]), column(gain_e[...])
    head = [wg_all[h].astype(F32) + wg_all[16 + h].astype(F32) for h in range(16)]
    total = jnp.zeros((32, 128), F32)
    for ref, weight, lanes, seats in (
        (grad_q, query_w, slice(0, 64), range(16)),
        (grad_k, key_w, slice(64, 128), range(0, 16, 2)),
        (grad_v, value_w, slice(64, 128), range(1, 16, 2)),
    ):
        for j in range(len(seats) // 2):
            part = jnp.concatenate([head[seats[2 * j]][:, lanes], head[seats[2 * j + 1]][:, lanes]], axis=1)
            cols = slice(128 * j, 128 * j + 128)
            ref[:, cols] = part * by_first
            total = total + part * weight[:, cols].astype(F32)
    grad_a[...] = as_row(jnp.sum(total, axis=1, keepdims=True))
    grad_o[...] = dwo_sum[:, 0:width].astype(F32)
    router = dwo_sum[:, width : width + 128].astype(F32)
    router = jnp.concatenate([router, jnp.zeros((96, 128), F32)], axis=0)
    router = jnp.transpose(router)[0:E, 0:32]
    grad_r[...] = router * gain_e[...].astype(F32)
    total = jnp.zeros((32 * E, 128), F32)
    for m, (ref, weight) in enumerate(((grad_gate, gate_w), (grad_up, up_w), (grad_down, None))):
        for b in range(F // 128):
            lanes = slice(b * 128, b * 128 + 128)
            for e in range(E):
                part = dw_all[m, e, :, lanes].astype(F32)
                spread[b, pl.ds(e, 32, stride=E), :] = part
            plain = spread[b]
            if m == 2:
                ref[:, :, lanes] = plain.reshape(32, E, 128)
            else:
                ref[:, :, lanes] = plain.reshape(32, E, 128) * by_second[:, :, None]
                total = total + plain * weight[:, :, lanes].astype(F32).reshape(32 * E, 128)
    sums = jnp.sum(jnp.sum(total.reshape(32, E, 128), axis=1), axis=1, keepdims=True)
    grad_e[...] = as_row(sums) + jnp.sum(router * router_w[...].astype(F32), axis=0, keepdims=True)


def frequencies(head_dim):
    halves = head_dim // 2
    return jnp.power(ROPE_BASE, -jnp.arange(halves, dtype=F32) * (2.0 / head_dim))


def sixteen_seats(
    tokens,
    attention_gain,
    expert_gain,
    query_weight,
    key_matrix,
    value_matrix,
    output_weight,
    router_weight,
    gate_weight,
    up_weight,
    down_weight,
    routes,
    segments,
    rope_index,
    cotangent,
):
    D = MODEL_WIDTH
    rows = tokens.shape[1]
    length = 16 * rows
    tok_mine = tokens.reshape(rows, D)
    cot_mine = cotangent.reshape(rows, D)
    powers = np.power(np.float32(ROPE_BASE), -np.arange(32, dtype=np.float32) * np.float32(2.0 / HEAD_SIZE))
    freq = jnp.asarray(np.broadcast_to(powers[:, None], (32, 128)).astype(np.float32))
    _, _, dw_all, grad_tokens, dwo_sum, wg_all, mix, residual = comm_call(
        layer,
        [sds((16, rows, D), BF), sds((16, rows, D), BF), sds((3, 16, 32, F), BF), sds((rows, D), F32)]
        + [sds((32, D + 128), BF), sds((32, 32, 128), BF), sds((rows, D), BF), sds((rows, D), F32)],
        [
            tok_mine,
            query_weight,
            key_matrix,
            value_matrix,
            output_weight,
            router_weight.T,
            gate_weight,
            up_weight,
            down_weight,
            attention_gain.reshape(1, 32),
            expert_gain.reshape(1, 32),
            segments.astype(jnp.int32),
            routes.reshape(rows, K).T,
            cot_mine,
            rope_index.astype(jnp.int32),
            freq,
        ],
        Reduce.SEMS * 3
        + GATHER_SEMS
        + GATHER_ALL_SEMS
        + GATHER_SEMS * 2
        + GATHER_ALL_SEMS
        + [DMA((16,))] * 6
        + [DMA((1,))] * 20
        + [DMA((2, 3)), DMA((16,)), pltpu.SemaphoreType.REGULAR],
        0,
        [VM((64, length), BF)] * 3
        + [VM((64, length), F32), VM((1, length), F32), VM((1, length), jnp.int32)]
        + [VM((32, length), F32)] * 2
        + [VM((rows, D), F32), VM((rows, 128), F32), VM((rows, D), BF), VM((rows, D), BF)]
        + [VM((rows, 128), F32), VM((rows, 128), F32), VM((64, D), BF), VM((rows, D), BF)]
        + [VM((16, 8, rows), F32)]
        + [
            VM((32, D + 128), BF),
            VM((E, 3, 32, F), BF),
            VM((32 * E, 128), F32),
            VM((8, rows), jnp.int32),
            VM((16, rows, D), BF),
            VM((2, 8, 2, 32, 256), BF),
            VM((16, 8, rows), jnp.int32),
            VM((64, length), BF),
            VM((16, 64, rows), BF),
            VM((length, 64), BF),
            VM((256, D), BF),
            VM((2, 16, 32, D + 128), BF),
            VM((3, 32, 32, F), BF),
            VM((16, rows, D), BF),
            VM((E, rows), F32),
            VM((16, E, rows), F32),
            VM((16, rows, D), BF),
            VM((4, rows, D), BF),
            VM((16, 8, rows), F32),
            VM((3, D, F), F32),
        ]
        + [
            VM((rows, D), F32),
            VM((D, rows), BF),
            VM((D, 128), BF),
            VM((16, 32, D + 128), BF),
            VM((16, 32, D + 128), BF),
            VM((2, 64, length), F32),
            VM((length, 64), BF),
            VM((1, length), F32),
            VM((64, length), F32),
            VM((2, 64, length), BF),
            VM((32, 32, 128), BF),
            VM((8, 2, 2, 64, rows), BF),
        ]
        + Reduce.bufs(rows, D)
        + Reduce.bufs(32, D + 128),
        [ANY] * 3 + [VM] * 5,
        [VM] * 14 + [SM, VM],
    )
    (
        mixed, grad_tokens, grad_a, grad_e, grad_q, grad_k, grad_v, grad_o, grad_r, grad_gate, grad_up, grad_down,
    ) = pl.pallas_call(
        finish,
        out_shape=[sds((rows, D), BF), sds((rows, D), F32), sds((1, 32), F32), sds((1, 32), F32)]
        + [sds((32, n), F32) for n in (D, 512, 512, D)]
        + [sds((E, 32), F32)]
        + [sds((32, E, F), F32)] * 3,
        scratch_shapes=[VM((F // 128, 32 * E, 128), F32)],
        compiler_params=pltpu.CompilerParams(vmem_limit_bytes=VMEM_LIMIT),
    )(
        wg_all,
        dwo_sum,
        dw_all,
        query_weight,
        key_matrix,
        value_matrix,
        router_weight.T,
        gate_weight,
        up_weight,
        attention_gain.reshape(1, 32),
        expert_gain.reshape(1, 32),
        mix,
        residual,
        grad_tokens,
    )
    return (
        mixed.reshape(tokens.shape),
        grad_tokens.reshape(tokens.shape),
        grad_a.reshape(32),
        grad_e.reshape(32),
        grad_q,
        grad_k,
        grad_v,
        grad_o,
        grad_r.T,
        grad_gate,
        grad_up,
        grad_down,
    )


def rms_scale(values):
    return lax.rsqrt(jnp.mean(values * values, axis=-1, keepdims=True) + EPSILON)


def apply_rotary(values, cosine_lookup, sine_lookup):
    halves = values.shape[-1] // 2
    first_half = values[..., :halves]
    second_half = values[..., halves:]
    return jnp.concatenate(
        [
            first_half * cosine_lookup - second_half * sine_lookup,
            second_half * cosine_lookup + first_half * sine_lookup,
        ],
        axis=-1,
    )


def unrotate(values, cosine_lookup, sine_lookup):
    halves = values.shape[-1] // 2
    first_half = values[..., :halves]
    second_half = values[..., halves:]
    return jnp.concatenate(
        [
            first_half * cosine_lookup + second_half * sine_lookup,
            second_half * cosine_lookup - first_half * sine_lookup,
        ],
        axis=-1,
    )


def block_mask(key_start, block_size, query_pos, query_seg, seg_block):
    key_pos = key_start + jnp.arange(block_size, dtype=jnp.int32)
    causal = key_pos[None, :] <= query_pos[:, None]
    same_doc = seg_block[:, None, :] == query_seg[:, :, None]
    return (causal[None] & same_doc)[:, None, None]


def attend_piece(running, pieces, first_key, queries, query_pos, query_seg, scaling):
    key_rows, value_rows, key_segments = pieces
    sequence_count, key_span = (key_rows.shape[0], key_rows.shape[1])
    block_size = math.gcd(key_span, 512)
    kv_heads, head_dim = (queries.shape[2], queries.shape[4])

    def advance(block_index, carried):
        top_score, denominator, numerator = carried
        offset = block_index * block_size
        key_block = lax.dynamic_slice_in_dim(key_rows, offset, block_size, 1).reshape(
            sequence_count, block_size, kv_heads, head_dim
        )
        value_block = lax.dynamic_slice_in_dim(value_rows, offset, block_size, 1).reshape(
            sequence_count, block_size, kv_heads, head_dim
        )
        seg_block = lax.dynamic_slice_in_dim(key_segments, offset, block_size, 1).astype(jnp.int32)
        allowed = block_mask(offset, block_size, query_pos, query_seg, seg_block)
        scores = (
            jnp.einsum("sqkgd,sjkd->skgqj", queries, key_block, preferred_element_type=jnp.float32)
            * scaling
        )
        fresh_top = jnp.maximum(top_score, jnp.max(jnp.where(allowed, scores, MASKED), axis=-1))
        weights = jnp.where(allowed, jnp.exp(scores - fresh_top[..., None]), 0.0)
        decay_factor = jnp.exp(top_score - fresh_top)
        denominator = denominator * decay_factor + jnp.sum(weights, axis=-1)
        numerator = numerator * decay_factor[..., None] + jnp.einsum(
            "skgqj,sjkd->skgqd",
            weights.astype(jnp.bfloat16),
            value_block,
            preferred_element_type=jnp.float32,
        )
        return (fresh_top, denominator, numerator)

    return lax.fori_loop(0, key_span // block_size, advance, running)


def attend_back(pieces, queries, query_pos, query_seg, grad_attn, log_total, row_delta, scaling):
    key_rows, value_rows, key_segments = pieces
    sequence_count, key_span, key_value_width = key_rows.shape
    block_size = math.gcd(key_span, 512)
    kv_heads, head_dim = (queries.shape[2], queries.shape[4])

    def advance(block_index, carried):
        grad_queries, gradient_couples = carried
        offset = block_index * block_size
        key_block = lax.dynamic_slice_in_dim(key_rows, offset, block_size, 1).reshape(
            sequence_count, block_size, kv_heads, head_dim
        )
        value_block = lax.dynamic_slice_in_dim(value_rows, offset, block_size, 1).reshape(
            sequence_count, block_size, kv_heads, head_dim
        )
        seg_block = lax.dynamic_slice_in_dim(key_segments, offset, block_size, 1).astype(jnp.int32)
        allowed = block_mask(offset, block_size, query_pos, query_seg, seg_block)
        scores = (
            jnp.einsum("sqkgd,sjkd->skgqj", queries, key_block, preferred_element_type=jnp.float32)
            * scaling
        )
        weights = jnp.where(allowed, jnp.exp(scores - log_total[..., None]), 0.0)
        grad_weights = jnp.einsum(
            "sqkgd,sjkd->skgqj", grad_attn, value_block, preferred_element_type=jnp.float32
        )
        grad_scores = (weights * (grad_weights - row_delta[..., None])).astype(jnp.bfloat16)
        grad_queries = grad_queries + jnp.einsum(
            "skgqj,sjkd->sqkgd", grad_scores, key_block, preferred_element_type=jnp.float32
        )
        grad_keys = (
            jnp.einsum(
                "skgqj,sqkgd->sjkd", grad_scores, queries, preferred_element_type=jnp.float32
            )
            * scaling
        )
        grad_values = jnp.einsum(
            "skgqj,sqkgd->sjkd",
            weights.astype(jnp.bfloat16),
            grad_attn,
            preferred_element_type=jnp.float32,
        )
        produced = jnp.concatenate(
            [
                grad_keys.reshape(sequence_count, block_size, key_value_width),
                grad_values.reshape(sequence_count, block_size, key_value_width),
            ],
            axis=-1,
        )
        return (
            grad_queries,
            lax.dynamic_update_slice_in_dim(gradient_couples, produced, offset, 1),
        )

    starting = (
        jnp.zeros(queries.shape, jnp.float32),
        jnp.zeros((sequence_count, key_span, 2 * key_value_width), jnp.float32),
    )
    grad_queries, gradient_couples = lax.fori_loop(0, key_span // block_size, advance, starting)
    return (grad_queries * scaling, gradient_couples)


def project_in(pieces, routed):
    gate_rows, up_rows = pieces
    return (
        jnp.einsum("erd,def->erf", routed, gate_rows, preferred_element_type=jnp.float32),
        jnp.einsum("erd,def->erf", routed, up_rows, preferred_element_type=jnp.float32),
    )


def project_out(down_rows, hidden):
    produced = jnp.einsum("erf,def->erd", hidden, down_rows, preferred_element_type=jnp.float32)
    return produced


def back_through_down(down_rows, grad_output):
    return jnp.einsum("erd,def->erf", grad_output, down_rows, preferred_element_type=jnp.float32)


def back_through_in(pieces, grad_gate, grad_up):
    gate_rows, up_rows = pieces
    produced = jnp.einsum(
        "erf,def->erd", grad_gate, gate_rows, preferred_element_type=jnp.float32
    ) + jnp.einsum("erf,def->erd", grad_up, up_rows, preferred_element_type=jnp.float32)
    return produced


def take_slots(slot_data, destination):
    experts, width = (slot_data.shape[0], slot_data.shape[-1])
    sequence_count, sequence_rows, picks = destination.shape
    flat = jnp.transpose(
        slot_data.reshape(experts, sequence_count, -1, width), (1, 0, 2, 3)
    ).reshape(sequence_count, -1, width)
    taken = jax.vmap(lambda table, spots: table[spots])(
        flat, destination.reshape(sequence_count, sequence_rows * picks)
    )
    return taken.reshape(sequence_count, sequence_rows, picks, width)


def place_slots(values, destination, experts, capacity):
    sequence_count, width = (values.shape[0], values.shape[-1])
    empty = jnp.zeros((sequence_count, experts * capacity, width), values.dtype)
    filled = jax.vmap(lambda table, spots, rows: table.at[spots].set(rows))(
        empty, destination.reshape(sequence_count, -1), values.reshape(sequence_count, -1, width)
    )
    return jnp.transpose(
        filled.reshape(sequence_count, experts, capacity, width), (1, 0, 2, 3)
    ).reshape(experts, sequence_count * capacity, width)


def any_seats(
    tokens,
    attention_gain,
    expert_gain,
    query_weight,
    key_matrix,
    value_matrix,
    output_weight,
    router_weight,
    gate_weight,
    up_weight,
    down_weight,
    routes,
    segments,
    rope_index,
    cotangent,
):
    sequence_count, sequence_rows = (tokens.shape[0], tokens.shape[1])
    queries_per_group = QUERY_HEADS // KEY_VALUE_HEADS
    key_value_width = KEY_VALUE_HEADS * HEAD_SIZE
    scaling = 1.0 / math.sqrt(HEAD_SIZE)
    experts_slots = E * CAP
    gathered = (
        lax.all_gather(attention_gain, ("row", "seq"), axis=0, tiled=True),
        lax.all_gather(expert_gain, ("row", "seq"), axis=0, tiled=True),
        lax.all_gather(query_weight, ("row", "seq"), axis=0, tiled=True),
        lax.all_gather(key_matrix, ("row", "seq"), axis=0, tiled=True),
        lax.all_gather(value_matrix, ("row", "seq"), axis=0, tiled=True),
        lax.all_gather(output_weight, ("row", "seq"), axis=0, tiled=True),
        lax.all_gather(router_weight, ("row", "seq"), axis=0, tiled=True),
    )
    gain_first = gathered[0].astype(jnp.float32)
    gain_second = gathered[1].astype(jnp.float32)
    full_query, full_key, full_value, full_output, full_router = gathered[2:]
    inputs = tokens.astype(jnp.float32)
    scale_first = rms_scale(inputs)
    normed_first = inputs * scale_first
    hidden_first = (normed_first * gain_first).astype(jnp.bfloat16)
    query_unrotated = jnp.einsum(
        "sqd,dc->sqc", hidden_first, full_query, preferred_element_type=jnp.float32
    )
    key_unrotated = jnp.einsum(
        "sqd,dc->sqc", hidden_first, full_key, preferred_element_type=jnp.float32
    )
    value_raw = jnp.einsum(
        "sqd,dc->sqc", hidden_first, full_value, preferred_element_type=jnp.float32
    )
    positions = lax.axis_index("seq") * sequence_rows + jnp.arange(sequence_rows, dtype=jnp.int32)
    factor = jnp.power(2.0, rope_index.astype(jnp.float32))
    angles = (positions.astype(jnp.float32)[None, :] / factor[:, None])[..., None] * frequencies(
        HEAD_SIZE
    )
    cosine_lookup = jnp.cos(angles)[:, :, None, :]
    sine_lookup = jnp.sin(angles)[:, :, None, :]
    query_turned = (
        apply_rotary(
            query_unrotated.reshape(sequence_count, sequence_rows, QUERY_HEADS, HEAD_SIZE),
            cosine_lookup,
            sine_lookup,
        )
        .astype(jnp.bfloat16)
        .reshape(sequence_count, sequence_rows, KEY_VALUE_HEADS, queries_per_group, HEAD_SIZE)
    )
    key_turned = (
        apply_rotary(
            key_unrotated.reshape(sequence_count, sequence_rows, KEY_VALUE_HEADS, HEAD_SIZE),
            cosine_lookup,
            sine_lookup,
        )
        .astype(jnp.bfloat16)
        .reshape(sequence_count, sequence_rows, key_value_width)
    )
    value_reduced = value_raw.astype(jnp.bfloat16)
    segment_low = segments.astype(jnp.float32).astype(jnp.bfloat16)
    statistic_shape = (sequence_count, KEY_VALUE_HEADS, queries_per_group, sequence_rows)
    starting = (
        jnp.full(statistic_shape, MASKED, jnp.float32),
        jnp.zeros(statistic_shape, jnp.float32),
        jnp.zeros(statistic_shape + (HEAD_SIZE,), jnp.float32),
    )
    attend = partial(
        attend_piece, queries=query_turned, query_pos=positions, query_seg=segments, scaling=scaling
    )
    top_score, denominator, numerator = attend(
        starting,
        (
            lax.all_gather(key_turned, "seq", axis=1, tiled=True),
            lax.all_gather(value_reduced, "seq", axis=1, tiled=True),
            lax.all_gather(segment_low, "seq", axis=1, tiled=True),
        ),
        jnp.int32(0),
    )
    attn_heads = numerator / denominator[..., None]
    log_total = top_score + jnp.log(denominator)
    attn_rows = jnp.transpose(attn_heads, (0, 3, 1, 2, 4))
    attn_low = attn_rows.astype(jnp.bfloat16).reshape(
        sequence_count, sequence_rows, QUERY_HEADS * HEAD_SIZE
    )
    branch = jnp.einsum("sqc,dc->sqd", attn_low, full_output, preferred_element_type=jnp.float32)
    residual = inputs + branch
    scale_second = rms_scale(residual)
    normed_second = residual * scale_second
    hidden_second = (normed_second * gain_second).astype(jnp.bfloat16)
    logits = jnp.einsum(
        "sqd,de->sqe", hidden_second, full_router, preferred_element_type=jnp.float32
    )
    router_probs = jax.nn.softmax(logits, axis=-1)
    picked = routes[..., None] == jnp.arange(E, dtype=jnp.int32)
    picked_int = picked.astype(jnp.int32).reshape(sequence_count, sequence_rows * K, E)
    earlier = jnp.cumsum(picked_int, axis=1, dtype=jnp.int32) - picked_int
    slot_ids = jnp.sum(earlier * picked_int, axis=-1, dtype=jnp.int32).reshape(
        sequence_count, sequence_rows, K
    )
    destination = routes * CAP + slot_ids
    chosen = destination[..., None] == jnp.arange(experts_slots, dtype=jnp.int32)
    gate_probs = jnp.sum(jnp.where(picked, router_probs[:, :, None, :], 0.0), axis=-1)
    dispatch = jnp.sum(chosen, axis=2, dtype=jnp.float32).reshape(
        sequence_count, sequence_rows, E, CAP
    )
    slot_rows = sequence_count * CAP
    routed = (
        jnp.einsum(
            "sqec,sqd->escd",
            dispatch.astype(jnp.bfloat16),
            hidden_second,
            preferred_element_type=jnp.float32,
        )
        .astype(jnp.bfloat16)
        .reshape(E, slot_rows, MODEL_WIDTH)
    )
    grad_mixed = cotangent.astype(jnp.float32)
    grad_slot_values = (gate_probs[..., None] * grad_mixed[:, :, None, :]).astype(jnp.bfloat16)
    grad_expert = place_slots(grad_slot_values, destination, E, CAP)
    groups = 4
    width = E // groups

    def some_experts(_, given):
        rows, grads, gate_part, up_part, down_part = given
        pieces = (
            lax.all_gather(gate_part, ("row", "seq"), axis=0, tiled=True),
            lax.all_gather(up_part, ("row", "seq"), axis=0, tiled=True),
        )
        down_rows = lax.all_gather(down_part, ("row", "seq"), axis=0, tiled=True)
        gate_pre, up_pre = project_in(pieces, routed=rows)
        hidden_low = (jax.nn.silu(gate_pre) * up_pre).astype(jnp.bfloat16)
        expert_out = project_out(down_rows, hidden=hidden_low)
        grad_hidden = back_through_down(down_rows, grad_output=grads)
        sigmoid_gate = jax.nn.sigmoid(gate_pre)
        grad_gate = (
            grad_hidden * up_pre * sigmoid_gate * (1.0 + gate_pre * (1.0 - sigmoid_gate))
        ).astype(jnp.bfloat16)
        grad_up = (grad_hidden * (gate_pre * sigmoid_gate)).astype(jnp.bfloat16)
        grad_routed = back_through_in(pieces, grad_gate=grad_gate, grad_up=grad_up)
        made = [
            lax.psum_scatter(
                jnp.einsum("erd,erf->def", left, right, preferred_element_type=jnp.float32),
                ("row", "seq"),
                scatter_dimension=0,
                tiled=True,
            )
            for left, right in ((rows, grad_gate), (rows, grad_up), (grads, hidden_low))
        ]
        return None, (expert_out, grad_routed, *made)

    def grouped(weight):
        return jnp.moveaxis(weight.reshape(weight.shape[0], groups, width, F), 1, 0)

    _, (expert_out, grad_routed, *expert_grads) = lax.scan(
        some_experts,
        None,
        (
            routed.reshape(groups, width, slot_rows, MODEL_WIDTH),
            grad_expert.reshape(groups, width, slot_rows, MODEL_WIDTH),
            grouped(gate_weight),
            grouped(up_weight),
            grouped(down_weight),
        ),
    )
    expert_out = expert_out.reshape(E, slot_rows, MODEL_WIDTH)
    grad_routed = grad_routed.reshape(E, slot_rows, MODEL_WIDTH)
    grad_gate_weight, grad_up_weight, grad_down_weight = [
        jnp.moveaxis(grad, 0, 1).reshape(gate_weight.shape) for grad in expert_grads
    ]
    taken_out = take_slots(expert_out, destination)
    expert_mix = jnp.sum(gate_probs[..., None] * taken_out, axis=2)
    mixed = (residual + expert_mix).astype(jnp.bfloat16)
    grad_gates = jnp.sum(taken_out * grad_mixed[:, :, None, :], axis=-1)
    grad_probs = jnp.sum(jnp.where(picked, grad_gates[..., None], 0.0), axis=2)
    grad_logits = (
        router_probs * (grad_probs - jnp.sum(router_probs * grad_probs, axis=-1, keepdims=True))
    ).astype(jnp.bfloat16)
    grad_second = jnp.sum(take_slots(grad_routed, destination), axis=2) + jnp.einsum(
        "sqe,de->sqd", grad_logits, full_router, preferred_element_type=jnp.float32
    )
    grad_gain_second = jnp.sum(grad_second * normed_second, axis=(0, 1))
    scaled_second = grad_second * gain_second
    grad_residual = grad_mixed + scale_second * (
        scaled_second
        - normed_second * jnp.mean(scaled_second * normed_second, axis=-1, keepdims=True)
    )
    grad_branch = grad_residual.astype(jnp.bfloat16)
    grad_attn = (
        jnp.einsum("sqd,dc->sqc", grad_branch, full_output, preferred_element_type=jnp.float32)
        .astype(jnp.bfloat16)
        .reshape(sequence_count, sequence_rows, KEY_VALUE_HEADS, queries_per_group, HEAD_SIZE)
    )
    row_delta = jnp.transpose(
        jnp.sum(grad_attn.astype(jnp.float32) * attn_rows, axis=-1), (0, 2, 3, 1)
    )
    keys_back = (
        lax.all_gather(key_turned, "seq", axis=1, tiled=True),
        lax.all_gather(value_reduced, "seq", axis=1, tiled=True),
        lax.all_gather(segment_low, "seq", axis=1, tiled=True),
    )
    grad_query_rot, grad_pair_rows = attend_back(
        keys_back, query_turned, positions, segments, grad_attn, log_total, row_delta, scaling
    )
    gradient_couples = lax.psum_scatter(grad_pair_rows, "seq", scatter_dimension=1, tiled=True)
    grad_query = (
        unrotate(
            grad_query_rot.reshape(sequence_count, sequence_rows, QUERY_HEADS, HEAD_SIZE),
            cosine_lookup,
            sine_lookup,
        )
        .astype(jnp.bfloat16)
        .reshape(sequence_count, sequence_rows, QUERY_HEADS * HEAD_SIZE)
    )
    grad_key = (
        unrotate(
            gradient_couples[..., :key_value_width].reshape(
                sequence_count, sequence_rows, KEY_VALUE_HEADS, HEAD_SIZE
            ),
            cosine_lookup,
            sine_lookup,
        )
        .astype(jnp.bfloat16)
        .reshape(sequence_count, sequence_rows, key_value_width)
    )
    grad_value = gradient_couples[..., key_value_width:].astype(jnp.bfloat16)
    grad_first = (
        jnp.einsum("sqc,dc->sqd", grad_query, full_query, preferred_element_type=jnp.float32)
        + jnp.einsum("sqc,dc->sqd", grad_key, full_key, preferred_element_type=jnp.float32)
        + jnp.einsum("sqc,dc->sqd", grad_value, full_value, preferred_element_type=jnp.float32)
    )
    grad_gain_first = jnp.sum(grad_first * normed_first, axis=(0, 1))
    scaled_first = grad_first * gain_first
    grad_tokens = grad_residual + scale_first * (
        scaled_first - normed_first * jnp.mean(scaled_first * normed_first, axis=-1, keepdims=True)
    )
    attention_grads = lax.psum_scatter(
        jnp.concatenate(
            [
                jnp.einsum(
                    "sqd,sqc->dc", hidden_first, grad_query, preferred_element_type=jnp.float32
                ),
                jnp.einsum(
                    "sqd,sqc->dc", hidden_first, grad_key, preferred_element_type=jnp.float32
                ),
                jnp.einsum(
                    "sqd,sqc->dc", hidden_first, grad_value, preferred_element_type=jnp.float32
                ),
                jnp.einsum(
                    "sqd,sqc->dc", grad_branch, attn_low, preferred_element_type=jnp.float32
                ),
                jnp.einsum(
                    "sqd,sqe->de", hidden_second, grad_logits, preferred_element_type=jnp.float32
                ),
                grad_gain_first[:, None],
                grad_gain_second[:, None],
            ],
            axis=1,
        ),
        ("row", "seq"),
        scatter_dimension=0,
        tiled=True,
    )
    query_cols = QUERY_HEADS * HEAD_SIZE
    edge_two = query_cols + key_value_width
    edge_three = edge_two + key_value_width
    edge_four = edge_three + query_cols
    edge_five = edge_four + E
    return (
        mixed,
        grad_tokens,
        attention_grads[:, edge_five],
        attention_grads[:, edge_five + 1],
        attention_grads[:, :query_cols],
        attention_grads[:, query_cols:edge_two],
        attention_grads[:, edge_two:edge_three],
        attention_grads[:, edge_three:edge_four],
        attention_grads[:, edge_four:edge_five],
        grad_gate_weight,
        grad_up_weight,
        grad_down_weight,
    )


def solution(mesh):
    first = P(("row", "seq"))
    in_specs = (
        (P("row", "seq", None), first, first)
        + (P(("row", "seq"), None),) * 5
        + (P(("row", "seq"), None, None),) * 3
        + (P("row", "seq", None), P("row", "seq"), P("row"), P("row", "seq", None))
    )
    out_specs = (
        (P("row", "seq", None), P("row", "seq", None), first, first)
        + (P(("row", "seq"), None),) * 5
        + (P(("row", "seq"), None, None),) * 3
    )
    body = sixteen_seats if dict(mesh.shape) == {"row": 2, "seq": 16} else any_seats
    return jax.shard_map(body, mesh=mesh, in_specs=in_specs, out_specs=out_specs, check_vma=False)
```

```python
from functools import partial
import math

import jax
import jax.numpy as jnp
import numpy as np
from jax import lax
from jax.experimental import pallas as pl
from jax.experimental.pallas import tpu as pltpu
from jax.sharding import PartitionSpec as P

MODEL_WIDTH = 1024
QUERY_HEADS = 16
KEY_VALUE_HEADS = 8
HEAD_SIZE = 64
F = 512
E = 16
K = 8
CAP = 96

EPSILON = 1e-05
ROPE_BASE = 10000.0
MASKED = -1e30
MESH = pl.DeviceIdType.MESH
VM = pltpu.VMEM
BF = jnp.bfloat16
F32 = jnp.float32
DMA = pltpu.SemaphoreType.DMA
UP, DOWN, SIDE, CORE, ACROSS = range(5)
VMEM_LIMIT = 60 * 1024 * 1024

NN = (((1,), (0,)), ((), ()))
NT = (((1,), (1,)), ((), ()))
TN = (((0,), (0,)), ((), ()))


def dot(a, b, dims=NN):
    return lax.dot_general(a, b, dims, preferred_element_type=F32)


def when(cond, f):
    if cond is None:
        f()
    else:
        pl.when(cond)(f)


def both(a, b):
    if a is None:
        return b
    return a if b is None else a & b


def place():
    x = lax.axis_index("row")
    s = lax.axis_index("seq")
    return x, s, s // 4, (s // 2) % 2, s % 2


def seat(z, y, c):
    return z * 4 + y * 2 + c


def remote(src, dst, send, recv, dev):
    return pltpu.make_async_remote_copy(src, dst, send, recv, device_id=dev, device_id_type=MESH)


def barrier_all():
    x, s = lax.axis_index("row"), lax.axis_index("seq")
    sem = pltpu.get_barrier_semaphore()
    for k in range(1, 16):
        pl.semaphore_signal(sem, inc=1, device_id=(x, (s + k) % 16), device_id_type=MESH)
    for k in range(16):
        pl.semaphore_signal(sem, inc=1, device_id=(1 - x, (s + k) % 16), device_id_type=MESH)
    pl.semaphore_wait(sem, 31)


def barrier_row(partner=False):
    x, s = lax.axis_index("row"), lax.axis_index("seq")
    sem = pltpu.get_barrier_semaphore()
    for k in range(1, 16):
        pl.semaphore_signal(sem, inc=1, device_id=(x, (s + k) % 16), device_id_type=MESH)
    if partner:
        pl.semaphore_signal(sem, inc=1, device_id=(1 - x, s), device_id_type=MESH)
    pl.semaphore_wait(sem, 16 if partner else 15)


def barrier_near():
    x, s, z, y, c = place()
    sem = pltpu.get_barrier_semaphore()
    for cond, dev in (
        (z < 3, (x, seat(z + 1, y, c))),
        (z > 0, (x, seat(z - 1, y, c))),
        (None, (x, seat(z, 1 - y, c))),
        (None, (x, seat(z, y, 1 - c))),
    ):
        when(cond, lambda dev=dev: pl.semaphore_signal(sem, inc=1, device_id=dev, device_id_type=MESH))
    pl.semaphore_wait(sem, 2 + (z < 3).astype(jnp.int32) + (z > 0).astype(jnp.int32))


QB = 512
TOKENS_CUT, COTS_CUT, HIDDEN_CUT = None, None, 64


def lane_block(i, size=QB):
    return pl.ds(pl.multiple_of(i * size, size), size)


class Gather:
    def __init__(self, own, at, send, recv, cut=None):
        self.own, self.at, self.send, self.recv, self.cut = own, at, send, recv, cut
        self.ending = False
        self.x, self.s, self.z, self.y, self.c = place()

    def device(self, k):
        x, z, y, c = self.x, self.z, self.y, self.c
        return {
            UP: (x, seat(z + 1, y, c)),
            DOWN: (x, seat(z - 1, y, c)),
            SIDE: (x, seat(z, 1 - y, c)),
            CORE: (x, seat(z, y, 1 - c)),
        }[k]

    def part(self, ref, p):
        if self.cut is None:
            return ref
        return ref.at[self.cut : ref.shape[0]] if p else ref.at[0 : self.cut]

    def copy(self, src, k, own=False, p=0):
        ref = self.own if own else self.at(src)
        send, recv = self.send.at[src, k, p], self.recv.at[src, p]
        return remote(self.part(ref, p), self.part(self.at(src), p), send, recv, self.device(k))

    def go(self, src, k, cond=None, own=False, p=0):
        if k == UP:
            cond = both(cond, self.z < 3)
        if k == DOWN:
            cond = both(cond, self.z > 0)
        act = (lambda c: c.wait_send()) if self.ending else (lambda c: c.start())
        when(cond, lambda: act(self.copy(src, k, own, p=p)))

    def wait(self, src, cond=None, p=0):
        if self.ending:
            return
        when(cond, lambda: self.copy(src, SIDE, p=p).wait_recv())

    def sides(self, t):
        if t == 0:
            return ((None, self.z, None),)
        return ((self.z - t >= 0, self.z - t, UP), (self.z + t <= 3, self.z + t, DOWN))

    def begin(self):
        if self.cut is not None:
            self.go(self.s, SIDE, own=True, p=1)
        for k in (UP, DOWN, SIDE, CORE):
            self.go(self.s, k, own=True)
        if self.cut is not None:
            for k in (UP, DOWN, CORE):
                self.go(self.s, k, own=True, p=1)

    def line(self, t):
        for cond, zz, k in self.sides(t):
            mine, other = seat(zz, self.y, self.c), seat(zz, 1 - self.y, self.c)
            parts = ((mine, 0, (k, SIDE, CORE)), (mine, 1, (k, CORE)), (other, 1, (k, CORE)))
            for src, p, ways in parts[: 1 if self.cut is None else 3]:
                self.wait(src, cond, p)
                for way in ways:
                    self.go(src, way, cond, p=p)

    def over(self, t):
        for cond, zz, _ in self.sides(t):
            src = seat(zz, 1 - self.y, self.c)
            if t == 0 and self.cut is not None:
                self.wait(src, cond, 1)
                for way in (UP, DOWN, CORE):
                    self.go(src, way, cond, p=1)
            self.wait(src, cond)
            self.go(src, CORE, cond)

    def done(self, t):
        for cond, zz, _ in self.sides(t):
            for yy in range(2):
                for p in range(1 if self.cut is None else 2):
                    self.wait(seat(zz, yy, 1 - self.c), cond, p)

    def end(self):
        self.ending = True
        self.begin()
        for t in range(4):
            if t:
                self.line(t)
            self.over(t)


GATHER_SEMS = [DMA((16, 4, 2)), DMA((16, 2))]


class GatherAll(Gather):
    first_y = False

    def device(self, k):
        return (1 - self.x, self.s) if k == ACROSS else Gather.device(self, k)

    def copy(self, src, k, own=False, x=None, p=0):
        x = self.x if x is None else x
        ref = self.own if own else self.at(x, src)
        return remote(ref, self.at(x, src), self.send.at[x, src, k], self.recv.at[x, src], self.device(k))

    def begin(self):
        for k in (UP, DOWN, SIDE, ACROSS, CORE):
            self.go(self.s, k, own=True)

    def line(self, t):
        for cond, zz, k in self.sides(t):
            mine, other = seat(zz, self.y, self.c), seat(zz, 1 - self.y, self.c)
            for src in (mine, other) if self.first_y else (mine,):
                self.wait(src, cond)
                for way in (k, ACROSS, CORE) if self.first_y else (k, SIDE, ACROSS, CORE):
                    self.go(src, way, cond)

    def over(self, t):
        if self.first_y and t:
            return
        for cond, zz, _ in self.sides(t):
            src = seat(zz, 1 - self.y, self.c)
            self.wait(src, cond)
            for way in (UP, DOWN, ACROSS, CORE) if self.first_y else (ACROSS, CORE):
                self.go(src, way, cond)

    def across(self, t):
        x = 1 - self.x
        for cond, zz, _ in self.sides(t):
            for yy in range(2):
                src = seat(zz, yy, self.c)
                if not self.ending:
                    when(cond, lambda: self.copy(src, SIDE, x=x).wait_recv())
                act = (lambda c: c.wait_send()) if self.ending else (lambda c: c.start())
                when(cond, lambda: act(self.copy(src, CORE, x=x)))

    def done(self, t):
        for cond, zz, _ in self.sides(t):
            for yy in range(2):
                src = seat(zz, yy, 1 - self.c)
                for x in (self.x, 1 - self.x):
                    when(cond, lambda: self.copy(src, SIDE, x=x).wait_recv())

    def end(self):
        Gather.end(self)
        for t in range(4):
            self.across(t)


class GatherAllY(GatherAll):
    first_y = True


GATHER_ALL_SEMS = [DMA((2, 16, 5)), DMA((2, 16))]


class Exchange:
    def __init__(self, src, dst, send, recv, wide=False):
        self.x, self.s, self.z, self.y, self.c = place()
        self.wide, self.n = wide, 32 if wide else 16
        self.src, self.dst, self.send, self.recv = src, dst, send, recv

    def seat(self, k, back=False):
        dz = (k // 4) % 4
        if back:
            dz = (4 - dz) % 4
        x = (self.x + k // 16) % 2
        s = seat((self.z + dz) % 4, (self.y + k // 2) % 2, (self.c + k) % 2)
        return x, s

    def index(self, seat_of):
        x, s = seat_of
        return x * 16 + s if self.wide else s

    def copy(self, k):
        to, me = self.seat(k), self.index((self.x, self.s))
        return remote(self.src(self.index(to)), self.dst(me), self.send.at[k], self.recv.at[k], to)

    def keep(self):
        me = self.index((self.x, self.s))
        return pltpu.make_async_copy(self.src(me), self.dst(me), self.recv.at[0])

    def begin(self, ks=None):
        for k in range(self.n) if ks is None else ks:
            if k == 0:
                self.keep().start()
            else:
                self.copy(k).start()

    def arrive(self, k):
        frm = self.seat(k, back=True)
        me = self.index((self.x, self.s))
        remote(self.src(me), self.dst(self.index(frm)), self.send.at[k], self.recv.at[k], frm).wait_recv()
        return self.index(frm)

    def end(self):
        self.keep().wait()
        for k in range(1, self.n):
            self.arrive(k)
        self.end_sends()

    def end_sends(self):
        for k in range(1, self.n):
            self.copy(k).wait_send()


class Swap(Exchange):
    def __init__(self, src, dst, whole, most, send, recv, wide=False):
        Exchange.__init__(self, src, dst, send, recv, wide)
        self.whole, self.most = whole, most

    def keep(self):
        me = self.index((self.x, self.s))
        return pltpu.make_async_copy(self.src(me), self.dst(me), self.recv.at[0])

    def copy(self, k):
        to, me = self.seat(k), self.index((self.x, self.s))
        return remote(self.src(self.index(to)), self.dst(me), self.send.at[0], self.recv.at[0], to)

    def arrived(self):
        remote(self.whole, self.whole, self.send.at[0], self.recv.at[0], self.seat(1)).wait_recv()

    def sent(self):
        remote(self.most, self.most, self.send.at[0], self.recv.at[0], self.seat(1)).wait_send()

    def end(self):
        self.arrived()
        self.sent()


class Slices:
    def __init__(self, src, got, send, recv):
        self.x, self.s, self.z, self.y, self.c = place()
        self.src, self.got, self.send, self.recv = src, got, send, recv

    def block(self, pair):
        return self.src.at[pl.ds((pair // 4) * 32, 32), lane_block(pair % 4, 256)]

    def copy(self, k):
        z, y = (self.z + k // 2) % 4, (self.y + k) % 2
        dst = self.got.at[self.x, self.s // 2, self.c]
        return remote(self.block(z * 2 + y), dst, self.send.at[k], self.recv.at[k], (self.x, seat(z, y, self.c)))

    def begin(self):
        self.local = pltpu.make_async_copy(
            self.block(self.s // 2), self.got.at[self.x, self.s // 2, self.c], self.recv.at[0]
        )
        self.local.start()
        for k in range(1, 8):
            self.copy(k).start()

    def over_x(self):
        ref = self.got.at[self.x, :, self.c]
        return remote(ref, ref, self.send.at[8], self.recv.at[8], (1 - self.x, self.s))

    def over_core(self, k):
        ref = self.got.at[self.x if k == 9 else 1 - self.x, :, self.c]
        return remote(ref, ref, self.send.at[k], self.recv.at[k], (self.x, seat(self.z, self.y, 1 - self.c)))

    def share(self):
        self.local.wait()
        for k in range(1, 8):
            z, y = (self.z + 4 - k // 2) % 4, (self.y + k) % 2
            dst = self.got.at[self.x, z * 2 + y, self.c]
            remote(
                self.block(z * 2 + y), dst, self.send.at[k], self.recv.at[k], (self.x, seat(z, y, self.c))
            ).wait_recv()
        self.over_x().start()
        self.over_core(9).start()

    def end(self):
        self.over_x().wait_recv()
        self.over_core(10).start()
        self.over_core(9).wait_recv()
        self.over_core(10).wait_recv()
        for k in range(1, 8):
            self.copy(k).wait_send()
        self.over_x().wait_send()
        self.over_core(9).wait_send()
        self.over_core(10).wait_send()


ANY = pl.ANY
SM = pltpu.SMEM


def comm_call(body, outs, ins, sems, cid, scratch=(), out_spaces=None, in_spaces=None):
    return pl.pallas_call(
        body,
        out_shape=outs,
        in_specs=[pl.BlockSpec(memory_space=m) for m in in_spaces or [VM] * len(ins)],
        out_specs=[pl.BlockSpec(memory_space=m) for m in out_spaces or [VM] * len(outs)],
        scratch_shapes=list(scratch) + list(sems),
        compiler_params=pltpu.CompilerParams(
            collective_id=cid, has_side_effects=True, vmem_limit_bytes=VMEM_LIMIT
        ),
    )(*ins)


def sds(shape, dtype):
    return jax.ShapeDtypeStruct(shape, dtype)


class Reduce:
    def __init__(self, part, out, bufs, sems, near=None):
        self.part, self.out = part, out
        self.near = part if near is None else near
        self.r1, self.ra, self.ua, self.da = bufs
        self.s1, self.q1, self.sa, self.qa, self.su, self.qu, self.sd, self.qd = sems
        self.x, self.s, self.z, self.y, self.c = place()

    @staticmethod
    def bufs(rows, width):
        return [VM((4, 2, rows, width), BF)] + [VM((4, rows, width), BF)] * 3

    SEMS = [DMA((4, 2))] * 8

    def add(self, dst, src):
        dst[...] = (dst[...].astype(F32) + src[...].astype(F32)).astype(BF)

    def piece(self, p):
        rows = self.ra.shape[1] // 2
        return slice(p * rows, p * rows + rows)

    def first(self, zz, yy):
        return remote(
            self.part.at[seat(zz, yy, 1 - self.c)],
            self.r1.at[zz, yy],
            self.s1.at[zz, yy],
            self.q1.at[zz, yy],
            (self.x, seat(self.z, self.y, 1 - self.c)),
        )

    def side(self, zz, p):
        part = self.piece(p)
        return remote(
            self.r1.at[zz, 1 - self.y, part],
            self.ra.at[zz, part],
            self.sa.at[zz, p],
            self.qa.at[zz, p],
            (self.x, seat(self.z, 1 - self.y, self.c)),
        )

    def line(self, zz, p, up):
        z, y, c = self.z, self.y, self.c
        src = self.ra.at[zz, self.piece(p)]
        dst = (self.ua if up else self.da).at[zz, self.piece(p)]
        send, recv = (self.su, self.qu) if up else (self.sd, self.qd)
        return remote(src, dst, send.at[zz, p], recv.at[zz, p], (self.x, seat(z + 1 if up else z - 1, y, c)))

    def order(self):
        z = self.z
        for t in (3, 2, 1):
            yield z + t <= 3, z + t, True
            yield z - t >= 0, z - t, False
        yield None, z, None

    def begin_plane(self, zz, cond=None):
        for yy in range(2):
            when(cond, lambda: self.first(zz, yy).start())

    def begin(self):
        for cond, zz, _ in self.order():
            self.begin_plane(zz, cond)

    def fold(self, zz, cond=None):
        def go():
            for yy in range(2):
                self.first(zz, yy).wait_recv()
                self.add(self.r1.at[zz, yy], self.near.at[seat(zz, yy, self.c)])
            for p in range(2):
                self.side(zz, p).start()

        when(cond, go)

    def take(self, zz, p, up):
        self.line(zz, p, up).wait_recv()
        part = self.piece(p)
        self.add(self.ra.at[zz, part], (self.ua if up else self.da).at[zz, part])

    def flow_plane(self, cond, zz, up):
        z = self.z

        def go():
            for p in range(2):
                part = self.piece(p)
                self.side(zz, p).wait_recv()
                self.add(self.ra.at[zz, part], self.r1.at[zz, self.y, part])
                if up is not None:
                    pl.when(z > 0 if up else z < 3)(lambda: self.take(zz, p, up))
                    self.line(zz, p, up).start()

        when(cond, go)

    def flow(self):
        z = self.z
        for cond, zz, up in self.order():
            self.flow_plane(cond, zz, up)
        for up, cond in ((True, z > 0), (False, z < 3)):
            for p in range(2):
                when(cond, lambda: self.take(z, p, up))
        self.out[...] = self.ra[z]

    def run(self):
        for cond, zz, _ in self.order():
            self.fold(zz, cond)
        self.flow()

    def end(self):
        for cond, zz, up in self.order():
            for yy in range(2):
                when(cond, lambda: self.first(zz, yy).wait_send())
            for p in range(2):
                when(cond, lambda: self.side(zz, p).wait_send())
                if up is not None:
                    when(cond, lambda: self.line(zz, p, up).wait_send())


NBUF = 4
NSEM = 8
TB = 512


def allowed_mask(first_key, first_query, start_row):
    key = first_key + lax.broadcasted_iota(jnp.int32, (QB, QB), 0)
    query = first_query + lax.broadcasted_iota(jnp.int32, (QB, QB), 1)
    return (key <= query) & (key >= start_row)


SCORE = math.log2(math.e) / math.sqrt(HEAD_SIZE)


def as_row(col):
    n = col.shape[0]
    same = lax.broadcasted_iota(jnp.int32, (n, n), 0) == lax.broadcasted_iota(jnp.int32, (n, n), 1)
    return jnp.sum(jnp.where(same, jnp.broadcast_to(col, (n, n)), 0.0), axis=0, keepdims=True)


def column(line):
    n = line.shape[1]
    same = lax.broadcasted_iota(jnp.int32, (n, n), 0) == lax.broadcasted_iota(jnp.int32, (n, n), 1)
    return jnp.sum(jnp.where(same, jnp.broadcast_to(line.astype(F32), (n, n)), 0.0), axis=1, keepdims=True)


def layer(
    tok, query_w, key_w, value_w, out_w, router_w, gate_w, up_w, down_w, gain_a, gain_e, seg, routes, cot, rope, freq,
    hid, mixp, dw_all, grad_tokens, dwo_sum, wg_all, mix, residual,
    q_t, k_t, v_t, o_t, lse, start, cos, sin, normed, scale_out, h2, att, probs, picked, wperm, back, g_all,
    wo, w3, spread, seg_mine, row_all, w_mine, seg_all, o_low, att_t, k_n, w_t, wo_v,
    wexp, cot_all, p_t, p_all, backp, mix_v, gg, acc,
    g_res, grad_t, router_t, dwo, dwo_x, gkv, v_n, delta, got, g_t, wg, g_mine,
    *rest,
):
    bufs, bufs_o, sems = rest[:NBUF], rest[NBUF : 2 * NBUF], rest[2 * NBUF :]
    (
        t_send, t_recv, o_send, o_recv, c_send, c_recv, h_send, h_recv, q_send, q_recv, w_send, w_recv, e_send, e_recv,
        x_send, x_recv, g_send, g_recv, a_send, a_recv, p_send, p_recv, y_send, y_recv, b_send, b_recv, r_send, r_recv,
        v_send, v_recv, w0s, w0r, w1s, w1r, w2s, w2r, d_sem, x_sem, free,
    ) = sems[3 * NSEM :]
    x, s, z, y, c = place()
    rows, width = tok.shape
    length = 16 * rows
    barrier_all()
    tokens = Gather(tok, lambda src: row_all.at[src], t_send, t_recv, TOKENS_CUT)
    tokens.begin()
    keep_tok = pltpu.make_async_copy(tok, row_all.at[s], x_sem.at[2])
    keep_tok.start()
    seg_mine[...] = jnp.broadcast_to(seg[...], seg_mine.shape)
    documents = Swap(lambda r: seg_mine, lambda r: seg_all.at[r], seg_all, seg_all.at[0:15], g_send, g_recv)
    documents.begin()
    by_first = column(gain_a[...])
    for j in range(8):
        part, lane = slice(32 * (j // 4), 32 * (j // 4) + 32), 256 * (j % 4)
        wperm[part, lane : lane + 128] = (query_w[:, 128 * j : 128 * j + 128].astype(F32) * by_first).astype(BF)
        pair = [ref[:, 64 * j : 64 * j + 64].astype(F32) for ref in (key_w, value_w)]
        wperm[part, lane + 128 : lane + 256] = (jnp.concatenate(pair, axis=1) * by_first).astype(BF)
    slices = Slices(wperm, w_mine, w_send, w_recv)
    slices.begin()
    by_second = column(gain_e[...])
    wo[:, 0:width] = out_w[...]
    router = router_w[...].astype(F32) * gain_e[...].astype(F32)
    router = jnp.concatenate([jnp.concatenate([router, jnp.zeros((128 - E, 32), F32)], axis=0), jnp.zeros((128, 96), F32)], axis=1)
    wo[:, width : width + 128] = jnp.transpose(router)[0:32].astype(BF)
    outw = GatherAll(wo, lambda x, src: wo_v.at[x, src], o_send, o_recv)
    keep = pltpu.make_async_copy(wo, wo_v.at[x, s], x_sem.at[3])
    keep.start()
    for m, ref in enumerate((gate_w, up_w, down_w)):
        plain = ref[...].astype(F32).reshape(32 * E, F)
        for b in range(F // 128):
            lanes = slice(b * 128, b * 128 + 128)
            spread[...] = plain[:, lanes]
            for e in range(E):
                part = spread[pl.ds(e, 32, stride=E), :]
                w3[e, m, :, lanes] = (part * by_second if m < 2 else part).astype(BF)
    weights = Exchange(lambda e: w3.at[e], lambda r: wexp.at[:, x * 16 + r], e_send, e_recv)
    cots = Gather(cot, lambda src: cot_all.at[src], c_send, c_recv, COTS_CUT)

    def cross_copy(k, back=False):
        row = weights.index(weights.seat(k, back=True))
        src = w3.at[s] if k == 0 else wexp.at[:, x * 16 + row]
        dst = wexp.at[:, (1 - x if back else x) * 16 + row]
        return remote(src, dst, x_send.at[k], x_recv.at[k], (1 - x, s))

    def cross(k):
        if k:
            weights.arrive(k)
        cross_copy(k).start()

    factor = jnp.exp2(rope[0].astype(F32))
    for b in range(length // 128):
        position = (b * 128 + lax.broadcasted_iota(jnp.int32, (32, 128), 1)).astype(F32)
        angle = position / factor * freq[...]
        cos[:, b * 128 : b * 128 + 128] = jnp.cos(angle)
        sin[:, b * 128 : b * 128 + 128] = jnp.sin(angle)
    tokens.over(0)
    tokens.line(1)
    slices.share()
    tokens.over(1)
    outw.begin()
    tokens.line(2)
    weights.begin(range(8))
    slices.end()
    w_t[...] = jnp.transpose(w_mine[...].reshape(width, 256).astype(F32)).astype(BF)
    tokens.over(2)
    tokens.line(3)
    outw.over(0)
    outw.line(1)
    weights.begin(range(8, 12))
    documents.end()
    numbers = seg_all[:, 0, :]
    ends = [jnp.sum((numbers < n).astype(jnp.int32)) for n in (1, 2)]
    for b in range(16):
        line = numbers[b : b + 1]
        start[:, b * 128 : b * 128 + 128] = jnp.where(line == 0, 0, jnp.where(line == 1, ends[0], ends[1]))
    tokens.over(3)
    for t in range(4):
        tokens.done(t)
    keep_tok.wait()
    tokens.end()
    acc[...] = jnp.zeros(acc.shape, F32)
    for k in range(4):
        cross(k)

    def project(i, _):
        cols = lane_block(i, 512)
        values = row_all[pl.ds(i * 4, 4)].reshape(512, width).astype(F32)
        scale = lax.rsqrt(jnp.mean(values * values, axis=-1, keepdims=True) + EPSILON)
        hidden = (values * scale).astype(BF)
        row_all[pl.ds(i * 4, 4)] = hidden.reshape(4, rows, width)
        made = dot(w_t[...], hidden, NT)
        co, si = cos[:, cols], sin[:, cols]
        own = jnp.where(c == 0, made[0:64], made[64:128])
        for ref, part in ((q_t, own), (k_t, made[128:192])):
            a, b = part[:32], part[32:]
            ref[0:32, cols] = (a * co - b * si).astype(BF)
            ref[32:64, cols] = (b * co + a * si).astype(BF)
        v_t[:, cols] = made[192:256].astype(BF)
        k_n[cols, :] = jnp.transpose(k_t[:, cols].astype(F32)).astype(BF)
        return 0

    lax.fori_loop(0, length // 512, project, 0)
    keep_hid = pltpu.make_async_copy(row_all, hid, x_sem.at[4])
    keep_hid.start()

    def query_block(i, _):
        @pl.when(i == 1)
        def _():
            outw.over(1)
            outw.line(2)

        @pl.when(i == 3)
        def _():
            outw.over(2)
            outw.line(3)
            cots.begin()

        cols = lane_block(i)
        queries = q_t[:, cols]
        begin = start[:, cols]

        def key_block(j, carried):
            top, total, acc = carried
            keys = lane_block(j)
            scores = dot(k_n[keys, :], queries) * SCORE
            scores = jnp.where(allowed_mask(j * QB, i * QB, begin), scores, MASKED)
            fresh = jnp.maximum(top, jnp.max(scores, axis=0, keepdims=True))
            powers = jnp.exp2(scores - fresh)
            decay = jnp.exp2(top - fresh)
            total = total * decay + jnp.sum(powers, axis=0, keepdims=True)
            acc = acc * decay + dot(v_t[:, keys], powers.astype(BF))
            return fresh, total, acc

        top, total, acc = lax.fori_loop(
            0,
            i + 1,
            key_block,
            (jnp.full((1, QB), MASKED, F32), jnp.zeros((1, QB), F32), jnp.zeros((HEAD_SIZE, QB), F32)),
        )
        out = acc / total
        o_t[:, cols] = out
        o_low[:, cols] = out.astype(BF)
        lse[:, cols] = top + jnp.log2(total)
        return 0

    lax.fori_loop(0, length // QB, query_block, 0)
    outw.over(3)
    for k in range(4, 8):
        cross(k)
    keep_hid.wait()
    heads = Swap(
        lambda t: o_low.at[:, lane_block(t, 128)], lambda h: att_t.at[h], att_t, att_t.at[0:15], a_send, a_recv
    )
    heads.begin()
    keep_cot = pltpu.make_async_copy(cot, cot_all.at[s], x_sem.at[6])
    keep_cot.start()
    for t in range(4):
        outw.across(t)
    for t in range(4):
        outw.done(t)
    keep.wait()
    cots.over(0)
    cots.line(1)
    weights.begin(range(12, 16))
    heads.end()
    for k in range(8, 12):
        cross(k)

    att[...] = jnp.transpose(att_t[...].reshape(width, rows).astype(F32)).astype(BF)
    res = tok[...].astype(F32) + dot(att[...], wo_v[:, :, :, 0:width].reshape(width, width), NT)
    residual[...] = res
    scale = lax.rsqrt(jnp.mean(res * res, axis=-1, keepdims=True) + EPSILON)
    norm = res * scale
    normed[...] = norm
    scale_out[...] = jnp.broadcast_to(scale, scale_out.shape)
    hidden = norm.astype(BF)
    h2[...] = hidden
    lanes = lax.broadcasted_iota(jnp.int32, (128, 128), 1)
    logits = jnp.where(lanes < E, dot(hidden, wo_v[:, :, :, width : width + 128].reshape(width, 128)), MASKED)
    top = jnp.max(logits, axis=-1, keepdims=True)
    powers = jnp.exp(logits - top)
    prob = powers / jnp.sum(powers, axis=-1, keepdims=True)
    probs[...] = prob
    names = lax.broadcasted_iota(jnp.int32, (128, 128), 0)
    mask = jnp.zeros((128, 128), F32)
    for k in range(K):
        mask = mask + jnp.where(names == routes[k : k + 1, :], 1.0, 0.0)
    mask = jnp.transpose(mask)
    picked[...] = mask
    p_t[...] = jnp.transpose(prob * mask)[0:E, :]

    hidden = Gather(h2, lambda src: row_all.at[src], h_send, h_recv, HIDDEN_CUT)
    hidden.begin()
    keep = pltpu.make_async_copy(h2, row_all.at[s], x_sem.at[8])
    keep.start()
    minor = Swap(lambda r: p_t, lambda r: p_all.at[r], p_all, p_all.at[0:15], p_send, p_recv)
    minor.begin()
    one = Reduce(backp, back, bufs, sems[:NSEM])
    hidden.over(0)
    keep.wait()
    keep_cot.wait()
    weights.end_sends()
    weights.keep().wait()
    cross_copy(0).wait_send()
    for k in range(12, 16):
        cross(k)
    minor.end()
    hidden.line(1)
    for k in range(16):
        if k:
            cross_copy(k).wait_send()
        cross_copy(k, back=True).wait_recv()
    cots.done(0)
    hidden.done(0)
    far = z // 2
    order = (z, z + 1 - 2 * far, 2 - 2 * z + 5 * far, 3 - 3 * far)

    def chunk(i, _):
        zz = jnp.where(i == 0, order[0], jnp.where(i == 1, order[1], jnp.where(i == 2, order[2], order[3])))

        for t in (1, 2, 3):

            @pl.when(i == t)
            def _():
                cots.done(t)
                hidden.done(t)

        four = pl.ds(zz * 4, 4)
        some = row_all[four].reshape(4 * rows, width)
        grad = cot_all[four].reshape(4 * rows, width)
        cols = [jnp.broadcast_to(p_all[zz * 4 + b, pl.ds(s, 1), :], (128, 128)) for b in range(4)]
        prob = jnp.concatenate([jnp.transpose(v)[:, 0:1] for v in cols], axis=0)
        gate = dot(some, wexp[0].reshape(width, F))
        up = dot(some, wexp[1].reshape(width, F))

        @pl.when(i == 0)
        def _():
            hidden.over(1)
            hidden.line(2)
            cots.over(1)

        @pl.when(i == 1)
        def _():
            hidden.over(2)
            hidden.line(3)

        @pl.when(i == 2)
        def _():
            one.fold(order[0])
            one.fold(order[1])
            hidden.over(3)

        sig = 1.0 / (1.0 + jnp.exp(-gate))
        silu = gate * sig
        low = (silu * up).astype(BF)
        moved = dot(grad, wexp[2].reshape(width, F))
        seen = jnp.sum(low.astype(F32) * moved, axis=-1, keepdims=True)
        for b in range(4):
            line = jnp.transpose(jnp.broadcast_to(seen[b * 128 : b * 128 + 128], (128, 128)))[0:8]
            gg[zz * 4 + b] = line
        grad_hidden = moved * prob
        grad_gate = (grad_hidden * up * (sig * (1.0 + gate * (1.0 - sig)))).astype(BF)
        grad_up = (grad_hidden * silu).astype(BF)
        below = dot(grad_gate, wexp[0].reshape(width, F), NT) + dot(
            grad_up, wexp[1].reshape(width, F), NT
        )
        backp[four] = below.astype(BF).reshape(4, rows, width)
        one.begin_plane(zz)

        @pl.when(i == 0)
        def _():
            cots.line(2)

        @pl.when(i == 1)
        def _():
            cots.over(2)

        @pl.when(i == 2)
        def _():
            cots.over(3)

        @pl.when(i == 3)
        def _():
            one.fold(order[2])

        out = dot(low, wexp[2].reshape(width, F), NT)
        keep_mix = pltpu.make_async_copy(mix_v, mixp.at[four], x_sem.at[7])
        pl.when(i > 0)(lambda: keep_mix.wait())
        mix_v[...] = (prob * out).astype(BF).reshape(4, rows, width)
        keep_mix.start()
        acc[0] += dot(some, grad_gate, TN)
        acc[1] += dot(some, grad_up, TN)
        acc[2] += dot(grad, (prob * low.astype(F32)).astype(BF), TN)

        @pl.when(i == 1)
        def _():
            cots.line(3)

        return 0

    lax.fori_loop(0, 4, chunk, 0)
    one.fold(order[3])
    seen_out = Swap(lambda r: gg.at[r], lambda r: g_all.at[r], g_all, g_all.at[0:15], y_send, y_recv)
    seen_out.begin()

    def over_d(m):
        part = wexp.at[m, pl.ds((1 - x) * 16, 16)]
        return remote(part, w3.at[:, m], d_sem.at[0, m], d_sem.at[1, m], (1 - x, s))

    for m in range(3):
        wexp[m] = acc[m].astype(BF).reshape(wexp.shape[1:])
        over_d(m).start()
    owners = [
        Swap(
            lambda r, m=m: w3.at[r, m],
            lambda e, m=m: dw_all.at[m, e],
            dw_all.at[m],
            dw_all.at[m, 0:15],
            (w0s, w1s, w2s)[m],
            (w0r, w1r, w2r)[m],
        )
        for m in range(3)
    ]

    def to_owners(m):
        over_d(m).wait()
        w3[:, m] = (w3[:, m].astype(F32) + wexp[m, pl.ds(x * 16, 16)].astype(F32)).astype(BF)
        owners[m].begin()

    for g in (outw, cots, hidden):
        g.end()
    one.flow()
    one.end()
    pltpu.make_async_copy(mix_v, mixp.at[pl.ds(0, 4)], x_sem.at[7]).wait()
    near = (
        (z < 3, (x, seat(z + 1, y, c))),
        (z > 0, (x, seat(z - 1, y, c))),
        (None, (x, seat(z, 1 - y, c))),
        (None, (x, seat(z, y, 1 - c))),
        (None, (1 - x, s)),
    )
    for cond, dev in near:
        when(cond, lambda dev=dev: pl.semaphore_signal(free, inc=1, device_id=dev, device_id_type=MESH))
    loads = [
        pltpu.make_async_copy(hid, row_all, x_sem.at[9]),
        pltpu.make_async_copy(mixp, backp, x_sem.at[10]),
    ]
    for copy in loads:
        copy.start()
    seen_out.end()
    pl.semaphore_wait(free, 3 + (z < 3).astype(jnp.int32) + (z > 0).astype(jnp.int32))
    me = x * 16 + s
    columns_all = GatherAll(
        wperm, lambda x_, src: cot_all.at[x_ * 8 + src // 2, pl.ds((src % 2) * 64, 64)], q_send, q_recv
    )
    columns_all.begin()
    keep_w = pltpu.make_async_copy(wperm, cot_all.at[me // 2, pl.ds((me % 2) * 64, 64)], x_sem.at[11])
    keep_w.start()
    two = Reduce(mixp, mix, bufs, sems[NSEM : 2 * NSEM], backp)
    two.begin()

    seen = jnp.concatenate([g_all[e, 0:1, :] for e in range(E)] + [jnp.zeros((128 - E, 128), F32)], axis=0)
    grad_probs = jnp.transpose(seen) * picked[...]
    prob = probs[...]
    grad_logits = (prob * (grad_probs - jnp.sum(prob * grad_probs, axis=-1, keepdims=True))).astype(BF)
    u = back[...].astype(F32) + dot(
        grad_logits, wo_v[:, :, :, width : width + 128].reshape(width, 128), NT
    )
    norm = normed[...]
    grad = cot[...].astype(F32) + scale_out[:, 0:1] * (u - norm * jnp.mean(u * norm, axis=-1, keepdims=True))
    g_res[...] = grad
    branch = grad.astype(BF)
    att_t[...] = jnp.transpose(dot(branch, wo_v[:, :, :, 0:width].reshape(width, width))).astype(BF).reshape(att_t.shape)
    heads = Swap(
        lambda h: att_t.at[h], lambda t: o_low.at[:, lane_block(t, 128)], o_low, att_t.at[0:15], b_send, b_recv
    )
    heads.begin()
    columns_all.over(0)
    columns_all.line(1)
    loads[1].wait()
    for cond, zz, _ in two.order():
        two.fold(zz, cond)
    grad_t[...] = jnp.transpose(grad).astype(BF)
    other = pl.ds((1 - x) * (width // 2), width // 2)
    router_t[...] = dot(h2[...], grad_logits, TN).astype(BF)
    dwo[:, :, 0:width] = dot(grad_t[other, :], att[...]).astype(BF).reshape(16, 32, width)
    dwo[:, :, width : width + 128] = router_t[other, :].reshape(16, 32, 128)
    over_o = remote(dwo, dwo_x, x_sem.at[12], x_sem.at[13], (1 - x, s))
    over_o.start()
    to_owners(0)
    to_owners(1)
    v_n[...] = jnp.transpose(v_t[...].astype(F32)).astype(BF)
    gkv[...] = jnp.zeros(gkv.shape, F32)
    heads.end()
    delta[...] = jnp.sum(o_low[...].astype(F32) * o_t[...], axis=0, keepdims=True)

    def query_block(i, _):
        @pl.when(i == 2)
        def _():
            two.flow()

        @pl.when(i == 3)
        def _():
            columns_all.over(1)
            to_owners(2)
            columns_all.line(2)

        cols = lane_block(i)
        queries, grads = q_t[:, cols], o_low[:, cols]
        begin, log_total, shift = start[:, cols], lse[:, cols], delta[:, cols]

        def key_block(j, sofar):
            rows = lane_block(j)
            scores = dot(k_n[rows, :], queries) * SCORE
            powers = jnp.where(allowed_mask(j * QB, i * QB, begin), jnp.exp2(scores - log_total), 0.0)
            moved = dot(v_n[rows, :], grads)
            grad_scores = (powers * (moved - shift)).astype(BF)
            gkv[0, :, rows] += dot(queries, grad_scores, NT)
            gkv[1, :, rows] += dot(grads, powers.astype(BF), NT)
            return sofar + dot(k_t[:, rows], grad_scores)

        o_t[:, cols] = lax.fori_loop(0, i + 1, key_block, jnp.zeros((HEAD_SIZE, QB), F32))
        return 0

    lax.fori_loop(0, length // QB, query_block, 0)
    columns_all.over(2)

    pair = remote(gkv.at[1 - c], got, x_sem.at[14], x_sem.at[15], (x, seat(z, y, 1 - c)))
    pair.start()
    columns_all.line(3)
    over_o.wait_recv()
    own = pl.ds(x * (width // 2), width // 2)
    mine = dot(grad_t[own, :], att[...]).reshape(16, 32, width)
    dwo_x[:, :, 0:width] = (dwo_x[:, :, 0:width].astype(F32) + mine).astype(BF)
    mine = router_t[own, :].reshape(16, 32, 128).astype(F32)
    dwo_x[:, :, width : width + 128] = (dwo_x[:, :, width : width + 128].astype(F32) + mine).astype(BF)
    out = Reduce(dwo_x, dwo_sum, bufs_o, sems[2 * NSEM : 3 * NSEM])
    out.begin()
    scaling = 1.0 / math.sqrt(HEAD_SIZE)
    co, si = cos[...], sin[...]

    def unturn(part):
        a, b = part[:32], part[32:]
        return jnp.concatenate([a * co + b * si, b * co - a * si], axis=0)

    g_t[0] = unturn(o_t[...] * scaling).astype(BF)
    pair.wait()
    mine = gkv[c] + got[...]
    g_t[1] = jnp.where(c == 0, unturn(mine * scaling), mine).astype(BF)
    tokens = Swap(
        lambda t: g_t.at[:, :, lane_block(t, 128)],
        lambda h: g_mine.at[h // 2, :, h % 2],
        g_mine,
        g_t.at[:, :, 0 : length - 128],
        r_send,
        r_recv,
    )
    tokens.begin()
    loads[0].wait()
    wg[...] = jnp.transpose(dot(g_t[...].reshape(128, length), row_all[...].reshape(length, width))).astype(BF).reshape(
        wg.shape
    )
    columns = Swap(lambda r: wg.at[r], lambda r: wg_all.at[r], wg_all, wg_all.at[0:31], v_send, v_recv, wide=True)
    columns.begin()
    columns_all.over(3)
    for t in range(4):
        columns_all.across(t)
    for t in range(4):
        columns_all.done(t)
    keep_w.wait()
    for cond, zz, _ in out.order():
        out.fold(zz, cond)
    tokens.end()
    halves = cot_all[...].reshape(32, 2, 32, width)
    w = sum(dot(halves[:, h].reshape(width, width), g_mine[4 * h : 4 * h + 4].reshape(width, 128)) for h in range(2))
    w = jnp.transpose(w)
    values = tok[...].astype(F32)
    scale_first = lax.rsqrt(jnp.mean(values * values, axis=-1, keepdims=True) + EPSILON)
    norm = values * scale_first
    grad_tokens[...] = g_res[...] + scale_first * (w - norm * jnp.mean(w * norm, axis=-1, keepdims=True))
    out.flow()
    out.end()
    columns.end()
    for owner in owners:
        owner.end()
    over_o.wait_send()
    two.end()
    columns_all.end()


def finish(
    wg_all, dwo_sum, dw_all, query_w, key_w, value_w, router_w, gate_w, up_w, gain_a, gain_e, mix, residual, g_tok,
    mixed, grad_tokens, grad_a, grad_e, grad_q, grad_k, grad_v, grad_o, grad_r, grad_gate, grad_up, grad_down,
    spread,
):
    width = grad_o.shape[1]
    mixed[...] = (residual[...] + mix[...].astype(F32)).astype(BF)
    grad_tokens[...] = g_tok[...]
    by_first, by_second = column(gain_a[...]), column(gain_e[...])
    head = [wg_all[h].astype(F32) + wg_all[16 + h].astype(F32) for h in range(16)]
    total = jnp.zeros((32, 128), F32)
    for ref, weight, lanes, seats in (
        (grad_q, query_w, slice(0, 64), range(16)),
        (grad_k, key_w, slice(64, 128), range(0, 16, 2)),
        (grad_v, value_w, slice(64, 128), range(1, 16, 2)),
    ):
        for j in range(len(seats) // 2):
            part = jnp.concatenate([head[seats[2 * j]][:, lanes], head[seats[2 * j + 1]][:, lanes]], axis=1)
            cols = slice(128 * j, 128 * j + 128)
            ref[:, cols] = part * by_first
            total = total + part * weight[:, cols].astype(F32)
    grad_a[...] = as_row(jnp.sum(total, axis=1, keepdims=True))
    grad_o[...] = dwo_sum[:, 0:width].astype(F32)
    router = dwo_sum[:, width : width + 128].astype(F32)
    router = jnp.concatenate([router, jnp.zeros((96, 128), F32)], axis=0)
    router = jnp.transpose(router)[0:E, 0:32]
    grad_r[...] = router * gain_e[...].astype(F32)
    total = jnp.zeros((32 * E, 128), F32)
    for m, (ref, weight) in enumerate(((grad_gate, gate_w), (grad_up, up_w), (grad_down, None))):
        for b in range(F // 128):
            lanes = slice(b * 128, b * 128 + 128)
            for e in range(E):
                part = dw_all[m, e, :, lanes].astype(F32)
                spread[b, pl.ds(e, 32, stride=E), :] = part
            plain = spread[b]
            if m == 2:
                ref[:, :, lanes] = plain.reshape(32, E, 128)
            else:
                ref[:, :, lanes] = plain.reshape(32, E, 128) * by_second[:, :, None]
                total = total + plain * weight[:, :, lanes].astype(F32).reshape(32 * E, 128)
    sums = jnp.sum(jnp.sum(total.reshape(32, E, 128), axis=1), axis=1, keepdims=True)
    grad_e[...] = as_row(sums) + jnp.sum(router * router_w[...].astype(F32), axis=0, keepdims=True)


def frequencies(head_dim):
    halves = head_dim // 2
    return jnp.power(ROPE_BASE, -jnp.arange(halves, dtype=F32) * (2.0 / head_dim))


def sixteen_seats(
    tokens,
    attention_gain,
    expert_gain,
    query_weight,
    key_matrix,
    value_matrix,
    output_weight,
    router_weight,
    gate_weight,
    up_weight,
    down_weight,
    routes,
    segments,
    rope_index,
    cotangent,
):
    D = MODEL_WIDTH
    rows = tokens.shape[1]
    length = 16 * rows
    tok_mine = tokens.reshape(rows, D)
    cot_mine = cotangent.reshape(rows, D)
    powers = np.power(np.float32(ROPE_BASE), -np.arange(32, dtype=np.float32) * np.float32(2.0 / HEAD_SIZE))
    freq = jnp.asarray(np.broadcast_to(powers[:, None], (32, 128)).astype(np.float32))
    _, _, dw_all, grad_tokens, dwo_sum, wg_all, mix, residual = comm_call(
        layer,
        [sds((16, rows, D), BF), sds((16, rows, D), BF), sds((3, 16, 32, F), BF), sds((rows, D), F32)]
        + [sds((32, D + 128), BF), sds((32, 32, 128), BF), sds((rows, D), BF), sds((rows, D), F32)],
        [
            tok_mine,
            query_weight,
            key_matrix,
            value_matrix,
            output_weight,
            router_weight.T,
            gate_weight,
            up_weight,
            down_weight,
            attention_gain.reshape(1, 32),
            expert_gain.reshape(1, 32),
            segments.astype(jnp.int32),
            routes.reshape(rows, K).T,
            cot_mine,
            rope_index.astype(jnp.int32),
            freq,
        ],
        Reduce.SEMS * 3
        + GATHER_SEMS
        + GATHER_ALL_SEMS
        + GATHER_SEMS * 2
        + GATHER_ALL_SEMS
        + [DMA((16,))] * 6
        + [DMA((1,))] * 20
        + [DMA((2, 3)), DMA((16,)), pltpu.SemaphoreType.REGULAR],
        0,
        [VM((64, length), BF)] * 3
        + [VM((64, length), F32), VM((1, length), F32), VM((1, length), jnp.int32)]
        + [VM((32, length), F32)] * 2
        + [VM((rows, D), F32), VM((rows, 128), F32), VM((rows, D), BF), VM((rows, D), BF)]
        + [VM((rows, 128), F32), VM((rows, 128), F32), VM((64, D), BF), VM((rows, D), BF)]
        + [VM((16, 8, rows), F32)]
        + [
            VM((32, D + 128), BF),
            VM((E, 3, 32, F), BF),
            VM((32 * E, 128), F32),
            VM((8, rows), jnp.int32),
            VM((16, rows, D), BF),
            VM((2, 8, 2, 32, 256), BF),
            VM((16, 8, rows), jnp.int32),
            VM((64, length), BF),
            VM((16, 64, rows), BF),
            VM((length, 64), BF),
            VM((256, D), BF),
            VM((2, 16, 32, D + 128), BF),
            VM((3, 32, 32, F), BF),
            VM((16, rows, D), BF),
            VM((E, rows), F32),
            VM((16, E, rows), F32),
            VM((16, rows, D), BF),
            VM((4, rows, D), BF),
            VM((16, 8, rows), F32),
            VM((3, D, F), F32),
        ]
        + [
            VM((rows, D), F32),
            VM((D, rows), BF),
            VM((D, 128), BF),
            VM((16, 32, D + 128), BF),
            VM((16, 32, D + 128), BF),
            VM((2, 64, length), F32),
            VM((length, 64), BF),
            VM((1, length), F32),
            VM((64, length), F32),
            VM((2, 64, length), BF),
            VM((32, 32, 128), BF),
            VM((8, 2, 2, 64, rows), BF),
        ]
        + Reduce.bufs(rows, D)
        + Reduce.bufs(32, D + 128),
        [ANY] * 3 + [VM] * 5,
        [VM] * 14 + [SM, VM],
    )
    (
        mixed, grad_tokens, grad_a, grad_e, grad_q, grad_k, grad_v, grad_o, grad_r, grad_gate, grad_up, grad_down,
    ) = pl.pallas_call(
        finish,
        out_shape=[sds((rows, D), BF), sds((rows, D), F32), sds((1, 32), F32), sds((1, 32), F32)]
        + [sds((32, n), F32) for n in (D, 512, 512, D)]
        + [sds((E, 32), F32)]
        + [sds((32, E, F), F32)] * 3,
        scratch_shapes=[VM((F // 128, 32 * E, 128), F32)],
        compiler_params=pltpu.CompilerParams(vmem_limit_bytes=VMEM_LIMIT),
    )(
        wg_all,
        dwo_sum,
        dw_all,
        query_weight,
        key_matrix,
        value_matrix,
        router_weight.T,
        gate_weight,
        up_weight,
        attention_gain.reshape(1, 32),
        expert_gain.reshape(1, 32),
        mix,
        residual,
        grad_tokens,
    )
    return (
        mixed.reshape(tokens.shape),
        grad_tokens.reshape(tokens.shape),
        grad_a.reshape(32),
        grad_e.reshape(32),
        grad_q,
        grad_k,
        grad_v,
        grad_o,
        grad_r.T,
        grad_gate,
        grad_up,
        grad_down,
    )


def rms_scale(values):
    return lax.rsqrt(jnp.mean(values * values, axis=-1, keepdims=True) + EPSILON)


def apply_rotary(values, cosine_lookup, sine_lookup):
    halves = values.shape[-1] // 2
    first_half = values[..., :halves]
    second_half = values[..., halves:]
    return jnp.concatenate(
        [
            first_half * cosine_lookup - second_half * sine_lookup,
            second_half * cosine_lookup + first_half * sine_lookup,
        ],
        axis=-1,
    )


def unrotate(values, cosine_lookup, sine_lookup):
    halves = values.shape[-1] // 2
    first_half = values[..., :halves]
    second_half = values[..., halves:]
    return jnp.concatenate(
        [
            first_half * cosine_lookup + second_half * sine_lookup,
            second_half * cosine_lookup - first_half * sine_lookup,
        ],
        axis=-1,
    )


def block_mask(key_start, block_size, query_pos, query_seg, seg_block):
    key_pos = key_start + jnp.arange(block_size, dtype=jnp.int32)
    causal = key_pos[None, :] <= query_pos[:, None]
    same_doc = seg_block[:, None, :] == query_seg[:, :, None]
    return (causal[None] & same_doc)[:, None, None]


def attend_piece(running, pieces, first_key, queries, query_pos, query_seg, scaling):
    key_rows, value_rows, key_segments = pieces
    sequence_count, key_span = (key_rows.shape[0], key_rows.shape[1])
    block_size = math.gcd(key_span, 512)
    kv_heads, head_dim = (queries.shape[2], queries.shape[4])

    def advance(block_index, carried):
        top_score, denominator, numerator = carried
        offset = block_index * block_size
        key_block = lax.dynamic_slice_in_dim(key_rows, offset, block_size, 1).reshape(
            sequence_count, block_size, kv_heads, head_dim
        )
        value_block = lax.dynamic_slice_in_dim(value_rows, offset, block_size, 1).reshape(
            sequence_count, block_size, kv_heads, head_dim
        )
        seg_block = lax.dynamic_slice_in_dim(key_segments, offset, block_size, 1).astype(jnp.int32)
        allowed = block_mask(offset, block_size, query_pos, query_seg, seg_block)
        scores = (
            jnp.einsum("sqkgd,sjkd->skgqj", queries, key_block, preferred_element_type=jnp.float32)
            * scaling
        )
        fresh_top = jnp.maximum(top_score, jnp.max(jnp.where(allowed, scores, MASKED), axis=-1))
        weights = jnp.where(allowed, jnp.exp(scores - fresh_top[..., None]), 0.0)
        decay_factor = jnp.exp(top_score - fresh_top)
        denominator = denominator * decay_factor + jnp.sum(weights, axis=-1)
        numerator = numerator * decay_factor[..., None] + jnp.einsum(
            "skgqj,sjkd->skgqd",
            weights.astype(jnp.bfloat16),
            value_block,
            preferred_element_type=jnp.float32,
        )
        return (fresh_top, denominator, numerator)

    return lax.fori_loop(0, key_span // block_size, advance, running)


def attend_back(pieces, queries, query_pos, query_seg, grad_attn, log_total, row_delta, scaling):
    key_rows, value_rows, key_segments = pieces
    sequence_count, key_span, key_value_width = key_rows.shape
    block_size = math.gcd(key_span, 512)
    kv_heads, head_dim = (queries.shape[2], queries.shape[4])

    def advance(block_index, carried):
        grad_queries, gradient_couples = carried
        offset = block_index * block_size
        key_block = lax.dynamic_slice_in_dim(key_rows, offset, block_size, 1).reshape(
            sequence_count, block_size, kv_heads, head_dim
        )
        value_block = lax.dynamic_slice_in_dim(value_rows, offset, block_size, 1).reshape(
            sequence_count, block_size, kv_heads, head_dim
        )
        seg_block = lax.dynamic_slice_in_dim(key_segments, offset, block_size, 1).astype(jnp.int32)
        allowed = block_mask(offset, block_size, query_pos, query_seg, seg_block)
        scores = (
            jnp.einsum("sqkgd,sjkd->skgqj", queries, key_block, preferred_element_type=jnp.float32)
            * scaling
        )
        weights = jnp.where(allowed, jnp.exp(scores - log_total[..., None]), 0.0)
        grad_weights = jnp.einsum(
            "sqkgd,sjkd->skgqj", grad_attn, value_block, preferred_element_type=jnp.float32
        )
        grad_scores = (weights * (grad_weights - row_delta[..., None])).astype(jnp.bfloat16)
        grad_queries = grad_queries + jnp.einsum(
            "skgqj,sjkd->sqkgd", grad_scores, key_block, preferred_element_type=jnp.float32
        )
        grad_keys = (
            jnp.einsum(
                "skgqj,sqkgd->sjkd", grad_scores, queries, preferred_element_type=jnp.float32
            )
            * scaling
        )
        grad_values = jnp.einsum(
            "skgqj,sqkgd->sjkd",
            weights.astype(jnp.bfloat16),
            grad_attn,
            preferred_element_type=jnp.float32,
        )
        produced = jnp.concatenate(
            [
                grad_keys.reshape(sequence_count, block_size, key_value_width),
                grad_values.reshape(sequence_count, block_size, key_value_width),
            ],
            axis=-1,
        )
        return (
            grad_queries,
            lax.dynamic_update_slice_in_dim(gradient_couples, produced, offset, 1),
        )

    starting = (
        jnp.zeros(queries.shape, jnp.float32),
        jnp.zeros((sequence_count, key_span, 2 * key_value_width), jnp.float32),
    )
    grad_queries, gradient_couples = lax.fori_loop(0, key_span // block_size, advance, starting)
    return (grad_queries * scaling, gradient_couples)


def project_in(pieces, routed):
    gate_rows, up_rows = pieces
    return (
        jnp.einsum("erd,def->erf", routed, gate_rows, preferred_element_type=jnp.float32),
        jnp.einsum("erd,def->erf", routed, up_rows, preferred_element_type=jnp.float32),
    )


def project_out(down_rows, hidden):
    produced = jnp.einsum("erf,def->erd", hidden, down_rows, preferred_element_type=jnp.float32)
    return produced


def back_through_down(down_rows, grad_output):
    return jnp.einsum("erd,def->erf", grad_output, down_rows, preferred_element_type=jnp.float32)


def back_through_in(pieces, grad_gate, grad_up):
    gate_rows, up_rows = pieces
    produced = jnp.einsum(
        "erf,def->erd", grad_gate, gate_rows, preferred_element_type=jnp.float32
    ) + jnp.einsum("erf,def->erd", grad_up, up_rows, preferred_element_type=jnp.float32)
    return produced


def take_slots(slot_data, destination):
    experts, width = (slot_data.shape[0], slot_data.shape[-1])
    sequence_count, sequence_rows, picks = destination.shape
    flat = jnp.transpose(
        slot_data.reshape(experts, sequence_count, -1, width), (1, 0, 2, 3)
    ).reshape(sequence_count, -1, width)
    taken = jax.vmap(lambda table, spots: table[spots])(
        flat, destination.reshape(sequence_count, sequence_rows * picks)
    )
    return taken.reshape(sequence_count, sequence_rows, picks, width)


def place_slots(values, destination, experts, capacity):
    sequence_count, width = (values.shape[0], values.shape[-1])
    empty = jnp.zeros((sequence_count, experts * capacity, width), values.dtype)
    filled = jax.vmap(lambda table, spots, rows: table.at[spots].set(rows))(
        empty, destination.reshape(sequence_count, -1), values.reshape(sequence_count, -1, width)
    )
    return jnp.transpose(
        filled.reshape(sequence_count, experts, capacity, width), (1, 0, 2, 3)
    ).reshape(experts, sequence_count * capacity, width)


def any_seats(
    tokens,
    attention_gain,
    expert_gain,
    query_weight,
    key_matrix,
    value_matrix,
    output_weight,
    router_weight,
    gate_weight,
    up_weight,
    down_weight,
    routes,
    segments,
    rope_index,
    cotangent,
):
    sequence_count, sequence_rows = (tokens.shape[0], tokens.shape[1])
    queries_per_group = QUERY_HEADS // KEY_VALUE_HEADS
    key_value_width = KEY_VALUE_HEADS * HEAD_SIZE
    scaling = 1.0 / math.sqrt(HEAD_SIZE)
    experts_slots = E * CAP
    gathered = (
        lax.all_gather(attention_gain, ("row", "seq"), axis=0, tiled=True),
        lax.all_gather(expert_gain, ("row", "seq"), axis=0, tiled=True),
        lax.all_gather(query_weight, ("row", "seq"), axis=0, tiled=True),
        lax.all_gather(key_matrix, ("row", "seq"), axis=0, tiled=True),
        lax.all_gather(value_matrix, ("row", "seq"), axis=0, tiled=True),
        lax.all_gather(output_weight, ("row", "seq"), axis=0, tiled=True),
        lax.all_gather(router_weight, ("row", "seq"), axis=0, tiled=True),
    )
    gain_first = gathered[0].astype(jnp.float32)
    gain_second = gathered[1].astype(jnp.float32)
    full_query, full_key, full_value, full_output, full_router = gathered[2:]
    inputs = tokens.astype(jnp.float32)
    scale_first = rms_scale(inputs)
    normed_first = inputs * scale_first
    hidden_first = (normed_first * gain_first).astype(jnp.bfloat16)
    query_unrotated = jnp.einsum(
        "sqd,dc->sqc", hidden_first, full_query, preferred_element_type=jnp.float32
    )
    key_unrotated = jnp.einsum(
        "sqd,dc->sqc", hidden_first, full_key, preferred_element_type=jnp.float32
    )
    value_raw = jnp.einsum(
        "sqd,dc->sqc", hidden_first, full_value, preferred_element_type=jnp.float32
    )
    positions = lax.axis_index("seq") * sequence_rows + jnp.arange(sequence_rows, dtype=jnp.int32)
    factor = jnp.power(2.0, rope_index.astype(jnp.float32))
    angles = (positions.astype(jnp.float32)[None, :] / factor[:, None])[..., None] * frequencies(
        HEAD_SIZE
    )
    cosine_lookup = jnp.cos(angles)[:, :, None, :]
    sine_lookup = jnp.sin(angles)[:, :, None, :]
    query_turned = (
        apply_rotary(
            query_unrotated.reshape(sequence_count, sequence_rows, QUERY_HEADS, HEAD_SIZE),
            cosine_lookup,
            sine_lookup,
        )
        .astype(jnp.bfloat16)
        .reshape(sequence_count, sequence_rows, KEY_VALUE_HEADS, queries_per_group, HEAD_SIZE)
    )
    key_turned = (
        apply_rotary(
            key_unrotated.reshape(sequence_count, sequence_rows, KEY_VALUE_HEADS, HEAD_SIZE),
            cosine_lookup,
            sine_lookup,
        )
        .astype(jnp.bfloat16)
        .reshape(sequence_count, sequence_rows, key_value_width)
    )
    value_reduced = value_raw.astype(jnp.bfloat16)
    segment_low = segments.astype(jnp.float32).astype(jnp.bfloat16)
    statistic_shape = (sequence_count, KEY_VALUE_HEADS, queries_per_group, sequence_rows)
    starting = (
        jnp.full(statistic_shape, MASKED, jnp.float32),
        jnp.zeros(statistic_shape, jnp.float32),
        jnp.zeros(statistic_shape + (HEAD_SIZE,), jnp.float32),
    )
    attend = partial(
        attend_piece, queries=query_turned, query_pos=positions, query_seg=segments, scaling=scaling
    )
    top_score, denominator, numerator = attend(
        starting,
        (
            lax.all_gather(key_turned, "seq", axis=1, tiled=True),
            lax.all_gather(value_reduced, "seq", axis=1, tiled=True),
            lax.all_gather(segment_low, "seq", axis=1, tiled=True),
        ),
        jnp.int32(0),
    )
    attn_heads = numerator / denominator[..., None]
    log_total = top_score + jnp.log(denominator)
    attn_rows = jnp.transpose(attn_heads, (0, 3, 1, 2, 4))
    attn_low = attn_rows.astype(jnp.bfloat16).reshape(
        sequence_count, sequence_rows, QUERY_HEADS * HEAD_SIZE
    )
    branch = jnp.einsum("sqc,dc->sqd", attn_low, full_output, preferred_element_type=jnp.float32)
    residual = inputs + branch
    scale_second = rms_scale(residual)
    normed_second = residual * scale_second
    hidden_second = (normed_second * gain_second).astype(jnp.bfloat16)
    logits = jnp.einsum(
        "sqd,de->sqe", hidden_second, full_router, preferred_element_type=jnp.float32
    )
    router_probs = jax.nn.softmax(logits, axis=-1)
    picked = routes[..., None] == jnp.arange(E, dtype=jnp.int32)
    picked_int = picked.astype(jnp.int32).reshape(sequence_count, sequence_rows * K, E)
    earlier = jnp.cumsum(picked_int, axis=1, dtype=jnp.int32) - picked_int
    slot_ids = jnp.sum(earlier * picked_int, axis=-1, dtype=jnp.int32).reshape(
        sequence_count, sequence_rows, K
    )
    destination = routes * CAP + slot_ids
    chosen = destination[..., None] == jnp.arange(experts_slots, dtype=jnp.int32)
    gate_probs = jnp.sum(jnp.where(picked, router_probs[:, :, None, :], 0.0), axis=-1)
    dispatch = jnp.sum(chosen, axis=2, dtype=jnp.float32).reshape(
        sequence_count, sequence_rows, E, CAP
    )
    slot_rows = sequence_count * CAP
    routed = (
        jnp.einsum(
            "sqec,sqd->escd",
            dispatch.astype(jnp.bfloat16),
            hidden_second,
            preferred_element_type=jnp.float32,
        )
        .astype(jnp.bfloat16)
        .reshape(E, slot_rows, MODEL_WIDTH)
    )
    grad_mixed = cotangent.astype(jnp.float32)
    grad_slot_values = (gate_probs[..., None] * grad_mixed[:, :, None, :]).astype(jnp.bfloat16)
    grad_expert = place_slots(grad_slot_values, destination, E, CAP)
    groups = 4
    width = E // groups

    def some_experts(_, given):
        rows, grads, gate_part, up_part, down_part = given
        pieces = (
            lax.all_gather(gate_part, ("row", "seq"), axis=0, tiled=True),
            lax.all_gather(up_part, ("row", "seq"), axis=0, tiled=True),
        )
        down_rows = lax.all_gather(down_part, ("row", "seq"), axis=0, tiled=True)
        gate_pre, up_pre = project_in(pieces, routed=rows)
        hidden_low = (jax.nn.silu(gate_pre) * up_pre).astype(jnp.bfloat16)
        expert_out = project_out(down_rows, hidden=hidden_low)
        grad_hidden = back_through_down(down_rows, grad_output=grads)
        sigmoid_gate = jax.nn.sigmoid(gate_pre)
        grad_gate = (
            grad_hidden * up_pre * sigmoid_gate * (1.0 + gate_pre * (1.0 - sigmoid_gate))
        ).astype(jnp.bfloat16)
        grad_up = (grad_hidden * (gate_pre * sigmoid_gate)).astype(jnp.bfloat16)
        grad_routed = back_through_in(pieces, grad_gate=grad_gate, grad_up=grad_up)
        made = [
            lax.psum_scatter(
                jnp.einsum("erd,erf->def", left, right, preferred_element_type=jnp.float32),
                ("row", "seq"),
                scatter_dimension=0,
                tiled=True,
            )
            for left, right in ((rows, grad_gate), (rows, grad_up), (grads, hidden_low))
        ]
        return None, (expert_out, grad_routed, *made)

    def grouped(weight):
        return jnp.moveaxis(weight.reshape(weight.shape[0], groups, width, F), 1, 0)

    _, (expert_out, grad_routed, *expert_grads) = lax.scan(
        some_experts,
        None,
        (
            routed.reshape(groups, width, slot_rows, MODEL_WIDTH),
            grad_expert.reshape(groups, width, slot_rows, MODEL_WIDTH),
            grouped(gate_weight),
            grouped(up_weight),
            grouped(down_weight),
        ),
    )
    expert_out = expert_out.reshape(E, slot_rows, MODEL_WIDTH)
    grad_routed = grad_routed.reshape(E, slot_rows, MODEL_WIDTH)
    grad_gate_weight, grad_up_weight, grad_down_weight = [
        jnp.moveaxis(grad, 0, 1).reshape(gate_weight.shape) for grad in expert_grads
    ]
    taken_out = take_slots(expert_out, destination)
    expert_mix = jnp.sum(gate_probs[..., None] * taken_out, axis=2)
    mixed = (residual + expert_mix).astype(jnp.bfloat16)
    grad_gates = jnp.sum(taken_out * grad_mixed[:, :, None, :], axis=-1)
    grad_probs = jnp.sum(jnp.where(picked, grad_gates[..., None], 0.0), axis=2)
    grad_logits = (
        router_probs * (grad_probs - jnp.sum(router_probs * grad_probs, axis=-1, keepdims=True))
    ).astype(jnp.bfloat16)
    grad_second = jnp.sum(take_slots(grad_routed, destination), axis=2) + jnp.einsum(
        "sqe,de->sqd", grad_logits, full_router, preferred_element_type=jnp.float32
    )
    grad_gain_second = jnp.sum(grad_second * normed_second, axis=(0, 1))
    scaled_second = grad_second * gain_second
    grad_residual = grad_mixed + scale_second * (
        scaled_second
        - normed_second * jnp.mean(scaled_second * normed_second, axis=-1, keepdims=True)
    )
    grad_branch = grad_residual.astype(jnp.bfloat16)
    grad_attn = (
        jnp.einsum("sqd,dc->sqc", grad_branch, full_output, preferred_element_type=jnp.float32)
        .astype(jnp.bfloat16)
        .reshape(sequence_count, sequence_rows, KEY_VALUE_HEADS, queries_per_group, HEAD_SIZE)
    )
    row_delta = jnp.transpose(
        jnp.sum(grad_attn.astype(jnp.float32) * attn_rows, axis=-1), (0, 2, 3, 1)
    )
    keys_back = (
        lax.all_gather(key_turned, "seq", axis=1, tiled=True),
        lax.all_gather(value_reduced, "seq", axis=1, tiled=True),
        lax.all_gather(segment_low, "seq", axis=1, tiled=True),
    )
    grad_query_rot, grad_pair_rows = attend_back(
        keys_back, query_turned, positions, segments, grad_attn, log_total, row_delta, scaling
    )
    gradient_couples = lax.psum_scatter(grad_pair_rows, "seq", scatter_dimension=1, tiled=True)
    grad_query = (
        unrotate(
            grad_query_rot.reshape(sequence_count, sequence_rows, QUERY_HEADS, HEAD_SIZE),
            cosine_lookup,
            sine_lookup,
        )
        .astype(jnp.bfloat16)
        .reshape(sequence_count, sequence_rows, QUERY_HEADS * HEAD_SIZE)
    )
    grad_key = (
        unrotate(
            gradient_couples[..., :key_value_width].reshape(
                sequence_count, sequence_rows, KEY_VALUE_HEADS, HEAD_SIZE
            ),
            cosine_lookup,
            sine_lookup,
        )
        .astype(jnp.bfloat16)
        .reshape(sequence_count, sequence_rows, key_value_width)
    )
    grad_value = gradient_couples[..., key_value_width:].astype(jnp.bfloat16)
    grad_first = (
        jnp.einsum("sqc,dc->sqd", grad_query, full_query, preferred_element_type=jnp.float32)
        + jnp.einsum("sqc,dc->sqd", grad_key, full_key, preferred_element_type=jnp.float32)
        + jnp.einsum("sqc,dc->sqd", grad_value, full_value, preferred_element_type=jnp.float32)
    )
    grad_gain_first = jnp.sum(grad_first * normed_first, axis=(0, 1))
    scaled_first = grad_first * gain_first
    grad_tokens = grad_residual + scale_first * (
        scaled_first - normed_first * jnp.mean(scaled_first * normed_first, axis=-1, keepdims=True)
    )
    attention_grads = lax.psum_scatter(
        jnp.concatenate(
            [
                jnp.einsum(
                    "sqd,sqc->dc", hidden_first, grad_query, preferred_element_type=jnp.float32
                ),
                jnp.einsum(
                    "sqd,sqc->dc", hidden_first, grad_key, preferred_element_type=jnp.float32
                ),
                jnp.einsum(
                    "sqd,sqc->dc", hidden_first, grad_value, preferred_element_type=jnp.float32
                ),
                jnp.einsum(
                    "sqd,sqc->dc", grad_branch, attn_low, preferred_element_type=jnp.float32
                ),
                jnp.einsum(
                    "sqd,sqe->de", hidden_second, grad_logits, preferred_element_type=jnp.float32
                ),
                grad_gain_first[:, None],
                grad_gain_second[:, None],
            ],
            axis=1,
        ),
        ("row", "seq"),
        scatter_dimension=0,
        tiled=True,
    )
    query_cols = QUERY_HEADS * HEAD_SIZE
    edge_two = query_cols + key_value_width
    edge_three = edge_two + key_value_width
    edge_four = edge_three + query_cols
    edge_five = edge_four + E
    return (
        mixed,
        grad_tokens,
        attention_grads[:, edge_five],
        attention_grads[:, edge_five + 1],
        attention_grads[:, :query_cols],
        attention_grads[:, query_cols:edge_two],
        attention_grads[:, edge_two:edge_three],
        attention_grads[:, edge_three:edge_four],
        attention_grads[:, edge_four:edge_five],
        grad_gate_weight,
        grad_up_weight,
        grad_down_weight,
    )


def solution(mesh):
    first = P(("row", "seq"))
    in_specs = (
        (P("row", "seq", None), first, first)
        + (P(("row", "seq"), None),) * 5
        + (P(("row", "seq"), None, None),) * 3
        + (P("row", "seq", None), P("row", "seq"), P("row"), P("row", "seq", None))
    )
    out_specs = (
        (P("row", "seq", None), P("row", "seq", None), first, first)
        + (P(("row", "seq"), None),) * 5
        + (P(("row", "seq"), None, None),) * 3
    )
    body = sixteen_seats if dict(mesh.shape) == {"row": 2, "seq": 16} else any_seats
    return jax.shard_map(body, mesh=mesh, in_specs=in_specs, out_specs=out_specs, check_vma=False)
```

```python
from functools import partial
import math

import jax
import jax.numpy as jnp
import numpy as np
from jax import lax
from jax.experimental import pallas as pl
from jax.experimental.pallas import tpu as pltpu
from jax.sharding import PartitionSpec as P

MODEL_WIDTH = 1024
QUERY_HEADS = 16
KEY_VALUE_HEADS = 8
HEAD_SIZE = 64
F = 512
E = 16
K = 8
CAP = 96

EPSILON = 1e-05
ROPE_BASE = 10000.0
MASKED = -1e30
MESH = pl.DeviceIdType.MESH
VM = pltpu.VMEM
BF = jnp.bfloat16
F32 = jnp.float32
DMA = pltpu.SemaphoreType.DMA
UP, DOWN, SIDE, CORE, ACROSS = range(5)
VMEM_LIMIT = 60 * 1024 * 1024

NN = (((1,), (0,)), ((), ()))
NT = (((1,), (1,)), ((), ()))
TN = (((0,), (0,)), ((), ()))


def dot(a, b, dims=NN):
    return lax.dot_general(a, b, dims, preferred_element_type=F32)


def when(cond, f):
    if cond is None:
        f()
    else:
        pl.when(cond)(f)


def both(a, b):
    if a is None:
        return b
    return a if b is None else a & b


def place():
    x = lax.axis_index("row")
    s = lax.axis_index("seq")
    return x, s, s // 4, (s // 2) % 2, s % 2


def seat(z, y, c):
    return z * 4 + y * 2 + c


def remote(src, dst, send, recv, dev):
    return pltpu.make_async_remote_copy(src, dst, send, recv, device_id=dev, device_id_type=MESH)


def barrier_all():
    x, s = lax.axis_index("row"), lax.axis_index("seq")
    sem = pltpu.get_barrier_semaphore()
    for k in range(1, 16):
        pl.semaphore_signal(sem, inc=1, device_id=(x, (s + k) % 16), device_id_type=MESH)
    for k in range(16):
        pl.semaphore_signal(sem, inc=1, device_id=(1 - x, (s + k) % 16), device_id_type=MESH)
    pl.semaphore_wait(sem, 31)


def barrier_row(partner=False):
    x, s = lax.axis_index("row"), lax.axis_index("seq")
    sem = pltpu.get_barrier_semaphore()
    for k in range(1, 16):
        pl.semaphore_signal(sem, inc=1, device_id=(x, (s + k) % 16), device_id_type=MESH)
    if partner:
        pl.semaphore_signal(sem, inc=1, device_id=(1 - x, s), device_id_type=MESH)
    pl.semaphore_wait(sem, 16 if partner else 15)


def barrier_near():
    x, s, z, y, c = place()
    sem = pltpu.get_barrier_semaphore()
    for cond, dev in (
        (z < 3, (x, seat(z + 1, y, c))),
        (z > 0, (x, seat(z - 1, y, c))),
        (None, (x, seat(z, 1 - y, c))),
        (None, (x, seat(z, y, 1 - c))),
    ):
        when(cond, lambda dev=dev: pl.semaphore_signal(sem, inc=1, device_id=dev, device_id_type=MESH))
    pl.semaphore_wait(sem, 2 + (z < 3).astype(jnp.int32) + (z > 0).astype(jnp.int32))


QB = 512
TOKENS_CUT, COTS_CUT, HIDDEN_CUT = None, None, 64


def lane_block(i, size=QB):
    return pl.ds(pl.multiple_of(i * size, size), size)


class Gather:
    def __init__(self, own, at, send, recv, cut=None):
        self.own, self.at, self.send, self.recv, self.cut = own, at, send, recv, cut
        self.ending = False
        self.x, self.s, self.z, self.y, self.c = place()

    def device(self, k):
        x, z, y, c = self.x, self.z, self.y, self.c
        return {
            UP: (x, seat(z + 1, y, c)),
            DOWN: (x, seat(z - 1, y, c)),
            SIDE: (x, seat(z, 1 - y, c)),
            CORE: (x, seat(z, y, 1 - c)),
        }[k]

    def part(self, ref, p):
        if self.cut is None:
            return ref
        return ref.at[self.cut : ref.shape[0]] if p else ref.at[0 : self.cut]

    def copy(self, src, k, own=False, p=0):
        ref = self.own if own else self.at(src)
        send, recv = self.send.at[src, k, p], self.recv.at[src, p]
        return remote(self.part(ref, p), self.part(self.at(src), p), send, recv, self.device(k))

    def go(self, src, k, cond=None, own=False, p=0):
        if k == UP:
            cond = both(cond, self.z < 3)
        if k == DOWN:
            cond = both(cond, self.z > 0)
        act = (lambda c: c.wait_send()) if self.ending else (lambda c: c.start())
        when(cond, lambda: act(self.copy(src, k, own, p=p)))

    def wait(self, src, cond=None, p=0):
        if self.ending:
            return
        when(cond, lambda: self.copy(src, SIDE, p=p).wait_recv())

    def sides(self, t):
        if t == 0:
            return ((None, self.z, None),)
        return ((self.z - t >= 0, self.z - t, UP), (self.z + t <= 3, self.z + t, DOWN))

    def begin(self):
        if self.cut is not None:
            self.go(self.s, SIDE, own=True, p=1)
        for k in (UP, DOWN, SIDE, CORE):
            self.go(self.s, k, own=True)
        if self.cut is not None:
            for k in (UP, DOWN, CORE):
                self.go(self.s, k, own=True, p=1)

    def line(self, t):
        for cond, zz, k in self.sides(t):
            mine, other = seat(zz, self.y, self.c), seat(zz, 1 - self.y, self.c)
            parts = ((mine, 0, (k, SIDE, CORE)), (mine, 1, (k, CORE)), (other, 1, (k, CORE)))
            for src, p, ways in parts[: 1 if self.cut is None else 3]:
                self.wait(src, cond, p)
                for way in ways:
                    self.go(src, way, cond, p=p)

    def over(self, t):
        for cond, zz, _ in self.sides(t):
            src = seat(zz, 1 - self.y, self.c)
            if t == 0 and self.cut is not None:
                self.wait(src, cond, 1)
                for way in (UP, DOWN, CORE):
                    self.go(src, way, cond, p=1)
            self.wait(src, cond)
            self.go(src, CORE, cond)

    def done(self, t):
        for cond, zz, _ in self.sides(t):
            for yy in range(2):
                for p in range(1 if self.cut is None else 2):
                    self.wait(seat(zz, yy, 1 - self.c), cond, p)

    def end(self):
        self.ending = True
        self.begin()
        for t in range(4):
            if t:
                self.line(t)
            self.over(t)


GATHER_SEMS = [DMA((16, 4, 2)), DMA((16, 2))]


class GatherAll(Gather):
    first_y = False

    def device(self, k):
        return (1 - self.x, self.s) if k == ACROSS else Gather.device(self, k)

    def copy(self, src, k, own=False, x=None, p=0):
        x = self.x if x is None else x
        ref = self.own if own else self.at(x, src)
        return remote(ref, self.at(x, src), self.send.at[x, src, k], self.recv.at[x, src], self.device(k))

    def begin(self):
        for k in (UP, DOWN, SIDE, ACROSS, CORE):
            self.go(self.s, k, own=True)

    def line(self, t):
        for cond, zz, k in self.sides(t):
            mine, other = seat(zz, self.y, self.c), seat(zz, 1 - self.y, self.c)
            for src in (mine, other) if self.first_y else (mine,):
                self.wait(src, cond)
                for way in (k, ACROSS, CORE) if self.first_y else (k, SIDE, ACROSS, CORE):
                    self.go(src, way, cond)

    def over(self, t):
        if self.first_y and t:
            return
        for cond, zz, _ in self.sides(t):
            src = seat(zz, 1 - self.y, self.c)
            self.wait(src, cond)
            for way in (UP, DOWN, ACROSS, CORE) if self.first_y else (ACROSS, CORE):
                self.go(src, way, cond)

    def across(self, t):
        x = 1 - self.x
        for cond, zz, _ in self.sides(t):
            for yy in range(2):
                src = seat(zz, yy, self.c)
                if not self.ending:
                    when(cond, lambda: self.copy(src, SIDE, x=x).wait_recv())
                act = (lambda c: c.wait_send()) if self.ending else (lambda c: c.start())
                when(cond, lambda: act(self.copy(src, CORE, x=x)))

    def done(self, t):
        for cond, zz, _ in self.sides(t):
            for yy in range(2):
                src = seat(zz, yy, 1 - self.c)
                for x in (self.x, 1 - self.x):
                    when(cond, lambda: self.copy(src, SIDE, x=x).wait_recv())

    def end(self):
        Gather.end(self)
        for t in range(4):
            self.across(t)


class GatherAllY(GatherAll):
    first_y = True


GATHER_ALL_SEMS = [DMA((2, 16, 5)), DMA((2, 16))]


class Exchange:
    def __init__(self, src, dst, send, recv, wide=False):
        self.x, self.s, self.z, self.y, self.c = place()
        self.wide, self.n = wide, 32 if wide else 16
        self.src, self.dst, self.send, self.recv = src, dst, send, recv

    def seat(self, k, back=False):
        dz = (k // 4) % 4
        if back:
            dz = (4 - dz) % 4
        x = (self.x + k // 16) % 2
        s = seat((self.z + dz) % 4, (self.y + k // 2) % 2, (self.c + k) % 2)
        return x, s

    def index(self, seat_of):
        x, s = seat_of
        return x * 16 + s if self.wide else s

    def copy(self, k):
        to, me = self.seat(k), self.index((self.x, self.s))
        return remote(self.src(self.index(to)), self.dst(me), self.send.at[k], self.recv.at[k], to)

    def keep(self):
        me = self.index((self.x, self.s))
        return pltpu.make_async_copy(self.src(me), self.dst(me), self.recv.at[0])

    def begin(self, ks=None):
        for k in range(self.n) if ks is None else ks:
            if k == 0:
                self.keep().start()
            else:
                self.copy(k).start()

    def arrive(self, k):
        frm = self.seat(k, back=True)
        me = self.index((self.x, self.s))
        remote(self.src(me), self.dst(self.index(frm)), self.send.at[k], self.recv.at[k], frm).wait_recv()
        return self.index(frm)

    def end(self):
        self.keep().wait()
        for k in range(1, self.n):
            self.arrive(k)
        self.end_sends()

    def end_sends(self):
        for k in range(1, self.n):
            self.copy(k).wait_send()


class Swap(Exchange):
    def __init__(self, src, dst, whole, most, send, recv, wide=False):
        Exchange.__init__(self, src, dst, send, recv, wide)
        self.whole, self.most = whole, most

    def keep(self):
        me = self.index((self.x, self.s))
        return pltpu.make_async_copy(self.src(me), self.dst(me), self.recv.at[0])

    def copy(self, k):
        to, me = self.seat(k), self.index((self.x, self.s))
        return remote(self.src(self.index(to)), self.dst(me), self.send.at[0], self.recv.at[0], to)

    def arrived(self):
        remote(self.whole, self.whole, self.send.at[0], self.recv.at[0], self.seat(1)).wait_recv()

    def sent(self):
        remote(self.most, self.most, self.send.at[0], self.recv.at[0], self.seat(1)).wait_send()

    def end(self):
        self.arrived()
        self.sent()


class Slices:
    def __init__(self, src, got, send, recv):
        self.x, self.s, self.z, self.y, self.c = place()
        self.src, self.got, self.send, self.recv = src, got, send, recv

    def block(self, pair):
        return self.src.at[pl.ds((pair // 4) * 32, 32), lane_block(pair % 4, 256)]

    def copy(self, k):
        z, y = (self.z + k // 2) % 4, (self.y + k) % 2
        dst = self.got.at[self.x, self.s // 2, self.c]
        return remote(self.block(z * 2 + y), dst, self.send.at[k], self.recv.at[k], (self.x, seat(z, y, self.c)))

    def begin(self):
        self.local = pltpu.make_async_copy(
            self.block(self.s // 2), self.got.at[self.x, self.s // 2, self.c], self.recv.at[0]
        )
        self.local.start()
        for k in range(1, 8):
            self.copy(k).start()

    def over_x(self):
        ref = self.got.at[self.x, :, self.c]
        return remote(ref, ref, self.send.at[8], self.recv.at[8], (1 - self.x, self.s))

    def over_core(self, k):
        ref = self.got.at[self.x if k == 9 else 1 - self.x, :, self.c]
        return remote(ref, ref, self.send.at[k], self.recv.at[k], (self.x, seat(self.z, self.y, 1 - self.c)))

    def share(self):
        self.local.wait()
        for k in range(1, 8):
            z, y = (self.z + 4 - k // 2) % 4, (self.y + k) % 2
            dst = self.got.at[self.x, z * 2 + y, self.c]
            remote(
                self.block(z * 2 + y), dst, self.send.at[k], self.recv.at[k], (self.x, seat(z, y, self.c))
            ).wait_recv()
        self.over_x().start()
        self.over_core(9).start()

    def end(self):
        self.over_x().wait_recv()
        self.over_core(10).start()
        self.over_core(9).wait_recv()
        self.over_core(10).wait_recv()
        for k in range(1, 8):
            self.copy(k).wait_send()
        self.over_x().wait_send()
        self.over_core(9).wait_send()
        self.over_core(10).wait_send()


ANY = pl.ANY
SM = pltpu.SMEM


def comm_call(body, outs, ins, sems, cid, scratch=(), out_spaces=None, in_spaces=None):
    return pl.pallas_call(
        body,
        out_shape=outs,
        in_specs=[pl.BlockSpec(memory_space=m) for m in in_spaces or [VM] * len(ins)],
        out_specs=[pl.BlockSpec(memory_space=m) for m in out_spaces or [VM] * len(outs)],
        scratch_shapes=list(scratch) + list(sems),
        compiler_params=pltpu.CompilerParams(
            collective_id=cid, has_side_effects=True, vmem_limit_bytes=VMEM_LIMIT
        ),
    )(*ins)


def sds(shape, dtype):
    return jax.ShapeDtypeStruct(shape, dtype)


class Reduce:
    def __init__(self, part, out, bufs, sems, near=None):
        self.part, self.out = part, out
        self.near = part if near is None else near
        self.r1, self.ra, self.ua, self.da = bufs
        self.s1, self.q1, self.sa, self.qa, self.su, self.qu, self.sd, self.qd = sems
        self.x, self.s, self.z, self.y, self.c = place()

    @staticmethod
    def bufs(rows, width):
        return [VM((4, 2, rows, width), BF)] + [VM((4, rows, width), BF)] * 3

    SEMS = [DMA((4, 2))] * 8

    def add(self, dst, src):
        dst[...] = (dst[...].astype(F32) + src[...].astype(F32)).astype(BF)

    def piece(self, p):
        rows = self.ra.shape[1] // 2
        return slice(p * rows, p * rows + rows)

    def first(self, zz, yy):
        return remote(
            self.part.at[seat(zz, yy, 1 - self.c)],
            self.r1.at[zz, yy],
            self.s1.at[zz, yy],
            self.q1.at[zz, yy],
            (self.x, seat(self.z, self.y, 1 - self.c)),
        )

    def side(self, zz, p):
        part = self.piece(p)
        return remote(
            self.r1.at[zz, 1 - self.y, part],
            self.ra.at[zz, part],
            self.sa.at[zz, p],
            self.qa.at[zz, p],
            (self.x, seat(self.z, 1 - self.y, self.c)),
        )

    def line(self, zz, p, up):
        z, y, c = self.z, self.y, self.c
        src = self.ra.at[zz, self.piece(p)]
        dst = (self.ua if up else self.da).at[zz, self.piece(p)]
        send, recv = (self.su, self.qu) if up else (self.sd, self.qd)
        return remote(src, dst, send.at[zz, p], recv.at[zz, p], (self.x, seat(z + 1 if up else z - 1, y, c)))

    def order(self):
        z = self.z
        for t in (3, 2, 1):
            yield z + t <= 3, z + t, True
            yield z - t >= 0, z - t, False
        yield None, z, None

    def begin_plane(self, zz, cond=None):
        for yy in range(2):
            when(cond, lambda: self.first(zz, yy).start())

    def begin(self):
        for cond, zz, _ in self.order():
            self.begin_plane(zz, cond)

    def fold(self, zz, cond=None):
        def go():
            for yy in range(2):
                self.first(zz, yy).wait_recv()
                self.add(self.r1.at[zz, yy], self.near.at[seat(zz, yy, self.c)])
            for p in range(2):
                self.side(zz, p).start()

        when(cond, go)

    def take(self, zz, p, up):
        self.line(zz, p, up).wait_recv()
        part = self.piece(p)
        self.add(self.ra.at[zz, part], (self.ua if up else self.da).at[zz, part])

    def flow_plane(self, cond, zz, up):
        z = self.z

        def go():
            for p in range(2):
                part = self.piece(p)
                self.side(zz, p).wait_recv()
                self.add(self.ra.at[zz, part], self.r1.at[zz, self.y, part])
                if up is not None:
                    pl.when(z > 0 if up else z < 3)(lambda: self.take(zz, p, up))
                    self.line(zz, p, up).start()

        when(cond, go)

    def flow(self):
        z = self.z
        for cond, zz, up in self.order():
            self.flow_plane(cond, zz, up)
        for up, cond in ((True, z > 0), (False, z < 3)):
            for p in range(2):
                when(cond, lambda: self.take(z, p, up))
        self.out[...] = self.ra[z]

    def run(self):
        for cond, zz, _ in self.order():
            self.fold(zz, cond)
        self.flow()

    def end(self):
        for cond, zz, up in self.order():
            for yy in range(2):
                when(cond, lambda: self.first(zz, yy).wait_send())
            for p in range(2):
                when(cond, lambda: self.side(zz, p).wait_send())
                if up is not None:
                    when(cond, lambda: self.line(zz, p, up).wait_send())


NBUF = 4
NSEM = 8
TB = 512


def allowed_mask(first_key, first_query, start_row):
    key = first_key + lax.broadcasted_iota(jnp.int32, (QB, QB), 0)
    query = first_query + lax.broadcasted_iota(jnp.int32, (QB, QB), 1)
    return (key <= query) & (key >= start_row)


SCORE = math.log2(math.e) / math.sqrt(HEAD_SIZE)


def as_row(col):
    n = col.shape[0]
    same = lax.broadcasted_iota(jnp.int32, (n, n), 0) == lax.broadcasted_iota(jnp.int32, (n, n), 1)
    return jnp.sum(jnp.where(same, jnp.broadcast_to(col, (n, n)), 0.0), axis=0, keepdims=True)


def column(line):
    n = line.shape[1]
    same = lax.broadcasted_iota(jnp.int32, (n, n), 0) == lax.broadcasted_iota(jnp.int32, (n, n), 1)
    return jnp.sum(jnp.where(same, jnp.broadcast_to(line.astype(F32), (n, n)), 0.0), axis=1, keepdims=True)


def layer(
    tok, query_w, key_w, value_w, out_w, router_w, gate_w, up_w, down_w, gain_a, gain_e, seg, routes, cot, rope, freq,
    hid, mixp, dw_all, grad_tokens, dwo_sum, wg_all, mix, residual,
    q_t, k_t, v_t, o_t, lse, start, cos, sin, normed, scale_out, h2, att, probs, picked, wperm, back, g_all,
    wo, w3, spread, seg_mine, row_all, w_mine, seg_all, o_low, att_t, k_n, w_t, wo_v,
    wexp, cot_all, p_t, p_all, backp, mix_v, gg, acc,
    g_res, grad_t, router_t, dwo, dwo_x, gkv, v_n, delta, got, g_t, wg, g_mine,
    *rest,
):
    bufs, bufs_o, sems = rest[:NBUF], rest[NBUF : 2 * NBUF], rest[2 * NBUF :]
    (
        t_send, t_recv, o_send, o_recv, c_send, c_recv, h_send, h_recv, q_send, q_recv, w_send, w_recv, e_send, e_recv,
        x_send, x_recv, g_send, g_recv, a_send, a_recv, p_send, p_recv, y_send, y_recv, b_send, b_recv, r_send, r_recv,
        v_send, v_recv, w0s, w0r, w1s, w1r, w2s, w2r, d_sem, x_sem, free,
    ) = sems[3 * NSEM :]
    x, s, z, y, c = place()
    rows, width = tok.shape
    length = 16 * rows
    barrier_all()
    tokens = Gather(tok, lambda src: row_all.at[src], t_send, t_recv, TOKENS_CUT)
    tokens.begin()
    keep_tok = pltpu.make_async_copy(tok, row_all.at[s], x_sem.at[2])
    keep_tok.start()
    seg_mine[...] = jnp.broadcast_to(seg[...], seg_mine.shape)
    documents = Swap(lambda r: seg_mine, lambda r: seg_all.at[r], seg_all, seg_all.at[0:15], g_send, g_recv)
    documents.begin()
    by_first = column(gain_a[...])
    for j in range(8):
        part, lane = slice(32 * (j // 4), 32 * (j // 4) + 32), 256 * (j % 4)
        wperm[part, lane : lane + 128] = (query_w[:, 128 * j : 128 * j + 128].astype(F32) * by_first).astype(BF)
        pair = [ref[:, 64 * j : 64 * j + 64].astype(F32) for ref in (key_w, value_w)]
        wperm[part, lane + 128 : lane + 256] = (jnp.concatenate(pair, axis=1) * by_first).astype(BF)
    slices = Slices(wperm, w_mine, w_send, w_recv)
    slices.begin()
    by_second = column(gain_e[...])
    wo[:, 0:width] = out_w[...]
    router = router_w[...].astype(F32) * gain_e[...].astype(F32)
    router = jnp.concatenate([jnp.concatenate([router, jnp.zeros((128 - E, 32), F32)], axis=0), jnp.zeros((128, 96), F32)], axis=1)
    wo[:, width : width + 128] = jnp.transpose(router)[0:32].astype(BF)
    outw = GatherAll(wo, lambda x, src: wo_v.at[x, src], o_send, o_recv)
    keep = pltpu.make_async_copy(wo, wo_v.at[x, s], x_sem.at[3])
    keep.start()
    for m, ref in enumerate((gate_w, up_w, down_w)):
        plain = ref[...].astype(F32).reshape(32 * E, F)
        for b in range(F // 128):
            lanes = slice(b * 128, b * 128 + 128)
            spread[...] = plain[:, lanes]
            for e in range(E):
                part = spread[pl.ds(e, 32, stride=E), :]
                w3[e, m, :, lanes] = (part * by_second if m < 2 else part).astype(BF)
    weights = Exchange(lambda e: w3.at[e], lambda r: wexp.at[:, x * 16 + r], e_send, e_recv)
    cots = Gather(cot, lambda src: cot_all.at[src], c_send, c_recv, COTS_CUT)

    def cross_copy(k, back=False):
        row = weights.index(weights.seat(k, back=True))
        src = w3.at[s] if k == 0 else wexp.at[:, x * 16 + row]
        dst = wexp.at[:, (1 - x if back else x) * 16 + row]
        return remote(src, dst, x_send.at[k], x_recv.at[k], (1 - x, s))

    def cross(k):
        if k:
            weights.arrive(k)
        cross_copy(k).start()

    factor = jnp.exp2(rope[0].astype(F32))
    for b in range(length // 128):
        position = (b * 128 + lax.broadcasted_iota(jnp.int32, (32, 128), 1)).astype(F32)
        angle = position / factor * freq[...]
        cos[:, b * 128 : b * 128 + 128] = jnp.cos(angle)
        sin[:, b * 128 : b * 128 + 128] = jnp.sin(angle)
    tokens.over(0)
    tokens.line(1)
    slices.share()
    tokens.over(1)
    outw.begin()
    tokens.line(2)
    weights.begin(range(8))
    slices.end()
    w_t[...] = jnp.transpose(w_mine[...].reshape(width, 256).astype(F32)).astype(BF)
    tokens.over(2)
    tokens.line(3)
    outw.over(0)
    outw.line(1)
    weights.begin(range(8, 12))
    documents.end()
    numbers = seg_all[:, 0, :]
    ends = [jnp.sum((numbers < n).astype(jnp.int32)) for n in (1, 2)]
    for b in range(16):
        line = numbers[b : b + 1]
        start[:, b * 128 : b * 128 + 128] = jnp.where(line == 0, 0, jnp.where(line == 1, ends[0], ends[1]))
    tokens.over(3)
    for t in range(4):
        tokens.done(t)
    keep_tok.wait()
    tokens.end()
    acc[...] = jnp.zeros(acc.shape, F32)
    for k in range(4):
        cross(k)

    def project(i, _):
        cols = lane_block(i, 512)
        values = row_all[pl.ds(i * 4, 4)].reshape(512, width).astype(F32)
        scale = lax.rsqrt(jnp.mean(values * values, axis=-1, keepdims=True) + EPSILON)
        hidden = (values * scale).astype(BF)
        row_all[pl.ds(i * 4, 4)] = hidden.reshape(4, rows, width)
        made = dot(w_t[...], hidden, NT)
        co, si = cos[:, cols], sin[:, cols]
        own = jnp.where(c == 0, made[0:64], made[64:128])
        for ref, part in ((q_t, own), (k_t, made[128:192])):
            a, b = part[:32], part[32:]
            ref[0:32, cols] = (a * co - b * si).astype(BF)
            ref[32:64, cols] = (b * co + a * si).astype(BF)
        v_t[:, cols] = made[192:256].astype(BF)
        k_n[cols, :] = jnp.transpose(k_t[:, cols].astype(F32)).astype(BF)
        return 0

    lax.fori_loop(0, length // 512, project, 0)
    keep_hid = pltpu.make_async_copy(row_all, hid, x_sem.at[4])
    keep_hid.start()

    def query_block(i, _):
        @pl.when(i == 1)
        def _():
            outw.over(1)
            outw.line(2)

        @pl.when(i == 3)
        def _():
            outw.over(2)
            outw.line(3)
            cots.begin()

        cols = lane_block(i)
        queries = q_t[:, cols]
        begin = start[:, cols]

        def key_block(j, carried):
            top, total, acc = carried
            keys = lane_block(j)
            scores = dot(k_n[keys, :], queries) * SCORE
            scores = jnp.where(allowed_mask(j * QB, i * QB, begin), scores, MASKED)
            fresh = jnp.maximum(top, jnp.max(scores, axis=0, keepdims=True))
            powers = jnp.exp2(scores - fresh)
            decay = jnp.exp2(top - fresh)
            total = total * decay + jnp.sum(powers, axis=0, keepdims=True)
            acc = acc * decay + dot(v_t[:, keys], powers.astype(BF))
            return fresh, total, acc

        top, total, acc = lax.fori_loop(
            0,
            i + 1,
            key_block,
            (jnp.full((1, QB), MASKED, F32), jnp.zeros((1, QB), F32), jnp.zeros((HEAD_SIZE, QB), F32)),
        )
        out = acc / total
        o_t[:, cols] = out
        o_low[:, cols] = out.astype(BF)
        lse[:, cols] = top + jnp.log2(total)
        return 0

    lax.fori_loop(0, length // QB, query_block, 0)
    outw.over(3)
    for k in range(4, 8):
        cross(k)
    keep_hid.wait()
    heads = Swap(
        lambda t: o_low.at[:, lane_block(t, 128)], lambda h: att_t.at[h], att_t, att_t.at[0:15], a_send, a_recv
    )
    heads.begin()
    keep_cot = pltpu.make_async_copy(cot, cot_all.at[s], x_sem.at[6])
    keep_cot.start()
    for t in range(4):
        outw.across(t)
    for t in range(4):
        outw.done(t)
    keep.wait()
    cots.over(0)
    cots.line(1)
    weights.begin(range(12, 16))
    heads.end()
    for k in range(8, 12):
        cross(k)

    att[...] = jnp.transpose(att_t[...].reshape(width, rows).astype(F32)).astype(BF)
    res = tok[...].astype(F32) + dot(att[...], wo_v[:, :, :, 0:width].reshape(width, width), NT)
    residual[...] = res
    scale = lax.rsqrt(jnp.mean(res * res, axis=-1, keepdims=True) + EPSILON)
    norm = res * scale
    normed[...] = norm
    scale_out[...] = jnp.broadcast_to(scale, scale_out.shape)
    hidden = norm.astype(BF)
    h2[...] = hidden
    lanes = lax.broadcasted_iota(jnp.int32, (128, 128), 1)
    logits = jnp.where(lanes < E, dot(hidden, wo_v[:, :, :, width : width + 128].reshape(width, 128)), MASKED)
    top = jnp.max(logits, axis=-1, keepdims=True)
    powers = jnp.exp(logits - top)
    prob = powers / jnp.sum(powers, axis=-1, keepdims=True)
    probs[...] = prob
    names = lax.broadcasted_iota(jnp.int32, (128, 128), 0)
    mask = jnp.zeros((128, 128), F32)
    for k in range(K):
        mask = mask + jnp.where(names == routes[k : k + 1, :], 1.0, 0.0)
    mask = jnp.transpose(mask)
    picked[...] = mask
    p_t[...] = jnp.transpose(prob * mask)[0:E, :]

    hidden = Gather(h2, lambda src: row_all.at[src], h_send, h_recv, HIDDEN_CUT)
    hidden.begin()
    keep = pltpu.make_async_copy(h2, row_all.at[s], x_sem.at[8])
    keep.start()
    minor = Swap(lambda r: p_t, lambda r: p_all.at[r], p_all, p_all.at[0:15], p_send, p_recv)
    minor.begin()
    one = Reduce(backp, back, bufs, sems[:NSEM])
    hidden.over(0)
    keep.wait()
    keep_cot.wait()
    weights.end_sends()
    weights.keep().wait()
    cross_copy(0).wait_send()
    for k in range(12, 16):
        cross(k)
    minor.end()
    hidden.line(1)
    for k in range(16):
        if k:
            cross_copy(k).wait_send()
        cross_copy(k, back=True).wait_recv()
    cots.done(0)
    hidden.done(0)
    far = z // 2
    order = (z, z + 1 - 2 * far, 2 - 2 * z + 5 * far, 3 - 3 * far)

    def chunk(i, _):
        zz = jnp.where(i == 0, order[0], jnp.where(i == 1, order[1], jnp.where(i == 2, order[2], order[3])))

        for t in (1, 2, 3):

            @pl.when(i == t)
            def _():
                cots.done(t)
                hidden.done(t)

        four = pl.ds(zz * 4, 4)
        some = row_all[four].reshape(4 * rows, width)
        grad = cot_all[four].reshape(4 * rows, width)
        cols = [jnp.broadcast_to(p_all[zz * 4 + b, pl.ds(s, 1), :], (128, 128)) for b in range(4)]
        prob = jnp.concatenate([jnp.transpose(v)[:, 0:1] for v in cols], axis=0)
        gate = dot(some, wexp[0].reshape(width, F))
        up = dot(some, wexp[1].reshape(width, F))

        @pl.when(i == 0)
        def _():
            hidden.over(1)
            hidden.line(2)
            cots.over(1)

        @pl.when(i == 1)
        def _():
            hidden.over(2)
            hidden.line(3)

        @pl.when(i == 2)
        def _():
            one.fold(order[0])
            one.fold(order[1])
            hidden.over(3)

        sig = 1.0 / (1.0 + jnp.exp(-gate))
        silu = gate * sig
        low = (silu * up).astype(BF)
        moved = dot(grad, wexp[2].reshape(width, F))
        seen = jnp.sum(low.astype(F32) * moved, axis=-1, keepdims=True)
        for b in range(4):
            line = jnp.transpose(jnp.broadcast_to(seen[b * 128 : b * 128 + 128], (128, 128)))[0:8]
            gg[zz * 4 + b] = line
        grad_hidden = moved * prob
        grad_gate = (grad_hidden * up * (sig * (1.0 + gate * (1.0 - sig)))).astype(BF)
        grad_up = (grad_hidden * silu).astype(BF)
        below = dot(grad_gate, wexp[0].reshape(width, F), NT) + dot(
            grad_up, wexp[1].reshape(width, F), NT
        )
        backp[four] = below.astype(BF).reshape(4, rows, width)
        one.begin_plane(zz)

        @pl.when(i == 0)
        def _():
            cots.line(2)

        @pl.when(i == 1)
        def _():
            cots.over(2)

        @pl.when(i == 2)
        def _():
            cots.over(3)

        @pl.when(i == 3)
        def _():
            one.fold(order[2])

        out = dot(low, wexp[2].reshape(width, F), NT)
        keep_mix = pltpu.make_async_copy(mix_v, mixp.at[four], x_sem.at[7])
        pl.when(i > 0)(lambda: keep_mix.wait())
        mix_v[...] = (prob * out).astype(BF).reshape(4, rows, width)
        keep_mix.start()
        acc[0] += dot(some, grad_gate, TN)
        acc[1] += dot(some, grad_up, TN)
        acc[2] += dot(grad, (prob * low.astype(F32)).astype(BF), TN)

        @pl.when(i == 1)
        def _():
            cots.line(3)

        return 0

    lax.fori_loop(0, 4, chunk, 0)
    one.fold(order[3])
    seen_out = Swap(lambda r: gg.at[r], lambda r: g_all.at[r], g_all, g_all.at[0:15], y_send, y_recv)
    seen_out.begin()

    def over_d(m):
        part = wexp.at[m, pl.ds((1 - x) * 16, 16)]
        return remote(part, w3.at[:, m], d_sem.at[0, m], d_sem.at[1, m], (1 - x, s))

    for m in range(3):
        wexp[m] = acc[m].astype(BF).reshape(wexp.shape[1:])
        over_d(m).start()
    owners = [
        Swap(
            lambda r, m=m: w3.at[r, m],
            lambda e, m=m: dw_all.at[m, e],
            dw_all.at[m],
            dw_all.at[m, 0:15],
            (w0s, w1s, w2s)[m],
            (w0r, w1r, w2r)[m],
        )
        for m in range(3)
    ]

    def to_owners(m):
        over_d(m).wait()
        w3[:, m] = (w3[:, m].astype(F32) + wexp[m, pl.ds(x * 16, 16)].astype(F32)).astype(BF)
        owners[m].begin()

    for g in (outw, cots, hidden):
        g.end()
    one.flow()
    one.end()
    pltpu.make_async_copy(mix_v, mixp.at[pl.ds(0, 4)], x_sem.at[7]).wait()
    near = (
        (z < 3, (x, seat(z + 1, y, c))),
        (z > 0, (x, seat(z - 1, y, c))),
        (None, (x, seat(z, 1 - y, c))),
        (None, (x, seat(z, y, 1 - c))),
        (None, (1 - x, s)),
    )
    for cond, dev in near:
        when(cond, lambda dev=dev: pl.semaphore_signal(free, inc=1, device_id=dev, device_id_type=MESH))
    loads = [
        pltpu.make_async_copy(hid, row_all, x_sem.at[9]),
        pltpu.make_async_copy(mixp, backp, x_sem.at[10]),
    ]
    for copy in loads:
        copy.start()
    seen_out.end()
    pl.semaphore_wait(free, 3 + (z < 3).astype(jnp.int32) + (z > 0).astype(jnp.int32))
    me = x * 16 + s
    columns_all = GatherAll(
        wperm, lambda x_, src: cot_all.at[x_ * 8 + src // 2, pl.ds((src % 2) * 64, 64)], q_send, q_recv
    )
    columns_all.begin()
    keep_w = pltpu.make_async_copy(wperm, cot_all.at[me // 2, pl.ds((me % 2) * 64, 64)], x_sem.at[11])
    keep_w.start()
    two = Reduce(mixp, mix, bufs, sems[NSEM : 2 * NSEM], backp)
    two.begin()

    seen = jnp.concatenate([g_all[e, 0:1, :] for e in range(E)] + [jnp.zeros((128 - E, 128), F32)], axis=0)
    grad_probs = jnp.transpose(seen) * picked[...]
    prob = probs[...]
    grad_logits = (prob * (grad_probs - jnp.sum(prob * grad_probs, axis=-1, keepdims=True))).astype(BF)
    u = back[...].astype(F32) + dot(
        grad_logits, wo_v[:, :, :, width : width + 128].reshape(width, 128), NT
    )
    norm = normed[...]
    grad = cot[...].astype(F32) + scale_out[:, 0:1] * (u - norm * jnp.mean(u * norm, axis=-1, keepdims=True))
    g_res[...] = grad
    branch = grad.astype(BF)
    att_t[...] = jnp.transpose(dot(branch, wo_v[:, :, :, 0:width].reshape(width, width))).astype(BF).reshape(att_t.shape)
    heads = Swap(
        lambda h: att_t.at[h], lambda t: o_low.at[:, lane_block(t, 128)], o_low, att_t.at[0:15], b_send, b_recv
    )
    heads.begin()
    columns_all.over(0)
    columns_all.line(1)
    loads[1].wait()
    for cond, zz, _ in two.order():
        two.fold(zz, cond)
    grad_t[...] = jnp.transpose(grad).astype(BF)
    other = pl.ds((1 - x) * (width // 2), width // 2)
    router_t[...] = dot(h2[...], grad_logits, TN).astype(BF)
    dwo[:, :, 0:width] = dot(grad_t[other, :], att[...]).astype(BF).reshape(16, 32, width)
    dwo[:, :, width : width + 128] = router_t[other, :].reshape(16, 32, 128)
    over_o = remote(dwo, dwo_x, x_sem.at[12], x_sem.at[13], (1 - x, s))
    over_o.start()
    to_owners(0)
    to_owners(1)
    v_n[...] = jnp.transpose(v_t[...].astype(F32)).astype(BF)
    gkv[...] = jnp.zeros(gkv.shape, F32)
    heads.end()
    delta[...] = jnp.sum(o_low[...].astype(F32) * o_t[...], axis=0, keepdims=True)

    def query_block(i, _):
        @pl.when(i == 2)
        def _():
            two.flow()

        @pl.when(i == 3)
        def _():
            columns_all.over(1)
            to_owners(2)
            columns_all.line(2)

        cols = lane_block(i)
        queries, grads = q_t[:, cols], o_low[:, cols]
        begin, log_total, shift = start[:, cols], lse[:, cols], delta[:, cols]

        def key_block(j, sofar):
            rows = lane_block(j)
            scores = dot(k_n[rows, :], queries) * SCORE
            powers = jnp.where(allowed_mask(j * QB, i * QB, begin), jnp.exp2(scores - log_total), 0.0)
            moved = dot(v_n[rows, :], grads)
            grad_scores = (powers * (moved - shift)).astype(BF)
            gkv[0, :, rows] += dot(queries, grad_scores, NT)
            gkv[1, :, rows] += dot(grads, powers.astype(BF), NT)
            return sofar + dot(k_t[:, rows], grad_scores)

        o_t[:, cols] = lax.fori_loop(0, i + 1, key_block, jnp.zeros((HEAD_SIZE, QB), F32))
        return 0

    lax.fori_loop(0, length // QB, query_block, 0)
    columns_all.over(2)

    pair = remote(gkv.at[1 - c], got, x_sem.at[14], x_sem.at[15], (x, seat(z, y, 1 - c)))
    pair.start()
    columns_all.line(3)
    over_o.wait_recv()
    own = pl.ds(x * (width // 2), width // 2)
    mine = dot(grad_t[own, :], att[...]).reshape(16, 32, width)
    dwo_x[:, :, 0:width] = (dwo_x[:, :, 0:width].astype(F32) + mine).astype(BF)
    mine = router_t[own, :].reshape(16, 32, 128).astype(F32)
    dwo_x[:, :, width : width + 128] = (dwo_x[:, :, width : width + 128].astype(F32) + mine).astype(BF)
    out = Reduce(dwo_x, dwo_sum, bufs_o, sems[2 * NSEM : 3 * NSEM])
    out.begin()
    scaling = 1.0 / math.sqrt(HEAD_SIZE)
    co, si = cos[...], sin[...]

    def unturn(part):
        a, b = part[:32], part[32:]
        return jnp.concatenate([a * co + b * si, b * co - a * si], axis=0)

    g_t[0] = unturn(o_t[...] * scaling).astype(BF)
    pair.wait()
    mine = gkv[c] + got[...]
    g_t[1] = jnp.where(c == 0, unturn(mine * scaling), mine).astype(BF)
    tokens = Swap(
        lambda t: g_t.at[:, :, lane_block(t, 128)],
        lambda h: g_mine.at[h // 2, :, h % 2],
        g_mine,
        g_t.at[:, :, 0 : length - 128],
        r_send,
        r_recv,
    )
    tokens.begin()
    loads[0].wait()
    wg[...] = jnp.transpose(dot(g_t[...].reshape(128, length), row_all[...].reshape(length, width))).astype(BF).reshape(
        wg.shape
    )
    columns = Swap(lambda r: wg.at[r], lambda r: wg_all.at[r], wg_all, wg_all.at[0:31], v_send, v_recv, wide=True)
    columns.begin()
    columns_all.over(3)
    for t in range(4):
        columns_all.across(t)
    for t in range(4):
        columns_all.done(t)
    keep_w.wait()
    for cond, zz, _ in out.order():
        out.fold(zz, cond)
    tokens.end()
    halves = cot_all[...].reshape(32, 2, 32, width)
    w = sum(dot(halves[:, h].reshape(width, width), g_mine[4 * h : 4 * h + 4].reshape(width, 128)) for h in range(2))
    w = jnp.transpose(w)
    values = tok[...].astype(F32)
    scale_first = lax.rsqrt(jnp.mean(values * values, axis=-1, keepdims=True) + EPSILON)
    norm = values * scale_first
    grad_tokens[...] = g_res[...] + scale_first * (w - norm * jnp.mean(w * norm, axis=-1, keepdims=True))
    out.flow()
    out.end()
    columns.end()
    for owner in owners:
        owner.end()
    over_o.wait_send()
    two.end()
    columns_all.end()


def finish(
    wg_all, dwo_sum, dw_all, query_w, key_w, value_w, router_w, gate_w, up_w, gain_a, gain_e, mix, residual, g_tok,
    mixed, grad_tokens, grad_a, grad_e, grad_q, grad_k, grad_v, grad_o, grad_r, grad_gate, grad_up, grad_down,
    spread, arrived, staged, sem,
):
    width = grad_o.shape[1]
    outs = (grad_gate, grad_up, grad_down)
    loads = [pltpu.make_async_copy(dw_all.at[m], arrived.at[m], sem.at[0, m]) for m in range(3)]
    stores = [pltpu.make_async_copy(staged.at[m], outs[m], sem.at[1, m]) for m in range(3)]
    for copy in loads:
        copy.start()
    mixed[...] = (residual[...] + mix[...].astype(F32)).astype(BF)
    grad_tokens[...] = g_tok[...]
    by_first, by_second = column(gain_a[...]), column(gain_e[...])
    head = [wg_all[h].astype(F32) + wg_all[16 + h].astype(F32) for h in range(16)]
    total = jnp.zeros((32, 128), F32)
    for ref, weight, lanes, seats in (
        (grad_q, query_w, slice(0, 64), range(16)),
        (grad_k, key_w, slice(64, 128), range(0, 16, 2)),
        (grad_v, value_w, slice(64, 128), range(1, 16, 2)),
    ):
        for j in range(len(seats) // 2):
            part = jnp.concatenate([head[seats[2 * j]][:, lanes], head[seats[2 * j + 1]][:, lanes]], axis=1)
            cols = slice(128 * j, 128 * j + 128)
            ref[:, cols] = part * by_first
            total = total + part * weight[:, cols].astype(F32)
    grad_a[...] = as_row(jnp.sum(total, axis=1, keepdims=True))
    grad_o[...] = dwo_sum[:, 0:width].astype(F32)
    router = dwo_sum[:, width : width + 128].astype(F32)
    router = jnp.concatenate([router, jnp.zeros((96, 128), F32)], axis=0)
    router = jnp.transpose(router)[0:E, 0:32]
    grad_r[...] = router * gain_e[...].astype(F32)
    total = jnp.zeros((32 * E, 128), F32)
    for m, weight in enumerate((gate_w, up_w, None)):
        loads[m].wait()
        ref = staged.at[m]
        for b in range(F // 128):
            lanes = slice(b * 128, b * 128 + 128)
            for e in range(E):
                part = arrived[m, e, :, lanes].astype(F32)
                spread[b, pl.ds(e, 32, stride=E), :] = part
            plain = spread[b]
            if m == 2:
                ref[:, :, lanes] = plain.reshape(32, E, 128)
            else:
                ref[:, :, lanes] = plain.reshape(32, E, 128) * by_second[:, :, None]
                total = total + plain * weight[:, :, lanes].astype(F32).reshape(32 * E, 128)
        stores[m].start()
    sums = jnp.sum(jnp.sum(total.reshape(32, E, 128), axis=1), axis=1, keepdims=True)
    grad_e[...] = as_row(sums) + jnp.sum(router * router_w[...].astype(F32), axis=0, keepdims=True)
    for copy in stores:
        copy.wait()


def frequencies(head_dim):
    halves = head_dim // 2
    return jnp.power(ROPE_BASE, -jnp.arange(halves, dtype=F32) * (2.0 / head_dim))


def sixteen_seats(
    tokens,
    attention_gain,
    expert_gain,
    query_weight,
    key_matrix,
    value_matrix,
    output_weight,
    router_weight,
    gate_weight,
    up_weight,
    down_weight,
    routes,
    segments,
    rope_index,
    cotangent,
):
    D = MODEL_WIDTH
    rows = tokens.shape[1]
    length = 16 * rows
    tok_mine = tokens.reshape(rows, D)
    cot_mine = cotangent.reshape(rows, D)
    powers = np.power(np.float32(ROPE_BASE), -np.arange(32, dtype=np.float32) * np.float32(2.0 / HEAD_SIZE))
    freq = jnp.asarray(np.broadcast_to(powers[:, None], (32, 128)).astype(np.float32))
    _, _, dw_all, grad_tokens, dwo_sum, wg_all, mix, residual = comm_call(
        layer,
        [sds((16, rows, D), BF), sds((16, rows, D), BF), sds((3, 16, 32, F), BF), sds((rows, D), F32)]
        + [sds((32, D + 128), BF), sds((32, 32, 128), BF), sds((rows, D), BF), sds((rows, D), F32)],
        [
            tok_mine,
            query_weight,
            key_matrix,
            value_matrix,
            output_weight,
            router_weight.T,
            gate_weight,
            up_weight,
            down_weight,
            attention_gain.reshape(1, 32),
            expert_gain.reshape(1, 32),
            segments.astype(jnp.int32),
            routes.reshape(rows, K).T,
            cot_mine,
            rope_index.astype(jnp.int32),
            freq,
        ],
        Reduce.SEMS * 3
        + GATHER_SEMS
        + GATHER_ALL_SEMS
        + GATHER_SEMS * 2
        + GATHER_ALL_SEMS
        + [DMA((16,))] * 6
        + [DMA((1,))] * 20
        + [DMA((2, 3)), DMA((16,)), pltpu.SemaphoreType.REGULAR],
        0,
        [VM((64, length), BF)] * 3
        + [VM((64, length), F32), VM((1, length), F32), VM((1, length), jnp.int32)]
        + [VM((32, length), F32)] * 2
        + [VM((rows, D), F32), VM((rows, 128), F32), VM((rows, D), BF), VM((rows, D), BF)]
        + [VM((rows, 128), F32), VM((rows, 128), F32), VM((64, D), BF), VM((rows, D), BF)]
        + [VM((16, 8, rows), F32)]
        + [
            VM((32, D + 128), BF),
            VM((E, 3, 32, F), BF),
            VM((32 * E, 128), F32),
            VM((8, rows), jnp.int32),
            VM((16, rows, D), BF),
            VM((2, 8, 2, 32, 256), BF),
            VM((16, 8, rows), jnp.int32),
            VM((64, length), BF),
            VM((16, 64, rows), BF),
            VM((length, 64), BF),
            VM((256, D), BF),
            VM((2, 16, 32, D + 128), BF),
            VM((3, 32, 32, F), BF),
            VM((16, rows, D), BF),
            VM((E, rows), F32),
            VM((16, E, rows), F32),
            VM((16, rows, D), BF),
            VM((4, rows, D), BF),
            VM((16, 8, rows), F32),
            VM((3, D, F), F32),
        ]
        + [
            VM((rows, D), F32),
            VM((D, rows), BF),
            VM((D, 128), BF),
            VM((16, 32, D + 128), BF),
            VM((16, 32, D + 128), BF),
            VM((2, 64, length), F32),
            VM((length, 64), BF),
            VM((1, length), F32),
            VM((64, length), F32),
            VM((2, 64, length), BF),
            VM((32, 32, 128), BF),
            VM((8, 2, 2, 64, rows), BF),
        ]
        + Reduce.bufs(rows, D)
        + Reduce.bufs(32, D + 128),
        [ANY] * 3 + [VM] * 5,
        [VM] * 14 + [SM, VM],
    )
    (
        mixed, grad_tokens, grad_a, grad_e, grad_q, grad_k, grad_v, grad_o, grad_r, grad_gate, grad_up, grad_down,
    ) = pl.pallas_call(
        finish,
        out_shape=[sds((rows, D), BF), sds((rows, D), F32), sds((1, 32), F32), sds((1, 32), F32)]
        + [sds((32, n), F32) for n in (D, 512, 512, D)]
        + [sds((E, 32), F32)]
        + [sds((32, E, F), F32)] * 3,
        in_specs=[pl.BlockSpec(memory_space=m) for m in [VM] * 2 + [ANY] + [VM] * 11],
        out_specs=[pl.BlockSpec(memory_space=m) for m in [VM] * 9 + [ANY] * 3],
        scratch_shapes=[
            VM((F // 128, 32 * E, 128), F32),
            VM((3, E, 32, F), BF),
            VM((3, 32, E, F), F32),
            DMA((2, 3)),
        ],
        compiler_params=pltpu.CompilerParams(vmem_limit_bytes=VMEM_LIMIT),
    )(
        wg_all,
        dwo_sum,
        dw_all,
        query_weight,
        key_matrix,
        value_matrix,
        router_weight.T,
        gate_weight,
        up_weight,
        attention_gain.reshape(1, 32),
        expert_gain.reshape(1, 32),
        mix,
        residual,
        grad_tokens,
    )
    return (
        mixed.reshape(tokens.shape),
        grad_tokens.reshape(tokens.shape),
        grad_a.reshape(32),
        grad_e.reshape(32),
        grad_q,
        grad_k,
        grad_v,
        grad_o,
        grad_r.T,
        grad_gate,
        grad_up,
        grad_down,
    )


def rms_scale(values):
    return lax.rsqrt(jnp.mean(values * values, axis=-1, keepdims=True) + EPSILON)


def apply_rotary(values, cosine_lookup, sine_lookup):
    halves = values.shape[-1] // 2
    first_half = values[..., :halves]
    second_half = values[..., halves:]
    return jnp.concatenate(
        [
            first_half * cosine_lookup - second_half * sine_lookup,
            second_half * cosine_lookup + first_half * sine_lookup,
        ],
        axis=-1,
    )


def unrotate(values, cosine_lookup, sine_lookup):
    halves = values.shape[-1] // 2
    first_half = values[..., :halves]
    second_half = values[..., halves:]
    return jnp.concatenate(
        [
            first_half * cosine_lookup + second_half * sine_lookup,
            second_half * cosine_lookup - first_half * sine_lookup,
        ],
        axis=-1,
    )


def block_mask(key_start, block_size, query_pos, query_seg, seg_block):
    key_pos = key_start + jnp.arange(block_size, dtype=jnp.int32)
    causal = key_pos[None, :] <= query_pos[:, None]
    same_doc = seg_block[:, None, :] == query_seg[:, :, None]
    return (causal[None] & same_doc)[:, None, None]


def attend_piece(running, pieces, first_key, queries, query_pos, query_seg, scaling):
    key_rows, value_rows, key_segments = pieces
    sequence_count, key_span = (key_rows.shape[0], key_rows.shape[1])
    block_size = math.gcd(key_span, 512)
    kv_heads, head_dim = (queries.shape[2], queries.shape[4])

    def advance(block_index, carried):
        top_score, denominator, numerator = carried
        offset = block_index * block_size
        key_block = lax.dynamic_slice_in_dim(key_rows, offset, block_size, 1).reshape(
            sequence_count, block_size, kv_heads, head_dim
        )
        value_block = lax.dynamic_slice_in_dim(value_rows, offset, block_size, 1).reshape(
            sequence_count, block_size, kv_heads, head_dim
        )
        seg_block = lax.dynamic_slice_in_dim(key_segments, offset, block_size, 1).astype(jnp.int32)
        allowed = block_mask(offset, block_size, query_pos, query_seg, seg_block)
        scores = (
            jnp.einsum("sqkgd,sjkd->skgqj", queries, key_block, preferred_element_type=jnp.float32)
            * scaling
        )
        fresh_top = jnp.maximum(top_score, jnp.max(jnp.where(allowed, scores, MASKED), axis=-1))
        weights = jnp.where(allowed, jnp.exp(scores - fresh_top[..., None]), 0.0)
        decay_factor = jnp.exp(top_score - fresh_top)
        denominator = denominator * decay_factor + jnp.sum(weights, axis=-1)
        numerator = numerator * decay_factor[..., None] + jnp.einsum(
            "skgqj,sjkd->skgqd",
            weights.astype(jnp.bfloat16),
            value_block,
            preferred_element_type=jnp.float32,
        )
        return (fresh_top, denominator, numerator)

    return lax.fori_loop(0, key_span // block_size, advance, running)


def attend_back(pieces, queries, query_pos, query_seg, grad_attn, log_total, row_delta, scaling):
    key_rows, value_rows, key_segments = pieces
    sequence_count, key_span, key_value_width = key_rows.shape
    block_size = math.gcd(key_span, 512)
    kv_heads, head_dim = (queries.shape[2], queries.shape[4])

    def advance(block_index, carried):
        grad_queries, gradient_couples = carried
        offset = block_index * block_size
        key_block = lax.dynamic_slice_in_dim(key_rows, offset, block_size, 1).reshape(
            sequence_count, block_size, kv_heads, head_dim
        )
        value_block = lax.dynamic_slice_in_dim(value_rows, offset, block_size, 1).reshape(
            sequence_count, block_size, kv_heads, head_dim
        )
        seg_block = lax.dynamic_slice_in_dim(key_segments, offset, block_size, 1).astype(jnp.int32)
        allowed = block_mask(offset, block_size, query_pos, query_seg, seg_block)
        scores = (
            jnp.einsum("sqkgd,sjkd->skgqj", queries, key_block, preferred_element_type=jnp.float32)
            * scaling
        )
        weights = jnp.where(allowed, jnp.exp(scores - log_total[..., None]), 0.0)
        grad_weights = jnp.einsum(
            "sqkgd,sjkd->skgqj", grad_attn, value_block, preferred_element_type=jnp.float32
        )
        grad_scores = (weights * (grad_weights - row_delta[..., None])).astype(jnp.bfloat16)
        grad_queries = grad_queries + jnp.einsum(
            "skgqj,sjkd->sqkgd", grad_scores, key_block, preferred_element_type=jnp.float32
        )
        grad_keys = (
            jnp.einsum(
                "skgqj,sqkgd->sjkd", grad_scores, queries, preferred_element_type=jnp.float32
            )
            * scaling
        )
        grad_values = jnp.einsum(
            "skgqj,sqkgd->sjkd",
            weights.astype(jnp.bfloat16),
            grad_attn,
            preferred_element_type=jnp.float32,
        )
        produced = jnp.concatenate(
            [
                grad_keys.reshape(sequence_count, block_size, key_value_width),
                grad_values.reshape(sequence_count, block_size, key_value_width),
            ],
            axis=-1,
        )
        return (
            grad_queries,
            lax.dynamic_update_slice_in_dim(gradient_couples, produced, offset, 1),
        )

    starting = (
        jnp.zeros(queries.shape, jnp.float32),
        jnp.zeros((sequence_count, key_span, 2 * key_value_width), jnp.float32),
    )
    grad_queries, gradient_couples = lax.fori_loop(0, key_span // block_size, advance, starting)
    return (grad_queries * scaling, gradient_couples)


def project_in(pieces, routed):
    gate_rows, up_rows = pieces
    return (
        jnp.einsum("erd,def->erf", routed, gate_rows, preferred_element_type=jnp.float32),
        jnp.einsum("erd,def->erf", routed, up_rows, preferred_element_type=jnp.float32),
    )


def project_out(down_rows, hidden):
    produced = jnp.einsum("erf,def->erd", hidden, down_rows, preferred_element_type=jnp.float32)
    return produced


def back_through_down(down_rows, grad_output):
    return jnp.einsum("erd,def->erf", grad_output, down_rows, preferred_element_type=jnp.float32)


def back_through_in(pieces, grad_gate, grad_up):
    gate_rows, up_rows = pieces
    produced = jnp.einsum(
        "erf,def->erd", grad_gate, gate_rows, preferred_element_type=jnp.float32
    ) + jnp.einsum("erf,def->erd", grad_up, up_rows, preferred_element_type=jnp.float32)
    return produced


def take_slots(slot_data, destination):
    experts, width = (slot_data.shape[0], slot_data.shape[-1])
    sequence_count, sequence_rows, picks = destination.shape
    flat = jnp.transpose(
        slot_data.reshape(experts, sequence_count, -1, width), (1, 0, 2, 3)
    ).reshape(sequence_count, -1, width)
    taken = jax.vmap(lambda table, spots: table[spots])(
        flat, destination.reshape(sequence_count, sequence_rows * picks)
    )
    return taken.reshape(sequence_count, sequence_rows, picks, width)


def place_slots(values, destination, experts, capacity):
    sequence_count, width = (values.shape[0], values.shape[-1])
    empty = jnp.zeros((sequence_count, experts * capacity, width), values.dtype)
    filled = jax.vmap(lambda table, spots, rows: table.at[spots].set(rows))(
        empty, destination.reshape(sequence_count, -1), values.reshape(sequence_count, -1, width)
    )
    return jnp.transpose(
        filled.reshape(sequence_count, experts, capacity, width), (1, 0, 2, 3)
    ).reshape(experts, sequence_count * capacity, width)


def any_seats(
    tokens,
    attention_gain,
    expert_gain,
    query_weight,
    key_matrix,
    value_matrix,
    output_weight,
    router_weight,
    gate_weight,
    up_weight,
    down_weight,
    routes,
    segments,
    rope_index,
    cotangent,
):
    sequence_count, sequence_rows = (tokens.shape[0], tokens.shape[1])
    queries_per_group = QUERY_HEADS // KEY_VALUE_HEADS
    key_value_width = KEY_VALUE_HEADS * HEAD_SIZE
    scaling = 1.0 / math.sqrt(HEAD_SIZE)
    experts_slots = E * CAP
    gathered = (
        lax.all_gather(attention_gain, ("row", "seq"), axis=0, tiled=True),
        lax.all_gather(expert_gain, ("row", "seq"), axis=0, tiled=True),
        lax.all_gather(query_weight, ("row", "seq"), axis=0, tiled=True),
        lax.all_gather(key_matrix, ("row", "seq"), axis=0, tiled=True),
        lax.all_gather(value_matrix, ("row", "seq"), axis=0, tiled=True),
        lax.all_gather(output_weight, ("row", "seq"), axis=0, tiled=True),
        lax.all_gather(router_weight, ("row", "seq"), axis=0, tiled=True),
    )
    gain_first = gathered[0].astype(jnp.float32)
    gain_second = gathered[1].astype(jnp.float32)
    full_query, full_key, full_value, full_output, full_router = gathered[2:]
    inputs = tokens.astype(jnp.float32)
    scale_first = rms_scale(inputs)
    normed_first = inputs * scale_first
    hidden_first = (normed_first * gain_first).astype(jnp.bfloat16)
    query_unrotated = jnp.einsum(
        "sqd,dc->sqc", hidden_first, full_query, preferred_element_type=jnp.float32
    )
    key_unrotated = jnp.einsum(
        "sqd,dc->sqc", hidden_first, full_key, preferred_element_type=jnp.float32
    )
    value_raw = jnp.einsum(
        "sqd,dc->sqc", hidden_first, full_value, preferred_element_type=jnp.float32
    )
    positions = lax.axis_index("seq") * sequence_rows + jnp.arange(sequence_rows, dtype=jnp.int32)
    factor = jnp.power(2.0, rope_index.astype(jnp.float32))
    angles = (positions.astype(jnp.float32)[None, :] / factor[:, None])[..., None] * frequencies(
        HEAD_SIZE
    )
    cosine_lookup = jnp.cos(angles)[:, :, None, :]
    sine_lookup = jnp.sin(angles)[:, :, None, :]
    query_turned = (
        apply_rotary(
            query_unrotated.reshape(sequence_count, sequence_rows, QUERY_HEADS, HEAD_SIZE),
            cosine_lookup,
            sine_lookup,
        )
        .astype(jnp.bfloat16)
        .reshape(sequence_count, sequence_rows, KEY_VALUE_HEADS, queries_per_group, HEAD_SIZE)
    )
    key_turned = (
        apply_rotary(
            key_unrotated.reshape(sequence_count, sequence_rows, KEY_VALUE_HEADS, HEAD_SIZE),
            cosine_lookup,
            sine_lookup,
        )
        .astype(jnp.bfloat16)
        .reshape(sequence_count, sequence_rows, key_value_width)
    )
    value_reduced = value_raw.astype(jnp.bfloat16)
    segment_low = segments.astype(jnp.float32).astype(jnp.bfloat16)
    statistic_shape = (sequence_count, KEY_VALUE_HEADS, queries_per_group, sequence_rows)
    starting = (
        jnp.full(statistic_shape, MASKED, jnp.float32),
        jnp.zeros(statistic_shape, jnp.float32),
        jnp.zeros(statistic_shape + (HEAD_SIZE,), jnp.float32),
    )
    attend = partial(
        attend_piece, queries=query_turned, query_pos=positions, query_seg=segments, scaling=scaling
    )
    top_score, denominator, numerator = attend(
        starting,
        (
            lax.all_gather(key_turned, "seq", axis=1, tiled=True),
            lax.all_gather(value_reduced, "seq", axis=1, tiled=True),
            lax.all_gather(segment_low, "seq", axis=1, tiled=True),
        ),
        jnp.int32(0),
    )
    attn_heads = numerator / denominator[..., None]
    log_total = top_score + jnp.log(denominator)
    attn_rows = jnp.transpose(attn_heads, (0, 3, 1, 2, 4))
    attn_low = attn_rows.astype(jnp.bfloat16).reshape(
        sequence_count, sequence_rows, QUERY_HEADS * HEAD_SIZE
    )
    branch = jnp.einsum("sqc,dc->sqd", attn_low, full_output, preferred_element_type=jnp.float32)
    residual = inputs + branch
    scale_second = rms_scale(residual)
    normed_second = residual * scale_second
    hidden_second = (normed_second * gain_second).astype(jnp.bfloat16)
    logits = jnp.einsum(
        "sqd,de->sqe", hidden_second, full_router, preferred_element_type=jnp.float32
    )
    router_probs = jax.nn.softmax(logits, axis=-1)
    picked = routes[..., None] == jnp.arange(E, dtype=jnp.int32)
    picked_int = picked.astype(jnp.int32).reshape(sequence_count, sequence_rows * K, E)
    earlier = jnp.cumsum(picked_int, axis=1, dtype=jnp.int32) - picked_int
    slot_ids = jnp.sum(earlier * picked_int, axis=-1, dtype=jnp.int32).reshape(
        sequence_count, sequence_rows, K
    )
    destination = routes * CAP + slot_ids
    chosen = destination[..., None] == jnp.arange(experts_slots, dtype=jnp.int32)
    gate_probs = jnp.sum(jnp.where(picked, router_probs[:, :, None, :], 0.0), axis=-1)
    dispatch = jnp.sum(chosen, axis=2, dtype=jnp.float32).reshape(
        sequence_count, sequence_rows, E, CAP
    )
    slot_rows = sequence_count * CAP
    routed = (
        jnp.einsum(
            "sqec,sqd->escd",
            dispatch.astype(jnp.bfloat16),
            hidden_second,
            preferred_element_type=jnp.float32,
        )
        .astype(jnp.bfloat16)
        .reshape(E, slot_rows, MODEL_WIDTH)
    )
    grad_mixed = cotangent.astype(jnp.float32)
    grad_slot_values = (gate_probs[..., None] * grad_mixed[:, :, None, :]).astype(jnp.bfloat16)
    grad_expert = place_slots(grad_slot_values, destination, E, CAP)
    groups = 4
    width = E // groups

    def some_experts(_, given):
        rows, grads, gate_part, up_part, down_part = given
        pieces = (
            lax.all_gather(gate_part, ("row", "seq"), axis=0, tiled=True),
            lax.all_gather(up_part, ("row", "seq"), axis=0, tiled=True),
        )
        down_rows = lax.all_gather(down_part, ("row", "seq"), axis=0, tiled=True)
        gate_pre, up_pre = project_in(pieces, routed=rows)
        hidden_low = (jax.nn.silu(gate_pre) * up_pre).astype(jnp.bfloat16)
        expert_out = project_out(down_rows, hidden=hidden_low)
        grad_hidden = back_through_down(down_rows, grad_output=grads)
        sigmoid_gate = jax.nn.sigmoid(gate_pre)
        grad_gate = (
            grad_hidden * up_pre * sigmoid_gate * (1.0 + gate_pre * (1.0 - sigmoid_gate))
        ).astype(jnp.bfloat16)
        grad_up = (grad_hidden * (gate_pre * sigmoid_gate)).astype(jnp.bfloat16)
        grad_routed = back_through_in(pieces, grad_gate=grad_gate, grad_up=grad_up)
        made = [
            lax.psum_scatter(
                jnp.einsum("erd,erf->def", left, right, preferred_element_type=jnp.float32),
                ("row", "seq"),
                scatter_dimension=0,
                tiled=True,
            )
            for left, right in ((rows, grad_gate), (rows, grad_up), (grads, hidden_low))
        ]
        return None, (expert_out, grad_routed, *made)

    def grouped(weight):
        return jnp.moveaxis(weight.reshape(weight.shape[0], groups, width, F), 1, 0)

    _, (expert_out, grad_routed, *expert_grads) = lax.scan(
        some_experts,
        None,
        (
            routed.reshape(groups, width, slot_rows, MODEL_WIDTH),
            grad_expert.reshape(groups, width, slot_rows, MODEL_WIDTH),
            grouped(gate_weight),
            grouped(up_weight),
            grouped(down_weight),
        ),
    )
    expert_out = expert_out.reshape(E, slot_rows, MODEL_WIDTH)
    grad_routed = grad_routed.reshape(E, slot_rows, MODEL_WIDTH)
    grad_gate_weight, grad_up_weight, grad_down_weight = [
        jnp.moveaxis(grad, 0, 1).reshape(gate_weight.shape) for grad in expert_grads
    ]
    taken_out = take_slots(expert_out, destination)
    expert_mix = jnp.sum(gate_probs[..., None] * taken_out, axis=2)
    mixed = (residual + expert_mix).astype(jnp.bfloat16)
    grad_gates = jnp.sum(taken_out * grad_mixed[:, :, None, :], axis=-1)
    grad_probs = jnp.sum(jnp.where(picked, grad_gates[..., None], 0.0), axis=2)
    grad_logits = (
        router_probs * (grad_probs - jnp.sum(router_probs * grad_probs, axis=-1, keepdims=True))
    ).astype(jnp.bfloat16)
    grad_second = jnp.sum(take_slots(grad_routed, destination), axis=2) + jnp.einsum(
        "sqe,de->sqd", grad_logits, full_router, preferred_element_type=jnp.float32
    )
    grad_gain_second = jnp.sum(grad_second * normed_second, axis=(0, 1))
    scaled_second = grad_second * gain_second
    grad_residual = grad_mixed + scale_second * (
        scaled_second
        - normed_second * jnp.mean(scaled_second * normed_second, axis=-1, keepdims=True)
    )
    grad_branch = grad_residual.astype(jnp.bfloat16)
    grad_attn = (
        jnp.einsum("sqd,dc->sqc", grad_branch, full_output, preferred_element_type=jnp.float32)
        .astype(jnp.bfloat16)
        .reshape(sequence_count, sequence_rows, KEY_VALUE_HEADS, queries_per_group, HEAD_SIZE)
    )
    row_delta = jnp.transpose(
        jnp.sum(grad_attn.astype(jnp.float32) * attn_rows, axis=-1), (0, 2, 3, 1)
    )
    keys_back = (
        lax.all_gather(key_turned, "seq", axis=1, tiled=True),
        lax.all_gather(value_reduced, "seq", axis=1, tiled=True),
        lax.all_gather(segment_low, "seq", axis=1, tiled=True),
    )
    grad_query_rot, grad_pair_rows = attend_back(
        keys_back, query_turned, positions, segments, grad_attn, log_total, row_delta, scaling
    )
    gradient_couples = lax.psum_scatter(grad_pair_rows, "seq", scatter_dimension=1, tiled=True)
    grad_query = (
        unrotate(
            grad_query_rot.reshape(sequence_count, sequence_rows, QUERY_HEADS, HEAD_SIZE),
            cosine_lookup,
            sine_lookup,
        )
        .astype(jnp.bfloat16)
        .reshape(sequence_count, sequence_rows, QUERY_HEADS * HEAD_SIZE)
    )
    grad_key = (
        unrotate(
            gradient_couples[..., :key_value_width].reshape(
                sequence_count, sequence_rows, KEY_VALUE_HEADS, HEAD_SIZE
            ),
            cosine_lookup,
            sine_lookup,
        )
        .astype(jnp.bfloat16)
        .reshape(sequence_count, sequence_rows, key_value_width)
    )
    grad_value = gradient_couples[..., key_value_width:].astype(jnp.bfloat16)
    grad_first = (
        jnp.einsum("sqc,dc->sqd", grad_query, full_query, preferred_element_type=jnp.float32)
        + jnp.einsum("sqc,dc->sqd", grad_key, full_key, preferred_element_type=jnp.float32)
        + jnp.einsum("sqc,dc->sqd", grad_value, full_value, preferred_element_type=jnp.float32)
    )
    grad_gain_first = jnp.sum(grad_first * normed_first, axis=(0, 1))
    scaled_first = grad_first * gain_first
    grad_tokens = grad_residual + scale_first * (
        scaled_first - normed_first * jnp.mean(scaled_first * normed_first, axis=-1, keepdims=True)
    )
    attention_grads = lax.psum_scatter(
        jnp.concatenate(
            [
                jnp.einsum(
                    "sqd,sqc->dc", hidden_first, grad_query, preferred_element_type=jnp.float32
                ),
                jnp.einsum(
                    "sqd,sqc->dc", hidden_first, grad_key, preferred_element_type=jnp.float32
                ),
                jnp.einsum(
                    "sqd,sqc->dc", hidden_first, grad_value, preferred_element_type=jnp.float32
                ),
                jnp.einsum(
                    "sqd,sqc->dc", grad_branch, attn_low, preferred_element_type=jnp.float32
                ),
                jnp.einsum(
                    "sqd,sqe->de", hidden_second, grad_logits, preferred_element_type=jnp.float32
                ),
                grad_gain_first[:, None],
                grad_gain_second[:, None],
            ],
            axis=1,
        ),
        ("row", "seq"),
        scatter_dimension=0,
        tiled=True,
    )
    query_cols = QUERY_HEADS * HEAD_SIZE
    edge_two = query_cols + key_value_width
    edge_three = edge_two + key_value_width
    edge_four = edge_three + query_cols
    edge_five = edge_four + E
    return (
        mixed,
        grad_tokens,
        attention_grads[:, edge_five],
        attention_grads[:, edge_five + 1],
        attention_grads[:, :query_cols],
        attention_grads[:, query_cols:edge_two],
        attention_grads[:, edge_two:edge_three],
        attention_grads[:, edge_three:edge_four],
        attention_grads[:, edge_four:edge_five],
        grad_gate_weight,
        grad_up_weight,
        grad_down_weight,
    )


def solution(mesh):
    first = P(("row", "seq"))
    in_specs = (
        (P("row", "seq", None), first, first)
        + (P(("row", "seq"), None),) * 5
        + (P(("row", "seq"), None, None),) * 3
        + (P("row", "seq", None), P("row", "seq"), P("row"), P("row", "seq", None))
    )
    out_specs = (
        (P("row", "seq", None), P("row", "seq", None), first, first)
        + (P(("row", "seq"), None),) * 5
        + (P(("row", "seq"), None, None),) * 3
    )
    body = sixteen_seats if dict(mesh.shape) == {"row": 2, "seq": 16} else any_seats
    return jax.shard_map(body, mesh=mesh, in_specs=in_specs, out_specs=out_specs, check_vma=False)
```
